32 devices in a mesh: dp: 8 (over z, x), seq: 4 (over y, core).
Axes of the slice: x: 2, y: 2, z: 4, core: 2. Of those that a mesh axis runs over, the one named last changes fastest.
Arguments:
- tokens: bfloat16 [8, 8192, 768], P('dp', 'seq'), may hold values from -6 to 6
- cotangent: bfloat16 [8, 8192, 768], P('dp', 'seq'), may hold values from -6 to 6
- norm_gain: bfloat16 [768], P(('dp', 'seq')), may hold values from 0.5 to 1.5
- in_weight: bfloat16 [768, 3352], P(('dp', 'seq')), may hold values from -0.21875 to 0.21875
- conv_weight: bfloat16 [1792, 4], P(('dp', 'seq')), may hold values from -3 to 3
- conv_bias: bfloat16 [1792], P(('dp', 'seq')), may hold values from -3 to 3
- step_bias: float32 [24], replicated, may hold values from -9 to -4
- decay_log: float32 [24], replicated, may hold values from 0 to 1.5
- skip_gain: float32 [24], replicated, may hold values from 0.5 to 1.5
- gate_gain: bfloat16 [1536], P(('dp', 'seq')), may hold values from 0.5 to 1.5
- out_weight: bfloat16 [1536, 768], P(('dp', 'seq')), may hold values from -0.15625 to 0.15625
Outputs:
- mixed: bfloat16 [8, 8192, 768], P('dp', 'seq')
- tokens_grad: bfloat16 [8, 8192, 768], P('dp', 'seq')
- norm_gain_grad: float32 [768], P(('dp', 'seq'))
- in_weight_grad: float32 [768, 3352], P(('dp', 'seq'))
- conv_weight_grad: float32 [1792, 4], P(('dp', 'seq'))
- conv_bias_grad: float32 [1792], P(('dp', 'seq'))
- step_bias_grad: float32 [24], replicated
- decay_log_grad: float32 [24], replicated
- skip_gain_grad: float32 [24], replicated
- gate_gain_grad: float32 [1536], P(('dp', 'seq'))
- out_weight_grad: float32 [1536, 768], P(('dp', 'seq'))
The draws below stay inside these ranges and needn't reach their ends.
All inputs are finite; a program needn't handle non-finite values.
Results may differ from the reference program's by a relative error of at most 0.012.
Values may be sent and summed in bfloat16 or wider, within the bound.
A program may use at most 384 MiB of HBM per device.

```python
import jax
import jax.numpy as jnp
from jax import lax

D = 768
HEADS = 24
HEADDIM = 64
NSTATE = 128
CONV = 4
BLOCK = 128
D_INNER = 1536
CHANNELS = 1792
PROJ = 3352
LENGTH = 8192
SEQS = 8


def shard_levels(stream_key, extent, shards, low, largest):
    def one(axis_at, blocks):
        draws = jax.random.uniform(jax.random.fold_in(jax.random.fold_in(stream_key, 6), axis_at), (blocks,), jnp.float32, low / len(shards), largest / len(shards))
        return jnp.repeat(jnp.exp(draws), extent[axis_at] // blocks).reshape((-1,) + (1,) * (len(extent) - axis_at - 1))

    level = one(*shards[0])
    for cut in shards[1:]:
        level = level * one(*cut)
    return level


def scatter_about(stream_key, dims, spread, bound, cuts=(), dtype=jnp.bfloat16):
    entries = spread * jax.random.normal(stream_key, dims, jnp.float32)
    if cuts:
        entries = entries * shard_levels(stream_key, dims, cuts, -0.22, 0.18)
    return jnp.clip(entries, -bound, bound).astype(dtype)


def setup_inputs(seed: int = 0) -> dict:
    key_list = jax.random.split(jax.random.key(seed), 12)
    tokens = scatter_about(key_list[0], (SEQS, LENGTH, D), 1.0, 6.0, ((0, 8), (1, 4)))
    cotangent = scatter_about(key_list[1], (SEQS, LENGTH, D), 1.0, 6.0, ((0, 8), (1, 4)))
    norm_gain = jnp.clip(1.0 + 0.1 * jax.random.normal(key_list[2], (D,), jnp.float32), 0.5, 1.5).astype(jnp.bfloat16)
    in_weight = scatter_about(key_list[3], (D, PROJ), D ** -0.5, 0.21875, ((0, 32),))
    conv_weight = scatter_about(key_list[4], (CHANNELS, CONV), CONV ** -0.5, 3.0, ((0, 32),))
    conv_bias = scatter_about(key_list[5], (CHANNELS,), 0.5, 3.0, ((0, 32),))
    step_bias = jnp.clip(jax.random.uniform(key_list[6], (HEADS,), jnp.float32, -9.0, -4.0), -9.0, -4.0)
    decay_log = jnp.clip(jax.random.uniform(key_list[7], (HEADS,), jnp.float32, 0.0, 1.5), 0.0, 1.5)
    skip_gain = jnp.clip(jax.random.uniform(key_list[8], (HEADS,), jnp.float32, 0.5, 1.5), 0.5, 1.5)
    gate_gain = jnp.clip(1.0 + 0.1 * jax.random.normal(key_list[9], (D_INNER,), jnp.float32), 0.5, 1.5).astype(jnp.bfloat16)
    out_weight = scatter_about(key_list[10], (D_INNER, D), D_INNER ** -0.5, 0.15625, ((0, 32),))
    return dict(tokens=tokens, cotangent=cotangent, norm_gain=norm_gain, in_weight=in_weight, conv_weight=conv_weight, conv_bias=conv_bias, step_bias=step_bias, decay_log=decay_log, skip_gain=skip_gain, gate_gain=gate_gain, out_weight=out_weight)


EPSILON = 1e-05
HIGHEST = lax.Precision.HIGHEST

@jax.custom_vjp
def low(v):
    return lax.optimization_barrier(v.astype(jnp.bfloat16)).astype(jnp.float32)

@jax.custom_vjp
def low_back(v):
    return v

def low_keep(v):
    return (low(v), None)

def low_pass(kept, grad):
    return (grad,)

def back_keep(v):
    return (v, None)

def back_low(kept, grad):
    return (low(grad),)
low.defvjp(low_keep, low_pass)
low_back.defvjp(back_keep, back_low)

def norm_input(tok_rows, gain_vec):
    inv_scale = lax.rsqrt(lax.optimization_barrier(jnp.mean(tok_rows * tok_rows, axis=-1, keepdims=True)) + EPSILON)
    return tok_rows * inv_scale * gain_vec

def conv_apply(extended, weight, bias_vec):
    seq_len = extended.shape[0] - weight.shape[1] + 1
    total_sum = bias_vec
    for offset in range(weight.shape[1]):
        total_sum = total_sum + extended[offset:offset + seq_len] * weight[:, offset]
    return jax.nn.silu(total_sum)

def make_steps(raw_steps, step_bias, decay_log):
    step_vals = jax.nn.softplus(raw_steps + step_bias)
    cumulative = jnp.cumsum(step_vals * -jnp.exp(decay_log), axis=1)
    return (step_vals, cumulative)

def causal_decay(cumulative):
    across = jnp.swapaxes(cumulative, 1, 2)
    gap_log = across[:, :, :, None] - across[:, :, None, :]
    span_len = cumulative.shape[1]
    lower_mask = lax.broadcasted_iota(jnp.int32, (span_len, span_len), 0) >= lax.broadcasted_iota(jnp.int32, (span_len, span_len), 1)
    return jnp.exp(jnp.where(lower_mask, gap_log, -jnp.inf))

def score_terms(inner_prod, step_vals, cumulative):
    return inner_prod[:, None] * causal_decay(cumulative) * jnp.swapaxes(step_vals, 1, 2)[:, :, None, :]

def weight_terms(values, step_vals, cumulative):
    return values * (jnp.exp(cumulative[:, -1:, :] - cumulative) * step_vals)[..., None]

def gated_norm(mixed_in, gate_in, gain_vec):
    gated = mixed_in * jax.nn.silu(gate_in)
    inv_scale = lax.rsqrt(lax.optimization_barrier(jnp.mean(gated * gated, axis=-1, keepdims=True)) + EPSILON)
    return gated * inv_scale * gain_vec

def sequence(params, tok_rows):
    norm_gain, in_weight, conv_weight, conv_bias, step_bias, decay_log, skip_gain, gate_gain, out_weight = params
    seq_len = tok_rows.shape[0]
    block_count = seq_len // BLOCK
    normed = low(norm_input(tok_rows, norm_gain))
    projected = low(low_back(jnp.dot(normed, in_weight, precision=HIGHEST)))
    gate_rows = projected[:, :D_INNER]
    conv_in = projected[:, D_INNER:D_INNER + CHANNELS]
    raw_steps = projected[:, D_INNER + CHANNELS:].reshape(block_count, BLOCK, HEADS)
    extended = jnp.concatenate([jnp.zeros((CONV - 1, CHANNELS), jnp.float32), conv_in], axis=0)
    activated = low(conv_apply(extended, conv_weight, conv_bias))
    values = activated[:, :D_INNER].reshape(block_count, BLOCK, HEADS, HEADDIM)
    write_mat = activated[:, D_INNER:D_INNER + NSTATE].reshape(block_count, BLOCK, NSTATE)
    read_mat = activated[:, D_INNER + NSTATE:].reshape(block_count, BLOCK, NSTATE)
    step_vals, cumulative = make_steps(raw_steps, step_bias, decay_log)
    inner_prod = low_back(jnp.einsum('btn,bsn->bts', read_mat, write_mat, precision=HIGHEST))
    scores = low(score_terms(inner_prod, step_vals, cumulative))
    diagonal = jnp.einsum('bhts,bshp->bthp', scores, values, precision=HIGHEST)
    weighted = low(weight_terms(values, step_vals, cumulative))
    block_states = low_back(jnp.einsum('bshp,bsn->bhpn', weighted, write_mat, precision=HIGHEST))

    def advance(state_now, pieces):
        decay_now, update = pieces
        return (jnp.exp(decay_now)[:, None, None] * state_now + update, state_now)
    start_state = jnp.zeros((HEADS, HEADDIM, NSTATE), jnp.float32)
    _, entering = lax.scan(advance, start_state, (cumulative[:, -1, :], block_states))
    read_out = low_back(jnp.einsum('btn,bhpn->bthp', read_mat, low(entering), precision=HIGHEST))
    mixed_sum = low_back(diagonal + jnp.exp(cumulative)[..., None] * read_out + skip_gain[:, None] * values)
    normed_out = low(gated_norm(mixed_sum.reshape(seq_len, D_INNER), gate_rows, gate_gain))
    return tok_rows + jnp.dot(normed_out, out_weight, precision=HIGHEST)

def reference(tokens, cotangent, norm_gain, in_weight, conv_weight, conv_bias, step_bias, decay_log, skip_gain, gate_gain, out_weight):
    params = tuple((member.astype(jnp.float32) for member in (norm_gain, in_weight, conv_weight, conv_bias, step_bias, decay_log, skip_gain, gate_gain, out_weight)))
    tok_rows = tokens.astype(jnp.float32)

    def forward(params_in, all_rows):
        return lax.map(lambda single: jax.checkpoint(sequence)(params_in, single), all_rows)
    result, pullback = jax.vjp(forward, params, tok_rows)
    param_grads, rows_grad = pullback(cotangent.astype(jnp.float32))
    return (result.astype(jnp.bfloat16), rows_grad.astype(jnp.bfloat16), param_grads[0], param_grads[1], param_grads[2], param_grads[3], param_grads[4], param_grads[5], param_grads[6], param_grads[7], param_grads[8])
```

```python
import functools

import jax
import jax.numpy as jnp
import numpy as np
from jax import lax
from jax.experimental import pallas as pl
from jax.experimental.pallas import tpu as pltpu
from jax.sharding import PartitionSpec as P

D = 768
HEADS = 24
HEADDIM = 64
NSTATE = 128
CONV = 4
BLOCK = 128
DI = 1536
CH = 1792
PAIRS = HEADS // 2
EPS = 1e-05
LOG2E = 1.4426950408889634
F32 = jnp.float32
BF16 = jnp.bfloat16
NT = (((1,), (1,)), ((), ()))
VMEM_LIMIT = 60 * 1024 * 1024


def dot(a, b):
    return jnp.dot(a, b, preferred_element_type=F32)


def dot_nt(a, b):
    return lax.dot_general(a, b, NT, preferred_element_type=F32)


def dot_exact(a, b):
    return jnp.dot(a, b, preferred_element_type=F32, precision=lax.Precision.HIGHEST)


def sigmoid(v):
    return 0.5 * jnp.tanh(0.5 * v) + 0.5


def iota(shape, dim):
    return lax.broadcasted_iota(jnp.int32, shape, dim)


def lane_lo():
    return iota((BLOCK, BLOCK), 1) < HEADDIM


def expand_pair(x, j, lo):
    rows = x.shape[0]
    a = jnp.broadcast_to(x[:, 2 * j : 2 * j + 1], (rows, BLOCK))
    b = jnp.broadcast_to(x[:, 2 * j + 1 : 2 * j + 2], (rows, BLOCK))
    return jnp.where(lo, a, b), a, b


def block_diag(v):
    lo = iota(v.shape, 1) < HEADDIM
    zero = jnp.zeros_like(v)
    return jnp.concatenate([jnp.where(lo, v, zero), jnp.where(lo, zero, v)], axis=0)


def pair(j):
    return slice(j * BLOCK, (j + 1) * BLOCK)


def rms_rows(tok, gain):
    x = tok.astype(F32)
    inv = lax.rsqrt(jnp.mean(x * x, axis=-1, keepdims=True) + EPS)
    return (x * inv * gain).astype(BF16)


def first_kernel(
    T, tok_ref, halo_ref, wc_ref, gain_ref, conv_ref, head_ref,
    normed_ref, convin_ref, act_ref, dt_ref, cum_ref, sig_ref, bst_ref, leave_ref, tot_ref,
    ext, state, weighted,
):
    i = pl.program_id(0)

    @pl.when(i == 0)
    def _():
        hn = rms_rows(halo_ref[...], gain_ref[...])
        hp = dot(hn, wc_ref[:, :CH]).astype(BF16).astype(F32)
        ext[0:8] = hp[8:16]
        state[...] = jnp.zeros_like(state)
        tot_ref[...] = jnp.zeros_like(tot_ref)

    @pl.when(i > 0)
    def _():
        ext[0:8] = ext[T : T + 8]

    normed = rms_rows(tok_ref[...], gain_ref[...])
    normed_ref[...] = normed
    for c in range(CH // 256):
        cs = slice(c * 256, (c + 1) * 256)
        p = dot(normed, wc_ref[:, cs]).astype(BF16)
        convin_ref[:, cs] = p
        ext[8 : 8 + T, cs] = p.astype(F32)
        total = conv_ref[4:5, cs]
        for k in range(CONV):
            total = total + ext[5 + k : 5 + k + T, cs] * conv_ref[k : k + 1, cs]
        act_ref[:, cs] = (total * sigmoid(total)).astype(BF16)
    raw = dot(normed, wc_ref[:, CH:]).astype(BF16).astype(F32) + head_ref[0:1]
    dt_all = jnp.maximum(raw, 0.0) + jnp.log1p(jnp.exp(-jnp.abs(raw)))
    dt_ref[...] = dt_all
    sig_ref[...] = sigmoid_exact(raw)
    tril = (iota((BLOCK, BLOCK), 0) >= iota((BLOCK, BLOCK), 1)).astype(F32)
    lo = lane_lo()
    for blk in range(T // BLOCK):
        rows = slice(blk * BLOCK, (blk + 1) * BLOCK)
        dt = dt_all[rows]
        cum = dot_exact(tril, dt * head_ref[1:2]) * LOG2E
        cum_ref[rows] = cum
        end = cum[BLOCK - 1 : BLOCK]
        tot_ref[...] += jnp.broadcast_to(end, tot_ref.shape)
        wfac = jnp.exp2(end - cum) * dt
        decay = jnp.broadcast_to(jnp.exp2(end), (8, BLOCK))
        write_t = act_ref[rows, DI : DI + NSTATE].T
        for j in range(PAIRS):
            w, _, _ = expand_pair(wfac, j, lo)
            weighted[:, pair(j)] = (act_ref[rows, pair(j)].astype(F32) * w).astype(BF16)
        for q in range(PAIRS // 2):
            cs = slice(q * 256, (q + 1) * 256)
            new = dot(write_t, weighted[:, cs])
            bst_ref[blk, :, cs] = new.astype(BF16)
            d0, _, _ = expand_pair(decay, 2 * q, lo[:8])
            d1, _, _ = expand_pair(decay, 2 * q + 1, lo[:8])
            dd = jnp.concatenate([d0, d1], axis=1)[0:1]
            state[:, cs] = state[:, cs] * dd + new

    @pl.when(i == pl.num_programs(0) - 1)
    def _():
        leave_ref[...] = state[...]


def sigmoid_exact(v):
    return 1.0 / (1.0 + jnp.exp(-v))


def second_kernel(
    T, normed_ref, act_ref, dt_ref, cum_ref, bst_ref, inc_ref, tok_ref, cot_ref, wg_ref, wo_ref, row_ref, et_ref,
    mixed_ref, nout_ref, ggrad_ref, mlow_ref, dcum_ref, ent_ref, egrad_ref, rg_ref, leave_ref, back_ref, cols_ref,
    gate_s, ng, ms, growth, rlow, prod, plow, state, exg, lows,
):
    i = pl.program_id(0)

    @pl.when(i == 0)
    def _():
        state[...] = inc_ref[...]
        exg[...] = jnp.ones_like(exg)
        back_ref[...] = jnp.zeros_like(back_ref)
        cols_ref[...] = jnp.zeros_like(cols_ref)

    lo = lane_lo()
    for c in range(DI // 256):
        cs = slice(c * 256, (c + 1) * 256)
        gate_s[:, cs] = dot(normed_ref[...], wg_ref[:, cs]).astype(BF16)
        ng[:, cs] = dot_nt(cot_ref[...], wo_ref[cs, :])
    lower = iota((BLOCK, BLOCK), 0) >= iota((BLOCK, BLOCK), 1)
    nblk = T // BLOCK
    for blk in range(nblk):
        rows = slice(blk * BLOCK, (blk + 1) * BLOCK)
        cum = cum_ref[rows]
        cum_t = cum.T
        dt = dt_ref[rows]
        write = act_ref[rows, DI : DI + NSTATE]
        read = act_ref[rows, DI + NSTATE :]
        inner = jnp.where(lower, dot_nt(read, write), 0.0)
        lows[blk] = state[...].astype(BF16)
        ent_ref[blk] = lows[blk]
        for j in range(PAIRS):
            cols, a, b = expand_pair(cum, j, lo)
            ga = jnp.exp2(jnp.minimum(a - cum_t[2 * j : 2 * j + 1], 0.0)) * inner
            gb = jnp.exp2(jnp.minimum(b - cum_t[2 * j + 1 : 2 * j + 2], 0.0)) * inner
            scores = jnp.concatenate([ga.astype(BF16), gb.astype(BF16)], axis=1)
            vals = act_ref[rows, pair(j)].astype(F32)
            dtp, _, _ = expand_pair(dt, j, lo)
            vdt = (vals * dtp).astype(BF16)
            grow = jnp.exp2(cols)
            growth[rows, pair(j)] = grow
            diag = dot(scores, block_diag(vdt))
            out = dot(read, lows[blk, :, pair(j)])
            ms[rows, pair(j)] = diag + grow * out + row_ref[1:2, pair(j)] * vals
            dec = grow[BLOCK - 1 : BLOCK]
            state[:, pair(j)] = state[:, pair(j)] * dec + bst_ref[blk, :, pair(j)].astype(F32)

    sq = jnp.zeros((T, BLOCK), F32)
    ug = jnp.zeros((T, BLOCK), F32)
    for j in range(PAIRS):
        g = gate_s[:, pair(j)].astype(F32)
        gated = ms[:, pair(j)] * (g * sigmoid(g))
        sq = sq + gated * gated
        ug = ug + gated * (ng[:, pair(j)] * row_ref[0:1, pair(j)])
    inv = lax.rsqrt(jnp.sum(sq, axis=-1, keepdims=True) * (1.0 / DI) + EPS)
    coef = jnp.sum(ug, axis=-1, keepdims=True) * (1.0 / DI) * (inv * inv * inv)
    for j in range(PAIRS):
        g = gate_s[:, pair(j)].astype(F32)
        sg = sigmoid(g)
        silu = g * sg
        m = ms[:, pair(j)]
        gated = m * silu
        n = ng[:, pair(j)]
        gain = row_ref[0:1, pair(j)]
        gi = gated * inv
        nout_ref[:, pair(j)] = (gi * gain).astype(BF16)
        dg = inv * (n * gain) - gated * coef
        low = (dg * silu).astype(BF16)
        mlow_ref[:, pair(j)] = low
        ggrad_ref[:, pair(j)] = (dg * m * (sg + silu * (1.0 - sg))).astype(BF16)
        vals = act_ref[:, pair(j)].astype(F32)
        lowf = low.astype(F32)
        mv = lowf * vals
        pr = lowf * m - row_ref[1:2, pair(j)] * mv
        hi = pr.astype(BF16)
        prod[:, pair(j)] = hi
        plow[:, pair(j)] = (pr - hi.astype(F32)).astype(BF16)
        rlow[:, pair(j)] = (lowf * growth[:, pair(j)]).astype(BF16)
        cols_ref[0:8, pair(j)] += jnp.sum((n * gi).reshape(T // 8, 8, BLOCK), axis=0)
        cols_ref[8:16, pair(j)] += jnp.sum(mv.reshape(T // 8, 8, BLOCK), axis=0)
    dcum_ref[...] = dot(prod[...], et_ref[...]) + dot(plow[...], et_ref[...])
    mixed_ref[...] = (tok_ref[...].astype(F32) + dot(nout_ref[...], wo_ref[...])).astype(BF16)
    for blk in range(nblk):
        rows = slice(blk * BLOCK, (blk + 1) * BLOCK)
        read_t = act_ref[rows, DI + NSTATE :].T
        for q in range(PAIRS // 2):
            cs = slice(q * 256, (q + 1) * 256)
            eg = dot(read_t, rlow[rows, cs])
            egrad_ref[blk, :, cs] = eg.astype(BF16)
            back_ref[:, cs] += eg * exg[0:1, cs]
        exg[...] = exg[...] * growth[blk * BLOCK + BLOCK - 1 : blk * BLOCK + BLOCK, :]
        rg_ref[rows] = dot_nt(rlow[rows, :], lows[blk])

    @pl.when(i == pl.num_programs(0) - 1)
    def _():
        leave_ref[...] = state[...].astype(BF16)


def third_kernel(
    T, act_ref, convin_ref, prev_ref, halo_ref, dt_ref, cum_ref, sig_ref, dcum_ref, mlow_ref, ent_ref, leave_ref,
    egrad_ref, rg_ref, inc_ref, row_ref, conv_ref, head_ref, et_ref,
    pg_ref, raw_ref, cgrad_ref, hgrad_ref, gfirst_ref, glast_ref,
    carry, dact, vprod, prod, plow, weighted, lows, dec, nxt, gext, cext,
):
    i = pl.program_id(0)
    steps = pl.num_programs(0)

    @pl.when(i == 0)
    def _():
        carry[...] = inc_ref[...]
        nxt[...] = leave_ref[...]
        cgrad_ref[...] = jnp.zeros_like(cgrad_ref)
        hgrad_ref[...] = jnp.zeros_like(hgrad_ref)
        gext[T : T + 8] = jnp.zeros((8, CH), F32)

    @pl.when(i > 0)
    def _():
        gext[T : T + 8] = gext[0:8]

    @pl.when(i == steps - 1)
    def _():
        cext[0:16] = halo_ref[...].astype(F32)

    @pl.when(i < steps - 1)
    def _():
        cext[0:16] = prev_ref[...].astype(F32)

    lo = lane_lo()
    upper = iota((BLOCK, BLOCK), 0) <= iota((BLOCK, BLOCK), 1)
    triu = upper.astype(F32)
    last = iota((BLOCK, BLOCK), 0) == BLOCK - 1
    for blk in reversed(range(T // BLOCK)):
        rows = slice(blk * BLOCK, (blk + 1) * BLOCK)
        cum = cum_ref[rows]
        cum_t = cum.T
        dt = dt_ref[rows]
        end = cum[BLOCK - 1 : BLOCK]
        rest = end - cum
        write = act_ref[rows, DI : DI + NSTATE]
        read = act_ref[rows, DI + NSTATE :]
        inner = jnp.where(upper, dot_nt(write, read), 0.0)
        lows[...] = carry[...].astype(BF16)
        acc = jnp.zeros((BLOCK, BLOCK), F32)
        for j in range(PAIRS):
            cols, a, b = expand_pair(cum, j, lo)
            wexp, _, _ = expand_pair(rest, j, lo)
            wexp = jnp.exp2(wexp)
            da = jnp.exp2(jnp.minimum(cum_t[2 * j : 2 * j + 1] - a, 0.0))
            db = jnp.exp2(jnp.minimum(cum_t[2 * j + 1 : 2 * j + 2] - b, 0.0))
            scores = jnp.concatenate([(da * inner).astype(BF16), (db * inner).astype(BF16)], axis=1)
            m = mlow_ref[rows, pair(j)]
            diag = block_diag(m)
            z = dot(scores, diag)
            vals = act_ref[rows, pair(j)].astype(F32)
            dtp, _, _ = expand_pair(dt, j, lo)
            vdt = vals * dtp
            vdtb = vdt.astype(BF16)
            wtb = (vdt * wexp).astype(BF16)
            g = dot_nt(vdtb, diag)
            acc = acc + g[:, :BLOCK] * da + g[:, BLOCK:] * db
            wg = dot(write, lows[:, pair(j)])
            pr = vdtb.astype(F32) * z + wtb.astype(F32) * wg
            z = z + wg * wexp
            dact[rows, pair(j)] = row_ref[1:2, pair(j)] * m.astype(F32) + dtp * z
            vprod[:, pair(j)] = (vals * z).astype(BF16)
            hi = pr.astype(BF16)
            prod[:, pair(j)] = hi
            plow[:, pair(j)] = (pr - hi.astype(F32)).astype(BF16)
            weighted[:, pair(j)] = wtb
            dec[0:1, pair(j)] = jnp.exp2(cols[BLOCK - 1 : BLOCK])
        low = jnp.where(upper, acc, 0.0).astype(BF16)
        dact[rows, DI : DI + NSTATE] = dot_nt(weighted[...], lows[...]) + dot(low, read)
        dact[rows, DI + NSTATE :] = rg_ref[rows] + dot(low.T, write)
        c = dot(vprod[...], et_ref[...])
        used = dot(prod[...], et_ref[...]) + dot(plow[...], et_ref[...])
        ends = jnp.sum((lows[...].astype(F32) * nxt[...].astype(F32)).reshape(16, 8, DI), axis=0)
        ends_hi = ends.astype(BF16)
        ends_lo = (ends - ends_hi.astype(F32)).astype(BF16)
        de = jnp.sum(dot(ends_hi, et_ref[...]) + dot(ends_lo, et_ref[...]), axis=0, keepdims=True)
        dc = dcum_ref[rows] - used + jnp.where(last, de, 0.0)
        da_log = dot_exact(triu, dc)
        draw = (c + da_log * head_ref[1:2]) * sig_ref[rows]
        raw_ref[rows] = draw.astype(BF16)
        hgrad_ref[0:8] += jnp.sum(draw.reshape(16, 8, BLOCK), axis=0)
        hgrad_ref[8:16] += jnp.sum((da_log * dt).reshape(16, 8, BLOCK), axis=0) * head_ref[1:2]
        nxt[...] = ent_ref[blk]
        for q in range(PAIRS // 2):
            cs = slice(q * 256, (q + 1) * 256)
            carry[:, cs] = carry[:, cs] * dec[0:1, cs] + egrad_ref[blk, :, cs].astype(F32)

    for c in range(CH // 128):
        cs = slice(c * 128, (c + 1) * 128)
        cext[16 : 16 + T, cs] = convin_ref[:, cs].astype(F32)
        taps = [cext[13 + k : 13 + k + T, cs] for k in range(CONV)]
        pre = conv_ref[4:5, cs]
        for k in range(CONV):
            pre = pre + taps[k] * conv_ref[k : k + 1, cs]
        sg = sigmoid(pre)
        g = dact[:, cs] * (sg * (1.0 + pre * (1.0 - sg)))
        gext[0:T, cs] = g
        for k in range(CONV):
            cgrad_ref[8 * k : 8 * k + 8, cs] += jnp.sum((g * taps[k]).reshape(T // 8, 8, BLOCK), axis=0)
        cgrad_ref[32:40, cs] += jnp.sum(g.reshape(T // 8, 8, BLOCK), axis=0)
        back = g * conv_ref[3:4, cs]
        for k in range(CONV - 1):
            back = back + gext[3 - k : 3 - k + T, cs] * conv_ref[k : k + 1, cs]
        pg_ref[:, cs] = back.astype(BF16)

        @pl.when(i == 0)
        def _():
            glast_ref[:, cs] = back[T - 8 :]

    @pl.when(i == steps - 1)
    def _():
        gfirst_ref[...] = gext[0:8]


def full(shape):
    return pl.BlockSpec(shape, lambda i: (0,) * len(shape))


def params():
    return pltpu.CompilerParams(dimension_semantics=("arbitrary",), vmem_limit_bytes=VMEM_LIMIT)


def head_columns():
    et = np.zeros((DI, BLOCK), np.float32)
    et[np.arange(DI), np.arange(DI) // HEADDIM] = 1.0
    return et


def sds(shape, dtype):
    return jax.ShapeDtypeStruct(shape, dtype)


def first_pass(tok, halo, wc, gain, conv, head, T=256):
    L = tok.shape[0]
    nb, per = L // BLOCK, T // BLOCK
    row = lambda w: pl.BlockSpec((T, w), lambda i: (i, 0))
    return pl.pallas_call(
        functools.partial(first_kernel, T),
        grid=(L // T,),
        in_specs=[row(D), full((16, D)), full((D, CH + BLOCK)), full((1, D)), full((8, CH)), full((8, BLOCK))],
        out_specs=[
            row(D), row(CH), row(CH), row(BLOCK), row(BLOCK), row(BLOCK),
            pl.BlockSpec((per, NSTATE, DI), lambda i: (i, 0, 0)), full((NSTATE, DI)), full((8, BLOCK)),
        ],
        out_shape=[
            sds((L, D), BF16), sds((L, CH), BF16), sds((L, CH), BF16), sds((L, BLOCK), F32), sds((L, BLOCK), F32),
            sds((L, BLOCK), F32), sds((nb, NSTATE, DI), BF16), sds((NSTATE, DI), F32), sds((8, BLOCK), F32),
        ],
        scratch_shapes=[
            pltpu.VMEM((T + 8, CH), F32), pltpu.VMEM((NSTATE, DI), F32), pltpu.VMEM((BLOCK, DI), BF16),
        ],
        compiler_params=params(),
        name="first_pass",
    )(tok, halo, wc, gain, conv, head)


def second_pass(normed, act, dt, cum, bst, inc, tok, cot, wg, wo, rows, et, T=256):
    L = tok.shape[0]
    nb, per = L // BLOCK, T // BLOCK
    row = lambda w: pl.BlockSpec((T, w), lambda i: (i, 0))
    blk = pl.BlockSpec((per, NSTATE, DI), lambda i: (i, 0, 0))
    return pl.pallas_call(
        functools.partial(second_kernel, T),
        grid=(L // T,),
        in_specs=[
            row(D), row(CH), row(BLOCK), row(BLOCK), blk, full((NSTATE, DI)), row(D), row(D), full((D, DI)),
            full((DI, D)), full((8, DI)), full((DI, BLOCK)),
        ],
        out_specs=[
            row(D), row(DI), row(DI), row(DI), row(BLOCK), blk, blk, row(BLOCK), full((NSTATE, DI)),
            full((NSTATE, DI)), full((16, DI)),
        ],
        out_shape=[
            sds((L, D), BF16), sds((L, DI), BF16), sds((L, DI), BF16), sds((L, DI), BF16), sds((L, BLOCK), F32),
            sds((nb, NSTATE, DI), BF16), sds((nb, NSTATE, DI), BF16), sds((L, BLOCK), F32), sds((NSTATE, DI), BF16),
            sds((NSTATE, DI), F32), sds((16, DI), F32),
        ],
        scratch_shapes=[
            pltpu.VMEM((T, DI), BF16), pltpu.VMEM((T, DI), F32), pltpu.VMEM((T, DI), F32), pltpu.VMEM((T, DI), F32),
            pltpu.VMEM((T, DI), BF16), pltpu.VMEM((T, DI), BF16), pltpu.VMEM((T, DI), BF16), pltpu.VMEM((NSTATE, DI), F32),
            pltpu.VMEM((8, DI), F32), pltpu.VMEM((per, NSTATE, DI), BF16),
        ],
        compiler_params=params(),
        name="second_pass",
    )(normed, act, dt, cum, bst, inc, tok, cot, wg, wo, rows, et)


def third_pass(act, convin, halo, dt, cum, sig, dcum, mlow, ent, leave, egrad, rg, inc, rows, conv, head, et, T=256):
    L = act.shape[0]
    n, per = L // T, T // BLOCK
    row = lambda w: pl.BlockSpec((T, w), lambda i: (n - 1 - i, 0))
    blk = pl.BlockSpec((per, NSTATE, DI), lambda i: (n - 1 - i, 0, 0))
    prev = pl.BlockSpec((16, CH), lambda i: (jnp.maximum((n - 1 - i) * (T // 16) - 1, 0), 0))
    return pl.pallas_call(
        functools.partial(third_kernel, T),
        grid=(n,),
        in_specs=[
            row(CH), row(CH), prev, full((16, CH)), row(BLOCK), row(BLOCK), row(BLOCK), row(BLOCK), row(DI), blk,
            full((NSTATE, DI)), blk, row(BLOCK), full((NSTATE, DI)), full((8, DI)), full((8, CH)), full((8, BLOCK)),
            full((DI, BLOCK)),
        ],
        out_specs=[row(CH), row(BLOCK), full((40, CH)), full((16, BLOCK)), full((8, CH)), full((8, CH))],
        out_shape=[
            sds((L, CH), BF16), sds((L, BLOCK), BF16), sds((40, CH), F32), sds((16, BLOCK), F32), sds((8, CH), F32),
            sds((8, CH), F32),
        ],
        scratch_shapes=[
            pltpu.VMEM((NSTATE, DI), F32), pltpu.VMEM((T, CH), F32), pltpu.VMEM((BLOCK, DI), BF16), pltpu.VMEM((BLOCK, DI), BF16), pltpu.VMEM((BLOCK, DI), BF16),
            pltpu.VMEM((BLOCK, DI), BF16), pltpu.VMEM((NSTATE, DI), BF16), pltpu.VMEM((8, DI), F32),
            pltpu.VMEM((NSTATE, DI), BF16), pltpu.VMEM((T + 8, CH), F32), pltpu.VMEM((T + 16, CH), F32),
        ],
        compiler_params=params(),
        name="third_pass",
    )(act, convin, convin, halo, dt, cum, sig, dcum, mlow, ent, leave, egrad, rg, inc, rows, conv, head, et)


def from_behind(x, axis, by):
    peers = lax.axis_size(axis)
    pairs = [(i, i + by) for i in range(peers) if 0 <= i + by < peers]
    return lax.ppermute(x, axis, pairs)


def chain(total, leaving, axis, reverse):
    peers, index = lax.axis_size(axis), lax.axis_index(axis)
    decays = lax.all_gather(total, axis)
    states = lax.all_gather(leaving.astype(BF16), axis)
    acc = jnp.zeros(leaving.shape, F32)
    for k in range(peers):
        at = peers - 1 - k if reverse else k
        reached = (at > index) if reverse else (at < index)
        acc = jnp.where(reached, acc * decays[at] + states[at].astype(F32), acc)
    return acc


def pad_lanes(x, width):
    return jnp.pad(x, ((0, 0), (0, width - x.shape[1])))


def on_device(
    tokens, cotangent, norm_gain, in_weight, conv_weight, conv_bias, step_bias, decay_log, skip_gain, gate_gain,
    out_weight,
):
    both = ("dp", "seq")
    gather = functools.partial(lax.all_gather, axis_name=both, axis=0, tiled=True)
    w_in = gather(in_weight)
    wo = gather(out_weight)
    taps = gather(conv_weight)
    small = gather(norm_gain), gather(conv_bias), gather(gate_gain)
    tok, cot = tokens[0], cotangent[0]
    L = tok.shape[0]
    wg = w_in[:, :DI]
    wc = jnp.pad(w_in[:, DI:], ((0, 0), (0, DI + CH + BLOCK - w_in.shape[1])))
    gain = small[0].astype(F32)[None]
    conv = jnp.concatenate([taps.astype(F32).T, small[1].astype(F32)[None], jnp.zeros((3, CH), F32)], axis=0)
    head = pad_lanes(jnp.stack([step_bias, -jnp.exp(decay_log)] + [jnp.zeros_like(step_bias)] * 6), BLOCK)
    skip = jnp.repeat(skip_gain, HEADDIM)[None]
    rows = jnp.concatenate([small[2].astype(F32)[None], skip, jnp.zeros((6, DI), F32)], axis=0)
    et = jnp.asarray(head_columns(), BF16)

    halo = from_behind(tok[L - 16 :], "seq", 1)
    normed, convin, act, dt, cum, sig, bst, leave, tot = first_pass(tok, halo, wc, gain, conv, head)
    total = jnp.repeat(jnp.exp2(tot[0, :HEADS]), HEADDIM)[None]
    inc = chain(total, leave, "seq", False)
    mixed, nout, ggrad, mlow, dcum, ent, egrad, rg, leave2, back, cols = second_pass(
        normed, act, dt, cum, bst, inc, tok, cot, wg, wo, rows, et
    )
    g_out = lax.dot_general(nout, cot, (((0,), (0,)), ((), ())), preferred_element_type=F32)
    g_gate = lax.dot_general(normed, ggrad, (((0,), (0,)), ((), ())), preferred_element_type=F32)
    later = chain(total, back, "seq", True)
    halo_conv = from_behind(convin[L - 16 :], "seq", 1)
    pg, raw, cgrad, hgrad, gfirst, glast = third_pass(
        act, convin, halo_conv, dt, cum, sig, dcum, mlow, ent, leave2, egrad, rg, later, rows, conv, head, et
    )
    after = from_behind(gfirst, "seq", -1)
    fix = [sum(conv[k] * after[i - k] for k in range(i + 1)) for i in range(CONV - 1)]
    tail = glast[5:8] + jnp.stack(fix)
    pg = lax.dynamic_update_slice(pg, tail.astype(BF16), (L - 3, 0))
    g_conv = lax.dot_general(normed, pg, (((0,), (0,)), ((), ())), preferred_element_type=F32)
    g_step = lax.dot_general(normed, raw, (((0,), (0,)), ((), ())), preferred_element_type=F32)
    nig = dot_nt(ggrad, wg) + dot_nt(pg, wc[:, :CH]) + dot_nt(raw, wc[:, CH:])
    x = tok.astype(F32)
    inv = lax.rsqrt(jnp.mean(x * x, axis=-1, keepdims=True) + EPS)
    u = nig * gain
    tgrad = (cot.astype(F32) + inv * u - x * (inv**3 * jnp.mean(u * x, axis=-1, keepdims=True))).astype(BF16)
    norm_gain_grad = jnp.sum(nig * x * inv, axis=0)
    in_grad = jnp.concatenate([g_gate, g_conv, g_step[:, :HEADS]], axis=1)
    cg = cgrad.reshape(5, 8, CH).sum(axis=1)
    scatter = functools.partial(lax.psum_scatter, axis_name=both, scatter_dimension=0, tiled=True)
    hg = hgrad.reshape(2, 8, BLOCK).sum(axis=1)[:, :HEADS]
    gg = cols.reshape(2, 8, DI).sum(axis=1)
    sums = lax.psum((hg[0], hg[1], gg[1].reshape(HEADS, HEADDIM).sum(axis=1)), both)
    return (
        mixed[None], tgrad[None], scatter(norm_gain_grad), scatter(in_grad), scatter(cg[:4].T), scatter(cg[4]),
        sums[0], sums[1], sums[2], scatter(gg[0]), scatter(g_out),
    )


def solution(mesh):
    both = ("dp", "seq")
    vec, mat, tok, rep = P(both), P(both, None), P("dp", "seq", None), P()
    return jax.shard_map(
        on_device,
        mesh=mesh,
        in_specs=(tok, tok, vec, mat, mat, vec, rep, rep, rep, vec, mat),
        out_specs=(tok, tok, vec, mat, mat, vec, rep, rep, rep, vec, mat),
        check_vma=False,
    )
```

```python
import functools

import jax
import jax.numpy as jnp
import numpy as np
from jax import lax
from jax.experimental import pallas as pl
from jax.experimental.pallas import tpu as pltpu
from jax.sharding import PartitionSpec as P

D = 768
HEADS = 24
HEADDIM = 64
NSTATE = 128
CONV = 4
BLOCK = 128
DI = 1536
CH = 1792
PAIRS = HEADS // 2
EPS = 1e-05
LOG2E = 1.4426950408889634
F32 = jnp.float32
BF16 = jnp.bfloat16
NT = (((1,), (1,)), ((), ()))
VMEM_LIMIT = 60 * 1024 * 1024


def dot(a, b):
    return jnp.dot(a, b, preferred_element_type=F32)


def dot_nt(a, b):
    return lax.dot_general(a, b, NT, preferred_element_type=F32)


def dot_exact(a, b):
    return jnp.dot(a, b, preferred_element_type=F32, precision=lax.Precision.HIGHEST)


def sigmoid(v):
    return 0.5 * jnp.tanh(0.5 * v) + 0.5


def iota(shape, dim):
    return lax.broadcasted_iota(jnp.int32, shape, dim)


def lane_lo():
    return iota((BLOCK, BLOCK), 1) < HEADDIM


def expand_pair(x, j, lo):
    rows = x.shape[0]
    a = jnp.broadcast_to(x[:, 2 * j : 2 * j + 1], (rows, BLOCK))
    b = jnp.broadcast_to(x[:, 2 * j + 1 : 2 * j + 2], (rows, BLOCK))
    return jnp.where(lo, a, b), a, b


def block_diag(v):
    lo = iota(v.shape, 1) < HEADDIM
    zero = jnp.zeros_like(v)
    return jnp.concatenate([jnp.where(lo, v, zero), jnp.where(lo, zero, v)], axis=0)


def pair(j):
    return slice(j * BLOCK, (j + 1) * BLOCK)


MESH = pl.DeviceIdType.MESH
ANY = pl.BlockSpec(memory_space=pl.ANY)
WC = CH + BLOCK
TN = (((0,), (0,)), ((), ()))


def dot_tn(a, b):
    return lax.dot_general(a, b, TN, preferred_element_type=F32)


def sizes():
    return {"z": lax.axis_size("dp") // 2, "x": 2, "y": lax.axis_size("seq") // 2, "c": 2}


def place():
    dp, seq = lax.axis_index("dp"), lax.axis_index("seq")
    return {"z": dp // 2, "x": lax.rem(dp, 2), "y": seq // 2, "c": lax.rem(seq, 2)}


def device(at):
    return {"dp": at["z"] * 2 + at["x"], "seq": at["y"] * 2 + at["c"]}


def peers(at, axis):
    n = sizes()[axis]
    return [dict(at, **{axis: lax.rem(at[axis] + o, n)}) for o in range(1, n)]


def greet(at, axes, by=0):
    sem = pltpu.get_barrier_semaphore()
    count = 0
    for axis in axes:
        for peer in peers(at, axis):
            pl.semaphore_signal(sem, inc=1, device_id=device(peer), device_id_type=MESH)
            count += 1
    if not by:
        pl.semaphore_wait(sem, count)
        return
    seq, n = lax.axis_index("seq"), lax.axis_size("seq")

    @pl.when((seq + by >= 0) & (seq + by < n))
    def _():
        pl.semaphore_signal(sem, inc=1, device_id={"seq": seq + by}, device_id_type=MESH)

    heard = (seq - by >= 0) & (seq - by < n)

    @pl.when(heard)
    def _():
        pl.semaphore_wait(sem, count + 1)

    @pl.when(jnp.logical_not(heard))
    def _():
        pl.semaphore_wait(sem, count)


def greet_neighbours():
    seq, n = lax.axis_index("seq"), lax.axis_size("seq")
    sem = pltpu.get_barrier_semaphore()

    @pl.when(seq > 0)
    def _():
        pl.semaphore_signal(sem, inc=1, device_id={"seq": seq - 1}, device_id_type=MESH)

    @pl.when(seq < n - 1)
    def _():
        pl.semaphore_signal(sem, inc=1, device_id={"seq": seq + 1}, device_id_type=MESH)

    @pl.when((seq > 0) & (seq < n - 1))
    def _():
        pl.semaphore_wait(sem, 2)

    @pl.when((seq == 0) | (seq == n - 1))
    def _():
        pl.semaphore_wait(sem, 1)


def remote(src, dst, send, recv, peer):
    return pltpu.make_async_remote_copy(
        src_ref=src, dst_ref=dst, send_sem=send, recv_sem=recv, device_id=device(peer), device_id_type=MESH
    )


class Gather:
    def __init__(self, slab, buf, order, sems, lanes=slice(None)):
        self.slab, self.buf, self.order, self.lanes = slab, buf, order, lanes
        self.send, self.recv, self.local = sems
        self.at = place()
        self.count = 0

    def spot(self, index):
        return self.buf.at[index["z"], index["x"], index["y"], index["c"], :, self.lanes]

    def copies(self, stage):
        at, (a, b) = self.at, self.order
        n = sizes()
        out = []
        every = slice(None)
        nz = n["z"] - 1
        if stage == 0:
            src, dst = self.slab.at[:, self.lanes], self.spot(at)
            for o, peer in enumerate(peers(at, "z")):
                out.append((src, dst, o, peer))
        elif stage == 1:
            index = dict(at, z=every)
            out.append((self.spot(index), self.spot(index), nz, peers(at, a)[0]))
        elif stage == 2:
            index = dict(at, z=every)
            index[a] = every
            for o, peer in enumerate(peers(at, b)):
                out.append((self.spot(index), self.spot(index), nz + 1 + o, peer))
            out.append((self.spot(index), self.spot(index), nz + 1 + n[b] - 1, peers(at, "c")[0]))
        else:
            for o in range(1, n[b]):
                index = dict(at, z=every)
                index[a] = every
                index[b] = lax.rem(at[b] + o, n[b])
                out.append((self.spot(index), self.spot(index), nz + 1 + n[b] + o - 1, peers(at, "c")[0]))
        return [remote(s, d, self.send.at[k], self.recv.at[k], p) for s, d, k, p in out]

    def own(self):
        return pltpu.make_async_copy(self.slab.at[:, self.lanes], self.spot(self.at), self.local)

    def start(self, stage):
        if stage == 0:
            self.own().start()
        for c in self.copies(stage):
            c.start()

    def wait(self, stage):
        for c in self.copies(stage):
            c.wait()
        if stage == 0:
            self.own().wait()


def gather_sems():
    count = sizes()["z"] + 2 * sizes()["y"] + 4
    return [pltpu.SemaphoreType.DMA((count,)), pltpu.SemaphoreType.DMA((count,)), pltpu.SemaphoreType.DMA(())]


class Scatter:
    def __init__(self, grads, out, order, scratch):
        self.grads, self.out, self.order = grads, out, order
        self.own, self.rc, self.r1, self.r2, self.rz, self.send, self.recv, self.local = scratch
        self.at = place()

    def copies(self, stage):
        at, (a, b) = self.at, self.order
        every = slice(None)
        out = []

        def spot(index):
            return self.own.at[index["z"], index["x"], index["y"]]

        if stage == 0:
            out.append((self.grads.at[:, :, :, 1 - at["c"]], self.rc, 0, peers(at, "c")[0]))
        elif stage == 1:
            index = {"z": every, "x": every, "y": every}
            index[a] = 1 - at[a]
            out.append((spot(index), self.r1, 1, peers(at, a)[0]))
        elif stage == 2:
            index = {"z": every, a: at[a], b: 1 - at[b]}
            out.append((spot(index), self.r2, 2, peers(at, b)[0]))
        else:
            for o, peer in enumerate(peers(at, "z")):
                out.append((self.own.at[peer["z"], at["x"], at["y"]], self.rz.at[o], 3 + o, peer))
        return [remote(s, d, self.send.at[k], self.recv.at[k], p) for s, d, k, p in out]

    def mine(self):
        return pltpu.make_async_copy(self.grads.at[:, :, :, self.at["c"]], self.own, self.local)

    def start(self, stage):
        if stage == 0:
            self.mine().start()
        for c in self.copies(stage):
            c.start()

    def finish(self, stage):
        at, (a, b) = self.at, self.order
        for c in self.copies(stage):
            c.wait()
        nz = sizes()["z"]

        def add(x, y):
            return (x.astype(F32) + y.astype(F32)).astype(BF16)

        if stage == 0:
            self.mine().wait()

            def body(z, _):
                for x in range(2):
                    for y in range(2):
                        self.own[z, x, y] = add(self.own[z, x, y], self.rc[z, x, y])
                return _

            lax.fori_loop(0, nz, body, 0)
        elif stage == 1:

            def body(z, _):
                for k in range(2):
                    index = {a: at[a], b: k}
                    got = self.own[z, index["x"], index["y"]]
                    self.own[z, index["x"], index["y"]] = add(got, self.r1[z, k])
                return _

            lax.fori_loop(0, nz, body, 0)
        elif stage == 2:

            def body(z, _):
                self.own[z, at["x"], at["y"]] = add(self.own[z, at["x"], at["y"]], self.r2[z])
                return _

            lax.fori_loop(0, nz, body, 0)
        else:
            total = self.own[at["z"], at["x"], at["y"]].astype(F32)
            for o in range(nz - 1):
                total = total + self.rz[o].astype(F32)
            self.out[...] = total


def scatter_scratch(rows, width):
    nz = sizes()["z"]
    return [
        pltpu.VMEM((nz, 2, 2, rows, width), BF16), pltpu.VMEM((nz, 2, 2, rows, width), BF16),
        pltpu.VMEM((nz, 2, rows, width), BF16), pltpu.VMEM((nz, rows, width), BF16),
        pltpu.VMEM((nz - 1, rows, width), BF16), pltpu.SemaphoreType.DMA((nz + 2,)), pltpu.SemaphoreType.DMA((nz + 2,)),
        pltpu.SemaphoreType.DMA(()),
    ]


NSC = 8


class Chain:
    def __init__(self, leave, inc, decay, bufs, reverse):
        self.leave, self.inc, self.decay, self.reverse = leave, inc, decay, reverse
        self.got, self.put, self.send, self.recv = bufs
        self.n = lax.axis_size("seq")
        seq = lax.axis_index("seq")
        self.rank = self.n - 1 - seq if reverse else seq
        self.to = seq - 1 if reverse else seq + 1

    def copy(self):
        return pltpu.make_async_remote_copy(
            src_ref=self.put, dst_ref=self.got, send_sem=self.send, recv_sem=self.recv,
            device_id={"seq": self.to}, device_id_type=MESH,
        )

    def step(self, k):
        @pl.when(self.rank == k)
        def _():
            if k == 0:
                self.inc[...] = jnp.zeros_like(self.inc)
                self.put[...] = self.leave[...].astype(BF16)
            else:
                self.copy().wait_recv()
                got = self.got[...].astype(F32)
                self.inc[...] = got
                if k < self.n - 1:
                    self.put[...] = (got * self.decay[0:1] + self.leave[...]).astype(BF16)
            if k < self.n - 1:
                self.copy().start()

    def done(self):
        @pl.when(self.rank < self.n - 1)
        def _():
            self.copy().wait_send()


def chain_scratch():
    return [
        pltpu.VMEM((NSTATE, DI), BF16), pltpu.VMEM((NSTATE, DI), BF16), pltpu.SemaphoreType.DMA(()),
        pltpu.SemaphoreType.DMA(()),
    ]


def expand_row(row, dst):
    lo = iota((8, BLOCK), 1) < HEADDIM
    wide = jnp.broadcast_to(row, (8, BLOCK))
    for j in range(PAIRS):
        dst[:, pair(j)] = expand_pair(wide, j, lo)[0]


def weights_kernel(slab, last, buf, halo, *sems):
    at = place()
    seq, n = lax.axis_index("seq"), lax.axis_size("seq")
    greet(at, "zxyc", -1)
    hsend, hrecv = sems[6], sems[7]
    copy = pltpu.make_async_remote_copy(
        src_ref=last, dst_ref=halo, send_sem=hsend, recv_sem=hrecv, device_id={"seq": seq + 1}, device_id_type=MESH
    )
    a = Gather(slab, buf, "xy", sems[0:3], slice(0, 1024))
    b = Gather(slab, buf, "yx", sems[3:6], slice(1024, WC))
    a.start(0)
    b.start(0)

    @pl.when(seq < n - 1)
    def _():
        copy.start()

    for stage in range(3):
        a.wait(stage)
        a.start(stage + 1)
        b.wait(stage)
        b.start(stage + 1)
    a.wait(3)
    b.wait(3)

    @pl.when(seq < n - 1)
    def _():
        copy.wait_send()

    @pl.when(seq > 0)
    def _():
        copy.wait_recv()

    @pl.when(seq == 0)
    def _():
        halo[...] = jnp.zeros_like(halo)


def gather_weights(slab, last):
    n = sizes()
    shape = (n["z"], n["x"], n["y"], n["c"]) + slab.shape
    vm = pl.BlockSpec(memory_space=pltpu.VMEM)
    return pl.pallas_call(
        weights_kernel,
        in_specs=[ANY, vm],
        out_specs=[ANY, vm],
        out_shape=[sds(shape, BF16), sds(last.shape, BF16)],
        scratch_shapes=gather_sems() + gather_sems() + [pltpu.SemaphoreType.DMA(()), pltpu.SemaphoreType.DMA(())],
        compiler_params=pltpu.CompilerParams(collective_id=0, has_side_effects=True),
        name="gather_weights",
    )(slab, last)


def gate_kernel(normed_ref, wg_ref, leave_ref, tot_ref, gate_ref, inc_ref, decay, *bufs):
    i = pl.program_id(0)
    chain = Chain(leave_ref, inc_ref, decay, bufs, False)
    last = pl.num_programs(0) - 1

    @pl.when(i == 0)
    def _():
        expand_row(jnp.exp2(tot_ref[0:1]), decay)
        greet_neighbours()
        chain.step(0)

    for c in range(DI // 256):
        cs = slice(c * 256, (c + 1) * 256)
        gate_ref[:, cs] = dot(normed_ref[...], wg_ref[:, cs]).astype(BF16)
    for k in range(1, chain.n):
        @pl.when(i == jnp.minimum(k, last))
        def _():
            chain.step(k)

    @pl.when(i == last)
    def _():
        chain.done()


def gate_pass(normed, wg, leave, tot, T=512):
    L = normed.shape[0]
    row = lambda w: pl.BlockSpec((T, w), lambda i: (i, 0))
    return pl.pallas_call(
        gate_kernel,
        grid=(L // T,),
        in_specs=[row(D), full((D, DI)), full((NSTATE, DI)), full((8, BLOCK))],
        out_specs=[row(DI), full((NSTATE, DI))],
        out_shape=[sds((L, DI), BF16), sds((NSTATE, DI), F32)],
        scratch_shapes=[pltpu.VMEM((8, DI), F32)] + chain_scratch(),
        compiler_params=params(collective_id=2),
        name="gate_pass",
    )(normed, wg, leave, tot)


def grads_kernel(nout_ref, cot_ref, normed_ref, ggrad_ref, back_ref, tot_ref, gout_ref, ggate_ref, inc_ref, decay, *bufs):
    i = pl.program_id(0)
    chain = Chain(back_ref, inc_ref, decay, bufs, True)
    last = pl.num_programs(0) - 1

    @pl.when(i == 0)
    def _():
        expand_row(jnp.exp2(tot_ref[0:1]), decay)
        greet_neighbours()
        chain.step(0)

    gout_ref[...] = dot_tn(nout_ref[...], cot_ref[...]).astype(BF16)
    ggate_ref[...] = dot_tn(normed_ref[...], ggrad_ref[...]).astype(BF16)
    for k in range(1, chain.n):
        @pl.when(i == jnp.minimum(k, last))
        def _():
            chain.step(k)

    @pl.when(i == last)
    def _():
        chain.done()


def grads_pass(nout, cot, normed, ggrad, back, tot):
    L = nout.shape[0]
    col = lambda w: pl.BlockSpec((L, w), lambda i: (0, i))
    return pl.pallas_call(
        grads_kernel,
        grid=(6,),
        in_specs=[col(256), full((L, D)), col(128), full((L, DI)), full((NSTATE, DI)), full((8, BLOCK))],
        out_specs=[
            pl.BlockSpec((256, D), lambda i: (i, 0)), pl.BlockSpec((128, DI), lambda i: (i, 0)), full((NSTATE, DI)),
        ],
        out_shape=[sds((DI, D), BF16), sds((D, DI), BF16), sds((NSTATE, DI), F32)],
        scratch_shapes=[pltpu.VMEM((8, DI), F32)] + chain_scratch(),
        compiler_params=params(collective_id=3),
        name="grads_pass",
    )(nout, cot, normed, ggrad, back, tot)


def conv_grad_kernel(normed_ref, pg_ref, tnormed_ref, tail_ref, out_ref):
    for c in range(WC // 384):
        cs = slice(c * 384, (c + 1) * 384)
        g = dot_tn(normed_ref[...], pg_ref[:, cs])
        out_ref[:, cs] = (g + dot_tn(tnormed_ref[...], tail_ref[:, cs])).astype(BF16)


def conv_grad(normed, pg, tail):
    L = normed.shape[0]
    return pl.pallas_call(
        conv_grad_kernel,
        grid=(3,),
        in_specs=[
            pl.BlockSpec((L, 256), lambda i: (0, i)), full((L, WC)), pl.BlockSpec((16, 256), lambda i: (L // 16 - 1, i)),
            full((16, WC)),
        ],
        out_specs=pl.BlockSpec((256, WC), lambda i: (i, 0)),
        out_shape=sds((D, WC), BF16),
        compiler_params=params(),
        name="conv_grad",
    )(normed, pg, normed, tail)


def last_kernel(
    T, ggrad_ref, pg_ref, tail_ref, tok_ref, cot_ref, wg_ref, wc_ref, gain_ref, small_ref, gconv_ref,
    tgrad_ref, gout_ref, sums_ref, ngain, packed, smalls, ssend, srecv, *scratch,
):
    i = pl.program_id(0)
    last = pl.num_programs(0) - 1
    at = place()
    sc = Scatter(gconv_ref, gout_ref, "yx", scratch)
    dp, seq = lax.axis_index("dp"), lax.axis_index("seq")
    n_dp, n_seq = lax.axis_size("dp"), lax.axis_size("seq")
    total = n_dp * n_seq
    me = dp * n_seq + seq

    def far(o):
        r = lax.rem(me + o, total)
        return r, {"dp": r // n_seq, "seq": lax.rem(r, n_seq)}

    @pl.when(i == 0)
    def _():
        ngain[...] = jnp.zeros_like(ngain)
        sem = pltpu.get_barrier_semaphore()
        for o in range(1, total):
            pl.semaphore_signal(sem, inc=1, device_id=far(o)[1], device_id_type=MESH)
        pl.semaphore_wait(sem, total - 1)
        sc.start(0)

    def part():
        nig = dot_nt(ggrad_ref[...], wg_ref[...]) + dot_nt(pg_ref[...], wc_ref[...])
        return nig

    x = tok_ref[...].astype(F32)
    inv = lax.rsqrt(jnp.mean(x * x, axis=-1, keepdims=True) + EPS)
    nig = part()
    fix = dot_nt(tail_ref[...], wc_ref[...])
    fix = jnp.where(i == last, fix, 0.0)
    nig = jnp.concatenate([nig[: T - 16], nig[T - 16 :] + fix], axis=0)
    u = nig * gain_ref[...]
    xi = x * inv
    coef = inv * jnp.mean(u * xi, axis=-1, keepdims=True)
    tgrad_ref[...] = (cot_ref[...].astype(F32) + inv * u - xi * coef).astype(BF16)
    ngain[...] += jnp.sum((nig * xi).reshape(T // 8, 8, D), axis=0)

    for k in range(3):
        @pl.when(i == jnp.minimum(k, last))
        def _():
            sc.finish(k)
            sc.start(k + 1)

    @pl.when(i == last)
    def _():
        row = jnp.sum(ngain[...], axis=0, keepdims=True)
        width = D // total
        which = iota((8, BLOCK), 0) == 5
        for r in range(total):
            piece = jnp.broadcast_to(row[:, r * width : (r + 1) * width], (8, width))
            piece = jnp.concatenate([piece, jnp.zeros((8, BLOCK - width), F32)], axis=1)
            packed[r] = jnp.where(which, piece, small_ref[r])
        copies = []
        for o in range(1, total):
            r, dev = far(o)
            c = pltpu.make_async_remote_copy(
                src_ref=packed.at[r], dst_ref=smalls.at[o - 1], send_sem=ssend.at[o - 1], recv_sem=srecv.at[o - 1],
                device_id=dev, device_id_type=MESH,
            )
            c.start()
            copies.append(c)
        sc.finish(3)
        for c in copies:
            c.wait()
        acc = packed[me]
        for o in range(1, total):
            acc = acc + smalls[o - 1]
        sums_ref[...] = acc


def last_pass(ggrad, pg, tail, tok, cot, wg, wc, gain, small, gconv, T=512):
    L = tok.shape[0]
    n = sizes()
    total = lax.axis_size("dp") * lax.axis_size("seq")
    rows = D // total
    row = lambda w: pl.BlockSpec((T, w), lambda i: (i, 0))
    gconv = gconv.reshape(n["z"], n["x"], n["y"], n["c"], rows, WC)
    return pl.pallas_call(
        functools.partial(last_kernel, T),
        grid=(L // T,),
        in_specs=[
            row(DI), row(WC), full((16, WC)), row(D), row(D), full((D, DI)), full((D, WC)), full((1, D)),
            full((total, 8, BLOCK)), ANY,
        ],
        out_specs=[row(D), full((rows, WC)), full((8, BLOCK))],
        out_shape=[sds((L, D), BF16), sds((rows, WC), F32), sds((8, BLOCK), F32)],
        scratch_shapes=[
            pltpu.VMEM((8, D), F32), pltpu.VMEM((total, 8, BLOCK), F32), pltpu.VMEM((total - 1, 8, BLOCK), F32),
            pltpu.SemaphoreType.DMA((total - 1,)), pltpu.SemaphoreType.DMA((total - 1,)),
        ] + scatter_scratch(rows, WC),
        compiler_params=params(collective_id=5),
        name="last_pass",
    )(ggrad, pg, tail, tok, cot, wg, wc, gain, small, gconv)


def rms_rows(tok, gain):
    x = tok.astype(F32)
    inv = lax.rsqrt(jnp.mean(x * x, axis=-1, keepdims=True) + EPS)
    return (x * inv * gain).astype(BF16)


def first_kernel(
    T, tok_ref, halo_ref, wc_ref, gain_ref, conv_ref, head_ref, sg_ref, so_ref,
    normed_ref, convin_ref, act_ref, dt_ref, cum_ref, sig_ref, bst_ref, leave_ref, tot_ref, hconv_ref, bg_ref, bo_ref,
    ext, state, weighted, *sems,
):
    i = pl.program_id(0)
    steps = pl.num_programs(0)
    ga = Gather(sg_ref, bg_ref, "xy", sems[0:3])
    gb = Gather(so_ref, bo_ref, "yx", sems[3:6])

    @pl.when(i == 0)
    def _():
        greet(place(), "zxyc")
        ga.start(0)
        gb.start(0)

    for stage, when in enumerate((3, 5)):
        @pl.when(i == when)
        def _():
            ga.wait(stage)
            ga.start(stage + 1)
            gb.wait(stage)
            gb.start(stage + 1)

    @pl.when(i == steps - 1)
    def _():
        ga.wait(2)
        ga.start(3)
        gb.wait(2)
        gb.start(3)

    @pl.when(i == 0)
    def _():
        hn = rms_rows(halo_ref[...], gain_ref[...])
        hp = dot(hn, wc_ref[:, :CH]).astype(BF16)
        hconv_ref[...] = hp
        ext[0:8] = hp.astype(F32)[8:16]
        state[...] = jnp.zeros_like(state)
        tot_ref[...] = jnp.zeros_like(tot_ref)

    @pl.when(i > 0)
    def _():
        ext[0:8] = ext[T : T + 8]

    normed = rms_rows(tok_ref[...], gain_ref[...])
    normed_ref[...] = normed
    for c in range(CH // 256):
        cs = slice(c * 256, (c + 1) * 256)
        p = dot(normed, wc_ref[:, cs]).astype(BF16)
        convin_ref[:, cs] = p
        ext[8 : 8 + T, cs] = p.astype(F32)
        total = conv_ref[4:5, cs]
        for k in range(CONV):
            total = total + ext[5 + k : 5 + k + T, cs] * conv_ref[k : k + 1, cs]
        act_ref[:, cs] = (total * sigmoid(total)).astype(BF16)
    raw = dot(normed, wc_ref[:, CH:]).astype(BF16).astype(F32) + head_ref[0:1]
    dt_all = jnp.maximum(raw, 0.0) + jnp.log1p(jnp.exp(-jnp.abs(raw)))
    dt_ref[...] = dt_all
    sig_ref[...] = sigmoid_exact(raw)
    tril = (iota((BLOCK, BLOCK), 0) >= iota((BLOCK, BLOCK), 1)).astype(F32)
    lo = lane_lo()
    for blk in range(T // BLOCK):
        rows = slice(blk * BLOCK, (blk + 1) * BLOCK)
        dt = dt_all[rows]
        cum = dot_exact(tril, dt * head_ref[1:2]) * LOG2E
        cum_ref[rows] = cum
        end = cum[BLOCK - 1 : BLOCK]
        tot_ref[...] += jnp.broadcast_to(end, tot_ref.shape)
        wfac = jnp.exp2(end - cum) * dt
        decay = jnp.broadcast_to(jnp.exp2(end), (8, BLOCK))
        write_t = act_ref[rows, DI : DI + NSTATE].T
        for j in range(PAIRS):
            w, _, _ = expand_pair(wfac, j, lo)
            weighted[:, pair(j)] = (act_ref[rows, pair(j)].astype(F32) * w).astype(BF16)
        for q in range(PAIRS // 2):
            cs = slice(q * 256, (q + 1) * 256)
            new = dot(write_t, weighted[:, cs])
            bst_ref[blk, :, cs] = new.astype(BF16)
            d0, _, _ = expand_pair(decay, 2 * q, lo[:8])
            d1, _, _ = expand_pair(decay, 2 * q + 1, lo[:8])
            dd = jnp.concatenate([d0, d1], axis=1)[0:1]
            state[:, cs] = state[:, cs] * dd + new

    @pl.when(i == pl.num_programs(0) - 1)
    def _():
        leave_ref[...] = state[...]
        ga.wait(3)
        gb.wait(3)


def sigmoid_exact(v):
    return 1.0 / (1.0 + jnp.exp(-v))


def second_kernel(
    T, gate_s, act_ref, dt_ref, cum_ref, bst_ref, inc_ref, tok_ref, cot_ref, wo_ref, row_ref, et_ref,
    mixed_ref, nout_ref, ggrad_ref, mlow_ref, dcum_ref, ent_ref, egrad_ref, rg_ref, leave_ref, back_ref, cols_ref,
    ng, ms, growth, rlow, prod, plow, state, exg, lows,
):
    i = pl.program_id(0)

    @pl.when(i == 0)
    def _():
        state[...] = inc_ref[...]
        exg[...] = jnp.ones_like(exg)
        back_ref[...] = jnp.zeros_like(back_ref)
        cols_ref[...] = jnp.zeros_like(cols_ref)

    lo = lane_lo()
    for c in range(DI // 256):
        cs = slice(c * 256, (c + 1) * 256)
        ng[:, cs] = dot_nt(cot_ref[...], wo_ref[cs, :])
    lower = iota((BLOCK, BLOCK), 0) >= iota((BLOCK, BLOCK), 1)
    nblk = T // BLOCK
    for blk in range(nblk):
        rows = slice(blk * BLOCK, (blk + 1) * BLOCK)
        cum = cum_ref[rows]
        cum_t = cum.T
        dt = dt_ref[rows]
        write = act_ref[rows, DI : DI + NSTATE]
        read = act_ref[rows, DI + NSTATE :]
        inner = jnp.where(lower, dot_nt(read, write), 0.0)
        lows[blk] = state[...].astype(BF16)
        ent_ref[blk] = lows[blk]
        for j in range(PAIRS):
            cols, a, b = expand_pair(cum, j, lo)
            ga = jnp.exp2(jnp.minimum(a - cum_t[2 * j : 2 * j + 1], 0.0)) * inner
            gb = jnp.exp2(jnp.minimum(b - cum_t[2 * j + 1 : 2 * j + 2], 0.0)) * inner
            scores = jnp.concatenate([ga.astype(BF16), gb.astype(BF16)], axis=1)
            vals = act_ref[rows, pair(j)].astype(F32)
            dtp, _, _ = expand_pair(dt, j, lo)
            vdt = (vals * dtp).astype(BF16)
            grow = jnp.exp2(cols)
            growth[rows, pair(j)] = grow
            diag = dot(scores, block_diag(vdt))
            out = dot(read, lows[blk, :, pair(j)])
            ms[rows, pair(j)] = diag + grow * out + row_ref[1:2, pair(j)] * vals
            dec = grow[BLOCK - 1 : BLOCK]
            state[:, pair(j)] = state[:, pair(j)] * dec + bst_ref[blk, :, pair(j)].astype(F32)

    sq = jnp.zeros((T, BLOCK), F32)
    ug = jnp.zeros((T, BLOCK), F32)
    for j in range(PAIRS):
        g = gate_s[:, pair(j)].astype(F32)
        gated = ms[:, pair(j)] * (g * sigmoid(g))
        sq = sq + gated * gated
        ug = ug + gated * (ng[:, pair(j)] * row_ref[0:1, pair(j)])
    inv = lax.rsqrt(jnp.sum(sq, axis=-1, keepdims=True) * (1.0 / DI) + EPS)
    coef = jnp.sum(ug, axis=-1, keepdims=True) * (1.0 / DI) * (inv * inv * inv)
    for j in range(PAIRS):
        g = gate_s[:, pair(j)].astype(F32)
        sg = sigmoid(g)
        silu = g * sg
        m = ms[:, pair(j)]
        gated = m * silu
        n = ng[:, pair(j)]
        gain = row_ref[0:1, pair(j)]
        gi = gated * inv
        nout_ref[:, pair(j)] = (gi * gain).astype(BF16)
        dg = inv * (n * gain) - gated * coef
        low = (dg * silu).astype(BF16)
        mlow_ref[:, pair(j)] = low
        ggrad_ref[:, pair(j)] = (dg * m * (sg + silu * (1.0 - sg))).astype(BF16)
        vals = act_ref[:, pair(j)].astype(F32)
        lowf = low.astype(F32)
        mv = lowf * vals
        pr = lowf * m - row_ref[1:2, pair(j)] * mv
        hi = pr.astype(BF16)
        prod[:, pair(j)] = hi
        plow[:, pair(j)] = (pr - hi.astype(F32)).astype(BF16)
        rlow[:, pair(j)] = (lowf * growth[:, pair(j)]).astype(BF16)
        cols_ref[0:8, pair(j)] += jnp.sum((n * gi).reshape(T // 8, 8, BLOCK), axis=0)
        cols_ref[8:16, pair(j)] += jnp.sum(mv.reshape(T // 8, 8, BLOCK), axis=0)
    dcum_ref[...] = dot(prod[...], et_ref[...]) + dot(plow[...], et_ref[...])
    mixed_ref[...] = (tok_ref[...].astype(F32) + dot(nout_ref[...], wo_ref[...])).astype(BF16)
    for blk in range(nblk):
        rows = slice(blk * BLOCK, (blk + 1) * BLOCK)
        read_t = act_ref[rows, DI + NSTATE :].T
        for q in range(PAIRS // 2):
            cs = slice(q * 256, (q + 1) * 256)
            eg = dot(read_t, rlow[rows, cs])
            egrad_ref[blk, :, cs] = eg.astype(BF16)
            back_ref[:, cs] += eg * exg[0:1, cs]
        exg[...] = exg[...] * growth[blk * BLOCK + BLOCK - 1 : blk * BLOCK + BLOCK, :]
        rg_ref[rows] = dot_nt(rlow[rows, :], lows[blk])

    @pl.when(i == pl.num_programs(0) - 1)
    def _():
        leave_ref[...] = state[...].astype(BF16)


def third_kernel(
    T, act_ref, convin_ref, prev_ref, halo_ref, dt_ref, cum_ref, sig_ref, dcum_ref, mlow_ref, ent_ref, leave_ref,
    egrad_ref, rg_ref, inc_ref, row_ref, conv_ref, head_ref, et_ref, go_ref, gg_ref,
    pg_ref, cgrad_ref, hgrad_ref, tail_ref, so_ref, sg_ref,
    glast, gafter, hsend, hrecv, carry, dact, vprod, prod, plow, weighted, lows, dec, nxt, gext, cext, *scratch,
):
    i = pl.program_id(0)
    steps = pl.num_programs(0)
    sca = Scatter(go_ref, so_ref, "yx", scratch[:NSC])
    scb = Scatter(gg_ref, sg_ref, "xy", scratch[NSC:])
    seq, nseq = lax.axis_index("seq"), lax.axis_size("seq")
    after = pltpu.make_async_remote_copy(
        src_ref=gext.at[0:8], dst_ref=gafter, send_sem=hsend, recv_sem=hrecv, device_id={"seq": seq - 1},
        device_id_type=MESH,
    )

    @pl.when(i == 0)
    def _():
        greet(place(), "zxyc", 1)
        sca.start(0)
        scb.start(0)

    for stage, when in enumerate((1, 4, 6)):
        @pl.when(i == when)
        def _():
            sca.finish(stage)
            sca.start(stage + 1)
            scb.finish(stage)
            scb.start(stage + 1)

    @pl.when(i == steps - 1)
    def _():
        sca.finish(3)
        scb.finish(3)

    @pl.when(i == 0)
    def _():
        carry[...] = inc_ref[...]
        nxt[...] = leave_ref[...]
        cgrad_ref[...] = jnp.zeros_like(cgrad_ref)
        hgrad_ref[...] = jnp.zeros_like(hgrad_ref)
        gext[T : T + 8] = jnp.zeros((8, CH), F32)

    @pl.when(i > 0)
    def _():
        gext[T : T + 8] = gext[0:8]

    @pl.when(i == steps - 1)
    def _():
        cext[0:16] = halo_ref[...].astype(F32)

    @pl.when(i < steps - 1)
    def _():
        cext[0:16] = prev_ref[...].astype(F32)

    lo = lane_lo()
    upper = iota((BLOCK, BLOCK), 0) <= iota((BLOCK, BLOCK), 1)
    triu = upper.astype(F32)
    last = iota((BLOCK, BLOCK), 0) == BLOCK - 1
    for blk in reversed(range(T // BLOCK)):
        rows = slice(blk * BLOCK, (blk + 1) * BLOCK)
        cum = cum_ref[rows]
        cum_t = cum.T
        dt = dt_ref[rows]
        end = cum[BLOCK - 1 : BLOCK]
        rest = end - cum
        write = act_ref[rows, DI : DI + NSTATE]
        read = act_ref[rows, DI + NSTATE :]
        inner = jnp.where(upper, dot_nt(write, read), 0.0)
        lows[...] = carry[...].astype(BF16)
        acc = jnp.zeros((BLOCK, BLOCK), F32)
        for j in range(PAIRS):
            cols, a, b = expand_pair(cum, j, lo)
            wexp, _, _ = expand_pair(rest, j, lo)
            wexp = jnp.exp2(wexp)
            da = jnp.exp2(jnp.minimum(cum_t[2 * j : 2 * j + 1] - a, 0.0))
            db = jnp.exp2(jnp.minimum(cum_t[2 * j + 1 : 2 * j + 2] - b, 0.0))
            scores = jnp.concatenate([(da * inner).astype(BF16), (db * inner).astype(BF16)], axis=1)
            m = mlow_ref[rows, pair(j)]
            diag = block_diag(m)
            z = dot(scores, diag)
            vals = act_ref[rows, pair(j)].astype(F32)
            dtp, _, _ = expand_pair(dt, j, lo)
            vdt = vals * dtp
            vdtb = vdt.astype(BF16)
            wtb = (vdt * wexp).astype(BF16)
            g = dot_nt(vdtb, diag)
            acc = acc + g[:, :BLOCK] * da + g[:, BLOCK:] * db
            wg = dot(write, lows[:, pair(j)])
            pr = vdtb.astype(F32) * z + wtb.astype(F32) * wg
            z = z + wg * wexp
            dact[rows, pair(j)] = row_ref[1:2, pair(j)] * m.astype(F32) + dtp * z
            vprod[:, pair(j)] = (vals * z).astype(BF16)
            hi = pr.astype(BF16)
            prod[:, pair(j)] = hi
            plow[:, pair(j)] = (pr - hi.astype(F32)).astype(BF16)
            weighted[:, pair(j)] = wtb
            dec[0:1, pair(j)] = jnp.exp2(cols[BLOCK - 1 : BLOCK])
        low = jnp.where(upper, acc, 0.0).astype(BF16)
        dact[rows, DI : DI + NSTATE] = dot_nt(weighted[...], lows[...]) + dot(low, read)
        dact[rows, DI + NSTATE :] = rg_ref[rows] + dot(low.T, write)
        c = dot(vprod[...], et_ref[...])
        used = dot(prod[...], et_ref[...]) + dot(plow[...], et_ref[...])
        ends = jnp.sum((lows[...].astype(F32) * nxt[...].astype(F32)).reshape(16, 8, DI), axis=0)
        ends_hi = ends.astype(BF16)
        ends_lo = (ends - ends_hi.astype(F32)).astype(BF16)
        de = jnp.sum(dot(ends_hi, et_ref[...]) + dot(ends_lo, et_ref[...]), axis=0, keepdims=True)
        dc = dcum_ref[rows] - used + jnp.where(last, de, 0.0)
        da_log = dot_exact(triu, dc)
        draw = (c + da_log * head_ref[1:2]) * sig_ref[rows]
        pg_ref[rows, CH:] = draw.astype(BF16)
        hgrad_ref[0:8] += jnp.sum(draw.reshape(16, 8, BLOCK), axis=0)
        hgrad_ref[8:16] += jnp.sum((da_log * dt).reshape(16, 8, BLOCK), axis=0) * head_ref[1:2]
        nxt[...] = ent_ref[blk]
        for q in range(PAIRS // 2):
            cs = slice(q * 256, (q + 1) * 256)
            carry[:, cs] = carry[:, cs] * dec[0:1, cs] + egrad_ref[blk, :, cs].astype(F32)

    for c in range(CH // 128):
        cs = slice(c * 128, (c + 1) * 128)
        cext[16 : 16 + T, cs] = convin_ref[:, cs].astype(F32)
        taps = [cext[13 + k : 13 + k + T, cs] for k in range(CONV)]
        pre = conv_ref[4:5, cs]
        for k in range(CONV):
            pre = pre + taps[k] * conv_ref[k : k + 1, cs]
        sg = sigmoid(pre)
        g = dact[:, cs] * (sg * (1.0 + pre * (1.0 - sg)))
        gext[0:T, cs] = g
        for k in range(CONV):
            cgrad_ref[8 * k : 8 * k + 8, cs] += jnp.sum((g * taps[k]).reshape(T // 8, 8, BLOCK), axis=0)
        cgrad_ref[32:40, cs] += jnp.sum(g.reshape(T // 8, 8, BLOCK), axis=0)
        back = g * conv_ref[3:4, cs]
        for k in range(CONV - 1):
            back = back + gext[3 - k : 3 - k + T, cs] * conv_ref[k : k + 1, cs]
        pg_ref[:, cs] = back.astype(BF16)

        @pl.when(i == 0)
        def _():
            glast[:, cs] = back[T - 16 :]
            pg_ref[T - 16 :, cs] = jnp.zeros((16, 128), BF16)

    @pl.when(i == steps - 1)
    def _():
        @pl.when(seq > 0)
        def _():
            after.start()

        @pl.when(seq == nseq - 1)
        def _():
            gafter[...] = jnp.zeros_like(gafter)

        @pl.when(seq < nseq - 1)
        def _():
            after.wait_recv()

        rows16 = iota((16, CH), 0)
        tail = glast[...]
        for i3 in range(CONV - 1):
            fix = jnp.zeros((1, CH), F32)
            for k in range(i3 + 1):
                fix = fix + conv_ref[k : k + 1] * gafter[i3 - k : i3 - k + 1]
            tail = tail + jnp.where(rows16 == 13 + i3, fix, 0.0)
        tail_ref[:, :CH] = tail.astype(BF16)
        tail_ref[:, CH:] = jnp.zeros((16, BLOCK), BF16)

        @pl.when(seq > 0)
        def _():
            after.wait_send()


def full(shape):
    return pl.BlockSpec(shape, lambda i: (0,) * len(shape))


def params(collective_id=None):
    return pltpu.CompilerParams(
        dimension_semantics=("arbitrary",), vmem_limit_bytes=VMEM_LIMIT, collective_id=collective_id,
        has_side_effects=collective_id is not None,
    )


def head_columns():
    et = np.zeros((DI, BLOCK), np.float32)
    et[np.arange(DI), np.arange(DI) // HEADDIM] = 1.0
    return et


def sds(shape, dtype):
    return jax.ShapeDtypeStruct(shape, dtype)


def first_pass(tok, halo, wc, gain, conv, head, slab_g, slab_o, T=256):
    L = tok.shape[0]
    nb, per = L // BLOCK, T // BLOCK
    n = sizes()
    row = lambda w: pl.BlockSpec((T, w), lambda i: (i, 0))
    dims = (n["z"], n["x"], n["y"], n["c"])
    return pl.pallas_call(
        functools.partial(first_kernel, T),
        grid=(L // T,),
        in_specs=[
            row(D), full((16, D)), full((D, WC)), full((1, D)), full((8, CH)), full((8, BLOCK)), ANY, ANY,
        ],
        out_specs=[
            row(D), row(CH), row(CH), row(BLOCK), row(BLOCK), row(BLOCK),
            pl.BlockSpec((per, NSTATE, DI), lambda i: (i, 0, 0)), full((NSTATE, DI)), full((8, BLOCK)),
            full((16, CH)), ANY, ANY,
        ],
        out_shape=[
            sds((L, D), BF16), sds((L, CH), BF16), sds((L, CH), BF16), sds((L, BLOCK), F32), sds((L, BLOCK), F32),
            sds((L, BLOCK), F32), sds((nb, NSTATE, DI), BF16), sds((NSTATE, DI), F32), sds((8, BLOCK), F32),
            sds((16, CH), BF16), sds(dims + slab_g.shape, BF16), sds(dims + slab_o.shape, BF16),
        ],
        scratch_shapes=[
            pltpu.VMEM((T + 8, CH), F32), pltpu.VMEM((NSTATE, DI), F32), pltpu.VMEM((BLOCK, DI), BF16),
        ] + gather_sems() + gather_sems(),
        compiler_params=params(collective_id=1),
        name="first_pass",
    )(tok, halo, wc, gain, conv, head, slab_g, slab_o)


def second_pass(gate, act, dt, cum, bst, inc, tok, cot, wo, rows, et, T=256):
    L = tok.shape[0]
    nb, per = L // BLOCK, T // BLOCK
    row = lambda w: pl.BlockSpec((T, w), lambda i: (i, 0))
    blk = pl.BlockSpec((per, NSTATE, DI), lambda i: (i, 0, 0))
    return pl.pallas_call(
        functools.partial(second_kernel, T),
        grid=(L // T,),
        in_specs=[
            row(DI), row(CH), row(BLOCK), row(BLOCK), blk, full((NSTATE, DI)), row(D), row(D),
            full((DI, D)), full((8, DI)), full((DI, BLOCK)),
        ],
        out_specs=[
            row(D), row(DI), row(DI), row(DI), row(BLOCK), blk, blk, row(BLOCK), full((NSTATE, DI)),
            full((NSTATE, DI)), full((16, DI)),
        ],
        out_shape=[
            sds((L, D), BF16), sds((L, DI), BF16), sds((L, DI), BF16), sds((L, DI), BF16), sds((L, BLOCK), F32),
            sds((nb, NSTATE, DI), BF16), sds((nb, NSTATE, DI), BF16), sds((L, BLOCK), F32), sds((NSTATE, DI), BF16),
            sds((NSTATE, DI), F32), sds((16, DI), F32),
        ],
        scratch_shapes=[
            pltpu.VMEM((T, DI), F32), pltpu.VMEM((T, DI), F32), pltpu.VMEM((T, DI), F32),
            pltpu.VMEM((T, DI), BF16), pltpu.VMEM((T, DI), BF16), pltpu.VMEM((T, DI), BF16), pltpu.VMEM((NSTATE, DI), F32),
            pltpu.VMEM((8, DI), F32), pltpu.VMEM((per, NSTATE, DI), BF16),
        ],
        compiler_params=params(),
        name="second_pass",
    )(gate, act, dt, cum, bst, inc, tok, cot, wo, rows, et)


def third_pass(
    act, convin, halo, dt, cum, sig, dcum, mlow, ent, leave, egrad, rg, inc, rows, conv, head, et, go, gg, T=256
):
    L = act.shape[0]
    m = sizes()
    dims = (m["z"], m["x"], m["y"], m["c"])
    total = m["z"] * m["y"] * 4
    ro, rg_rows = DI // total, D // total
    go = go.reshape(dims + (ro, D))
    gg = gg.reshape(dims + (rg_rows, DI))
    n, per = L // T, T // BLOCK
    row = lambda w: pl.BlockSpec((T, w), lambda i: (n - 1 - i, 0))
    blk = pl.BlockSpec((per, NSTATE, DI), lambda i: (n - 1 - i, 0, 0))
    prev = pl.BlockSpec((16, CH), lambda i: (jnp.maximum((n - 1 - i) * (T // 16) - 1, 0), 0))
    return pl.pallas_call(
        functools.partial(third_kernel, T),
        grid=(n,),
        in_specs=[
            row(CH), row(CH), prev, full((16, CH)), row(BLOCK), row(BLOCK), row(BLOCK), row(BLOCK), row(DI), blk,
            full((NSTATE, DI)), blk, row(BLOCK), full((NSTATE, DI)), full((8, DI)), full((8, CH)), full((8, BLOCK)),
            full((DI, BLOCK)), ANY, ANY,
        ],
        out_specs=[
            row(WC), full((40, CH)), full((16, BLOCK)), full((16, WC)), full((ro, D)), full((rg_rows, DI)),
        ],
        out_shape=[
            sds((L, WC), BF16), sds((40, CH), F32), sds((16, BLOCK), F32), sds((16, WC), BF16), sds((ro, D), F32),
            sds((rg_rows, DI), F32),
        ],
        scratch_shapes=[
            pltpu.VMEM((16, CH), F32), pltpu.VMEM((8, CH), F32), pltpu.SemaphoreType.DMA(()), pltpu.SemaphoreType.DMA(()),
            pltpu.VMEM((NSTATE, DI), F32), pltpu.VMEM((T, CH), F32), pltpu.VMEM((BLOCK, DI), BF16), pltpu.VMEM((BLOCK, DI), BF16), pltpu.VMEM((BLOCK, DI), BF16),
            pltpu.VMEM((BLOCK, DI), BF16), pltpu.VMEM((NSTATE, DI), BF16), pltpu.VMEM((8, DI), F32),
            pltpu.VMEM((NSTATE, DI), BF16), pltpu.VMEM((T + 8, CH), F32), pltpu.VMEM((T + 16, CH), F32),
        ] + scatter_scratch(ro, D) + scatter_scratch(rg_rows, DI),
        compiler_params=params(collective_id=4),
        name="third_pass",
    )(act, convin, convin, halo, dt, cum, sig, dcum, mlow, ent, leave, egrad, rg, inc, rows, conv, head, et, go, gg)


def pad_lanes(x, width):
    return jnp.pad(x, ((0, 0), (0, width - x.shape[1])))


def pad_block(x, rows, lanes):
    return jnp.pad(x, ((0, rows - x.shape[0]), (0, lanes - x.shape[1])))


def on_device(
    tokens, cotangent, norm_gain, in_weight, conv_weight, conv_bias, step_bias, decay_log, skip_gain, gate_gain,
    out_weight,
):
    tok, cot = tokens[0], cotangent[0]
    L = tok.shape[0]
    k_rows, c_rows, g_rows = in_weight.shape[0], conv_weight.shape[0], gate_gain.shape[0]
    spare = BLOCK - HEADS
    last_row = jnp.concatenate([norm_gain, gate_gain])[None]
    extra = jnp.concatenate(
        [pad_lanes(conv_weight.T, spare), pad_lanes(conv_bias[None], spare), pad_lanes(last_row, spare)], axis=0
    )
    slab_c = jnp.concatenate([in_weight[:, DI:], pad_block(extra, k_rows, spare)], axis=1)
    buf, halo = gather_weights(slab_c, tok[L - 16 :])
    total = D // k_rows
    wc = buf.reshape(D, WC)
    spread = buf.reshape(total, k_rows, WC)[:, :6, CH + HEADS :].astype(F32)
    conv = jnp.swapaxes(spread[:, :5, :c_rows], 0, 1).reshape(5, total * c_rows)
    conv = jnp.pad(conv, ((0, 3), (0, 0)))
    gain = spread[:, 5, :k_rows].reshape(1, D)
    ggain = spread[:, 5, k_rows : k_rows + g_rows].reshape(1, DI)
    head = pad_lanes(jnp.stack([step_bias, -jnp.exp(decay_log)] + [jnp.zeros_like(step_bias)] * 6), BLOCK)
    skip = jnp.repeat(skip_gain, HEADDIM)[None]
    rows = jnp.concatenate([ggain, skip, jnp.zeros((6, DI), F32)], axis=0)
    et = jnp.asarray(head_columns(), BF16)

    normed, convin, act, dt, cum, sig, bst, leave, tot, hconv, buf_g, buf_o = first_pass(
        tok, halo, wc, gain, conv, head, in_weight[:, :DI], out_weight
    )
    wg, wo = buf_g.reshape(D, DI), buf_o.reshape(DI, D)
    gate, inc = gate_pass(normed, wg, leave, tot)
    mixed, nout, ggrad, mlow, dcum, ent, egrad, rg, leave2, back, cols = second_pass(
        gate, act, dt, cum, bst, inc, tok, cot, wo, rows, et
    )
    g_out, g_gate, later = grads_pass(nout, cot, normed, ggrad, back, tot)
    pg, cgrad, hgrad, tail, out_grad, gate_cols = third_pass(
        act, convin, hconv, dt, cum, sig, dcum, mlow, ent, leave2, egrad, rg, later, rows, conv, head, et, g_out, g_gate
    )
    g_conv = conv_grad(normed, pg, tail)
    cg = cgrad.reshape(5, 8, CH).sum(axis=1)
    hg = hgrad.reshape(2, 8, BLOCK).sum(axis=1)[:, :HEADS]
    gg = cols.reshape(2, 8, DI).sum(axis=1)
    sums = jnp.concatenate([hg[0], hg[1], gg[1].reshape(HEADS, HEADDIM).sum(axis=1)])
    lanes = lambda x: jnp.pad(x, ((0, 0),) * (x.ndim - 1) + ((0, BLOCK - x.shape[-1]),))
    small = jnp.concatenate(
        [
            lanes(jnp.swapaxes(cg.reshape(5, total, c_rows), 0, 1)), jnp.zeros((total, 1, BLOCK), F32),
            lanes(gg[0].reshape(total, 1, g_rows)), jnp.broadcast_to(lanes(sums[None, None]), (total, 1, BLOCK)),
        ],
        axis=1,
    )
    tgrad, conv_cols, out = last_pass(ggrad, pg, tail, tok, cot, wg, wc, gain, small, g_conv)
    in_grad = jnp.concatenate([gate_cols, conv_cols[:, : CH + HEADS]], axis=1)
    return (
        mixed[None], tgrad[None], out[5, :k_rows], in_grad, out[:4, :c_rows].T, out[4, :c_rows],
        out[7, :HEADS], out[7, HEADS : 2 * HEADS], out[7, 2 * HEADS : 3 * HEADS], out[6, :g_rows], out_grad,
    )


def solution(mesh):
    both = ("dp", "seq")
    vec, mat, tok, rep = P(both), P(both, None), P("dp", "seq", None), P()
    return jax.shard_map(
        on_device,
        mesh=mesh,
        in_specs=(tok, tok, vec, mat, mat, vec, rep, rep, rep, vec, mat),
        out_specs=(tok, tok, vec, mat, mat, vec, rep, rep, rep, vec, mat),
        check_vma=False,
    )
```

```python
import functools

import jax
import jax.numpy as jnp
import numpy as np
from jax import lax
from jax.experimental import pallas as pl
from jax.experimental.pallas import tpu as pltpu
from jax.sharding import PartitionSpec as P

D = 768
HEADS = 24
HEADDIM = 64
NSTATE = 128
CONV = 4
BLOCK = 128
DI = 1536
CH = 1792
PAIRS = HEADS // 2
EPS = 1e-05
LOG2E = 1.4426950408889634
F32 = jnp.float32
BF16 = jnp.bfloat16
NT = (((1,), (1,)), ((), ()))
VMEM_LIMIT = 60 * 1024 * 1024


def dot(a, b):
    return jnp.dot(a, b, preferred_element_type=F32)


def dot_nt(a, b):
    return lax.dot_general(a, b, NT, preferred_element_type=F32)


def dot_exact(a, b):
    return jnp.dot(a, b, preferred_element_type=F32, precision=lax.Precision.HIGHEST)


def sigmoid(v):
    return 0.5 * jnp.tanh(0.5 * v) + 0.5


def iota(shape, dim):
    return lax.broadcasted_iota(jnp.int32, shape, dim)


def lane_lo():
    return iota((BLOCK, BLOCK), 1) < HEADDIM


def expand_pair(x, j, lo):
    rows = x.shape[0]
    a = jnp.broadcast_to(x[:, 2 * j : 2 * j + 1], (rows, BLOCK))
    b = jnp.broadcast_to(x[:, 2 * j + 1 : 2 * j + 2], (rows, BLOCK))
    return jnp.where(lo, a, b), a, b


def block_diag(v):
    lo = iota(v.shape, 1) < HEADDIM
    zero = jnp.zeros_like(v)
    return jnp.concatenate([jnp.where(lo, v, zero), jnp.where(lo, zero, v)], axis=0)


def pair(j):
    return slice(j * BLOCK, (j + 1) * BLOCK)


MESH = pl.DeviceIdType.MESH
ANY = pl.BlockSpec(memory_space=pl.ANY)
WC = CH + BLOCK
TN = (((0,), (0,)), ((), ()))


def dot_tn(a, b):
    return lax.dot_general(a, b, TN, preferred_element_type=F32)


def sizes():
    return {"z": lax.axis_size("dp") // 2, "x": 2, "y": lax.axis_size("seq") // 2, "c": 2}


def place():
    dp, seq = lax.axis_index("dp"), lax.axis_index("seq")
    return {"z": dp // 2, "x": lax.rem(dp, 2), "y": seq // 2, "c": lax.rem(seq, 2)}


def device(at):
    return {"dp": at["z"] * 2 + at["x"], "seq": at["y"] * 2 + at["c"]}


def peers(at, axis):
    n = sizes()[axis]
    return [dict(at, **{axis: lax.rem(at[axis] + o, n)}) for o in range(1, n)]


def greet(at, axes, by=0):
    sem = pltpu.get_barrier_semaphore()
    count = 0
    for axis in axes:
        for peer in peers(at, axis):
            pl.semaphore_signal(sem, inc=1, device_id=device(peer), device_id_type=MESH)
            count += 1
    if not by:
        pl.semaphore_wait(sem, count)
        return
    seq, n = lax.axis_index("seq"), lax.axis_size("seq")

    @pl.when((seq + by >= 0) & (seq + by < n))
    def _():
        pl.semaphore_signal(sem, inc=1, device_id={"seq": seq + by}, device_id_type=MESH)

    heard = (seq - by >= 0) & (seq - by < n)

    @pl.when(heard)
    def _():
        pl.semaphore_wait(sem, count + 1)

    @pl.when(jnp.logical_not(heard))
    def _():
        pl.semaphore_wait(sem, count)


def greet_neighbours():
    seq, n = lax.axis_index("seq"), lax.axis_size("seq")
    sem = pltpu.get_barrier_semaphore()

    @pl.when(seq > 0)
    def _():
        pl.semaphore_signal(sem, inc=1, device_id={"seq": seq - 1}, device_id_type=MESH)

    @pl.when(seq < n - 1)
    def _():
        pl.semaphore_signal(sem, inc=1, device_id={"seq": seq + 1}, device_id_type=MESH)

    @pl.when((seq > 0) & (seq < n - 1))
    def _():
        pl.semaphore_wait(sem, 2)

    @pl.when((seq == 0) | (seq == n - 1))
    def _():
        pl.semaphore_wait(sem, 1)


def remote(src, dst, send, recv, peer):
    return pltpu.make_async_remote_copy(
        src_ref=src, dst_ref=dst, send_sem=send, recv_sem=recv, device_id=device(peer), device_id_type=MESH
    )


class Gather:
    def __init__(self, slab, spot, order, sems):
        self.slab, self.spot, self.order = slab, spot, order
        self.send, self.recv = sems
        self.at = place()

    def copies(self, stage):
        at, (a, b) = self.at, self.order
        n = sizes()
        out = []
        every = slice(None)
        nz = n["z"] - 1
        if stage == 0:
            for o, peer in enumerate(peers(at, "z")):
                out.append((self.slab, self.spot(at), o, peer))
        elif stage == 1:
            index = dict(at, z=every)
            out.append((self.spot(index), self.spot(index), nz, peers(at, a)[0]))
        elif stage == 2:
            index = dict(at, z=every)
            index[a] = every
            for o, peer in enumerate(peers(at, b)):
                out.append((self.spot(index), self.spot(index), nz + 1 + o, peer))
            out.append((self.spot(index), self.spot(index), nz + 1 + n[b] - 1, peers(at, "c")[0]))
        else:
            for o in range(1, n[b]):
                index = dict(at, z=every)
                index[a] = every
                index[b] = lax.rem(at[b] + o, n[b])
                out.append((self.spot(index), self.spot(index), nz + 1 + n[b] + o - 1, peers(at, "c")[0]))
        return [remote(s, d, self.send.at[k], self.recv.at[k], p) for s, d, k, p in out]

    def start(self, stage):
        for c in self.copies(stage):
            c.start()

    def wait(self, stage):
        for c in self.copies(stage):
            c.wait()


def spots(buf, lanes=slice(None)):
    return lambda index: buf.at[index["z"], index["x"], index["y"], index["c"], :, lanes]


def gather_sems():
    count = sizes()["z"] + 2 * sizes()["y"] + 4
    return [pltpu.SemaphoreType.DMA((count,)), pltpu.SemaphoreType.DMA((count,))]


class Scatter:
    def __init__(self, grads, order, scratch, own=None, local=None):
        self.grads, self.order, self.own_ref, self.local = grads, order, own, local
        self.rc, self.r1, self.r2, self.rz, self.send, self.recv = scratch
        self.at = place()
        self.own = self

    def spot(self, z, x, y):
        if self.own_ref is not None:
            return self.own_ref.at[z, x, y]
        return self.grads.at[z, x, y, self.at["c"]]

    def add(self, z, x, y, got):
        mine = self.spot(z, x, y)
        mine[...] = (mine[...].astype(F32) + got.astype(F32)).astype(BF16)

    def copies(self, stage):
        at, (a, b) = self.at, self.order
        every = slice(None)
        out = []

        def spot(index):
            return self.spot(index["z"], index["x"], index["y"])

        if stage == 0:
            out.append((self.grads.at[:, :, :, 1 - at["c"]], self.rc, 0, peers(at, "c")[0]))
        elif stage == 1:
            index = {"z": every, "x": every, "y": every}
            index[a] = 1 - at[a]
            out.append((spot(index), self.r1, 1, peers(at, a)[0]))
        elif stage == 2:
            index = {"z": every, a: at[a], b: 1 - at[b]}
            out.append((spot(index), self.r2, 2, peers(at, b)[0]))
        else:
            for o, peer in enumerate(peers(at, "z")):
                out.append((self.spot(peer["z"], at["x"], at["y"]), self.rz.at[o], 3 + o, peer))
        return [remote(s, d, self.send.at[k], self.recv.at[k], p) for s, d, k, p in out]

    def mine(self):
        return pltpu.make_async_copy(self.grads.at[:, :, :, self.at["c"]], self.own_ref, self.local)

    def start(self, stage):
        if stage == 0 and self.own_ref is not None:
            self.mine().start()
        for c in self.copies(stage):
            c.start()

    def finish(self, stage):
        at, (a, b) = self.at, self.order
        for c in self.copies(stage):
            c.wait()
        nz = sizes()["z"]
        if stage == 0:
            if self.own_ref is not None:
                self.mine().wait()

            def body(z, _):
                for x in range(2):
                    for y in range(2):
                        self.add(z, x, y, self.rc[z, x, y])
                return _

        elif stage == 1:

            def body(z, _):
                for k in range(2):
                    index = {a: at[a], b: k}
                    self.add(z, index["x"], index["y"], self.r1[z, k])
                return _

        else:

            def body(z, _):
                self.add(z, at["x"], at["y"], self.r2[z])
                return _

        lax.fori_loop(0, nz, body, 0)

    def result(self):
        for c in self.copies(3):
            c.wait()
        total = self.spot(self.at["z"], self.at["x"], self.at["y"])[...].astype(F32)
        for o in range(sizes()["z"] - 1):
            total = total + self.rz[o].astype(F32)
        return total


def scatter_scratch(rows, width):
    nz = sizes()["z"]
    return [
        pltpu.VMEM((nz, 2, 2, rows, width), BF16), pltpu.VMEM((nz, 2, rows, width), BF16),
        pltpu.VMEM((nz, rows, width), BF16), pltpu.VMEM((nz - 1, rows, width), BF16),
        pltpu.SemaphoreType.DMA((nz + 2,)), pltpu.SemaphoreType.DMA((nz + 2,)),
    ]


NSC = 6


def own_scratch(rows, width):
    return [pltpu.VMEM((sizes()["z"], 2, 2, rows, width), BF16), pltpu.SemaphoreType.DMA(())]


class Chain:
    def __init__(self, leave, inc, decay, bufs, reverse):
        self.leave, self.inc, self.decay, self.reverse = leave, inc, decay, reverse
        self.got, self.put, self.send, self.recv = bufs
        self.n = lax.axis_size("seq")
        seq = lax.axis_index("seq")
        self.rank = self.n - 1 - seq if reverse else seq
        self.to = seq - 1 if reverse else seq + 1

    def copy(self):
        return pltpu.make_async_remote_copy(
            src_ref=self.put, dst_ref=self.got, send_sem=self.send, recv_sem=self.recv,
            device_id={"seq": self.to}, device_id_type=MESH,
        )

    def step(self, k):
        @pl.when(self.rank == k)
        def _():
            if k == 0:
                self.inc[...] = jnp.zeros_like(self.inc)
                self.put[...] = self.leave[...].astype(BF16)
            else:
                self.copy().wait_recv()
                got = self.got[...].astype(F32)
                self.inc[...] = got
                if k < self.n - 1:
                    self.put[...] = (got * self.decay[0:1] + self.leave[...]).astype(BF16)
            if k < self.n - 1:
                self.copy().start()

    def done(self):
        @pl.when(self.rank < self.n - 1)
        def _():
            self.copy().wait_send()


def chain_scratch():
    return [
        pltpu.VMEM((NSTATE, DI), BF16), pltpu.VMEM((NSTATE, DI), BF16), pltpu.SemaphoreType.DMA(()),
        pltpu.SemaphoreType.DMA(()),
    ]


def expand_row(row, dst):
    lo = iota((8, BLOCK), 1) < HEADDIM
    wide = jnp.broadcast_to(row, (8, BLOCK))
    for j in range(PAIRS):
        dst[:, pair(j)] = expand_pair(wide, j, lo)[0]


CHUNKS = ((0, 512), (512, 512), (1024, 512), (1536, 384))
ORDERS = ("xy", "yx", "xy", "yx")


def gate_kernel(normed_ref, wg_ref, cot_ref, wo_ref, gain_ref, leave_ref, tot_ref, gate_ref, ng_ref, inc_ref, decay, *bufs):
    i = pl.program_id(0)
    chain = Chain(leave_ref, inc_ref, decay, bufs, False)
    last = pl.num_programs(0) - 1

    @pl.when(i == 0)
    def _():
        expand_row(jnp.exp2(tot_ref[0:1]), decay)
        greet_neighbours()
        chain.step(0)

    for c in range(DI // 256):
        cs = slice(c * 256, (c + 1) * 256)
        gate_ref[:, cs] = dot(normed_ref[...], wg_ref[:, cs]).astype(BF16)
        ng_ref[:, cs] = (dot_nt(cot_ref[...], wo_ref[cs, :]) * gain_ref[0:1, cs]).astype(BF16)
    for k in range(1, chain.n):
        @pl.when(i == jnp.minimum(k, last))
        def _():
            chain.step(k)

    @pl.when(i == last)
    def _():
        chain.done()


def gate_pass(normed, wg, cot, wo, gain, leave, tot, T=512):
    L = normed.shape[0]
    row = lambda w: pl.BlockSpec((T, w), lambda i: (i, 0))
    return pl.pallas_call(
        gate_kernel,
        grid=(L // T,),
        in_specs=[
            row(D), full((D, DI)), row(D), full((DI, D)), full((8, DI)), full((NSTATE, DI)), full((8, BLOCK)),
        ],
        out_specs=[row(DI), row(DI), full((NSTATE, DI))],
        out_shape=[sds((L, DI), BF16), sds((L, DI), BF16), sds((NSTATE, DI), F32)],
        scratch_shapes=[pltpu.VMEM((8, DI), F32)] + chain_scratch(),
        compiler_params=params(collective_id=2),
        name="gate_pass",
    )(normed, wg, cot, wo, gain, leave, tot)


def grads_kernel(nout_ref, cot_ref, xt_ref, ggrad_ref, back_ref, tot_ref, gout_ref, ggate_ref, inc_ref, decay, *bufs):
    i = pl.program_id(0)
    chain = Chain(back_ref, inc_ref, decay, bufs, True)
    last = pl.num_programs(0) - 1

    @pl.when(i == 0)
    def _():
        expand_row(jnp.exp2(tot_ref[0:1]), decay)
        greet_neighbours()
        chain.step(0)

    gout_ref[...] = dot_tn(nout_ref[...], cot_ref[...]).astype(BF16)
    ggate_ref[...] = dot(xt_ref[...], ggrad_ref[...]).astype(BF16)
    for k in range(1, chain.n):
        @pl.when(i == jnp.minimum(k, last))
        def _():
            chain.step(k)

    @pl.when(i == last)
    def _():
        chain.done()


def grads_pass(nout, cot, xt, ggrad, back, tot):
    L = nout.shape[0]
    col = lambda w: pl.BlockSpec((L, w), lambda i: (0, i))
    return pl.pallas_call(
        grads_kernel,
        grid=(6,),
        in_specs=[
            col(256), full((L, D)), pl.BlockSpec((128, L), lambda i: (i, 0)), full((L, DI)), full((NSTATE, DI)),
            full((8, BLOCK)),
        ],
        out_specs=[
            pl.BlockSpec((256, D), lambda i: (i, 0)), pl.BlockSpec((128, DI), lambda i: (i, 0)), full((NSTATE, DI)),
        ],
        out_shape=[sds((DI, D), BF16), sds((D, DI), BF16), sds((NSTATE, DI), F32)],
        scratch_shapes=[pltpu.VMEM((8, DI), F32)] + chain_scratch(),
        compiler_params=params(collective_id=3),
        name="grads_pass",
    )(nout, cot, xt, ggrad, back, tot)


def last_kernel(
    T, xt_ref, pg_any, tail_ref, ggrad_ref, tok_ref, cot_ref, wg_ref, wc_ref, gain_ref, small_ref,
    tgrad_ref, gout_ref, sums_ref, pg, g0, g1, g2, g3, lsem, smalls, ssend, srecv, *scratch,
):
    i = pl.program_id(0)
    nc = len(CHUNKS)
    grads = (g0, g1, g2, g3)
    sc = [Scatter(grads[k], ORDERS[k][::-1], scratch[NSC * k : NSC * k + NSC]) for k in range(nc)]
    dp, seq = lax.axis_index("dp"), lax.axis_index("seq")
    n_dp, n_seq = lax.axis_size("dp"), lax.axis_size("seq")
    total = n_dp * n_seq
    me = dp * n_seq + seq
    L = pg.shape[0]

    def load(k):
        lanes = pl.ds(CHUNKS[k][0], CHUNKS[k][1])
        return pltpu.make_async_copy(pg_any.at[:, lanes], pg.at[:, lanes], lsem.at[k])

    def far(o):
        r = lax.rem(me + o, total)
        return {"dp": r // n_seq, "seq": lax.rem(r, n_seq)}

    def small(o):
        r = lax.rem(me + o, total)
        return pltpu.make_async_remote_copy(
            src_ref=small_ref.at[r], dst_ref=smalls.at[o - 1], send_sem=ssend.at[o - 1], recv_sem=srecv.at[o - 1],
            device_id=far(o), device_id_type=MESH,
        )

    @pl.when(i == 0)
    def _():
        for k in range(nc):
            load(k).start()
        sem = pltpu.get_barrier_semaphore()
        for o in range(1, total):
            pl.semaphore_signal(sem, inc=1, device_id=far(o), device_id_type=MESH)

    for k in range(nc):
        @pl.when(i == k)
        def _():
            lane, width = CHUNKS[k]
            load(k).wait()
            skip = BLOCK if k == 0 else 0
            pg[L - 16 :, lane + skip : lane + width] = tail_ref[:, lane + skip : lane + width]
            rows = grads[k].shape[4]
            for q in range(2):
                half = D // 2
                g = dot(xt_ref[q * half : (q + 1) * half], pg[:, lane : lane + width])
                for r in range(half // rows):
                    s = r + q * (half // rows)
                    grads[k][s // 8, (s // 4) % 2, (s // 2) % 2, s % 2] = g[r * rows : (r + 1) * rows].astype(BF16)
            if k == 0:
                pl.semaphore_wait(pltpu.get_barrier_semaphore(), total - 1)
                sc[0].start(0)
                for o in range(1, total):
                    small(o).start()
            else:
                sc[k - 1].finish(0)
                sc[k - 1].start(1)
                sc[k].start(0)

    @pl.when(i >= nc)
    def _():
        r0 = pl.multiple_of((i - nc) * T, T)
        u = dot_nt(ggrad_ref[...], wg_ref[...]) + dot_nt(pg[pl.ds(r0, T), :], wc_ref[...])
        u = u * gain_ref[0:1]
        x = tok_ref[...].astype(F32)
        inv = lax.rsqrt(jnp.mean(x * x, axis=-1, keepdims=True) + EPS)
        xi = x * inv
        coef = inv * jnp.mean(u * xi, axis=-1, keepdims=True)
        tgrad_ref[...] = (cot_ref[...].astype(F32) + inv * u - xi * coef).astype(BF16)

    def after(step, what):
        @pl.when(i == step)
        def _():
            for k, stage in what:
                sc[k].finish(stage)
                sc[k].start(stage + 1)

    after(nc, [(3, 0), (0, 1)])
    after(nc + 1, [(1, 1)])
    after(nc + 2, [(2, 1), (0, 2)])
    after(nc + 3, [(3, 1), (1, 2), (2, 2), (3, 2)])

    @pl.when(i == pl.num_programs(0) - 1)
    def _():
        for o in range(1, total):
            small(o).wait()
        acc = small_ref[me]
        for o in range(1, total):
            acc = acc + smalls[o - 1]
        sums_ref[...] = acc
        for k in range(nc):
            lane, width = CHUNKS[k]
            gout_ref[:, lane : lane + width] = sc[k].result()


def last_pass(xt, pg, tail, ggrad, tok, cot, wg, wc, gain, small, T=512):
    L = tok.shape[0]
    n = sizes()
    nc = len(CHUNKS)
    total = lax.axis_size("dp") * lax.axis_size("seq")
    rows = D // total
    row = lambda w: pl.BlockSpec((T, w), lambda i: (jnp.maximum(i - nc, 0), 0))
    scratch = []
    for _, w in CHUNKS:
        scratch += scatter_scratch(rows, w)
    return pl.pallas_call(
        functools.partial(last_kernel, T),
        grid=(nc + L // T,),
        in_specs=[
            once((D, L)), ANY, full((16, WC)), row(DI), row(D), row(D), once((D, DI)), once((D, WC)),
            once((8, D)), once((total, 8, BLOCK)),
        ],
        out_specs=[row(D), full((rows, WC)), full((8, BLOCK))],
        out_shape=[sds((L, D), BF16), sds((rows, WC), F32), sds((8, BLOCK), F32)],
        scratch_shapes=[pltpu.VMEM((L, WC), BF16)]
        + [pltpu.VMEM((n["z"], 2, n["y"], 2, rows, w), BF16) for _, w in CHUNKS]
        + [
            pltpu.SemaphoreType.DMA((nc,)), pltpu.VMEM((total - 1, 8, BLOCK), F32),
            pltpu.SemaphoreType.DMA((total - 1,)), pltpu.SemaphoreType.DMA((total - 1,)),
        ] + scratch,
        compiler_params=params(collective_id=5),
        name="last_pass",
    )(xt, pg, tail, ggrad, tok, cot, wg, wc, gain, small)


def finish_kernel(
    gate_ref, conv_ref, out_ref, sums_ref, w_ref, wo_ref, gain_ref, ggain_ref,
    in_grad, ngain, ggain, taps, bias, step, decay, skip,
):
    conv = conv_ref[...]
    raw = jnp.concatenate([gate_ref[...], conv[:, BLOCK:], conv[:, :HEADS]], axis=1)
    in_grad[...] = raw
    ngain[...] = jnp.sum(raw * w_ref[...].astype(F32), axis=1) / gain_ref[...]
    o = out_ref[...]
    ggain[...] = jnp.sum(o * wo_ref[...].astype(F32), axis=1) / ggain_ref[...]
    s = sums_ref[...]
    n = bias.shape[0]
    taps[...] = s.T[:n, :CONV]
    bias[...] = s[4, :n]
    step[...] = s[7, :HEADS]
    decay[...] = s[7, HEADS : 2 * HEADS]
    skip[...] = s[7, 2 * HEADS : 3 * HEADS]


def finish_pass(gate_cols, conv_cols, out_raw, sums, w, wo, gain, ggain, channels):
    vm = pl.BlockSpec(memory_space=pltpu.VMEM)
    vec = lambda n: sds((n,), F32)
    return pl.pallas_call(
        finish_kernel,
        in_specs=[vm] * 8,
        out_specs=[vm] * 8,
        out_shape=[
            sds(w.shape, F32), vec(w.shape[0]), vec(wo.shape[0]), sds((channels, CONV), F32),
            vec(channels), vec(HEADS), vec(HEADS), vec(HEADS),
        ],
        name="finish_pass",
    )(gate_cols, conv_cols, out_raw, sums, w, wo, gain, ggain)


def rms_rows(tok, gain):
    x = tok.astype(F32)
    return (x * lax.rsqrt(jnp.mean(x * x, axis=-1, keepdims=True) + EPS) * gain).astype(BF16)


def first_kernel(
    T, slab, small, tok_any, head_ref, sg_ref, so_ref,
    xhat_any, xt_any, wc_any, p_any, hp_ref, conv_ref, gain_ref, ggain_ref,
    act_ref, dt_ref, cum_ref, sig_ref, bst_ref, leave_ref, tot_ref, bg_ref, bo_ref,
    tok, halo, xhat, xt, wc, wide, p, smalls, b0, b1, b2, b3, ext, state, weighted, lsem, hsend, hrecv, ssend, srecv,
    *sems,
):
    i = pl.program_id(0)
    steps = pl.num_programs(0)
    at = place()
    seq, n = lax.axis_index("seq"), lax.axis_size("seq")
    L = tok.shape[0]
    bufs = (b0, b1, b2, b3)
    nc = len(CHUNKS)
    gets = []
    for (lane, width), order, buf, k in zip(CHUNKS, ORDERS, bufs, range(nc)):
        gets.append(Gather(slab.at[:, pl.ds(lane, width)], spots(buf), order, sems[2 * k : 2 * k + 2]))
    for k in range(4):
        src, buf = ((sg_ref, bg_ref), (so_ref, bo_ref))[k % 2]
        width = src.shape[1] // 2
        lanes = pl.ds((k // 2) * width, width)
        q = 2 * (nc + k)
        gets.append(Gather(src.at[:, lanes], spots(buf, lanes), ORDERS[k], sems[q : q + 2]))
    own = []
    for k, (src, buf) in enumerate(((sg_ref, bg_ref), (so_ref, bo_ref))):
        own.append(pltpu.make_async_copy(src, buf.at[at["z"], at["x"], at["y"], at["c"]], lsem.at[k]))
    halo_copy = pltpu.make_async_remote_copy(
        src_ref=tok_any.at[pl.ds(L - 16, 16)], dst_ref=halo, send_sem=hsend, recv_sem=hrecv,
        device_id={"seq": seq + 1}, device_id_type=MESH,
    )
    outs = [pltpu.make_async_copy(xhat, xhat_any, lsem.at[3]), pltpu.make_async_copy(xt, xt_any, lsem.at[4])]
    for k, (lane, width) in enumerate(CHUNKS):
        for j, (src, dst) in enumerate(((p, p_any), (wc, wc_any))):
            lanes = pl.ds(lane, width)
            outs.append(pltpu.make_async_copy(src.at[:, lanes], dst.at[:, lanes], lsem.at[5 + 2 * k + j]))

    def advance(*what):
        for k, stage in what:
            if stage > 0:
                gets[k].wait(stage - 1)
            if stage < 4:
                gets[k].start(stage)

    def project(k):
        lane, width = CHUNKS[k]
        buf = bufs[k]
        nz, rows_k = buf.shape[0], buf.shape[4]
        for z in range(nz):
            for m in range(8):
                r = z * 8 + m
                wide[r * rows_k : (r + 1) * rows_k, :width] = buf[z, m // 4, (m // 2) % 2, m % 2].astype(F32)
        wc[:, lane : lane + width] = wide[:, :width].astype(BF16)
        for r in range(L // 512):
            rows = slice(r * 512, (r + 1) * 512)
            p[rows, lane : lane + width] = dot(xhat[rows], wc[:, lane : lane + width]).astype(BF16)
        hp_ref[:, lane : lane + width] = dot(halo[...], wc[:, lane : lane + width]).astype(BF16)
        for c in outs[2 + 2 * k : 4 + 2 * k]:
            c.start()

    @pl.when(i == 0)
    def _():
        dp = lax.axis_index("dp")
        n_dp = lax.axis_size("dp")
        total = n_dp * n
        me = dp * n + seq
        load = pltpu.make_async_copy(tok_any, tok, lsem.at[2])
        load.start()
        sem = pltpu.get_barrier_semaphore()

        def far(o):
            r = lax.rem(me + o, total)
            return {"dp": r // n, "seq": lax.rem(r, n)}

        for o in range(1, total):
            pl.semaphore_signal(sem, inc=1, device_id=far(o), device_id_type=MESH)
        pl.semaphore_wait(sem, total - 1)
        advance((0, 0), (1, 0))

        @pl.when(seq < n - 1)
        def _():
            halo_copy.start()

        sends = []
        for o in range(1, total):
            c = pltpu.make_async_remote_copy(
                src_ref=small, dst_ref=smalls.at[me], send_sem=ssend.at[o - 1], recv_sem=srecv.at[o - 1],
                device_id=far(o), device_id_type=MESH,
            )
            c.start()
            sends.append(c)
        for c in own:
            c.start()
        smalls[me] = small[...]
        for (lane, width), buf in zip(CHUNKS, bufs):
            buf[at["z"], at["x"], at["y"], at["c"]] = slab[:, lane : lane + width]
        conv_ref[...] = jnp.zeros_like(conv_ref)
        state[...] = jnp.zeros_like(state)
        tot_ref[...] = jnp.zeros_like(tot_ref)
        load.wait()
        for c in sends:
            c.wait()
        taps, ks, gs = CH // total, D // total, DI // total
        for r in range(total):
            conv_ref[0:5, r * taps : (r + 1) * taps] = smalls[r, 0:5, :taps]
            gain_ref[:, r * ks : (r + 1) * ks] = jnp.broadcast_to(smalls[r, 5:6, :ks], (8, ks))
            ggain_ref[:, r * gs : (r + 1) * gs] = jnp.broadcast_to(smalls[r, 6:7, :gs], (8, gs))

        def norm(r, _):
            rows = pl.ds(pl.multiple_of(r * 256, 256), 256)
            h = rms_rows(tok[rows], gain_ref[0:1])
            xhat[rows] = h
            xt[:, rows] = h.T
            return _

        advance((0, 1), (2, 0), (1, 1), (3, 0))
        lax.fori_loop(0, L // 512, norm, 0)
        advance((0, 2), (1, 2))
        lax.fori_loop(L // 512, L // 256, norm, 0)
        for c in outs[:2]:
            c.start()

        @pl.when(seq == 0)
        def _():
            halo[...] = jnp.zeros_like(halo)

        @pl.when(seq > 0)
        def _():
            halo_copy.wait_recv()

        @pl.when(seq < n - 1)
        def _():
            halo_copy.wait_send()

        halo[...] = rms_rows(halo[...], gain_ref[0:1])
        for c in own:
            c.wait()
        advance((2, 1), (4, 0), (3, 1), (5, 0), (0, 3), (1, 3), (2, 2), (3, 2), (0, 4))
        project(0)
        advance((1, 4), (4, 1), (6, 0), (5, 1), (7, 0))
        project(1)
        advance((2, 3), (3, 3), (2, 4))
        project(2)
        advance((3, 4), (4, 2), (5, 2))
        project(3)
        ext[0:8] = hp_ref[...].astype(F32)[8:16, BLOCK:]

    def tile(r0):
        for c in range(CH // 256):
            cs = slice(c * 256, (c + 1) * 256)
            ext[8 : 8 + T, cs] = p[pl.ds(r0, T), BLOCK + c * 256 : BLOCK + (c + 1) * 256].astype(F32)
            total = conv_ref[4:5, cs]
            for k in range(CONV):
                total = total + ext[5 + k : 5 + k + T, cs] * conv_ref[k : k + 1, cs]
            act_ref[:, cs] = (total * sigmoid(total)).astype(BF16)
        raw = p[pl.ds(r0, T), :BLOCK].astype(F32) + head_ref[0:1]
        dt_all = jnp.maximum(raw, 0.0) + jnp.log1p(jnp.exp(-jnp.abs(raw)))
        dt_ref[...] = dt_all
        sig_ref[...] = sigmoid_exact(raw)
        tril = (iota((BLOCK, BLOCK), 0) >= iota((BLOCK, BLOCK), 1)).astype(F32)
        lo = lane_lo()
        for blk in range(T // BLOCK):
            rows = slice(blk * BLOCK, (blk + 1) * BLOCK)
            dt = dt_all[rows]
            cum = dot_exact(tril, dt * head_ref[1:2]) * LOG2E
            cum_ref[rows] = cum
            end = cum[BLOCK - 1 : BLOCK]
            tot_ref[...] += jnp.broadcast_to(end, tot_ref.shape)
            wfac = jnp.exp2(end - cum) * dt
            decay = jnp.broadcast_to(jnp.exp2(end), (8, BLOCK))
            write_t = act_ref[rows, DI : DI + NSTATE].T
            for j in range(PAIRS):
                w, _, _ = expand_pair(wfac, j, lo)
                weighted[:, pair(j)] = (act_ref[rows, pair(j)].astype(F32) * w).astype(BF16)
            for q in range(PAIRS // 2):
                cs = slice(q * 256, (q + 1) * 256)
                new = dot(write_t, weighted[:, cs])
                bst_ref[blk, :, cs] = new.astype(BF16)
                d0, _, _ = expand_pair(decay, 2 * q, lo[:8])
                d1, _, _ = expand_pair(decay, 2 * q + 1, lo[:8])
                dd = jnp.concatenate([d0, d1], axis=1)[0:1]
                state[:, cs] = state[:, cs] * dd + new

    def after(step, *what):
        @pl.when(i == step)
        def _():
            advance(*what)

    after(2, (6, 1), (7, 1))
    after(4, (4, 3), (5, 3), (6, 2), (7, 2))

    @pl.when(i > 1)
    def _():
        ext[0:8] = ext[T : T + 8]

    @pl.when(i > 0)
    def _():
        tile(pl.multiple_of((i - 1) * T, T))

    @pl.when(i == steps - 1)
    def _():
        leave_ref[...] = state[...]
        advance((4, 4), (5, 4), (6, 3), (7, 3), (6, 4), (7, 4))
        for c in outs:
            c.wait()


def sigmoid_exact(v):
    return 1.0 / (1.0 + jnp.exp(-v))


def second_kernel(
    T, gate_s, ng, act_ref, dt_ref, cum_ref, bst_ref, inc_ref, tok_ref, wo_ref, row_ref, et_ref,
    mixed_ref, nout_ref, ggrad_ref, mlow_ref, dcum_ref, ent_ref, egrad_ref, rg_ref, leave_ref, back_ref, cols_ref,
    ms, growth, rlow, prod, plow, state, exg, lows,
):
    i = pl.program_id(0)

    @pl.when(i == 0)
    def _():
        state[...] = inc_ref[...]
        exg[...] = jnp.ones_like(exg)
        back_ref[...] = jnp.zeros_like(back_ref)
        cols_ref[...] = jnp.zeros_like(cols_ref)

    lo = lane_lo()
    lower = iota((BLOCK, BLOCK), 0) >= iota((BLOCK, BLOCK), 1)
    nblk = T // BLOCK
    for blk in range(nblk):
        rows = slice(blk * BLOCK, (blk + 1) * BLOCK)
        cum = cum_ref[rows]
        cum_t = cum.T
        dt = dt_ref[rows]
        write = act_ref[rows, DI : DI + NSTATE]
        read = act_ref[rows, DI + NSTATE :]
        inner = jnp.where(lower, dot_nt(read, write), 0.0)
        lows[blk] = state[...].astype(BF16)
        ent_ref[blk] = lows[blk]
        for j in range(PAIRS):
            cols, a, b = expand_pair(cum, j, lo)
            ga = jnp.exp2(jnp.minimum(a - cum_t[2 * j : 2 * j + 1], 0.0)) * inner
            gb = jnp.exp2(jnp.minimum(b - cum_t[2 * j + 1 : 2 * j + 2], 0.0)) * inner
            scores = jnp.concatenate([ga.astype(BF16), gb.astype(BF16)], axis=1)
            vals = act_ref[rows, pair(j)].astype(F32)
            dtp, _, _ = expand_pair(dt, j, lo)
            vdt = (vals * dtp).astype(BF16)
            grow = jnp.exp2(cols)
            growth[rows, pair(j)] = grow
            diag = dot(scores, block_diag(vdt))
            out = dot(read, lows[blk, :, pair(j)])
            ms[rows, pair(j)] = diag + grow * out + row_ref[0:1, pair(j)] * vals
            dec = grow[BLOCK - 1 : BLOCK]
            state[:, pair(j)] = state[:, pair(j)] * dec + bst_ref[blk, :, pair(j)].astype(F32)

    sq = jnp.zeros((T, BLOCK), F32)
    ug = jnp.zeros((T, BLOCK), F32)
    for j in range(PAIRS):
        g = gate_s[:, pair(j)].astype(F32)
        gated = ms[:, pair(j)] * (g * sigmoid(g))
        sq = sq + gated * gated
        ug = ug + gated * ng[:, pair(j)].astype(F32)
    inv = lax.rsqrt(jnp.sum(sq, axis=-1, keepdims=True) * (1.0 / DI) + EPS)
    coef = jnp.sum(ug, axis=-1, keepdims=True) * (1.0 / DI) * (inv * inv * inv)
    for j in range(PAIRS):
        g = gate_s[:, pair(j)].astype(F32)
        sg = sigmoid(g)
        silu = g * sg
        m = ms[:, pair(j)]
        gated = m * silu
        nout_ref[:, pair(j)] = (gated * inv * row_ref[1:2, pair(j)]).astype(BF16)
        dg = inv * ng[:, pair(j)].astype(F32) - gated * coef
        low = (dg * silu).astype(BF16)
        mlow_ref[:, pair(j)] = low
        ggrad_ref[:, pair(j)] = (dg * m * (sg + silu * (1.0 - sg))).astype(BF16)
        vals = act_ref[:, pair(j)].astype(F32)
        lowf = low.astype(F32)
        mv = lowf * vals
        pr = lowf * m - row_ref[0:1, pair(j)] * mv
        hi = pr.astype(BF16)
        prod[:, pair(j)] = hi
        plow[:, pair(j)] = (pr - hi.astype(F32)).astype(BF16)
        rlow[:, pair(j)] = (lowf * growth[:, pair(j)]).astype(BF16)
        cols_ref[:, pair(j)] += jnp.sum(mv.reshape(T // 8, 8, BLOCK), axis=0)
    dcum_ref[...] = dot(prod[...], et_ref[...]) + dot(plow[...], et_ref[...])
    mixed_ref[...] = (tok_ref[...].astype(F32) + dot(nout_ref[...], wo_ref[...])).astype(BF16)
    for blk in range(nblk):
        rows = slice(blk * BLOCK, (blk + 1) * BLOCK)
        read_t = act_ref[rows, DI + NSTATE :].T
        for q in range(PAIRS // 2):
            cs = slice(q * 256, (q + 1) * 256)
            eg = dot(read_t, rlow[rows, cs])
            egrad_ref[blk, :, cs] = eg.astype(BF16)
            back_ref[:, cs] += eg * exg[0:1, cs]
        exg[...] = exg[...] * growth[blk * BLOCK + BLOCK - 1 : blk * BLOCK + BLOCK, :]
        rg_ref[rows] = dot_nt(rlow[rows, :], lows[blk])

    @pl.when(i == pl.num_programs(0) - 1)
    def _():
        leave_ref[...] = state[...].astype(BF16)


def third_kernel(
    T, act_ref, convin_ref, prev_ref, halo_ref, dt_ref, cum_ref, sig_ref, dcum_ref, mlow_ref, ent_ref, leave_ref,
    egrad_ref, rg_ref, inc_ref, row_ref, conv_ref, head_ref, et_ref, go_ref, gg_ref,
    pg_ref, cgrad_ref, hgrad_ref, tail_ref, so_ref, sg_ref,
    glast, gafter, hsend, hrecv, carry, dact, vprod, prod, plow, weighted, lows, dec, nxt, gext, cext, *scratch,
):
    i = pl.program_id(0)
    steps = pl.num_programs(0)
    sca = Scatter(go_ref, "yx", scratch[2 : 2 + NSC], *scratch[:2])
    scb = Scatter(gg_ref, "xy", scratch[4 + NSC :], *scratch[2 + NSC : 4 + NSC])
    seq, nseq = lax.axis_index("seq"), lax.axis_size("seq")
    after = pltpu.make_async_remote_copy(
        src_ref=gext.at[0:8], dst_ref=gafter, send_sem=hsend, recv_sem=hrecv, device_id={"seq": seq - 1},
        device_id_type=MESH,
    )

    @pl.when(i == 0)
    def _():
        greet(place(), "zxyc", 1)
        sca.start(0)
        scb.start(0)

    for stage, when in enumerate((1, 3, 5)):
        @pl.when(i == when)
        def _():
            sca.finish(stage)
            sca.start(stage + 1)
            scb.finish(stage)
            scb.start(stage + 1)

    @pl.when(i == steps - 1)
    def _():
        so_ref[...] = sca.result()
        sg_ref[...] = scb.result()

    @pl.when(i == 0)
    def _():
        carry[...] = inc_ref[...]
        nxt[...] = leave_ref[...]
        cgrad_ref[...] = jnp.zeros_like(cgrad_ref)
        hgrad_ref[...] = jnp.zeros_like(hgrad_ref)
        gext[T : T + 8] = jnp.zeros((8, CH), F32)

    @pl.when(i > 0)
    def _():
        gext[T : T + 8] = gext[0:8]

    @pl.when(i == steps - 1)
    def _():
        cext[0:16] = halo_ref[:, BLOCK:].astype(F32)

    @pl.when(i < steps - 1)
    def _():
        cext[0:16] = prev_ref[:, BLOCK:].astype(F32)

    lo = lane_lo()
    upper = iota((BLOCK, BLOCK), 0) <= iota((BLOCK, BLOCK), 1)
    triu = upper.astype(F32)
    last = iota((BLOCK, BLOCK), 0) == BLOCK - 1
    for blk in reversed(range(T // BLOCK)):
        rows = slice(blk * BLOCK, (blk + 1) * BLOCK)
        cum = cum_ref[rows]
        cum_t = cum.T
        dt = dt_ref[rows]
        end = cum[BLOCK - 1 : BLOCK]
        rest = end - cum
        write = act_ref[rows, DI : DI + NSTATE]
        read = act_ref[rows, DI + NSTATE :]
        inner = jnp.where(upper, dot_nt(write, read), 0.0)
        lows[...] = carry[...].astype(BF16)
        acc = jnp.zeros((BLOCK, BLOCK), F32)
        for j in range(PAIRS):
            cols, a, b = expand_pair(cum, j, lo)
            wexp, _, _ = expand_pair(rest, j, lo)
            wexp = jnp.exp2(wexp)
            da = jnp.exp2(jnp.minimum(cum_t[2 * j : 2 * j + 1] - a, 0.0))
            db = jnp.exp2(jnp.minimum(cum_t[2 * j + 1 : 2 * j + 2] - b, 0.0))
            scores = jnp.concatenate([(da * inner).astype(BF16), (db * inner).astype(BF16)], axis=1)
            m = mlow_ref[rows, pair(j)]
            diag = block_diag(m)
            z = dot(scores, diag)
            vals = act_ref[rows, pair(j)].astype(F32)
            dtp, _, _ = expand_pair(dt, j, lo)
            vdt = vals * dtp
            vdtb = vdt.astype(BF16)
            wtb = (vdt * wexp).astype(BF16)
            g = dot_nt(vdtb, diag)
            acc = acc + g[:, :BLOCK] * da + g[:, BLOCK:] * db
            wg = dot(write, lows[:, pair(j)])
            pr = vdtb.astype(F32) * z + wtb.astype(F32) * wg
            z = z + wg * wexp
            dact[rows, pair(j)] = row_ref[0:1, pair(j)] * m.astype(F32) + dtp * z
            vprod[:, pair(j)] = (vals * z).astype(BF16)
            hi = pr.astype(BF16)
            prod[:, pair(j)] = hi
            plow[:, pair(j)] = (pr - hi.astype(F32)).astype(BF16)
            weighted[:, pair(j)] = wtb
            dec[0:1, pair(j)] = jnp.exp2(cols[BLOCK - 1 : BLOCK])
        low = jnp.where(upper, acc, 0.0).astype(BF16)
        dact[rows, DI : DI + NSTATE] = dot_nt(weighted[...], lows[...]) + dot(low, read)
        dact[rows, DI + NSTATE :] = rg_ref[rows] + dot(low.T, write)
        c = dot(vprod[...], et_ref[...])
        used = dot(prod[...], et_ref[...]) + dot(plow[...], et_ref[...])
        ends = jnp.sum((lows[...].astype(F32) * nxt[...].astype(F32)).reshape(16, 8, DI), axis=0)
        ends_hi = ends.astype(BF16)
        ends_lo = (ends - ends_hi.astype(F32)).astype(BF16)
        de = jnp.sum(dot(ends_hi, et_ref[...]) + dot(ends_lo, et_ref[...]), axis=0, keepdims=True)
        dc = dcum_ref[rows] - used + jnp.where(last, de, 0.0)
        da_log = dot_exact(triu, dc)
        draw = (c + da_log * head_ref[1:2]) * sig_ref[rows]
        pg_ref[rows, :BLOCK] = draw.astype(BF16)
        hgrad_ref[0:8] += jnp.sum(draw.reshape(16, 8, BLOCK), axis=0)
        hgrad_ref[8:16] += jnp.sum((da_log * dt).reshape(16, 8, BLOCK), axis=0) * head_ref[1:2]
        nxt[...] = ent_ref[blk]
        for q in range(PAIRS // 2):
            cs = slice(q * 256, (q + 1) * 256)
            carry[:, cs] = carry[:, cs] * dec[0:1, cs] + egrad_ref[blk, :, cs].astype(F32)

    for c in range(CH // 128):
        cs = slice(c * 128, (c + 1) * 128)
        ps = slice(BLOCK + c * 128, BLOCK + (c + 1) * 128)
        cext[16 : 16 + T, cs] = convin_ref[:, ps].astype(F32)
        taps = [cext[13 + k : 13 + k + T, cs] for k in range(CONV)]
        pre = conv_ref[4:5, cs]
        for k in range(CONV):
            pre = pre + taps[k] * conv_ref[k : k + 1, cs]
        sg = sigmoid(pre)
        g = dact[:, cs] * (sg * (1.0 + pre * (1.0 - sg)))
        gext[0:T, cs] = g
        for k in range(CONV):
            cgrad_ref[8 * k : 8 * k + 8, cs] += jnp.sum((g * taps[k]).reshape(T // 8, 8, BLOCK), axis=0)
        cgrad_ref[32:40, cs] += jnp.sum(g.reshape(T // 8, 8, BLOCK), axis=0)
        back = g * conv_ref[3:4, cs]
        for k in range(CONV - 1):
            back = back + gext[3 - k : 3 - k + T, cs] * conv_ref[k : k + 1, cs]
        pg_ref[:, ps] = back.astype(BF16)

        @pl.when(i == 0)
        def _():
            glast[:, cs] = back[T - 16 :]

    @pl.when(i == steps - 1)
    def _():
        @pl.when(seq > 0)
        def _():
            after.start()

        @pl.when(seq == nseq - 1)
        def _():
            gafter[...] = jnp.zeros_like(gafter)

        @pl.when(seq < nseq - 1)
        def _():
            after.wait_recv()

        rows16 = iota((16, CH), 0)
        tail = glast[...]
        for i3 in range(CONV - 1):
            fix = jnp.zeros((1, CH), F32)
            for k in range(i3 + 1):
                fix = fix + conv_ref[k : k + 1] * gafter[i3 - k : i3 - k + 1]
            tail = tail + jnp.where(rows16 == 13 + i3, fix, 0.0)
        tail_ref[:, BLOCK:] = tail.astype(BF16)
        tail_ref[:, :BLOCK] = jnp.zeros((16, BLOCK), BF16)

        @pl.when(seq > 0)
        def _():
            after.wait_send()


def once(shape):
    return pl.BlockSpec(shape, lambda i: (0,) * len(shape), pipeline_mode=pl.Buffered(1))


def full(shape):
    return pl.BlockSpec(shape, lambda i: (0,) * len(shape))


def params(collective_id=None):
    return pltpu.CompilerParams(
        dimension_semantics=("arbitrary",), vmem_limit_bytes=VMEM_LIMIT, collective_id=collective_id,
        has_side_effects=collective_id is not None,
    )


def head_columns():
    et = np.zeros((DI, BLOCK), np.float32)
    et[np.arange(DI), np.arange(DI) // HEADDIM] = 1.0
    return et


def sds(shape, dtype):
    return jax.ShapeDtypeStruct(shape, dtype)


def first_pass(slab, small, tok, head, slab_g, slab_o, T=256):
    L = tok.shape[0]
    nb, per = L // BLOCK, T // BLOCK
    n = sizes()
    k_rows = slab.shape[0]
    total = lax.axis_size("dp") * lax.axis_size("seq")
    row = lambda w: pl.BlockSpec((T, w), lambda i: (jnp.maximum(i - 1, 0), 0))
    dims = (n["z"], n["x"], n["y"], n["c"])
    sems = []
    for _ in range(len(CHUNKS) + 4):
        sems += gather_sems()
    return pl.pallas_call(
        functools.partial(first_kernel, T),
        grid=(1 + L // T,),
        in_specs=[once(slab.shape), once((8, BLOCK)), ANY, once((8, BLOCK)), ANY, ANY],
        out_specs=[
            ANY, ANY, ANY, ANY, full((16, WC)), full((8, CH)), full((8, D)), full((8, DI)),
            row(CH), row(BLOCK), row(BLOCK), row(BLOCK),
            pl.BlockSpec((per, NSTATE, DI), lambda i: (jnp.maximum(i - 1, 0), 0, 0)), full((NSTATE, DI)),
            full((8, BLOCK)), ANY, ANY,
        ],
        out_shape=[
            sds((L, D), BF16), sds((D, L), BF16), sds((D, WC), BF16), sds((L, WC), BF16), sds((16, WC), BF16),
            sds((8, CH), F32), sds((8, D), F32), sds((8, DI), F32),
            sds((L, CH), BF16), sds((L, BLOCK), F32), sds((L, BLOCK), F32), sds((L, BLOCK), F32),
            sds((nb, NSTATE, DI), BF16), sds((NSTATE, DI), F32), sds((8, BLOCK), F32),
            sds(dims + slab_g.shape, BF16), sds(dims + slab_o.shape, BF16),
        ],
        scratch_shapes=[
            pltpu.VMEM((L, D), BF16), pltpu.VMEM((16, D), BF16), pltpu.VMEM((L, D), BF16), pltpu.VMEM((D, L), BF16),
            pltpu.VMEM((D, WC), BF16), pltpu.VMEM((D, 512), F32), pltpu.VMEM((L, WC), BF16),
            pltpu.VMEM((total, 8, BLOCK), F32),
        ] + [pltpu.VMEM(dims + (k_rows, w), BF16) for _, w in CHUNKS] + [
            pltpu.VMEM((T + 8, CH), F32), pltpu.VMEM((NSTATE, DI), F32), pltpu.VMEM((BLOCK, DI), BF16),
            pltpu.SemaphoreType.DMA((5 + 2 * len(CHUNKS),)), pltpu.SemaphoreType.DMA(()), pltpu.SemaphoreType.DMA(()),
            pltpu.SemaphoreType.DMA((total - 1,)), pltpu.SemaphoreType.DMA((total - 1,)),
        ] + sems,
        compiler_params=params(collective_id=1),
        name="first_pass",
    )(slab, small, tok, head, slab_g, slab_o)


def second_pass(gate, ng, act, dt, cum, bst, inc, tok, wo, rows, et, T=256):
    L = tok.shape[0]
    nb, per = L // BLOCK, T // BLOCK
    row = lambda w: pl.BlockSpec((T, w), lambda i: (i, 0))
    blk = pl.BlockSpec((per, NSTATE, DI), lambda i: (i, 0, 0))
    return pl.pallas_call(
        functools.partial(second_kernel, T),
        grid=(L // T,),
        in_specs=[
            row(DI), row(DI), row(CH), row(BLOCK), row(BLOCK), blk, full((NSTATE, DI)), row(D), full((DI, D)), full((8, DI)), full((DI, BLOCK)),
        ],
        out_specs=[
            row(D), row(DI), row(DI), row(DI), row(BLOCK), blk, blk, row(BLOCK), full((NSTATE, DI)),
            full((NSTATE, DI)), full((8, DI)),
        ],
        out_shape=[
            sds((L, D), BF16), sds((L, DI), BF16), sds((L, DI), BF16), sds((L, DI), BF16), sds((L, BLOCK), F32),
            sds((nb, NSTATE, DI), BF16), sds((nb, NSTATE, DI), BF16), sds((L, BLOCK), F32), sds((NSTATE, DI), BF16),
            sds((NSTATE, DI), F32), sds((8, DI), F32),
        ],
        scratch_shapes=[
            pltpu.VMEM((T, DI), F32), pltpu.VMEM((T, DI), F32),
            pltpu.VMEM((T, DI), BF16), pltpu.VMEM((T, DI), BF16), pltpu.VMEM((T, DI), BF16), pltpu.VMEM((NSTATE, DI), F32),
            pltpu.VMEM((8, DI), F32), pltpu.VMEM((per, NSTATE, DI), BF16),
        ],
        compiler_params=params(),
        name="second_pass",
    )(gate, ng, act, dt, cum, bst, inc, tok, wo, rows, et)


def third_pass(
    act, convin, halo, dt, cum, sig, dcum, mlow, ent, leave, egrad, rg, inc, rows, conv, head, et, go, gg, T=256
):
    L = act.shape[0]
    m = sizes()
    dims = (m["z"], m["x"], m["y"], m["c"])
    total = m["z"] * m["y"] * 4
    ro, rg_rows = DI // total, D // total
    go = go.reshape(dims + (ro, D))
    gg = gg.reshape(dims + (rg_rows, DI))
    n, per = L // T, T // BLOCK
    row = lambda w: pl.BlockSpec((T, w), lambda i: (n - 1 - i, 0))
    blk = pl.BlockSpec((per, NSTATE, DI), lambda i: (n - 1 - i, 0, 0))
    prev = pl.BlockSpec((16, WC), lambda i: (jnp.maximum((n - 1 - i) * (T // 16) - 1, 0), 0))
    return pl.pallas_call(
        functools.partial(third_kernel, T),
        grid=(n,),
        in_specs=[
            row(CH), row(WC), prev, full((16, WC)), row(BLOCK), row(BLOCK), row(BLOCK), row(BLOCK), row(DI), blk,
            full((NSTATE, DI)), blk, row(BLOCK), full((NSTATE, DI)), full((8, DI)), full((8, CH)), full((8, BLOCK)),
            full((DI, BLOCK)), ANY, ANY,
        ],
        out_specs=[
            row(WC), full((40, CH)), full((16, BLOCK)), full((16, WC)), full((ro, D)), full((rg_rows, DI)),
        ],
        out_shape=[
            sds((L, WC), BF16), sds((40, CH), F32), sds((16, BLOCK), F32), sds((16, WC), BF16), sds((ro, D), F32),
            sds((rg_rows, DI), F32),
        ],
        scratch_shapes=[
            pltpu.VMEM((16, CH), F32), pltpu.VMEM((8, CH), F32), pltpu.SemaphoreType.DMA(()), pltpu.SemaphoreType.DMA(()),
            pltpu.VMEM((NSTATE, DI), F32), pltpu.VMEM((T, CH), F32), pltpu.VMEM((BLOCK, DI), BF16), pltpu.VMEM((BLOCK, DI), BF16), pltpu.VMEM((BLOCK, DI), BF16),
            pltpu.VMEM((BLOCK, DI), BF16), pltpu.VMEM((NSTATE, DI), BF16), pltpu.VMEM((8, DI), F32),
            pltpu.VMEM((NSTATE, DI), BF16), pltpu.VMEM((T + 8, CH), F32), pltpu.VMEM((T + 16, CH), F32),
        ] + own_scratch(ro, D) + scatter_scratch(ro, D) + own_scratch(rg_rows, DI) + scatter_scratch(rg_rows, DI),
        compiler_params=params(collective_id=4),
        name="third_pass",
    )(act, convin, convin, halo, dt, cum, sig, dcum, mlow, ent, leave, egrad, rg, inc, rows, conv, head, et, go, gg)


def on_device(
    tokens, cotangent, norm_gain, in_weight, conv_weight, conv_bias, step_bias, decay_log, skip_gain, gate_gain,
    out_weight,
):
    tok, cot = tokens[0], cotangent[0]
    L = tok.shape[0]
    k_rows, c_rows = in_weight.shape[0], conv_weight.shape[0]
    total = D // k_rows
    lanes = lambda x: jnp.pad(x, ((0, 0),) * (x.ndim - 1) + ((0, BLOCK - x.shape[-1]),))
    wide = lambda x: lanes(x.astype(F32))
    own = jnp.concatenate(
        [wide(conv_weight.T), wide(conv_bias[None]), wide(norm_gain[None]), wide(gate_gain[None]), jnp.zeros((1, BLOCK))],
        axis=0,
    )
    slab_c = jnp.concatenate([lanes(in_weight[:, DI + CH :]), in_weight[:, DI : DI + CH]], axis=1)
    head = lanes(jnp.stack([step_bias, -jnp.exp(decay_log)] + [jnp.zeros_like(step_bias)] * 6))
    et = jnp.asarray(head_columns(), BF16)

    (xhat, xt, wc, p, hp, conv, gain, ggain, act, dt, cum, sig, bst, leave, tot, buf_g, buf_o) = first_pass(
        slab_c, own, tok, head, in_weight[:, :DI], out_weight
    )
    rows = jnp.concatenate([jnp.repeat(skip_gain, HEADDIM)[None], ggain[:7]], axis=0)
    wg, wo = buf_g.reshape(D, DI), buf_o.reshape(DI, D)
    gate, ng, inc = gate_pass(xhat, wg, cot, wo, ggain, leave, tot)
    mixed, nout, ggrad, mlow, dcum, ent, egrad, rg, leave2, back, cols = second_pass(
        gate, ng, act, dt, cum, bst, inc, tok, wo, rows, et
    )
    g_out, g_gate, later = grads_pass(nout, cot, xt, ggrad, back, tot)
    pg, cgrad, hgrad, tail, out_raw, gate_cols = third_pass(
        act, p, hp, dt, cum, sig, dcum, mlow, ent, leave2, egrad, rg, later, rows, conv, head, et, g_out, g_gate
    )
    cg = cgrad.reshape(5, 8, CH).sum(axis=1)
    hg = hgrad.reshape(2, 8, BLOCK).sum(axis=1)[:, :HEADS]
    sums = jnp.concatenate([hg[0], hg[1], cols.reshape(8, HEADS, HEADDIM).sum(axis=(0, 2))])
    small = jnp.concatenate(
        [
            lanes(jnp.swapaxes(cg.reshape(5, total, c_rows), 0, 1)), jnp.zeros((total, 2, BLOCK), F32),
            jnp.broadcast_to(lanes(sums[None, None]), (total, 1, BLOCK)),
        ],
        axis=1,
    )
    tgrad, conv_cols, sums = last_pass(xt, pg, tail, ggrad, tok, cot, wg, wc, gain, small)
    in_grad, ngain_grad, ggain_grad, taps, bias, step, decay, skip = finish_pass(
        gate_cols, conv_cols, out_raw, sums, in_weight, out_weight, norm_gain.astype(F32), gate_gain.astype(F32), c_rows
    )
    return (
        mixed[None], tgrad[None], ngain_grad, in_grad, taps, bias, step, decay, skip, ggain_grad, out_raw,
    )


def solution(mesh):
    both = ("dp", "seq")
    vec, mat, tok, rep = P(both), P(both, None), P("dp", "seq", None), P()
    return jax.shard_map(
        on_device,
        mesh=mesh,
        in_specs=(tok, tok, vec, mat, mat, vec, rep, rep, rep, vec, mat),
        out_specs=(tok, tok, vec, mat, mat, vec, rep, rep, rep, vec, mat),
        check_vma=False,
    )
```

```python
import functools

import jax
import jax.numpy as jnp
import numpy as np
from jax import lax
from jax.experimental import pallas as pl
from jax.experimental.pallas import tpu as pltpu
from jax.sharding import PartitionSpec as P

D = 768
HEADS = 24
HEADDIM = 64
NSTATE = 128
CONV = 4
BLOCK = 128
DI = 1536
CH = 1792
PAIRS = HEADS // 2
EPS = 1e-05
LOG2E = 1.4426950408889634
F32 = jnp.float32
BF16 = jnp.bfloat16
NT = (((1,), (1,)), ((), ()))
VMEM_LIMIT = 60 * 1024 * 1024


def dot(a, b):
    return jnp.dot(a, b, preferred_element_type=F32)


def dot_nt(a, b):
    return lax.dot_general(a, b, NT, preferred_element_type=F32)


def dot_exact(a, b):
    return jnp.dot(a, b, preferred_element_type=F32, precision=lax.Precision.HIGHEST)


def sigmoid(v):
    return 0.5 * jnp.tanh(0.5 * v) + 0.5


def iota(shape, dim):
    return lax.broadcasted_iota(jnp.int32, shape, dim)


def lane_lo():
    return iota((BLOCK, BLOCK), 1) < HEADDIM


def expand_pair(x, j, lo):
    rows = x.shape[0]
    a = jnp.broadcast_to(x[:, 2 * j : 2 * j + 1], (rows, BLOCK))
    b = jnp.broadcast_to(x[:, 2 * j + 1 : 2 * j + 2], (rows, BLOCK))
    return jnp.where(lo, a, b), a, b


def block_diag(v):
    lo = iota(v.shape, 1) < HEADDIM
    zero = jnp.zeros_like(v)
    return jnp.concatenate([jnp.where(lo, v, zero), jnp.where(lo, zero, v)], axis=0)


def pair(j):
    return slice(j * BLOCK, (j + 1) * BLOCK)


MESH = pl.DeviceIdType.MESH
ANY = pl.BlockSpec(memory_space=pl.ANY)
WC = CH + BLOCK
TN = (((0,), (0,)), ((), ()))


def dot_tn(a, b):
    return lax.dot_general(a, b, TN, preferred_element_type=F32)


def sizes():
    return {"z": lax.axis_size("dp") // 2, "x": 2, "y": lax.axis_size("seq") // 2, "c": 2}


def place():
    dp, seq = lax.axis_index("dp"), lax.axis_index("seq")
    return {"z": dp // 2, "x": lax.rem(dp, 2), "y": seq // 2, "c": lax.rem(seq, 2)}


def device(at):
    return {"dp": at["z"] * 2 + at["x"], "seq": at["y"] * 2 + at["c"]}


def peers(at, axis):
    n = sizes()[axis]
    return [dict(at, **{axis: lax.rem(at[axis] + o, n)}) for o in range(1, n)]


def greet(at, axes, by=0):
    sem = pltpu.get_barrier_semaphore()
    count = 0
    for axis in axes:
        for peer in peers(at, axis):
            pl.semaphore_signal(sem, inc=1, device_id=device(peer), device_id_type=MESH)
            count += 1
    if not by:
        pl.semaphore_wait(sem, count)
        return
    seq, n = lax.axis_index("seq"), lax.axis_size("seq")

    @pl.when((seq + by >= 0) & (seq + by < n))
    def _():
        pl.semaphore_signal(sem, inc=1, device_id={"seq": seq + by}, device_id_type=MESH)

    heard = (seq - by >= 0) & (seq - by < n)

    @pl.when(heard)
    def _():
        pl.semaphore_wait(sem, count + 1)

    @pl.when(jnp.logical_not(heard))
    def _():
        pl.semaphore_wait(sem, count)


def greet_neighbours():
    seq, n = lax.axis_index("seq"), lax.axis_size("seq")
    sem = pltpu.get_barrier_semaphore()

    @pl.when(seq > 0)
    def _():
        pl.semaphore_signal(sem, inc=1, device_id={"seq": seq - 1}, device_id_type=MESH)

    @pl.when(seq < n - 1)
    def _():
        pl.semaphore_signal(sem, inc=1, device_id={"seq": seq + 1}, device_id_type=MESH)

    @pl.when((seq > 0) & (seq < n - 1))
    def _():
        pl.semaphore_wait(sem, 2)

    @pl.when((seq == 0) | (seq == n - 1))
    def _():
        pl.semaphore_wait(sem, 1)


def remote(src, dst, send, recv, peer):
    return pltpu.make_async_remote_copy(
        src_ref=src, dst_ref=dst, send_sem=send, recv_sem=recv, device_id=device(peer), device_id_type=MESH
    )


class Gather:
    def __init__(self, slab, spot, order, sems):
        self.slab, self.spot, self.order = slab, spot, order
        self.send, self.recv = sems
        self.at = place()

    def copies(self, stage):
        at, (a, b) = self.at, self.order
        n = sizes()
        out = []
        every = slice(None)
        nz = n["z"] - 1
        if stage == 0:
            for o, peer in enumerate(peers(at, "z")):
                out.append((self.slab, self.spot(at), o, peer))
        elif stage == 1:
            index = dict(at, z=every)
            out.append((self.spot(index), self.spot(index), nz, peers(at, a)[0]))
        elif stage == 2:
            index = dict(at, z=every)
            index[a] = every
            for o, peer in enumerate(peers(at, b)):
                out.append((self.spot(index), self.spot(index), nz + 1 + o, peer))
            out.append((self.spot(index), self.spot(index), nz + 1 + n[b] - 1, peers(at, "c")[0]))
        else:
            for o in range(1, n[b]):
                index = dict(at, z=every)
                index[a] = every
                index[b] = lax.rem(at[b] + o, n[b])
                out.append((self.spot(index), self.spot(index), nz + 1 + n[b] + o - 1, peers(at, "c")[0]))
        return [remote(s, d, self.send.at[k], self.recv.at[k], p) for s, d, k, p in out]

    def start(self, stage):
        for c in self.copies(stage):
            c.start()

    def wait(self, stage):
        for c in self.copies(stage):
            c.wait()


def spots(buf, lanes=slice(None)):
    return lambda index: buf.at[index["z"], index["x"], index["y"], index["c"], :, lanes]


def gather_sems():
    count = sizes()["z"] + 2 * sizes()["y"] + 4
    return [pltpu.SemaphoreType.DMA((count,)), pltpu.SemaphoreType.DMA((count,))]


class Scatter:
    def __init__(self, grads, order, scratch, own=None, local=None):
        self.grads, self.order, self.own_ref, self.local = grads, order, own, local
        self.rc, self.r1, self.r2, self.rz, self.send, self.recv = scratch
        self.at = place()
        self.own = self

    def spot(self, z, x, y):
        if self.own_ref is not None:
            return self.own_ref.at[z, x, y]
        return self.grads.at[z, x, y, self.at["c"]]

    def add(self, z, x, y, got):
        mine = self.spot(z, x, y)
        mine[...] = (mine[...].astype(F32) + got.astype(F32)).astype(BF16)

    def copies(self, stage):
        at, (a, b) = self.at, self.order
        every = slice(None)
        out = []

        def spot(index):
            return self.spot(index["z"], index["x"], index["y"])

        if stage == 0:
            out.append((self.grads.at[:, :, :, 1 - at["c"]], self.rc, 0, peers(at, "c")[0]))
        elif stage == 1:
            index = {"z": every, "x": every, "y": every}
            index[a] = 1 - at[a]
            out.append((spot(index), self.r1, 1, peers(at, a)[0]))
        elif stage == 2:
            index = {"z": every, a: at[a], b: 1 - at[b]}
            out.append((spot(index), self.r2, 2, peers(at, b)[0]))
        else:
            for o, peer in enumerate(peers(at, "z")):
                out.append((self.spot(peer["z"], at["x"], at["y"]), self.rz.at[o], 3 + o, peer))
        return [remote(s, d, self.send.at[k], self.recv.at[k], p) for s, d, k, p in out]

    def mine(self):
        return pltpu.make_async_copy(self.grads.at[:, :, :, self.at["c"]], self.own_ref, self.local)

    def start(self, stage):
        if stage == 0 and self.own_ref is not None:
            self.mine().start()
        for c in self.copies(stage):
            c.start()

    def finish(self, stage):
        at, (a, b) = self.at, self.order
        for c in self.copies(stage):
            c.wait()
        nz = sizes()["z"]
        if stage == 0:
            if self.own_ref is not None:
                self.mine().wait()

            def body(z, _):
                for x in range(2):
                    for y in range(2):
                        self.add(z, x, y, self.rc[z, x, y])
                return _

        elif stage == 1:

            def body(z, _):
                for k in range(2):
                    index = {a: at[a], b: k}
                    self.add(z, index["x"], index["y"], self.r1[z, k])
                return _

        else:

            def body(z, _):
                self.add(z, at["x"], at["y"], self.r2[z])
                return _

        lax.fori_loop(0, nz, body, 0)

    def result(self):
        for c in self.copies(3):
            c.wait()
        total = self.spot(self.at["z"], self.at["x"], self.at["y"])[...].astype(F32)
        for o in range(sizes()["z"] - 1):
            total = total + self.rz[o].astype(F32)
        return total


def scatter_scratch(rows, width):
    nz = sizes()["z"]
    return [
        pltpu.VMEM((nz, 2, 2, rows, width), BF16), pltpu.VMEM((nz, 2, rows, width), BF16),
        pltpu.VMEM((nz, rows, width), BF16), pltpu.VMEM((nz - 1, rows, width), BF16),
        pltpu.SemaphoreType.DMA((nz + 2,)), pltpu.SemaphoreType.DMA((nz + 2,)),
    ]


NSC = 6


def own_scratch(rows, width):
    return [pltpu.VMEM((sizes()["z"], 2, 2, rows, width), BF16), pltpu.SemaphoreType.DMA(())]


class Chain:
    def __init__(self, leave, inc, decay, bufs, reverse):
        self.leave, self.inc, self.decay, self.reverse = leave, inc, decay, reverse
        self.got, self.put, self.send, self.recv = bufs
        self.n = lax.axis_size("seq")
        seq = lax.axis_index("seq")
        self.rank = self.n - 1 - seq if reverse else seq
        self.to = seq - 1 if reverse else seq + 1

    def copy(self):
        return pltpu.make_async_remote_copy(
            src_ref=self.put, dst_ref=self.got, send_sem=self.send, recv_sem=self.recv,
            device_id={"seq": self.to}, device_id_type=MESH,
        )

    def step(self, k):
        @pl.when(self.rank == k)
        def _():
            if k == 0:
                self.inc[...] = jnp.zeros_like(self.inc)
                self.put[...] = self.leave[...].astype(BF16)
            else:
                self.copy().wait_recv()
                got = self.got[...].astype(F32)
                self.inc[...] = got
                if k < self.n - 1:
                    self.put[...] = (got * self.decay[0:1] + self.leave[...]).astype(BF16)
            if k < self.n - 1:
                self.copy().start()

    def done(self):
        @pl.when(self.rank < self.n - 1)
        def _():
            self.copy().wait_send()


def chain_scratch():
    return [
        pltpu.VMEM((NSTATE, DI), BF16), pltpu.VMEM((NSTATE, DI), BF16), pltpu.SemaphoreType.DMA(()),
        pltpu.SemaphoreType.DMA(()),
    ]


def expand_row(row, dst):
    lo = iota((8, BLOCK), 1) < HEADDIM
    wide = jnp.broadcast_to(row, (8, BLOCK))
    for j in range(PAIRS):
        dst[:, pair(j)] = expand_pair(wide, j, lo)[0]


CHUNKS = ((0, 512), (512, 512), (1024, 512), (1536, 384))
ORDERS = ("xy", "yx", "xy", "yx")


def last_kernel(
    T, xt_ref, pg_any, tail_ref, ggrad_ref, tok_ref, cot_ref, wg_ref, wc_ref, gain_ref, small_ref,
    tgrad_ref, gout_ref, sums_ref, pg, g0, g1, g2, g3, lsem, smalls, ssend, srecv, *scratch,
):
    i = pl.program_id(0)
    nc = len(CHUNKS)
    grads = (g0, g1, g2, g3)
    sc = [Scatter(grads[k], ORDERS[k][::-1], scratch[NSC * k : NSC * k + NSC]) for k in range(nc)]
    dp, seq = lax.axis_index("dp"), lax.axis_index("seq")
    n_dp, n_seq = lax.axis_size("dp"), lax.axis_size("seq")
    total = n_dp * n_seq
    me = dp * n_seq + seq
    L = pg.shape[0]

    def load(k):
        lanes = pl.ds(CHUNKS[k][0], CHUNKS[k][1])
        return pltpu.make_async_copy(pg_any.at[:, lanes], pg.at[:, lanes], lsem.at[k])

    def far(o):
        r = lax.rem(me + o, total)
        return {"dp": r // n_seq, "seq": lax.rem(r, n_seq)}

    def small(o):
        r = lax.rem(me + o, total)
        return pltpu.make_async_remote_copy(
            src_ref=small_ref.at[r], dst_ref=smalls.at[o - 1], send_sem=ssend.at[o - 1], recv_sem=srecv.at[o - 1],
            device_id=far(o), device_id_type=MESH,
        )

    @pl.when(i == 0)
    def _():
        for k in range(nc):
            load(k).start()
        sem = pltpu.get_barrier_semaphore()
        for o in range(1, total):
            pl.semaphore_signal(sem, inc=1, device_id=far(o), device_id_type=MESH)

    for k in range(nc):
        @pl.when(i == k)
        def _():
            lane, width = CHUNKS[k]
            load(k).wait()
            skip = BLOCK if k == 0 else 0
            pg[L - 16 :, lane + skip : lane + width] = tail_ref[:, lane + skip : lane + width]
            rows = grads[k].shape[4]
            for q in range(2):
                half = D // 2
                g = dot(xt_ref[q * half : (q + 1) * half], pg[:, lane : lane + width])
                for r in range(half // rows):
                    s = r + q * (half // rows)
                    grads[k][s // 8, (s // 4) % 2, (s // 2) % 2, s % 2] = g[r * rows : (r + 1) * rows].astype(BF16)
            if k == 0:
                pl.semaphore_wait(pltpu.get_barrier_semaphore(), total - 1)
                sc[0].start(0)
                for o in range(1, total):
                    small(o).start()
            else:
                sc[k - 1].finish(0)
                sc[k - 1].start(1)
                sc[k].start(0)

    @pl.when(i >= nc)
    def _():
        r0 = pl.multiple_of((i - nc) * T, T)
        u = dot_nt(ggrad_ref[...], wg_ref[...]) + dot_nt(pg[pl.ds(r0, T), :], wc_ref[...])
        u = u * gain_ref[0:1]
        x = tok_ref[...].astype(F32)
        inv = lax.rsqrt(jnp.mean(x * x, axis=-1, keepdims=True) + EPS)
        xi = x * inv
        coef = inv * jnp.mean(u * xi, axis=-1, keepdims=True)
        tgrad_ref[...] = (cot_ref[...].astype(F32) + inv * u - xi * coef).astype(BF16)

    def after(step, what):
        @pl.when(i == step)
        def _():
            for k, stage in what:
                sc[k].finish(stage)
                sc[k].start(stage + 1)

    after(nc, [(3, 0), (0, 1)])
    after(nc + 1, [(1, 1)])
    after(nc + 2, [(2, 1), (0, 2)])
    after(nc + 3, [(3, 1), (1, 2), (2, 2), (3, 2)])

    @pl.when(i == pl.num_programs(0) - 1)
    def _():
        for o in range(1, total):
            small(o).wait()
        acc = small_ref[me]
        for o in range(1, total):
            acc = acc + smalls[o - 1]
        sums_ref[...] = acc
        for k in range(nc):
            lane, width = CHUNKS[k]
            gout_ref[:, lane : lane + width] = sc[k].result()


def last_pass(xt, pg, tail, ggrad, tok, cot, wg, wc, gain, small, T=512):
    L = tok.shape[0]
    n = sizes()
    nc = len(CHUNKS)
    total = lax.axis_size("dp") * lax.axis_size("seq")
    rows = D // total
    row = lambda w: pl.BlockSpec((T, w), lambda i: (jnp.maximum(i - nc, 0), 0))
    scratch = []
    for _, w in CHUNKS:
        scratch += scatter_scratch(rows, w)
    return pl.pallas_call(
        functools.partial(last_kernel, T),
        grid=(nc + L // T,),
        in_specs=[
            once((D, L)), ANY, full((16, WC)), row(DI), row(D), row(D), once((D, DI)), once((D, WC)),
            once((8, D)), once((total, 8, BLOCK)),
        ],
        out_specs=[row(D), full((rows, WC)), full((8, BLOCK))],
        out_shape=[sds((L, D), BF16), sds((rows, WC), F32), sds((8, BLOCK), F32)],
        scratch_shapes=[pltpu.VMEM((L, WC), BF16)]
        + [pltpu.VMEM((n["z"], 2, n["y"], 2, rows, w), BF16) for _, w in CHUNKS]
        + [
            pltpu.SemaphoreType.DMA((nc,)), pltpu.VMEM((total - 1, 8, BLOCK), F32),
            pltpu.SemaphoreType.DMA((total - 1,)), pltpu.SemaphoreType.DMA((total - 1,)),
        ] + scratch,
        compiler_params=params(collective_id=5),
        name="last_pass",
    )(xt, pg, tail, ggrad, tok, cot, wg, wc, gain, small)


def finish_kernel(
    gate_ref, conv_ref, out_ref, sums_ref, w_ref, wo_ref, gain_ref, ggain_ref, tgrad_ref, mixed_ref,
    in_grad, ngain, ggain, taps, bias, step, decay, skip, out_grad, tgrad_out, mixed_out,
):
    tgrad_out[...] = tgrad_ref[...]
    mixed_out[...] = mixed_ref[...]

    @pl.when(pl.program_id(0) == 0)
    def _():
        finish_small(
            gate_ref, conv_ref, out_ref, sums_ref, w_ref, wo_ref, gain_ref, ggain_ref, in_grad, ngain, ggain, taps, bias,
            step, decay, skip, out_grad,
        )


def finish_small(
    gate_ref, conv_ref, out_ref, sums_ref, w_ref, wo_ref, gain_ref, ggain_ref,
    in_grad, ngain, ggain, taps, bias, step, decay, skip, out_grad,
):
    conv = conv_ref[...]
    raw = jnp.concatenate([gate_ref[...], conv[:, BLOCK:], conv[:, :HEADS]], axis=1)
    in_grad[...] = raw
    ngain[...] = jnp.sum(raw * w_ref[...].astype(F32), axis=1) / gain_ref[...]
    o = out_ref[...]
    out_grad[...] = o
    ggain[...] = jnp.sum(o * wo_ref[...].astype(F32), axis=1) / ggain_ref[...]
    s = sums_ref[...]
    n = bias.shape[0]
    taps[...] = s.T[:n, :CONV]
    bias[...] = s[4, :n]
    step[...] = s[7, :HEADS]
    decay[...] = s[7, HEADS : 2 * HEADS]
    skip[...] = s[7, 2 * HEADS : 3 * HEADS]


def finish_pass(gate_cols, conv_cols, out_raw, sums, w, wo, gain, ggain, tgrad, mixed, channels):
    vec = lambda n: sds((n,), F32)
    rows = pl.BlockSpec((512, D), lambda i: (i, 0))
    small = [
        sds(w.shape, F32), vec(w.shape[0]), vec(wo.shape[0]), sds((channels, CONV), F32),
        vec(channels), vec(HEADS), vec(HEADS), vec(HEADS), sds(out_raw.shape, F32),
    ]
    ins = (gate_cols, conv_cols, out_raw, sums, w, wo, gain, ggain)
    return pl.pallas_call(
        finish_kernel,
        grid=(tgrad.shape[0] // 512,),
        in_specs=[once(x.shape) for x in ins] + [rows, rows],
        out_specs=[once(x.shape) for x in small] + [rows, rows],
        out_shape=small + [sds(tgrad.shape, BF16)] * 2,
        name="finish_pass",
    )(*ins, tgrad, mixed)


def rms_rows(tok, gain):
    x = tok.astype(F32)
    return (x * lax.rsqrt(jnp.mean(x * x, axis=-1, keepdims=True) + EPS) * gain).astype(BF16)


def first_kernel(
    T, win_ref, small, tok_any, so_ref,
    xhat_any, xt_any, wc_any, p_any, hp_ref, conv_ref, gain_ref, row_ref,
    act_ref, slope_ref, dt_ref, cum_ref, sig_ref, bst_ref, leave_ref, tot_ref, bg_ref, bo_ref,
    slab, tok, halo, xhat, xt, wc, wide, p, smalls, b0, b1, b2, b3, ext, state, weighted, lsem, hsend, hrecv, ssend, srecv,
    *sems,
):
    i = pl.program_id(0)
    steps = pl.num_programs(0)
    at = place()
    seq, n = lax.axis_index("seq"), lax.axis_size("seq")
    L = tok.shape[0]
    bufs = (b0, b1, b2, b3)
    nc = len(CHUNKS)
    gets = []
    for (lane, width), order, buf, k in zip(CHUNKS, ORDERS, bufs, range(nc)):
        gets.append(Gather(slab.at[:, pl.ds(lane, width)], spots(buf), order, sems[2 * k : 2 * k + 2]))
    for k in range(4):
        buf = (bg_ref, bo_ref)[k % 2]
        width = buf.shape[5] // 2
        lanes = pl.ds((k // 2) * width, width)
        q = 2 * (nc + k)
        src = win_ref if k % 2 == 0 else so_ref
        gets.append(Gather(src.at[:, lanes], spots(buf, lanes), ORDERS[k], sems[q : q + 2]))
    own = []
    for k, (src, buf) in enumerate(((win_ref.at[:, pl.ds(0, DI)], bg_ref), (so_ref, bo_ref))):
        own.append(pltpu.make_async_copy(src, buf.at[at["z"], at["x"], at["y"], at["c"]], lsem.at[k]))
    halo_copy = pltpu.make_async_remote_copy(
        src_ref=tok_any.at[pl.ds(L - 16, 16)], dst_ref=halo, send_sem=hsend, recv_sem=hrecv,
        device_id={"seq": seq + 1}, device_id_type=MESH,
    )
    outs = [pltpu.make_async_copy(xhat, xhat_any, lsem.at[3]), pltpu.make_async_copy(xt, xt_any, lsem.at[4])]
    for k, (lane, width) in enumerate(CHUNKS):
        for j, (src, dst) in enumerate(((p, p_any), (wc, wc_any))):
            lanes = pl.ds(lane, width)
            outs.append(pltpu.make_async_copy(src.at[:, lanes], dst.at[:, lanes], lsem.at[5 + 2 * k + j]))

    def advance(*what):
        for k, stage in what:
            if stage > 0:
                gets[k].wait(stage - 1)
            if stage < 4:
                gets[k].start(stage)

    def project(k):
        lane, width = CHUNKS[k]
        buf = bufs[k]
        nz, rows_k = buf.shape[0], buf.shape[4]
        for z in range(nz):
            for m in range(8):
                r = z * 8 + m
                wide[r * rows_k : (r + 1) * rows_k, :width] = buf[z, m // 4, (m // 2) % 2, m % 2].astype(F32)
        wc[:, lane : lane + width] = wide[:, :width].astype(BF16)
        for r in range(L // 512):
            rows = slice(r * 512, (r + 1) * 512)
            p[rows, lane : lane + width] = dot(xhat[rows], wc[:, lane : lane + width]).astype(BF16)
        hp_ref[:, lane : lane + width] = dot(halo[...], wc[:, lane : lane + width]).astype(BF16)
        for c in outs[2 + 2 * k : 4 + 2 * k]:
            c.start()

    @pl.when(i == 0)
    def _():
        dp = lax.axis_index("dp")
        n_dp = lax.axis_size("dp")
        total = n_dp * n
        me = dp * n + seq
        load = pltpu.make_async_copy(tok_any, tok, lsem.at[2])
        load.start()
        sem = pltpu.get_barrier_semaphore()
        k_rows = slab.shape[0]
        steps_w = win_ref[:, DI + CH :]
        slab[:, :BLOCK] = jnp.concatenate([steps_w, jnp.zeros((k_rows, BLOCK - HEADS), BF16)], axis=1)
        slab[:, BLOCK:] = win_ref[:, DI : DI + CH]

        def far(o):
            r = lax.rem(me + o, total)
            return {"dp": r // n, "seq": lax.rem(r, n)}

        for o in range(1, total):
            pl.semaphore_signal(sem, inc=1, device_id=far(o), device_id_type=MESH)
        pl.semaphore_wait(sem, total - 1)
        advance((0, 0), (1, 0))

        @pl.when(seq < n - 1)
        def _():
            halo_copy.start()

        sends = []
        for o in range(1, total):
            c = pltpu.make_async_remote_copy(
                src_ref=small.at[0], dst_ref=smalls.at[me], send_sem=ssend.at[o - 1], recv_sem=srecv.at[o - 1],
                device_id=far(o), device_id_type=MESH,
            )
            c.start()
            sends.append(c)
        for c in own:
            c.start()
        smalls[me] = small[0]
        expand_row(small[1, 2:3], row_ref)
        for (lane, width), buf in zip(CHUNKS, bufs):
            buf[at["z"], at["x"], at["y"], at["c"]] = slab[:, lane : lane + width]
        conv_ref[...] = jnp.zeros_like(conv_ref)
        state[...] = jnp.zeros_like(state)
        tot_ref[...] = jnp.zeros_like(tot_ref)
        advance((0, 1), (2, 0), (1, 1), (3, 0))
        load.wait()
        for c in sends:
            c.wait()
        taps, ks, gs = CH // total, D // total, DI // total
        for r in range(total):
            conv_ref[0:5, r * taps : (r + 1) * taps] = smalls[r, 0:5, :taps]
            gain_ref[:, r * ks : (r + 1) * ks] = jnp.broadcast_to(smalls[r, 5:6, :ks], (8, ks))
            row_ref[1:2, r * gs : (r + 1) * gs] = smalls[r, 6:7, :gs]

        def norm(r, _):
            rows = pl.ds(pl.multiple_of(r * 256, 256), 256)
            h = rms_rows(tok[rows], gain_ref[0:1])
            xhat[rows] = h
            xt[:, rows] = h.T
            return _

        lax.fori_loop(0, L // 512, norm, 0)
        advance((0, 2), (1, 2), (2, 1), (4, 0), (3, 1), (5, 0), (6, 0), (7, 0))
        lax.fori_loop(L // 512, L // 256, norm, 0)
        for c in outs[:2]:
            c.start()

        @pl.when(seq == 0)
        def _():
            halo[...] = jnp.zeros_like(halo)

        @pl.when(seq > 0)
        def _():
            halo_copy.wait_recv()

        @pl.when(seq < n - 1)
        def _():
            halo_copy.wait_send()

        halo[...] = rms_rows(halo[...], gain_ref[0:1])
        for c in own:
            c.wait()
        advance((0, 3), (1, 3), (2, 2), (3, 2), (0, 4))
        project(0)
        advance((1, 4), (4, 1), (5, 1))
        project(1)
        advance((2, 3), (3, 3), (4, 2), (5, 2), (6, 1), (7, 1), (2, 4))
        project(2)
        advance((3, 4))
        project(3)
        for c in range(CH // 128):
            ext[c, 0:8] = hp_ref[:, BLOCK + c * 128 : BLOCK + (c + 1) * 128].astype(F32)[8:16]

    def tile(r0):
        for c in range(CH // 128):
            cs = slice(c * 128, (c + 1) * 128)
            ext[c, 8 : 8 + T] = p[pl.ds(r0, T), BLOCK + c * 128 : BLOCK + (c + 1) * 128].astype(F32)
            for r in range(0, T, 64):
                total = conv_ref[4:5, cs]
                for k in range(CONV):
                    total = total + ext[c, 5 + k + r : 5 + k + r + 64] * conv_ref[k : k + 1, cs]
                sg = sigmoid(total)
                v = total * sg
                act_ref[r : r + 64, cs] = v.astype(BF16)
                slope_ref[r : r + 64, cs] = (sg + v * (1.0 - sg)).astype(BF16)
        raw = p[pl.ds(r0, T), :BLOCK].astype(F32) + small[1, 0:1]
        dt_all = jnp.maximum(raw, 0.0) + jnp.log1p(jnp.exp(-jnp.abs(raw)))
        dt_ref[...] = dt_all
        sig_ref[...] = sigmoid_exact(raw)
        tril = (iota((BLOCK, BLOCK), 0) >= iota((BLOCK, BLOCK), 1)).astype(F32)
        lo = lane_lo()
        for blk in range(T // BLOCK):
            rows = slice(blk * BLOCK, (blk + 1) * BLOCK)
            dt = dt_all[rows]
            cum = dot_exact(tril, dt * small[1, 1:2]) * LOG2E
            cum_ref[rows] = cum
            end = cum[BLOCK - 1 : BLOCK]
            tot_ref[...] += jnp.broadcast_to(end, tot_ref.shape)
            wfac = jnp.exp2(end - cum) * dt
            decay = jnp.broadcast_to(jnp.exp2(end), (8, BLOCK))
            write_t = act_ref[rows, DI : DI + NSTATE].T
            for j in range(PAIRS):
                w, _, _ = expand_pair(wfac, j, lo)
                weighted[:, pair(j)] = (act_ref[rows, pair(j)].astype(F32) * w).astype(BF16)
            for q in range(PAIRS // 2):
                cs = slice(q * 256, (q + 1) * 256)
                new = dot(write_t, weighted[:, cs])
                bst_ref[blk, :, cs] = new.astype(BF16)
                d0, _, _ = expand_pair(decay, 2 * q, lo[:8])
                d1, _, _ = expand_pair(decay, 2 * q + 1, lo[:8])
                dd = jnp.concatenate([d0, d1], axis=1)[0:1]
                state[:, cs] = state[:, cs] * dd + new

    def after(step, *what):
        @pl.when(i == step)
        def _():
            advance(*what)

    after(2, (6, 2), (7, 2))
    after(4, (4, 3), (5, 3))
    after(6, (6, 3), (7, 3))

    @pl.when(i > 1)
    def _():
        ext[:, 0:8] = ext[:, T : T + 8]

    @pl.when(i > 0)
    def _():
        tile(pl.multiple_of((i - 1) * T, T))

    @pl.when(i == steps - 1)
    def _():
        leave_ref[...] = state[...]
        advance((4, 4), (5, 4), (6, 4), (7, 4))
        for c in outs:
            c.wait()


def sigmoid_exact(v):
    return 1.0 / (1.0 + jnp.exp(-v))


def second_kernel(
    T, xhat_ref, cot_ref, wg_ref, wo_ref, leave1_ref, tot_ref, act_ref, dt_ref, cum_ref, bst_ref, tok_ref, row_ref, et_ref,
    mixed_ref, mlow_ref, dcum_ref, ent_ref, egrad_ref, rg_ref, leave_ref, later_ref, cols_ref, ggrad_any, gout_any, ggate_any,
    gate, ngrad, nout_t, nout, ms, growth, rlow, prod, plow, state, back, exg, lows, decay, osem, *bufs,
):
    i = pl.program_id(0)
    steps = pl.num_programs(0)
    L = gate.shape[0]
    first = Chain(leave1_ref, state, decay, bufs[:4], False)
    second = Chain(back, later_ref, decay, bufs[4:], True)
    parts = L // 512

    def keep(step):
        rows = pl.ds(pl.multiple_of((step - 1) * T, T), T)
        return pltpu.make_async_copy(gate.at[rows], ggrad_any.at[rows], osem.at[step - 1])

    @pl.when(i == 0)
    def _():
        expand_row(jnp.exp2(tot_ref[0:1]), decay)
        greet_neighbours()
        first.step(0)
        exg[...] = jnp.ones_like(exg)
        back[...] = jnp.zeros_like(back)
        cols_ref[...] = jnp.zeros_like(cols_ref)
        for r in range(parts):
            rows = slice(r * 512, (r + 1) * 512)
            for c in range(DI // 256):
                cs = slice(c * 256, (c + 1) * 256)
                gate[rows, cs] = dot(xhat_ref[rows], wg_ref[:, cs]).astype(BF16)
            for c in range(DI // 256):
                cs = slice(c * 256, (c + 1) * 256)
                ngrad[rows, cs] = (dot_nt(cot_ref[rows], wo_ref[cs, :]) * row_ref[1:2, cs]).astype(BF16)
            for k in range(1, first.n):
                if r == min(k, parts - 1):
                    first.step(k)
        first.done()

    def tile(r0):
        gate_s, ng = gate.at[pl.ds(r0, T)], ngrad.at[pl.ds(r0, T)]
        lo = lane_lo()
        lower = iota((BLOCK, BLOCK), 0) >= iota((BLOCK, BLOCK), 1)
        nblk = T // BLOCK
        for blk in range(nblk):
            rows = slice(blk * BLOCK, (blk + 1) * BLOCK)
            cum = cum_ref[rows]
            cum_t = cum.T
            dt = dt_ref[rows]
            write = act_ref[rows, DI : DI + NSTATE]
            read = act_ref[rows, DI + NSTATE :]
            inner = jnp.where(lower, dot_nt(read, write), 0.0)
            lows[blk] = state[...].astype(BF16)
            ent_ref[blk] = lows[blk]
            for j in range(PAIRS):
                cols, a, b = expand_pair(cum, j, lo)
                ga = jnp.exp2(jnp.minimum(a - cum_t[2 * j : 2 * j + 1], 0.0)) * inner
                gb = jnp.exp2(jnp.minimum(b - cum_t[2 * j + 1 : 2 * j + 2], 0.0)) * inner
                scores = jnp.concatenate([ga.astype(BF16), gb.astype(BF16)], axis=1)
                vals = act_ref[rows, pair(j)].astype(F32)
                dtp, _, _ = expand_pair(dt, j, lo)
                vdt = (vals * dtp).astype(BF16)
                grow = jnp.exp2(cols)
                growth[rows, pair(j)] = grow
                diag = dot(scores, block_diag(vdt))
                out = dot(read, lows[blk, :, pair(j)])
                ms[rows, pair(j)] = diag + grow * out + row_ref[0:1, pair(j)] * vals
                dec = grow[BLOCK - 1 : BLOCK]
                state[:, pair(j)] = state[:, pair(j)] * dec + bst_ref[blk, :, pair(j)].astype(F32)

        sq = jnp.zeros((T, BLOCK), F32)
        ug = jnp.zeros((T, BLOCK), F32)
        for j in range(PAIRS):
            g = gate_s[:, pair(j)].astype(F32)
            gated = ms[:, pair(j)] * (g * sigmoid(g))
            sq = sq + gated * gated
            ug = ug + gated * ng[:, pair(j)].astype(F32)
        inv = lax.rsqrt(jnp.sum(sq, axis=-1, keepdims=True) * (1.0 / DI) + EPS)
        coef = jnp.sum(ug, axis=-1, keepdims=True) * (1.0 / DI) * (inv * inv * inv)
        for j in range(PAIRS):
            g = gate_s[:, pair(j)].astype(F32)
            sg = sigmoid(g)
            silu = g * sg
            m = ms[:, pair(j)]
            gated = m * silu
            nout[:, pair(j)] = (gated * inv * row_ref[1:2, pair(j)]).astype(BF16)
            dg = inv * ng[:, pair(j)].astype(F32) - gated * coef
            low = (dg * silu).astype(BF16)
            mlow_ref[:, pair(j)] = low
            gate_s[:, pair(j)] = (dg * m * (sg + silu * (1.0 - sg))).astype(BF16)
            vals = act_ref[:, pair(j)].astype(F32)
            lowf = low.astype(F32)
            mv = lowf * vals
            pr = lowf * m - row_ref[0:1, pair(j)] * mv
            hi = pr.astype(BF16)
            prod[:, pair(j)] = hi
            plow[:, pair(j)] = (pr - hi.astype(F32)).astype(BF16)
            rlow[:, pair(j)] = (lowf * growth[:, pair(j)]).astype(BF16)
            cols_ref[:, pair(j)] += jnp.sum(mv.reshape(T // 8, 8, BLOCK), axis=0)
        dcum_ref[...] = dot(prod[...], et_ref[...]) + dot(plow[...], et_ref[...])
        mixed_ref[...] = (tok_ref[...].astype(F32) + dot(nout[...], wo_ref[...])).astype(BF16)
        nout_t[:, pl.ds(r0, T)] = nout[...].T
        for blk in range(nblk):
            rows = slice(blk * BLOCK, (blk + 1) * BLOCK)
            read_t = act_ref[rows, DI + NSTATE :].T
            for q in range(PAIRS // 2):
                cs = slice(q * 256, (q + 1) * 256)
                eg = dot(read_t, rlow[rows, cs])
                egrad_ref[blk, :, cs] = eg.astype(BF16)
                back[:, cs] += eg * exg[0:1, cs]
            exg[...] = exg[...] * growth[blk * BLOCK + BLOCK - 1 : blk * BLOCK + BLOCK, :]
            rg_ref[rows] = dot_nt(rlow[rows, :], lows[blk])

    @pl.when((i > 0) & (i < steps - 1))
    def _():
        tile(pl.multiple_of((i - 1) * T, T))
        keep(i).start()

    @pl.when(i == steps - 1)
    def _():
        leave_ref[...] = state[...].astype(BF16)
        second.step(0)
        done = 0
        writes = []
        base = L // T
        for r in range(DI // 256):
            rows = slice(r * 256, (r + 1) * 256)
            ngrad[rows, :D] = dot(nout_t[rows], cot_ref[...]).astype(BF16)
            writes.append((ngrad.at[rows, pl.ds(0, D)], gout_any.at[rows, :]))
            if r % 2 == 1 and r // 2 + 1 < second.n:
                done = r // 2 + 1
                second.step(done)
        for k in range(done + 1, second.n):
            second.step(k)
        for r in range(D // 256):
            src = slice(r * 256, (r + 1) * 256)
            for h in range(2):
                rows, lanes = slice(h * D + r * 256, h * D + (r + 1) * 256), pl.ds(h * D, D)
                part = dot_tn(xhat_ref[:, src], gate[:, h * D : (h + 1) * D])
                ngrad[rows, D:] = part.astype(BF16)
                writes.append((ngrad.at[rows, pl.ds(D, D)], ggate_any.at[src, lanes]))
        copies = [pltpu.make_async_copy(a, b, osem.at[base + k]) for k, (a, b) in enumerate(writes)]
        for c in copies:
            c.start()
        for k in range(1, base + 1):
            keep(k).wait()
        for c in copies:
            c.wait()
        second.done()


def third_kernel(
    T, act_ref, convin_ref, slope_ref, dt_ref, cum_ref, sig_ref, dcum_ref, mlow_ref, ent_ref, leave_ref,
    egrad_ref, rg_ref, inc_ref, row_ref, conv_ref, head_ref, et_ref, go_ref, gg_ref,
    pg_ref, cgrad_ref, hgrad_ref, tail_ref, so_ref, sg_ref,
    glast, xlast, gafter, hsend, hrecv, carry, dact, vprod, prod, plow, weighted, lows, dec, nxt, gext, *scratch,
):
    i = pl.program_id(0)
    steps = pl.num_programs(0)
    sca = Scatter(go_ref, "yx", scratch[2 : 2 + NSC], *scratch[:2])
    scb = Scatter(gg_ref, "xy", scratch[4 + NSC :], *scratch[2 + NSC : 4 + NSC])
    seq, nseq = lax.axis_index("seq"), lax.axis_size("seq")
    after = pltpu.make_async_remote_copy(
        src_ref=gext.at[:, pl.ds(0, 8)], dst_ref=gafter, send_sem=hsend, recv_sem=hrecv, device_id={"seq": seq - 1},
        device_id_type=MESH,
    )

    @pl.when(i == 0)
    def _():
        greet(place(), "zxyc", 1)
        sca.start(0)
        scb.start(0)

    for stage, when in enumerate((1, 3, 5)):
        @pl.when(i == when)
        def _():
            sca.finish(stage)
            sca.start(stage + 1)
            scb.finish(stage)
            scb.start(stage + 1)

    @pl.when(i == steps - 1)
    def _():
        so_ref[...] = sca.result()
        sg_ref[...] = scb.result()

    @pl.when(i == 0)
    def _():
        carry[...] = inc_ref[...]
        nxt[...] = leave_ref[...]
        cgrad_ref[...] = jnp.zeros_like(cgrad_ref)
        hgrad_ref[...] = jnp.zeros_like(hgrad_ref)

    lo = lane_lo()
    upper = iota((BLOCK, BLOCK), 0) <= iota((BLOCK, BLOCK), 1)
    triu = upper.astype(F32)
    last = iota((BLOCK, BLOCK), 0) == BLOCK - 1
    for blk in reversed(range(T // BLOCK)):
        rows = slice(blk * BLOCK, (blk + 1) * BLOCK)
        cum = cum_ref[rows]
        cum_t = cum.T
        dt = dt_ref[rows]
        end = cum[BLOCK - 1 : BLOCK]
        write = act_ref[rows, DI : DI + NSTATE]
        read = act_ref[rows, DI + NSTATE :]
        inner = jnp.where(upper, dot_nt(write, read), 0.0)
        lows[...] = carry[...].astype(BF16)
        acc = jnp.zeros((BLOCK, BLOCK), F32)
        for j in range(PAIRS):
            cols, a, b = expand_pair(cum, j, lo)
            ends = jnp.where(lo[:1], end[:, 2 * j : 2 * j + 1], end[:, 2 * j + 1 : 2 * j + 2])
            wexp = jnp.exp2(ends - cols)
            da = jnp.exp2(jnp.minimum(cum_t[2 * j : 2 * j + 1] - a, 0.0))
            db = jnp.exp2(jnp.minimum(cum_t[2 * j + 1 : 2 * j + 2] - b, 0.0))
            scores = jnp.concatenate([(da * inner).astype(BF16), (db * inner).astype(BF16)], axis=1)
            m = mlow_ref[rows, pair(j)]
            diag = block_diag(m)
            z = dot(scores, diag)
            vals = act_ref[rows, pair(j)].astype(F32)
            dtp, _, _ = expand_pair(dt, j, lo)
            vdt = vals * dtp
            vdtb = vdt.astype(BF16)
            wtb = (vdt * wexp).astype(BF16)
            g = dot_nt(vdtb, diag)
            acc = acc + g[:, :BLOCK] * da + g[:, BLOCK:] * db
            wg = dot(write, lows[:, pair(j)])
            pr = vdtb.astype(F32) * z + wtb.astype(F32) * wg
            z = z + wg * wexp
            dact[rows, pair(j)] = row_ref[0:1, pair(j)] * m.astype(F32) + dtp * z
            vprod[:, pair(j)] = (vals * z).astype(BF16)
            hi = pr.astype(BF16)
            prod[:, pair(j)] = hi
            plow[:, pair(j)] = (pr - hi.astype(F32)).astype(BF16)
            weighted[:, pair(j)] = wtb
            dec[0:1, pair(j)] = jnp.exp2(cols[BLOCK - 1 : BLOCK])
        low = jnp.where(upper, acc, 0.0).astype(BF16)
        dact[rows, DI : DI + NSTATE] = dot_nt(weighted[...], lows[...]) + dot(low, read)
        dact[rows, DI + NSTATE :] = rg_ref[rows] + dot(low.T, write)
        c = dot(vprod[...], et_ref[...])
        used = dot(prod[...], et_ref[...]) + dot(plow[...], et_ref[...])
        ends = jnp.sum((lows[...].astype(F32) * nxt[...].astype(F32)).reshape(16, 8, DI), axis=0)
        ends_hi = ends.astype(BF16)
        ends_lo = (ends - ends_hi.astype(F32)).astype(BF16)
        de = jnp.sum(dot(ends_hi, et_ref[...]) + dot(ends_lo, et_ref[...]), axis=0, keepdims=True)
        dc = dcum_ref[rows] - used + jnp.where(last, de, 0.0)
        da_log = dot_exact(triu, dc)
        draw = (c + da_log * head_ref[1, 1:2]) * sig_ref[rows]
        pg_ref[rows, :BLOCK] = draw.astype(BF16)
        hgrad_ref[0:8] += jnp.sum(draw.reshape(16, 8, BLOCK), axis=0)
        hgrad_ref[8:16] += jnp.sum((da_log * dt).reshape(16, 8, BLOCK), axis=0) * head_ref[1, 1:2]
        nxt[...] = ent_ref[blk]
        for q in range(PAIRS // 2):
            cs = slice(q * 256, (q + 1) * 256)
            carry[:, cs] = carry[:, cs] * dec[0:1, cs] + egrad_ref[blk, :, cs].astype(F32)

    for c in range(CH // 128):
        cs = slice(c * 128, (c + 1) * 128)
        ps = slice(BLOCK + c * 128, BLOCK + (c + 1) * 128)

        @pl.when(i == 0)
        def _():
            gext[c, T : T + 8] = jnp.zeros((8, 128), F32)
            xlast[:, cs] = convin_ref[T - 16 :, ps].astype(F32)

        @pl.when(i > 0)
        def _():
            gext[c, T : T + 8] = gext[c, 0:8]

        for r in range(0, T, 64):
            gext[c, r : r + 64] = dact[r : r + 64, cs] * slope_ref[r : r + 64, cs].astype(F32)
        sums = [jnp.zeros((8, 128), F32)] * 5
        for r in range(0, T, 64):
            x = convin_ref[r : r + 64, ps].astype(F32)
            g = gext[c, r : r + 64]
            back = g * conv_ref[3:4, cs]
            sums[4] = sums[4] + jnp.sum(g.reshape(8, 8, 128), axis=0)
            sums[3] = sums[3] + jnp.sum((g * x).reshape(8, 8, 128), axis=0)
            for k in range(CONV - 1):
                gk = gext[c, 3 - k + r : 3 - k + r + 64]
                back = back + gk * conv_ref[k : k + 1, cs]
                sums[k] = sums[k] + jnp.sum((gk * x).reshape(8, 8, 128), axis=0)
            pg_ref[r : r + 64, ps] = back.astype(BF16)
            if r + 64 == T:
                @pl.when(i == 0)
                def _():
                    glast[:, cs] = back[48:]
        for k in range(5):
            cgrad_ref[8 * k : 8 * k + 8, cs] += sums[k]

    @pl.when(i == steps - 1)
    def _():
        @pl.when(seq > 0)
        def _():
            after.start()

        @pl.when(seq == nseq - 1)
        def _():
            gafter[...] = jnp.zeros_like(gafter)

        @pl.when(seq < nseq - 1)
        def _():
            after.wait_recv()

        row16, row8 = iota((16, 128), 0), iota((8, 128), 0)
        for c in range(CH // 128):
            cs = slice(c * 128, (c + 1) * 128)
            ps = slice(BLOCK + c * 128, BLOCK + (c + 1) * 128)
            tail = glast[:, cs]
            for j in range(CONV - 1):
                for k in range(j + 1):
                    g = gafter[c, j - k : j - k + 1]
                    tail = tail + jnp.where(row16 == 13 + j, g * conv_ref[k : k + 1, cs], 0.0)
                    cgrad_ref[8 * k : 8 * k + 8, cs] += jnp.where(row8 == 0, g * xlast[13 + j : 14 + j, cs], 0.0)
            tail_ref[:, ps] = tail.astype(BF16)
        tail_ref[:, :BLOCK] = jnp.zeros((16, BLOCK), BF16)

        @pl.when(seq > 0)
        def _():
            after.wait_send()


def once(shape):
    return pl.BlockSpec(shape, lambda i: (0,) * len(shape), pipeline_mode=pl.Buffered(1))


def full(shape):
    return pl.BlockSpec(shape, lambda i: (0,) * len(shape))


def params(collective_id=None):
    return pltpu.CompilerParams(
        dimension_semantics=("arbitrary",), vmem_limit_bytes=VMEM_LIMIT, collective_id=collective_id,
        has_side_effects=collective_id is not None,
    )


def head_columns():
    et = np.zeros((DI, BLOCK), np.float32)
    et[np.arange(DI), np.arange(DI) // HEADDIM] = 1.0
    return et


def sds(shape, dtype):
    return jax.ShapeDtypeStruct(shape, dtype)


def first_pass(w_in, small, tok, slab_o, T=256):
    L = tok.shape[0]
    nb, per = L // BLOCK, T // BLOCK
    n = sizes()
    k_rows = w_in.shape[0]
    total = lax.axis_size("dp") * lax.axis_size("seq")
    row = lambda w: pl.BlockSpec((T, w), lambda i: (jnp.maximum(i - 1, 0), 0))
    dims = (n["z"], n["x"], n["y"], n["c"])
    sems = []
    for _ in range(len(CHUNKS) + 4):
        sems += gather_sems()
    return pl.pallas_call(
        functools.partial(first_kernel, T),
        grid=(1 + L // T,),
        in_specs=[once(w_in.shape), once((2, 8, BLOCK)), ANY, ANY],
        out_specs=[
            ANY, ANY, ANY, ANY, full((16, WC)), full((8, CH)), full((8, D)), full((8, DI)),
            row(CH), row(CH), row(BLOCK), row(BLOCK), row(BLOCK),
            pl.BlockSpec((per, NSTATE, DI), lambda i: (jnp.maximum(i - 1, 0), 0, 0)), full((NSTATE, DI)),
            full((8, BLOCK)), ANY, ANY,
        ],
        out_shape=[
            sds((L, D), BF16), sds((D, L), BF16), sds((D, WC), BF16), sds((L, WC), BF16), sds((16, WC), BF16),
            sds((8, CH), F32), sds((8, D), F32), sds((8, DI), F32),
            sds((L, CH), BF16), sds((L, CH), BF16), sds((L, BLOCK), F32), sds((L, BLOCK), F32), sds((L, BLOCK), F32),
            sds((nb, NSTATE, DI), BF16), sds((NSTATE, DI), F32), sds((8, BLOCK), F32),
            sds(dims + (k_rows, DI), BF16), sds(dims + slab_o.shape, BF16),
        ],
        scratch_shapes=[
            pltpu.VMEM((k_rows, WC), BF16), pltpu.VMEM((L, D), BF16), pltpu.VMEM((16, D), BF16), pltpu.VMEM((L, D), BF16), pltpu.VMEM((D, L), BF16),
            pltpu.VMEM((D, WC), BF16), pltpu.VMEM((D, 512), F32), pltpu.VMEM((L, WC), BF16),
            pltpu.VMEM((total, 8, BLOCK), F32),
        ] + [pltpu.VMEM(dims + (k_rows, w), BF16) for _, w in CHUNKS] + [
            pltpu.VMEM((CH // 128, T + 8, 128), F32), pltpu.VMEM((NSTATE, DI), F32), pltpu.VMEM((BLOCK, DI), BF16),
            pltpu.SemaphoreType.DMA((5 + 2 * len(CHUNKS),)), pltpu.SemaphoreType.DMA(()), pltpu.SemaphoreType.DMA(()),
            pltpu.SemaphoreType.DMA((total - 1,)), pltpu.SemaphoreType.DMA((total - 1,)),
        ] + sems,
        compiler_params=params(collective_id=1),
        name="first_pass",
    )(w_in, small, tok, slab_o)


def second_pass(xhat, cot, wg, wo, leave1, tot, act, dt, cum, bst, tok, rows, et, T=256):
    L = tok.shape[0]
    nb, per, nt = L // BLOCK, T // BLOCK, L // T
    at = lambda i: jnp.clip(i - 1, 0, nt - 1)
    row = lambda w: pl.BlockSpec((T, w), lambda i: (at(i), 0))
    blk = pl.BlockSpec((per, NSTATE, DI), lambda i: (at(i), 0, 0))
    return pl.pallas_call(
        functools.partial(second_kernel, T),
        grid=(nt + 2,),
        in_specs=[
            once((L, D)), once((L, D)), once((D, DI)), once((DI, D)), once((NSTATE, DI)), once((8, BLOCK)), row(CH),
            row(BLOCK), row(BLOCK), blk, row(D), once((8, DI)), once((DI, BLOCK)),
        ],
        out_specs=[
            row(D), row(DI), row(BLOCK), blk, blk, row(BLOCK), once((NSTATE, DI)), once((NSTATE, DI)), once((8, DI)),
            ANY, ANY, ANY,
        ],
        out_shape=[
            sds((L, D), BF16), sds((L, DI), BF16), sds((L, BLOCK), F32), sds((nb, NSTATE, DI), BF16),
            sds((nb, NSTATE, DI), BF16), sds((L, BLOCK), F32), sds((NSTATE, DI), BF16), sds((NSTATE, DI), F32),
            sds((8, DI), F32), sds((L, DI), BF16), sds((DI, D), BF16), sds((D, DI), BF16),
        ],
        scratch_shapes=[
            pltpu.VMEM((L, DI), BF16), pltpu.VMEM((L, DI), BF16), pltpu.VMEM((DI, L), BF16), pltpu.VMEM((T, DI), BF16),
            pltpu.VMEM((T, DI), F32), pltpu.VMEM((T, DI), F32), pltpu.VMEM((T, DI), BF16), pltpu.VMEM((T, DI), BF16),
            pltpu.VMEM((T, DI), BF16), pltpu.VMEM((NSTATE, DI), F32), pltpu.VMEM((NSTATE, DI), F32),
            pltpu.VMEM((8, DI), F32), pltpu.VMEM((per, NSTATE, DI), BF16), pltpu.VMEM((8, DI), F32),
            pltpu.SemaphoreType.DMA((nt + DI // 256 + 2 * (D // 256),)),
        ] + chain_scratch() + chain_scratch(),
        compiler_params=params(collective_id=2),
        name="second_pass",
    )(xhat, cot, wg, wo, leave1, tot, act, dt, cum, bst, tok, rows, et)


def third_pass(
    act, convin, slope, dt, cum, sig, dcum, mlow, ent, leave, egrad, rg, inc, rows, conv, head, et, go, gg, T=256
):
    L = act.shape[0]
    m = sizes()
    dims = (m["z"], m["x"], m["y"], m["c"])
    total = m["z"] * m["y"] * 4
    ro, rg_rows = DI // total, D // total
    go = go.reshape(dims + (ro, D))
    gg = gg.reshape(dims + (rg_rows, DI))
    n, per = L // T, T // BLOCK
    row = lambda w: pl.BlockSpec((T, w), lambda i: (n - 1 - i, 0))
    blk = pl.BlockSpec((per, NSTATE, DI), lambda i: (n - 1 - i, 0, 0))
    return pl.pallas_call(
        functools.partial(third_kernel, T),
        grid=(n,),
        in_specs=[
            row(CH), row(WC), row(CH), row(BLOCK), row(BLOCK), row(BLOCK), row(BLOCK), row(DI), blk,
            full((NSTATE, DI)), blk, row(BLOCK), full((NSTATE, DI)), full((8, DI)), full((8, CH)), full((2, 8, BLOCK)),
            full((DI, BLOCK)), ANY, ANY,
        ],
        out_specs=[
            row(WC), full((40, CH)), full((16, BLOCK)), full((16, WC)), full((ro, D)), full((rg_rows, DI)),
        ],
        out_shape=[
            sds((L, WC), BF16), sds((40, CH), F32), sds((16, BLOCK), F32), sds((16, WC), BF16), sds((ro, D), F32),
            sds((rg_rows, DI), F32),
        ],
        scratch_shapes=[
            pltpu.VMEM((16, CH), F32), pltpu.VMEM((16, CH), F32), pltpu.VMEM((CH // 128, 8, 128), F32),
            pltpu.SemaphoreType.DMA(()), pltpu.SemaphoreType.DMA(()),
            pltpu.VMEM((NSTATE, DI), F32), pltpu.VMEM((T, CH), F32), pltpu.VMEM((BLOCK, DI), BF16), pltpu.VMEM((BLOCK, DI), BF16), pltpu.VMEM((BLOCK, DI), BF16),
            pltpu.VMEM((BLOCK, DI), BF16), pltpu.VMEM((NSTATE, DI), BF16), pltpu.VMEM((8, DI), F32),
            pltpu.VMEM((NSTATE, DI), BF16), pltpu.VMEM((CH // 128, T + 8, 128), F32),
        ] + own_scratch(ro, D) + scatter_scratch(ro, D) + own_scratch(rg_rows, DI) + scatter_scratch(rg_rows, DI),
        compiler_params=params(collective_id=4),
        name="third_pass",
    )(act, convin, slope, dt, cum, sig, dcum, mlow, ent, leave, egrad, rg, inc, rows, conv, head, et, go, gg)


def on_device(
    tokens, cotangent, norm_gain, in_weight, conv_weight, conv_bias, step_bias, decay_log, skip_gain, gate_gain,
    out_weight,
):
    tok, cot = tokens[0], cotangent[0]
    L = tok.shape[0]
    k_rows, c_rows = in_weight.shape[0], conv_weight.shape[0]
    total = D // k_rows
    lanes = lambda x: jnp.pad(x, ((0, 0),) * (x.ndim - 1) + ((0, BLOCK - x.shape[-1]),))

    def put(x, row):
        x = x.astype(F32)
        return jnp.pad(x, ((row, 16 - row - x.shape[0]), (0, BLOCK - x.shape[1])))

    own = put(conv_weight.T, 0) + put(conv_bias[None], 4) + put(norm_gain[None], 5) + put(gate_gain[None], 6)
    own = own + put(step_bias[None], 8) + put(-jnp.exp(decay_log)[None], 9) + put(skip_gain[None], 10)
    own = own.reshape(2, 8, BLOCK)
    et = jnp.asarray(head_columns(), BF16)

    (xhat, xt, wc, p, hp, conv, gain, rows, act, slope, dt, cum, sig, bst, leave, tot, buf_g, buf_o) = first_pass(
        in_weight, own, tok, out_weight
    )
    wg, wo = buf_g.reshape(D, DI), buf_o.reshape(DI, D)
    mixed, mlow, dcum, ent, egrad, rg, leave2, later, cols, ggrad, g_out, g_gate = second_pass(
        xhat, cot, wg, wo, leave, tot, act, dt, cum, bst, tok, rows, et
    )
    pg, cgrad, hgrad, tail, out_raw, gate_cols = third_pass(
        act, p, slope, dt, cum, sig, dcum, mlow, ent, leave2, egrad, rg, later, rows, conv, own, et, g_out, g_gate
    )
    cg = cgrad.reshape(5, 8, CH).sum(axis=1)
    hg = hgrad.reshape(2, 8, BLOCK).sum(axis=1)[:, :HEADS]
    sums = jnp.concatenate([hg[0], hg[1], cols.reshape(8, HEADS, HEADDIM).sum(axis=(0, 2))])
    small = jnp.concatenate(
        [
            lanes(jnp.swapaxes(cg.reshape(5, total, c_rows), 0, 1)), jnp.zeros((total, 2, BLOCK), F32),
            jnp.broadcast_to(lanes(sums[None, None]), (total, 1, BLOCK)),
        ],
        axis=1,
    )
    tgrad, conv_cols, sums = last_pass(xt, pg, tail, ggrad, tok, cot, wg, wc, gain, small)
    in_grad, ngain_grad, ggain_grad, taps, bias, step, decay, skip, out_grad, tgrad, mixed = finish_pass(
        gate_cols, conv_cols, out_raw, sums, in_weight, out_weight, norm_gain.astype(F32), gate_gain.astype(F32), tgrad,
        mixed, c_rows,
    )
    return (
        mixed[None], tgrad[None], ngain_grad, in_grad, taps, bias, step, decay, skip, ggain_grad, out_grad,
    )


def solution(mesh):
    both = ("dp", "seq")
    vec, mat, tok, rep = P(both), P(both, None), P("dp", "seq", None), P()
    return jax.shard_map(
        on_device,
        mesh=mesh,
        in_specs=(tok, tok, vec, mat, mat, vec, rep, rep, rep, vec, mat),
        out_specs=(tok, tok, vec, mat, mat, vec, rep, rep, rep, vec, mat),
        check_vma=False,
    )
```

```python
import functools

import jax
import jax.numpy as jnp
import numpy as np
from jax import lax
from jax.experimental import pallas as pl
from jax.experimental.pallas import tpu as pltpu
from jax.sharding import PartitionSpec as P

D = 768
HEADS = 24
HEADDIM = 64
NSTATE = 128
CONV = 4
BLOCK = 128
DI = 1536
CH = 1792
PAIRS = HEADS // 2
EPS = 1e-05
LOG2E = 1.4426950408889634
F32 = jnp.float32
BF16 = jnp.bfloat16
NT = (((1,), (1,)), ((), ()))
VMEM_LIMIT = 60 * 1024 * 1024


def dot(a, b):
    return jnp.dot(a, b, preferred_element_type=F32)


def dot_nt(a, b):
    return lax.dot_general(a, b, NT, preferred_element_type=F32)


def dot_exact(a, b):
    return jnp.dot(a, b, preferred_element_type=F32, precision=lax.Precision.HIGHEST)


def sigmoid(v):
    return 0.5 * jnp.tanh(0.5 * v) + 0.5


def iota(shape, dim):
    return lax.broadcasted_iota(jnp.int32, shape, dim)


def lane_lo():
    return iota((BLOCK, BLOCK), 1) < HEADDIM


def expand_pair(x, j, lo):
    rows = x.shape[0]
    a = jnp.broadcast_to(x[:, 2 * j : 2 * j + 1], (rows, BLOCK))
    b = jnp.broadcast_to(x[:, 2 * j + 1 : 2 * j + 2], (rows, BLOCK))
    return jnp.where(lo, a, b), a, b


def block_diag(v):
    lo = iota(v.shape, 1) < HEADDIM
    zero = jnp.zeros_like(v)
    return jnp.concatenate([jnp.where(lo, v, zero), jnp.where(lo, zero, v)], axis=0)


def pair(j):
    return slice(j * BLOCK, (j + 1) * BLOCK)


MESH = pl.DeviceIdType.MESH
ANY = pl.BlockSpec(memory_space=pl.ANY)
WC = CH + BLOCK
TN = (((0,), (0,)), ((), ()))


def dot_tn(a, b):
    return lax.dot_general(a, b, TN, preferred_element_type=F32)


def sizes():
    return {"z": lax.axis_size("dp") // 2, "x": 2, "y": lax.axis_size("seq") // 2, "c": 2}


def place():
    dp, seq = lax.axis_index("dp"), lax.axis_index("seq")
    return {"z": dp // 2, "x": lax.rem(dp, 2), "y": seq // 2, "c": lax.rem(seq, 2)}


def device(at):
    return {"dp": at["z"] * 2 + at["x"], "seq": at["y"] * 2 + at["c"]}


def peers(at, axis):
    n = sizes()[axis]
    return [dict(at, **{axis: lax.rem(at[axis] + o, n)}) for o in range(1, n)]


def greet(at, axes, by=0):
    sem = pltpu.get_barrier_semaphore()
    count = 0
    for axis in axes:
        for peer in peers(at, axis):
            pl.semaphore_signal(sem, inc=1, device_id=device(peer), device_id_type=MESH)
            count += 1
    if not by:
        pl.semaphore_wait(sem, count)
        return
    seq, n = lax.axis_index("seq"), lax.axis_size("seq")

    @pl.when((seq + by >= 0) & (seq + by < n))
    def _():
        pl.semaphore_signal(sem, inc=1, device_id={"seq": seq + by}, device_id_type=MESH)

    heard = (seq - by >= 0) & (seq - by < n)

    @pl.when(heard)
    def _():
        pl.semaphore_wait(sem, count + 1)

    @pl.when(jnp.logical_not(heard))
    def _():
        pl.semaphore_wait(sem, count)


def greet_neighbours():
    seq, n = lax.axis_index("seq"), lax.axis_size("seq")
    sem = pltpu.get_barrier_semaphore()

    @pl.when(seq > 0)
    def _():
        pl.semaphore_signal(sem, inc=1, device_id={"seq": seq - 1}, device_id_type=MESH)

    @pl.when(seq < n - 1)
    def _():
        pl.semaphore_signal(sem, inc=1, device_id={"seq": seq + 1}, device_id_type=MESH)

    @pl.when((seq > 0) & (seq < n - 1))
    def _():
        pl.semaphore_wait(sem, 2)

    @pl.when((seq == 0) | (seq == n - 1))
    def _():
        pl.semaphore_wait(sem, 1)


def remote(src, dst, send, recv, peer):
    return pltpu.make_async_remote_copy(
        src_ref=src, dst_ref=dst, send_sem=send, recv_sem=recv, device_id=device(peer), device_id_type=MESH
    )


class Gather:
    def __init__(self, slab, spot, order, sems):
        self.slab, self.spot, self.order = slab, spot, order
        self.send, self.recv = sems
        self.at = place()

    def copies(self, stage):
        at, (a, b) = self.at, self.order
        n = sizes()
        out = []
        every = slice(None)
        nz = n["z"] - 1
        if stage == 0:
            for o, peer in enumerate(peers(at, "z")):
                out.append((self.slab, self.spot(at), o, peer))
        elif stage == 1:
            index = dict(at, z=every)
            out.append((self.spot(index), self.spot(index), nz, peers(at, a)[0]))
        elif stage == 2:
            index = dict(at, z=every)
            index[a] = every
            for o, peer in enumerate(peers(at, b)):
                out.append((self.spot(index), self.spot(index), nz + 1 + o, peer))
            out.append((self.spot(index), self.spot(index), nz + 1 + n[b] - 1, peers(at, "c")[0]))
        else:
            for o in range(1, n[b]):
                index = dict(at, z=every)
                index[a] = every
                index[b] = lax.rem(at[b] + o, n[b])
                out.append((self.spot(index), self.spot(index), nz + 1 + n[b] + o - 1, peers(at, "c")[0]))
        return [remote(s, d, self.send.at[k], self.recv.at[k], p) for s, d, k, p in out]

    def start(self, stage):
        for c in self.copies(stage):
            c.start()

    def wait(self, stage):
        for c in self.copies(stage):
            c.wait()


def spots(buf, lanes=slice(None)):
    return lambda index: buf.at[index["z"], index["x"], index["y"], index["c"], :, lanes]


def gather_sems():
    count = sizes()["z"] + 2 * sizes()["y"] + 4
    return [pltpu.SemaphoreType.DMA((count,)), pltpu.SemaphoreType.DMA((count,))]


class Scatter:
    def __init__(self, grads, order, scratch, own=None, local=None):
        self.grads, self.order, self.own_ref, self.local = grads, order, own, local
        self.rc, self.r1, self.r2, self.rz, self.send, self.recv = scratch
        self.at = place()
        self.own = self

    def spot(self, z, x, y):
        if self.own_ref is not None:
            return self.own_ref.at[z, x, y]
        return self.grads.at[z, x, y, self.at["c"]]

    def add(self, z, x, y, got):
        mine = self.spot(z, x, y)
        mine[...] = (mine[...].astype(F32) + got.astype(F32)).astype(BF16)

    def copies(self, stage):
        at, (a, b) = self.at, self.order
        every = slice(None)
        out = []

        def spot(index):
            return self.spot(index["z"], index["x"], index["y"])

        if stage == 0:
            out.append((self.grads.at[:, :, :, 1 - at["c"]], self.rc, 0, peers(at, "c")[0]))
        elif stage == 1:
            index = {"z": every, "x": every, "y": every}
            index[a] = 1 - at[a]
            out.append((spot(index), self.r1, 1, peers(at, a)[0]))
        elif stage == 2:
            index = {"z": every, a: at[a], b: 1 - at[b]}
            out.append((spot(index), self.r2, 2, peers(at, b)[0]))
        else:
            for o, peer in enumerate(peers(at, "z")):
                out.append((self.spot(peer["z"], at["x"], at["y"]), self.rz.at[o], 3 + o, peer))
        return [remote(s, d, self.send.at[k], self.recv.at[k], p) for s, d, k, p in out]

    def mine(self):
        return pltpu.make_async_copy(self.grads.at[:, :, :, self.at["c"]], self.own_ref, self.local)

    def start(self, stage):
        if stage == 0 and self.own_ref is not None:
            self.mine().start()
        for c in self.copies(stage):
            c.start()

    def finish(self, stage):
        at, (a, b) = self.at, self.order
        for c in self.copies(stage):
            c.wait()
        nz = sizes()["z"]
        if stage == 0:
            if self.own_ref is not None:
                self.mine().wait()

            def body(z, _):
                for x in range(2):
                    for y in range(2):
                        self.add(z, x, y, self.rc[z, x, y])
                return _

        elif stage == 1:

            def body(z, _):
                for k in range(2):
                    index = {a: at[a], b: k}
                    self.add(z, index["x"], index["y"], self.r1[z, k])
                return _

        else:

            def body(z, _):
                self.add(z, at["x"], at["y"], self.r2[z])
                return _

        lax.fori_loop(0, nz, body, 0)

    def result(self):
        for c in self.copies(3):
            c.wait()
        total = self.spot(self.at["z"], self.at["x"], self.at["y"])[...].astype(F32)
        for o in range(sizes()["z"] - 1):
            total = total + self.rz[o].astype(F32)
        return total


def scatter_scratch(rows, width):
    nz = sizes()["z"]
    return [
        pltpu.VMEM((nz, 2, 2, rows, width), BF16), pltpu.VMEM((nz, 2, rows, width), BF16),
        pltpu.VMEM((nz, rows, width), BF16), pltpu.VMEM((nz - 1, rows, width), BF16),
        pltpu.SemaphoreType.DMA((nz + 2,)), pltpu.SemaphoreType.DMA((nz + 2,)),
    ]


NSC = 6


def own_scratch(rows, width):
    return [pltpu.VMEM((sizes()["z"], 2, 2, rows, width), BF16), pltpu.SemaphoreType.DMA(())]


class Chain:
    def __init__(self, leave, inc, decay, bufs, reverse):
        self.leave, self.inc, self.decay, self.reverse = leave, inc, decay, reverse
        self.got, self.put, self.send, self.recv = bufs
        self.n = lax.axis_size("seq")
        seq = lax.axis_index("seq")
        self.rank = self.n - 1 - seq if reverse else seq
        self.to = seq - 1 if reverse else seq + 1

    def copy(self):
        return pltpu.make_async_remote_copy(
            src_ref=self.put, dst_ref=self.got, send_sem=self.send, recv_sem=self.recv,
            device_id={"seq": self.to}, device_id_type=MESH,
        )

    def step(self, k):
        @pl.when(self.rank == k)
        def _():
            if k == 0:
                self.inc[...] = jnp.zeros_like(self.inc)
                self.put[...] = self.leave[...].astype(BF16)
            else:
                self.copy().wait_recv()
                got = self.got[...].astype(F32)
                self.inc[...] = got
                if k < self.n - 1:
                    self.put[...] = (got * self.decay[0:1] + self.leave[...]).astype(BF16)
            if k < self.n - 1:
                self.copy().start()

    def done(self):
        @pl.when(self.rank < self.n - 1)
        def _():
            self.copy().wait_send()


def chain_scratch():
    return [
        pltpu.VMEM((NSTATE, DI), BF16), pltpu.VMEM((NSTATE, DI), BF16), pltpu.SemaphoreType.DMA(()),
        pltpu.SemaphoreType.DMA(()),
    ]


def expand_row(row, dst):
    lo = iota((8, BLOCK), 1) < HEADDIM
    wide = jnp.broadcast_to(row, (8, BLOCK))
    for j in range(PAIRS):
        dst[:, pair(j)] = expand_pair(wide, j, lo)[0]


CHUNKS = ((0, 512), (512, 512), (1024, 512), (1536, 384))
ORDERS = ("xy", "yx", "xy", "yx")


def gate_kernel(normed_ref, wg_ref, cot_ref, wo_ref, gain_ref, leave_ref, tot_ref, gate_ref, ng_ref, inc_ref, decay, *bufs):
    i = pl.program_id(0)
    chain = Chain(leave_ref, inc_ref, decay, bufs, False)
    last = pl.num_programs(0) - 1

    @pl.when(i == 0)
    def _():
        expand_row(jnp.exp2(tot_ref[0:1]), decay)
        greet_neighbours()
        chain.step(0)

    for c in range(DI // 256):
        cs = slice(c * 256, (c + 1) * 256)
        gate_ref[:, cs] = dot(normed_ref[...], wg_ref[:, cs]).astype(BF16)
        ng_ref[:, cs] = (dot_nt(cot_ref[...], wo_ref[cs, :]) * gain_ref[1:2, cs]).astype(BF16)
    for k in range(1, chain.n):
        @pl.when(i == (0, 2, 3)[min(k, 3) - 1])
        def _():
            chain.step(k)

    @pl.when(i == last)
    def _():
        chain.done()


def gate_pass(normed, wg, cot, wo, gain, leave, tot, T=512):
    L = normed.shape[0]
    row = lambda w: pl.BlockSpec((T, w), lambda i: (i, 0))
    return pl.pallas_call(
        gate_kernel,
        grid=(L // T,),
        in_specs=[
            row(D), full((D, DI)), row(D), full((DI, D)), full((8, DI)), full((NSTATE, DI)), full((8, BLOCK)),
        ],
        out_specs=[row(DI), row(DI), full((NSTATE, DI))],
        out_shape=[sds((L, DI), BF16), sds((L, DI), BF16), sds((NSTATE, DI), F32)],
        scratch_shapes=[pltpu.VMEM((8, DI), F32)] + chain_scratch(),
        compiler_params=params(collective_id=2),
        name="gate_pass",
    )(normed, wg, cot, wo, gain, leave, tot)


def grads_kernel(nout_ref, cot_ref, xt_ref, ggrad_ref, back_ref, tot_ref, gout_ref, ggate_ref, inc_ref, decay, *bufs):
    i = pl.program_id(0)
    chain = Chain(back_ref, inc_ref, decay, bufs, True)
    last = pl.num_programs(0) - 1

    @pl.when(i == 0)
    def _():
        expand_row(jnp.exp2(tot_ref[0:1]), decay)
        greet_neighbours()
        chain.step(0)

    gout_ref[...] = dot_tn(nout_ref[...], cot_ref[...]).astype(BF16)
    ggate_ref[...] = dot(xt_ref[...], ggrad_ref[...]).astype(BF16)
    for k in range(1, chain.n):
        @pl.when(i == (0, 3, 5)[min(k, 3) - 1])
        def _():
            chain.step(k)

    @pl.when(i == last)
    def _():
        chain.done()


def grads_pass(nout, cot, xt, ggrad, back, tot):
    L = nout.shape[0]
    col = lambda w: pl.BlockSpec((L, w), lambda i: (0, i))
    return pl.pallas_call(
        grads_kernel,
        grid=(6,),
        in_specs=[
            col(256), full((L, D)), pl.BlockSpec((128, L), lambda i: (i, 0)), full((L, DI)), full((NSTATE, DI)),
            full((8, BLOCK)),
        ],
        out_specs=[
            pl.BlockSpec((256, D), lambda i: (i, 0)), pl.BlockSpec((128, DI), lambda i: (i, 0)), full((NSTATE, DI)),
        ],
        out_shape=[sds((DI, D), BF16), sds((D, DI), BF16), sds((NSTATE, DI), F32)],
        scratch_shapes=[pltpu.VMEM((8, DI), F32)] + chain_scratch(),
        compiler_params=params(collective_id=3),
        name="grads_pass",
    )(nout, cot, xt, ggrad, back, tot)


def last_kernel(
    T, xt_any, pg_any, wg_any, wc_any, tail_ref, ggrad_ref, tok_ref, cot_ref, gain_ref, small_ref,
    tgrad_ref, gout_ref, sums_ref, xt, wg, wc, pg, g0, g1, g2, g3, lsem, smalls, ssend, srecv, *scratch,
):
    i = pl.program_id(0)
    nc = len(CHUNKS)
    grads = (g0, g1, g2, g3)
    sc = [Scatter(grads[k], ORDERS[k][::-1], scratch[NSC * k : NSC * k + NSC]) for k in range(nc)]
    dp, seq = lax.axis_index("dp"), lax.axis_index("seq")
    n_dp, n_seq = lax.axis_size("dp"), lax.axis_size("seq")
    total = n_dp * n_seq
    me = dp * n_seq + seq
    L = pg.shape[0]

    whole = ((xt_any, xt), (wg_any, wg), (wc_any, wc))

    def load(k):
        if k >= nc:
            return pltpu.make_async_copy(*whole[k - nc], lsem.at[k])
        lanes = pl.ds(CHUNKS[k][0], CHUNKS[k][1])
        return pltpu.make_async_copy(pg_any.at[:, lanes], pg.at[:, lanes], lsem.at[k])

    def far(o):
        r = lax.rem(me + o, total)
        return {"dp": r // n_seq, "seq": lax.rem(r, n_seq)}

    def small(o):
        r = lax.rem(me + o, total)
        return pltpu.make_async_remote_copy(
            src_ref=small_ref.at[r], dst_ref=smalls.at[o - 1], send_sem=ssend.at[o - 1], recv_sem=srecv.at[o - 1],
            device_id=far(o), device_id_type=MESH,
        )

    @pl.when(i == 0)
    def _():
        load(nc).start()
        load(0).start()
        sem = pltpu.get_barrier_semaphore()
        for o in range(1, total):
            pl.semaphore_signal(sem, inc=1, device_id=far(o), device_id_type=MESH)

    for k in range(nc):
        @pl.when(i == k)
        def _():
            lane, width = CHUNKS[k]
            if k == 0:
                load(nc).wait()
            load(k).wait()
            if k + 1 < nc:
                load(k + 1).start()
            if k >= nc - 2:
                load(nc + 1 + k - (nc - 2)).start()
            skip = BLOCK if k == 0 else 0
            pg[L - 16 :, lane + skip : lane + width] = tail_ref[:, lane + skip : lane + width]
            rows = grads[k].shape[4]
            for q in range(2):
                half = D // 2
                g = dot(xt[q * half : (q + 1) * half], pg[:, lane : lane + width])
                for r in range(half // rows):
                    s = r + q * (half // rows)
                    grads[k][s // 8, (s // 4) % 2, (s // 2) % 2, s % 2] = g[r * rows : (r + 1) * rows].astype(BF16)
            if k == 0:
                pl.semaphore_wait(pltpu.get_barrier_semaphore(), total - 1)
                sc[0].start(0)
                for o in range(1, total):
                    small(o).start()
            else:
                sc[k - 1].finish(0)
                sc[k - 1].start(1)
                sc[k].start(0)

    @pl.when(i >= nc)
    def _():
        r0 = pl.multiple_of((i - nc) * T, T)

        @pl.when(i == nc)
        def _():
            load(nc + 1).wait()
            load(nc + 2).wait()

        u = dot_nt(ggrad_ref[...], wg[...]) + dot_nt(pg[pl.ds(r0, T), :], wc[...])
        u = u * gain_ref[0:1]
        x = tok_ref[...].astype(F32)
        inv = lax.rsqrt(jnp.mean(x * x, axis=-1, keepdims=True) + EPS)
        xi = x * inv
        coef = inv * jnp.mean(u * xi, axis=-1, keepdims=True)
        tgrad_ref[...] = (cot_ref[...].astype(F32) + inv * u - xi * coef).astype(BF16)

    def after(step, what):
        @pl.when(i == step)
        def _():
            for k, stage in what:
                sc[k].finish(stage)
                sc[k].start(stage + 1)

    after(nc + 1, [(3, 0)])
    after(nc + 3, [(0, 1)])
    after(nc + 4, [(1, 1)])
    after(nc + 5, [(2, 1)])
    after(nc + 6, [(3, 1), (0, 2)])
    after(nc + 7, [(1, 2), (2, 2), (3, 2)])

    @pl.when(i == pl.num_programs(0) - 1)
    def _():
        for o in range(1, total):
            small(o).wait()
        acc = small_ref[me]
        for o in range(1, total):
            acc = acc + smalls[o - 1]
        sums_ref[...] = acc
        for k in range(nc):
            lane, width = CHUNKS[k]
            gout_ref[:, lane : lane + width] = sc[k].result()


def last_pass(xt, pg, tail, ggrad, tok, cot, wg, wc, gain, small):
    L = tok.shape[0]
    T = L // 8
    n = sizes()
    nc = len(CHUNKS)
    total = lax.axis_size("dp") * lax.axis_size("seq")
    rows = D // total
    row = lambda w: pl.BlockSpec((T, w), lambda i: (jnp.maximum(i - nc, 0), 0))
    scratch = []
    for _, w in CHUNKS:
        scratch += scatter_scratch(rows, w)
    return pl.pallas_call(
        functools.partial(last_kernel, T),
        grid=(nc + L // T,),
        in_specs=[
            ANY, ANY, ANY, ANY, once((16, WC)), row(DI), row(D), row(D), once((8, D)), once((total, 8, BLOCK)),
        ],
        out_specs=[row(D), full((rows, WC)), full((8, BLOCK))],
        out_shape=[sds((L, D), BF16), sds((rows, WC), F32), sds((8, BLOCK), F32)],
        scratch_shapes=[
            pltpu.VMEM((D, L), BF16), pltpu.VMEM((D, DI), BF16), pltpu.VMEM((D, WC), BF16), pltpu.VMEM((L, WC), BF16),
        ]
        + [pltpu.VMEM((n["z"], 2, n["y"], 2, rows, w), BF16) for _, w in CHUNKS]
        + [
            pltpu.SemaphoreType.DMA((nc + 3,)), pltpu.VMEM((total - 1, 8, BLOCK), F32),
            pltpu.SemaphoreType.DMA((total - 1,)), pltpu.SemaphoreType.DMA((total - 1,)),
        ] + scratch,
        compiler_params=params(collective_id=5),
        name="last_pass",
    )(xt, pg, wg, wc, tail, ggrad, tok, cot, gain, small)


def finish_kernel(
    gate_ref, conv_ref, out_ref, sums_ref, w_ref, wo_ref, gain_ref, ggain_ref, tgrad_ref,
    in_grad, ngain, ggain, taps, bias, step, decay, skip, out_grad, tgrad_out,
):
    tgrad_out[...] = tgrad_ref[...]

    @pl.when(pl.program_id(0) == 0)
    def _():
        finish_small(
            gate_ref, conv_ref, out_ref, sums_ref, w_ref, wo_ref, gain_ref, ggain_ref, in_grad, ngain, ggain, taps, bias,
            step, decay, skip, out_grad,
        )


def finish_small(
    gate_ref, conv_ref, out_ref, sums_ref, w_ref, wo_ref, gain_ref, ggain_ref,
    in_grad, ngain, ggain, taps, bias, step, decay, skip, out_grad,
):
    conv = conv_ref[...]
    raw = jnp.concatenate([gate_ref[...], conv[:, BLOCK:], conv[:, :HEADS]], axis=1)
    in_grad[...] = raw
    ngain[...] = jnp.sum(raw * w_ref[...].astype(F32), axis=1) / gain_ref[...]
    o = out_ref[...]
    out_grad[...] = o
    ggain[...] = jnp.sum(o * wo_ref[...].astype(F32), axis=1) / ggain_ref[...]
    s = sums_ref[...]
    n = bias.shape[0]
    taps[...] = s.T[:n, :CONV]
    bias[...] = s[4, :n]
    step[...] = s[7, :HEADS]
    decay[...] = s[7, HEADS : 2 * HEADS]
    skip[...] = s[7, 2 * HEADS : 3 * HEADS]


def finish_pass(gate_cols, conv_cols, out_raw, sums, w, wo, gain, ggain, tgrad, channels):
    vec = lambda n: sds((n,), F32)
    rows = pl.BlockSpec((512, D), lambda i: (i, 0))
    small = [
        sds(w.shape, F32), vec(w.shape[0]), vec(wo.shape[0]), sds((channels, CONV), F32),
        vec(channels), vec(HEADS), vec(HEADS), vec(HEADS), sds(out_raw.shape, F32),
    ]
    ins = (gate_cols, conv_cols, out_raw, sums, w, wo, gain, ggain)
    return pl.pallas_call(
        finish_kernel,
        grid=(tgrad.shape[0] // 512,),
        in_specs=[once(x.shape) for x in ins] + [rows],
        out_specs=[once(x.shape) for x in small] + [rows],
        out_shape=small + [sds(tgrad.shape, BF16)],
        name="finish_pass",
    )(*ins, tgrad)


def rms_rows(tok, gain):
    x = tok.astype(F32)
    return (x * lax.rsqrt(jnp.mean(x * x, axis=-1, keepdims=True) + EPS) * gain).astype(BF16)


def first_kernel(
    T, win_ref, small, tok_any, so_ref,
    xhat_any, xt_any, wc_any, p_any, hp_ref, conv_ref, gain_ref, row_ref,
    act_ref, slope_ref, dt_ref, cum_ref, sig_ref, bst_ref, leave_ref, tot_ref, bg_ref, bo_ref,
    slab, tok, halo, xhat, xt, wc, wide, p, smalls, b0, b1, b2, b3, ext, state, weighted, lsem, hsend, hrecv, ssend, srecv,
    *sems,
):
    i = pl.program_id(0)
    steps = pl.num_programs(0)
    at = place()
    seq, n = lax.axis_index("seq"), lax.axis_size("seq")
    L = tok.shape[0]
    bufs = (b0, b1, b2, b3)
    nc = len(CHUNKS)
    gets = []
    for (lane, width), order, buf, k in zip(CHUNKS, ORDERS, bufs, range(nc)):
        gets.append(Gather(slab.at[:, pl.ds(lane, width)], spots(buf), order, sems[2 * k : 2 * k + 2]))
    for k in range(4):
        buf = (bg_ref, bo_ref)[k % 2]
        width = buf.shape[5] // 2
        lanes = pl.ds((k // 2) * width, width)
        q = 2 * (nc + k)
        src = win_ref if k % 2 == 0 else so_ref
        gets.append(Gather(src.at[:, lanes], spots(buf, lanes), ORDERS[k], sems[q : q + 2]))
    own = []
    for k, (src, buf) in enumerate(((win_ref.at[:, pl.ds(0, DI)], bg_ref), (so_ref, bo_ref))):
        own.append(pltpu.make_async_copy(src, buf.at[at["z"], at["x"], at["y"], at["c"]], lsem.at[k]))
    halo_copy = pltpu.make_async_remote_copy(
        src_ref=tok_any.at[pl.ds(L - 16, 16)], dst_ref=halo, send_sem=hsend, recv_sem=hrecv,
        device_id={"seq": seq + 1}, device_id_type=MESH,
    )
    outs = [pltpu.make_async_copy(xhat, xhat_any, lsem.at[3]), pltpu.make_async_copy(xt, xt_any, lsem.at[4])]
    for k, (lane, width) in enumerate(CHUNKS):
        for j, (src, dst) in enumerate(((p, p_any), (wc, wc_any))):
            lanes = pl.ds(lane, width)
            outs.append(pltpu.make_async_copy(src.at[:, lanes], dst.at[:, lanes], lsem.at[5 + 2 * k + j]))

    def advance(*what):
        for k, stage in what:
            if stage > 0:
                gets[k].wait(stage - 1)
            if stage < 4:
                gets[k].start(stage)

    def project(k):
        lane, width = CHUNKS[k]
        buf = bufs[k]
        nz, rows_k = buf.shape[0], buf.shape[4]
        for z in range(nz):
            for m in range(8):
                r = z * 8 + m
                wide[r * rows_k : (r + 1) * rows_k, :width] = buf[z, m // 4, (m // 2) % 2, m % 2].astype(F32)
        wc[:, lane : lane + width] = wide[:, :width].astype(BF16)
        for r in range(L // 512):
            rows = slice(r * 512, (r + 1) * 512)
            p[rows, lane : lane + width] = dot(xhat[rows], wc[:, lane : lane + width]).astype(BF16)
        hp_ref[:, lane : lane + width] = dot(halo[...], wc[:, lane : lane + width]).astype(BF16)
        for c in outs[2 + 2 * k : 4 + 2 * k]:
            c.start()

    @pl.when(i == 0)
    def _():
        dp = lax.axis_index("dp")
        n_dp = lax.axis_size("dp")
        total = n_dp * n
        me = dp * n + seq
        load = pltpu.make_async_copy(tok_any, tok, lsem.at[2])
        load.start()
        sem = pltpu.get_barrier_semaphore()
        k_rows = slab.shape[0]
        steps_w = win_ref[:, DI + CH :]
        slab[:, :BLOCK] = jnp.concatenate([steps_w, jnp.zeros((k_rows, BLOCK - HEADS), BF16)], axis=1)
        slab[:, BLOCK:] = win_ref[:, DI : DI + CH]

        def far(o):
            r = lax.rem(me + o, total)
            return {"dp": r // n, "seq": lax.rem(r, n)}

        for o in range(1, total):
            pl.semaphore_signal(sem, inc=1, device_id=far(o), device_id_type=MESH)
        pl.semaphore_wait(sem, total - 1)
        advance((0, 0), (1, 0))

        @pl.when(seq < n - 1)
        def _():
            halo_copy.start()

        sends = []
        for o in range(1, total):
            c = pltpu.make_async_remote_copy(
                src_ref=small.at[0], dst_ref=smalls.at[me], send_sem=ssend.at[o - 1], recv_sem=srecv.at[o - 1],
                device_id=far(o), device_id_type=MESH,
            )
            c.start()
            sends.append(c)
        for c in own:
            c.start()
        smalls[me] = small[0]
        expand_row(small[1, 2:3], row_ref)
        for (lane, width), buf in zip(CHUNKS, bufs):
            buf[at["z"], at["x"], at["y"], at["c"]] = slab[:, lane : lane + width]
        conv_ref[...] = jnp.zeros_like(conv_ref)
        state[...] = jnp.zeros_like(state)
        tot_ref[...] = jnp.zeros_like(tot_ref)
        advance((0, 1), (2, 0), (1, 1), (3, 0))
        load.wait()
        for c in sends:
            c.wait()
        taps, ks, gs = CH // total, D // total, DI // total
        for r in range(total):
            conv_ref[0:5, r * taps : (r + 1) * taps] = smalls[r, 0:5, :taps]
            gain_ref[:, r * ks : (r + 1) * ks] = jnp.broadcast_to(smalls[r, 5:6, :ks], (8, ks))
            row_ref[1:2, r * gs : (r + 1) * gs] = smalls[r, 6:7, :gs]

        def norm(r, _):
            rows = pl.ds(pl.multiple_of(r * 256, 256), 256)
            h = rms_rows(tok[rows], gain_ref[0:1])
            xhat[rows] = h
            xt[:, rows] = h.T
            return _

        lax.fori_loop(0, L // 512, norm, 0)
        advance((0, 2), (1, 2), (2, 1), (4, 0), (3, 1), (5, 0), (6, 0), (7, 0))
        lax.fori_loop(L // 512, L // 256, norm, 0)
        for c in outs[:2]:
            c.start()

        @pl.when(seq == 0)
        def _():
            halo[...] = jnp.zeros_like(halo)

        @pl.when(seq > 0)
        def _():
            halo_copy.wait_recv()

        @pl.when(seq < n - 1)
        def _():
            halo_copy.wait_send()

        halo[...] = rms_rows(halo[...], gain_ref[0:1])
        for c in own:
            c.wait()
        advance((0, 3), (1, 3), (2, 2), (3, 2), (0, 4))
        project(0)
        advance((1, 4), (4, 1), (5, 1))
        project(1)
        advance((2, 3), (3, 3), (4, 2), (5, 2), (6, 1), (7, 1), (2, 4))
        project(2)
        advance((3, 4))
        project(3)
        for c in range(CH // 128):
            ext[c, 0:8] = hp_ref[:, BLOCK + c * 128 : BLOCK + (c + 1) * 128].astype(F32)[8:16]

    def tile(r0):
        for c in range(CH // 128):
            cs = slice(c * 128, (c + 1) * 128)
            ext[c, 8 : 8 + T] = p[pl.ds(r0, T), BLOCK + c * 128 : BLOCK + (c + 1) * 128].astype(F32)
            for r in range(0, T, 64):
                total = conv_ref[4:5, cs]
                for k in range(CONV):
                    total = total + ext[c, 5 + k + r : 5 + k + r + 64] * conv_ref[k : k + 1, cs]
                sg = sigmoid(total)
                v = total * sg
                act_ref[r : r + 64, cs] = v.astype(BF16)
                slope_ref[r : r + 64, cs] = (sg + v * (1.0 - sg)).astype(BF16)
        raw = p[pl.ds(r0, T), :BLOCK].astype(F32) + small[1, 0:1]
        dt_all = jnp.maximum(raw, 0.0) + jnp.log1p(jnp.exp(-jnp.abs(raw)))
        dt_ref[...] = dt_all
        sig_ref[...] = sigmoid_exact(raw)
        tril = (iota((BLOCK, BLOCK), 0) >= iota((BLOCK, BLOCK), 1)).astype(F32)
        lo = lane_lo()
        for blk in range(T // BLOCK):
            rows = slice(blk * BLOCK, (blk + 1) * BLOCK)
            dt = dt_all[rows]
            cum = dot_exact(tril, dt * small[1, 1:2]) * LOG2E
            cum_ref[rows] = cum
            end = cum[BLOCK - 1 : BLOCK]
            tot_ref[...] += jnp.broadcast_to(end, tot_ref.shape)
            wfac = jnp.exp2(end - cum) * dt
            decay = jnp.broadcast_to(jnp.exp2(end), (8, BLOCK))
            write_t = act_ref[rows, DI : DI + NSTATE].T
            for j in range(PAIRS):
                w, _, _ = expand_pair(wfac, j, lo)
                weighted[:, pair(j)] = (act_ref[rows, pair(j)].astype(F32) * w).astype(BF16)
            for q in range(PAIRS // 2):
                cs = slice(q * 256, (q + 1) * 256)
                new = dot(write_t, weighted[:, cs])
                bst_ref[blk, :, cs] = new.astype(BF16)
                d0, _, _ = expand_pair(decay, 2 * q, lo[:8])
                d1, _, _ = expand_pair(decay, 2 * q + 1, lo[:8])
                dd = jnp.concatenate([d0, d1], axis=1)[0:1]
                state[:, cs] = state[:, cs] * dd + new

    def after(step, *what):
        @pl.when(i == step)
        def _():
            advance(*what)

    after(2, (6, 2), (7, 2))
    after(4, (4, 3), (5, 3))
    after(6, (6, 3), (7, 3))

    @pl.when(i > 1)
    def _():
        ext[:, 0:8] = ext[:, T : T + 8]

    @pl.when(i > 0)
    def _():
        tile(pl.multiple_of((i - 1) * T, T))

    @pl.when(i == steps - 1)
    def _():
        leave_ref[...] = state[...]
        advance((4, 4), (5, 4), (6, 4), (7, 4))
        for c in outs:
            c.wait()


def sigmoid_exact(v):
    return 1.0 / (1.0 + jnp.exp(-v))


def second_kernel(
    T, gate_s, ng, act_ref, dt_ref, cum_ref, bst_ref, inc_ref, tok_ref, wo_ref, row_ref, et_ref,
    mixed_ref, nout_ref, ggrad_ref, mlow_ref, dcum_ref, ent_ref, egrad_ref, rg_ref, leave_ref, back_ref, cols_ref,
    ms, growth, rlow, prod, plow, state, exg, lows,
):
    i = pl.program_id(0)

    @pl.when(i == 0)
    def _():
        state[...] = inc_ref[...]
        exg[...] = jnp.ones_like(exg)
        back_ref[...] = jnp.zeros_like(back_ref)
        cols_ref[...] = jnp.zeros_like(cols_ref)

    lo = lane_lo()
    lower = iota((BLOCK, BLOCK), 0) >= iota((BLOCK, BLOCK), 1)
    nblk = T // BLOCK
    for blk in range(nblk):
        rows = slice(blk * BLOCK, (blk + 1) * BLOCK)
        cum = cum_ref[rows]
        cum_t = cum.T
        dt = dt_ref[rows]
        write = act_ref[rows, DI : DI + NSTATE]
        read = act_ref[rows, DI + NSTATE :]
        inner = jnp.where(lower, dot_nt(read, write), 0.0)
        lows[blk] = state[...].astype(BF16)
        ent_ref[blk] = lows[blk]
        for j in range(PAIRS):
            cols, a, b = expand_pair(cum, j, lo)
            ga = jnp.exp2(jnp.minimum(a - cum_t[2 * j : 2 * j + 1], 0.0)) * inner
            gb = jnp.exp2(jnp.minimum(b - cum_t[2 * j + 1 : 2 * j + 2], 0.0)) * inner
            scores = jnp.concatenate([ga.astype(BF16), gb.astype(BF16)], axis=1)
            vals = act_ref[rows, pair(j)].astype(F32)
            dtp, _, _ = expand_pair(dt, j, lo)
            vdt = (vals * dtp).astype(BF16)
            grow = jnp.exp2(cols)
            growth[rows, pair(j)] = grow
            diag = dot(scores, block_diag(vdt))
            out = dot(read, lows[blk, :, pair(j)])
            ms[rows, pair(j)] = diag + grow * out + row_ref[0:1, pair(j)] * vals
            dec = grow[BLOCK - 1 : BLOCK]
            state[:, pair(j)] = state[:, pair(j)] * dec + bst_ref[blk, :, pair(j)].astype(F32)

    sq = jnp.zeros((T, BLOCK), F32)
    ug = jnp.zeros((T, BLOCK), F32)
    for j in range(PAIRS):
        g = gate_s[:, pair(j)].astype(F32)
        gated = ms[:, pair(j)] * (g * sigmoid(g))
        sq = sq + gated * gated
        ug = ug + gated * ng[:, pair(j)].astype(F32)
    inv = lax.rsqrt(jnp.sum(sq, axis=-1, keepdims=True) * (1.0 / DI) + EPS)
    coef = jnp.sum(ug, axis=-1, keepdims=True) * (1.0 / DI) * (inv * inv * inv)
    for j in range(PAIRS):
        g = gate_s[:, pair(j)].astype(F32)
        sg = sigmoid(g)
        silu = g * sg
        m = ms[:, pair(j)]
        gated = m * silu
        nout_ref[:, pair(j)] = (gated * inv * row_ref[1:2, pair(j)]).astype(BF16)
        dg = inv * ng[:, pair(j)].astype(F32) - gated * coef
        low = (dg * silu).astype(BF16)
        mlow_ref[:, pair(j)] = low
        ggrad_ref[:, pair(j)] = (dg * m * (sg + silu * (1.0 - sg))).astype(BF16)
        vals = act_ref[:, pair(j)].astype(F32)
        lowf = low.astype(F32)
        mv = lowf * vals
        pr = lowf * m - row_ref[0:1, pair(j)] * mv
        hi = pr.astype(BF16)
        prod[:, pair(j)] = hi
        plow[:, pair(j)] = (pr - hi.astype(F32)).astype(BF16)
        rlow[:, pair(j)] = (lowf * growth[:, pair(j)]).astype(BF16)
        cols_ref[:, pair(j)] += jnp.sum(mv.reshape(T // 8, 8, BLOCK), axis=0)
    dcum_ref[...] = dot(prod[...], et_ref[...]) + dot(plow[...], et_ref[...])
    mixed_ref[...] = (tok_ref[...].astype(F32) + dot(nout_ref[...], wo_ref[...])).astype(BF16)
    for blk in range(nblk):
        rows = slice(blk * BLOCK, (blk + 1) * BLOCK)
        read_t = act_ref[rows, DI + NSTATE :].T
        for q in range(PAIRS // 2):
            cs = slice(q * 256, (q + 1) * 256)
            eg = dot(read_t, rlow[rows, cs])
            egrad_ref[blk, :, cs] = eg.astype(BF16)
            back_ref[:, cs] += eg * exg[0:1, cs]
        exg[...] = exg[...] * growth[blk * BLOCK + BLOCK - 1 : blk * BLOCK + BLOCK, :]
        rg_ref[rows] = dot_nt(rlow[rows, :], lows[blk])

    @pl.when(i == pl.num_programs(0) - 1)
    def _():
        leave_ref[...] = state[...].astype(BF16)


def third_kernel(
    T, act_ref, convin_ref, slope_ref, dt_ref, cum_ref, sig_ref, dcum_ref, mlow_ref, ent_ref, leave_ref,
    egrad_ref, rg_ref, inc_ref, row_ref, conv_ref, head_ref, et_ref, go_ref, gg_ref,
    pg_ref, cgrad_ref, hgrad_ref, tail_ref, so_ref, sg_ref,
    glast, xlast, gafter, hsend, hrecv, carry, dact, vprod, prod, plow, weighted, lows, dec, nxt, gext, *scratch,
):
    i = pl.program_id(0)
    steps = pl.num_programs(0)
    sca = Scatter(go_ref, "yx", scratch[2 : 2 + NSC], *scratch[:2])
    scb = Scatter(gg_ref, "xy", scratch[4 + NSC :], *scratch[2 + NSC : 4 + NSC])
    seq, nseq = lax.axis_index("seq"), lax.axis_size("seq")
    after = pltpu.make_async_remote_copy(
        src_ref=gext.at[:, pl.ds(0, 8)], dst_ref=gafter, send_sem=hsend, recv_sem=hrecv, device_id={"seq": seq - 1},
        device_id_type=MESH,
    )

    @pl.when(i == 0)
    def _():
        greet(place(), "zxyc", 1)
        sca.start(0)
        scb.start(0)

    for stage, when in enumerate((1, 3, 5)):
        @pl.when(i == when)
        def _():
            sca.finish(stage)
            sca.start(stage + 1)
            scb.finish(stage)
            scb.start(stage + 1)


    @pl.when(i == 0)
    def _():
        carry[...] = inc_ref[...]
        nxt[...] = leave_ref[...]
        cgrad_ref[...] = jnp.zeros_like(cgrad_ref)
        hgrad_ref[...] = jnp.zeros_like(hgrad_ref)

    lo = lane_lo()
    upper = iota((BLOCK, BLOCK), 0) <= iota((BLOCK, BLOCK), 1)
    triu = upper.astype(F32)
    last = iota((BLOCK, BLOCK), 0) == BLOCK - 1
    for blk in reversed(range(T // BLOCK)):
        rows = slice(blk * BLOCK, (blk + 1) * BLOCK)
        cum = cum_ref[rows]
        cum_t = cum.T
        dt = dt_ref[rows]
        end = cum[BLOCK - 1 : BLOCK]
        write = act_ref[rows, DI : DI + NSTATE]
        read = act_ref[rows, DI + NSTATE :]
        inner = jnp.where(upper, dot_nt(write, read), 0.0)
        lows[...] = carry[...].astype(BF16)
        acc = jnp.zeros((BLOCK, BLOCK), F32)
        for j in range(PAIRS):
            cols, a, b = expand_pair(cum, j, lo)
            ends = jnp.where(lo[:1], end[:, 2 * j : 2 * j + 1], end[:, 2 * j + 1 : 2 * j + 2])
            wexp = jnp.exp2(ends - cols)
            da = jnp.exp2(jnp.minimum(cum_t[2 * j : 2 * j + 1] - a, 0.0))
            db = jnp.exp2(jnp.minimum(cum_t[2 * j + 1 : 2 * j + 2] - b, 0.0))
            scores = jnp.concatenate([(da * inner).astype(BF16), (db * inner).astype(BF16)], axis=1)
            m = mlow_ref[rows, pair(j)]
            diag = block_diag(m)
            z = dot(scores, diag)
            vals = act_ref[rows, pair(j)].astype(F32)
            dtp, _, _ = expand_pair(dt, j, lo)
            vdt = vals * dtp
            vdtb = vdt.astype(BF16)
            wtb = (vdt * wexp).astype(BF16)
            g = dot_nt(vdtb, diag)
            acc = acc + g[:, :BLOCK] * da + g[:, BLOCK:] * db
            wg = dot(write, lows[:, pair(j)])
            pr = vdtb.astype(F32) * z + wtb.astype(F32) * wg
            z = z + wg * wexp
            dact[rows, pair(j)] = row_ref[0:1, pair(j)] * m.astype(F32) + dtp * z
            vprod[:, pair(j)] = (vals * z).astype(BF16)
            hi = pr.astype(BF16)
            prod[:, pair(j)] = hi
            plow[:, pair(j)] = (pr - hi.astype(F32)).astype(BF16)
            weighted[:, pair(j)] = wtb
            dec[0:1, pair(j)] = jnp.exp2(cols[BLOCK - 1 : BLOCK])
        low = jnp.where(upper, acc, 0.0).astype(BF16)
        dact[rows, DI : DI + NSTATE] = dot_nt(weighted[...], lows[...]) + dot(low, read)
        dact[rows, DI + NSTATE :] = rg_ref[rows] + dot(low.T, write)
        c = dot(vprod[...], et_ref[...])
        used = dot(prod[...], et_ref[...]) + dot(plow[...], et_ref[...])
        ends = jnp.sum((lows[...].astype(F32) * nxt[...].astype(F32)).reshape(16, 8, DI), axis=0)
        ends_hi = ends.astype(BF16)
        ends_lo = (ends - ends_hi.astype(F32)).astype(BF16)
        de = jnp.sum(dot(ends_hi, et_ref[...]) + dot(ends_lo, et_ref[...]), axis=0, keepdims=True)
        dc = dcum_ref[rows] - used + jnp.where(last, de, 0.0)
        da_log = dot_exact(triu, dc)
        draw = (c + da_log * head_ref[1, 1:2]) * sig_ref[rows]
        pg_ref[rows, :BLOCK] = draw.astype(BF16)
        hgrad_ref[0:8] += jnp.sum(draw.reshape(16, 8, BLOCK), axis=0)
        hgrad_ref[8:16] += jnp.sum((da_log * dt).reshape(16, 8, BLOCK), axis=0) * head_ref[1, 1:2]
        nxt[...] = ent_ref[blk]
        for q in range(PAIRS // 2):
            cs = slice(q * 256, (q + 1) * 256)
            carry[:, cs] = carry[:, cs] * dec[0:1, cs] + egrad_ref[blk, :, cs].astype(F32)

    for c in range(CH // 128):
        cs = slice(c * 128, (c + 1) * 128)
        ps = slice(BLOCK + c * 128, BLOCK + (c + 1) * 128)

        @pl.when(i == 0)
        def _():
            gext[c, T : T + 8] = jnp.zeros((8, 128), F32)
            xlast[:, cs] = convin_ref[T - 16 :, ps].astype(F32)

        @pl.when(i > 0)
        def _():
            gext[c, T : T + 8] = gext[c, 0:8]

        for r in range(0, T, 64):
            gext[c, r : r + 64] = dact[r : r + 64, cs] * slope_ref[r : r + 64, cs].astype(F32)
        sums = [jnp.zeros((8, 128), F32)] * 5
        for r in range(0, T, 64):
            x = convin_ref[r : r + 64, ps].astype(F32)
            g = gext[c, r : r + 64]
            back = g * conv_ref[3:4, cs]
            sums[4] = sums[4] + jnp.sum(g.reshape(8, 8, 128), axis=0)
            sums[3] = sums[3] + jnp.sum((g * x).reshape(8, 8, 128), axis=0)
            for k in range(CONV - 1):
                gk = gext[c, 3 - k + r : 3 - k + r + 64]
                back = back + gk * conv_ref[k : k + 1, cs]
                sums[k] = sums[k] + jnp.sum((gk * x).reshape(8, 8, 128), axis=0)
            pg_ref[r : r + 64, ps] = back.astype(BF16)
            if r + 64 == T:
                @pl.when(i == 0)
                def _():
                    glast[:, cs] = back[48:]
        for k in range(5):
            cgrad_ref[8 * k : 8 * k + 8, cs] += sums[k]

    @pl.when(i == steps - 1)
    def _():
        @pl.when(seq > 0)
        def _():
            after.start()

        so_ref[...] = sca.result()
        sg_ref[...] = scb.result()

        @pl.when(seq == nseq - 1)
        def _():
            gafter[...] = jnp.zeros_like(gafter)

        @pl.when(seq < nseq - 1)
        def _():
            after.wait_recv()

        row16, row8 = iota((16, 128), 0), iota((8, 128), 0)
        for c in range(CH // 128):
            cs = slice(c * 128, (c + 1) * 128)
            ps = slice(BLOCK + c * 128, BLOCK + (c + 1) * 128)
            tail = glast[:, cs]
            for j in range(CONV - 1):
                for k in range(j + 1):
                    g = gafter[c, j - k : j - k + 1]
                    tail = tail + jnp.where(row16 == 13 + j, g * conv_ref[k : k + 1, cs], 0.0)
                    cgrad_ref[8 * k : 8 * k + 8, cs] += jnp.where(row8 == 0, g * xlast[13 + j : 14 + j, cs], 0.0)
            tail_ref[:, ps] = tail.astype(BF16)
        tail_ref[:, :BLOCK] = jnp.zeros((16, BLOCK), BF16)

        @pl.when(seq > 0)
        def _():
            after.wait_send()


def once(shape):
    return pl.BlockSpec(shape, lambda i: (0,) * len(shape), pipeline_mode=pl.Buffered(1))


def full(shape):
    return pl.BlockSpec(shape, lambda i: (0,) * len(shape))


def params(collective_id=None):
    return pltpu.CompilerParams(
        dimension_semantics=("arbitrary",), vmem_limit_bytes=VMEM_LIMIT, collective_id=collective_id,
        has_side_effects=collective_id is not None,
    )


def head_columns():
    et = np.zeros((DI, BLOCK), np.float32)
    et[np.arange(DI), np.arange(DI) // HEADDIM] = 1.0
    return et


def sds(shape, dtype):
    return jax.ShapeDtypeStruct(shape, dtype)


def first_pass(w_in, small, tok, slab_o, T=256):
    L = tok.shape[0]
    nb, per = L // BLOCK, T // BLOCK
    n = sizes()
    k_rows = w_in.shape[0]
    total = lax.axis_size("dp") * lax.axis_size("seq")
    row = lambda w: pl.BlockSpec((T, w), lambda i: (jnp.maximum(i - 1, 0), 0))
    dims = (n["z"], n["x"], n["y"], n["c"])
    sems = []
    for _ in range(len(CHUNKS) + 4):
        sems += gather_sems()
    return pl.pallas_call(
        functools.partial(first_kernel, T),
        grid=(1 + L // T,),
        in_specs=[once(w_in.shape), once((2, 8, BLOCK)), ANY, ANY],
        out_specs=[
            ANY, ANY, ANY, ANY, full((16, WC)), full((8, CH)), full((8, D)), full((8, DI)),
            row(CH), row(CH), row(BLOCK), row(BLOCK), row(BLOCK),
            pl.BlockSpec((per, NSTATE, DI), lambda i: (jnp.maximum(i - 1, 0), 0, 0)), full((NSTATE, DI)),
            full((8, BLOCK)), ANY, ANY,
        ],
        out_shape=[
            sds((L, D), BF16), sds((D, L), BF16), sds((D, WC), BF16), sds((L, WC), BF16), sds((16, WC), BF16),
            sds((8, CH), F32), sds((8, D), F32), sds((8, DI), F32),
            sds((L, CH), BF16), sds((L, CH), BF16), sds((L, BLOCK), F32), sds((L, BLOCK), F32), sds((L, BLOCK), F32),
            sds((nb, NSTATE, DI), BF16), sds((NSTATE, DI), F32), sds((8, BLOCK), F32),
            sds(dims + (k_rows, DI), BF16), sds(dims + slab_o.shape, BF16),
        ],
        scratch_shapes=[
            pltpu.VMEM((k_rows, WC), BF16), pltpu.VMEM((L, D), BF16), pltpu.VMEM((16, D), BF16), pltpu.VMEM((L, D), BF16), pltpu.VMEM((D, L), BF16),
            pltpu.VMEM((D, WC), BF16), pltpu.VMEM((D, 512), F32), pltpu.VMEM((L, WC), BF16),
            pltpu.VMEM((total, 8, BLOCK), F32),
        ] + [pltpu.VMEM(dims + (k_rows, w), BF16) for _, w in CHUNKS] + [
            pltpu.VMEM((CH // 128, T + 8, 128), F32), pltpu.VMEM((NSTATE, DI), F32), pltpu.VMEM((BLOCK, DI), BF16),
            pltpu.SemaphoreType.DMA((5 + 2 * len(CHUNKS),)), pltpu.SemaphoreType.DMA(()), pltpu.SemaphoreType.DMA(()),
            pltpu.SemaphoreType.DMA((total - 1,)), pltpu.SemaphoreType.DMA((total - 1,)),
        ] + sems,
        compiler_params=params(collective_id=1),
        name="first_pass",
    )(w_in, small, tok, slab_o)


def second_pass(gate, ng, act, dt, cum, bst, inc, tok, wo, rows, et, T=256):
    L = tok.shape[0]
    nb, per = L // BLOCK, T // BLOCK
    row = lambda w: pl.BlockSpec((T, w), lambda i: (i, 0))
    blk = pl.BlockSpec((per, NSTATE, DI), lambda i: (i, 0, 0))
    return pl.pallas_call(
        functools.partial(second_kernel, T),
        grid=(L // T,),
        in_specs=[
            row(DI), row(DI), row(CH), row(BLOCK), row(BLOCK), blk, full((NSTATE, DI)), row(D), full((DI, D)), full((8, DI)), full((DI, BLOCK)),
        ],
        out_specs=[
            row(D), row(DI), row(DI), row(DI), row(BLOCK), blk, blk, row(BLOCK), full((NSTATE, DI)),
            full((NSTATE, DI)), full((8, DI)),
        ],
        out_shape=[
            sds((L, D), BF16), sds((L, DI), BF16), sds((L, DI), BF16), sds((L, DI), BF16), sds((L, BLOCK), F32),
            sds((nb, NSTATE, DI), BF16), sds((nb, NSTATE, DI), BF16), sds((L, BLOCK), F32), sds((NSTATE, DI), BF16),
            sds((NSTATE, DI), F32), sds((8, DI), F32),
        ],
        scratch_shapes=[
            pltpu.VMEM((T, DI), F32), pltpu.VMEM((T, DI), F32),
            pltpu.VMEM((T, DI), BF16), pltpu.VMEM((T, DI), BF16), pltpu.VMEM((T, DI), BF16), pltpu.VMEM((NSTATE, DI), F32),
            pltpu.VMEM((8, DI), F32), pltpu.VMEM((per, NSTATE, DI), BF16),
        ],
        compiler_params=params(),
        name="second_pass",
    )(gate, ng, act, dt, cum, bst, inc, tok, wo, rows, et)


def third_pass(
    act, convin, slope, dt, cum, sig, dcum, mlow, ent, leave, egrad, rg, inc, rows, conv, head, et, go, gg, T=256
):
    L = act.shape[0]
    m = sizes()
    dims = (m["z"], m["x"], m["y"], m["c"])
    total = m["z"] * m["y"] * 4
    ro, rg_rows = DI // total, D // total
    go = go.reshape(dims + (ro, D))
    gg = gg.reshape(dims + (rg_rows, DI))
    n, per = L // T, T // BLOCK
    row = lambda w: pl.BlockSpec((T, w), lambda i: (n - 1 - i, 0))
    blk = pl.BlockSpec((per, NSTATE, DI), lambda i: (n - 1 - i, 0, 0))
    return pl.pallas_call(
        functools.partial(third_kernel, T),
        grid=(n,),
        in_specs=[
            row(CH), row(WC), row(CH), row(BLOCK), row(BLOCK), row(BLOCK), row(BLOCK), row(DI), blk,
            full((NSTATE, DI)), blk, row(BLOCK), full((NSTATE, DI)), full((8, DI)), full((8, CH)), full((2, 8, BLOCK)),
            full((DI, BLOCK)), ANY, ANY,
        ],
        out_specs=[
            row(WC), full((40, CH)), full((16, BLOCK)), full((16, WC)), full((ro, D)), full((rg_rows, DI)),
        ],
        out_shape=[
            sds((L, WC), BF16), sds((40, CH), F32), sds((16, BLOCK), F32), sds((16, WC), BF16), sds((ro, D), F32),
            sds((rg_rows, DI), F32),
        ],
        scratch_shapes=[
            pltpu.VMEM((16, CH), F32), pltpu.VMEM((16, CH), F32), pltpu.VMEM((CH // 128, 8, 128), F32),
            pltpu.SemaphoreType.DMA(()), pltpu.SemaphoreType.DMA(()),
            pltpu.VMEM((NSTATE, DI), F32), pltpu.VMEM((T, CH), F32), pltpu.VMEM((BLOCK, DI), BF16), pltpu.VMEM((BLOCK, DI), BF16), pltpu.VMEM((BLOCK, DI), BF16),
            pltpu.VMEM((BLOCK, DI), BF16), pltpu.VMEM((NSTATE, DI), BF16), pltpu.VMEM((8, DI), F32),
            pltpu.VMEM((NSTATE, DI), BF16), pltpu.VMEM((CH // 128, T + 8, 128), F32),
        ] + own_scratch(ro, D) + scatter_scratch(ro, D) + own_scratch(rg_rows, DI) + scatter_scratch(rg_rows, DI),
        compiler_params=params(collective_id=4),
        name="third_pass",
    )(act, convin, slope, dt, cum, sig, dcum, mlow, ent, leave, egrad, rg, inc, rows, conv, head, et, go, gg)


def on_device(
    tokens, cotangent, norm_gain, in_weight, conv_weight, conv_bias, step_bias, decay_log, skip_gain, gate_gain,
    out_weight,
):
    tok, cot = tokens[0], cotangent[0]
    L = tok.shape[0]
    k_rows, c_rows = in_weight.shape[0], conv_weight.shape[0]
    total = D // k_rows
    lanes = lambda x: jnp.pad(x, ((0, 0),) * (x.ndim - 1) + ((0, BLOCK - x.shape[-1]),))

    def put(x, row):
        x = x.astype(F32)
        return jnp.pad(x, ((row, 16 - row - x.shape[0]), (0, BLOCK - x.shape[1])))

    own = put(conv_weight.T, 0) + put(conv_bias[None], 4) + put(norm_gain[None], 5) + put(gate_gain[None], 6)
    own = own + put(step_bias[None], 8) + put(-jnp.exp(decay_log)[None], 9) + put(skip_gain[None], 10)
    own = own.reshape(2, 8, BLOCK)
    et = jnp.asarray(head_columns(), BF16)

    (xhat, xt, wc, p, hp, conv, gain, rows, act, slope, dt, cum, sig, bst, leave, tot, buf_g, buf_o) = first_pass(
        in_weight, own, tok, out_weight
    )
    wg, wo = buf_g.reshape(D, DI), buf_o.reshape(DI, D)
    gate, ng, inc = gate_pass(xhat, wg, cot, wo, rows, leave, tot)
    mixed, nout, ggrad, mlow, dcum, ent, egrad, rg, leave2, back, cols = second_pass(
        gate, ng, act, dt, cum, bst, inc, tok, wo, rows, et
    )
    g_out, g_gate, later = grads_pass(nout, cot, xt, ggrad, back, tot)
    pg, cgrad, hgrad, tail, out_raw, gate_cols = third_pass(
        act, p, slope, dt, cum, sig, dcum, mlow, ent, leave2, egrad, rg, later, rows, conv, own, et, g_out, g_gate
    )
    cg = cgrad.reshape(5, 8, CH).sum(axis=1)
    hg = hgrad.reshape(2, 8, BLOCK).sum(axis=1)[:, :HEADS]
    sums = jnp.concatenate([hg[0], hg[1], cols.reshape(8, HEADS, HEADDIM).sum(axis=(0, 2))])
    small = jnp.concatenate(
        [
            lanes(jnp.swapaxes(cg.reshape(5, total, c_rows), 0, 1)), jnp.zeros((total, 2, BLOCK), F32),
            jnp.broadcast_to(lanes(sums[None, None]), (total, 1, BLOCK)),
        ],
        axis=1,
    )
    tgrad, conv_cols, sums = last_pass(xt, pg, tail, ggrad, tok, cot, wg, wc, gain, small)
    in_grad, ngain_grad, ggain_grad, taps, bias, step, decay, skip, out_grad, tgrad = finish_pass(
        gate_cols, conv_cols, out_raw, sums, in_weight, out_weight, norm_gain.astype(F32), gate_gain.astype(F32), tgrad,
        c_rows,
    )
    return (
        mixed[None], tgrad[None], ngain_grad, in_grad, taps, bias, step, decay, skip, ggain_grad, out_grad,
    )


def solution(mesh):
    both = ("dp", "seq")
    vec, mat, tok, rep = P(both), P(both, None), P("dp", "seq", None), P()
    return jax.shard_map(
        on_device,
        mesh=mesh,
        in_specs=(tok, tok, vec, mat, mat, vec, rep, rep, rep, vec, mat),
        out_specs=(tok, tok, vec, mat, mat, vec, rep, rep, rep, vec, mat),
        check_vma=False,
    )
```

```python
import functools

import jax
import jax.numpy as jnp
import numpy as np
from jax import lax
from jax.experimental import pallas as pl
from jax.experimental.pallas import tpu as pltpu
from jax.sharding import PartitionSpec as P

D = 768
HEADS = 24
HEADDIM = 64
NSTATE = 128
CONV = 4
BLOCK = 128
DI = 1536
CH = 1792
PAIRS = HEADS // 2
EPS = 1e-05
LOG2E = 1.4426950408889634
F32 = jnp.float32
BF16 = jnp.bfloat16
NT = (((1,), (1,)), ((), ()))
VMEM_LIMIT = 60 * 1024 * 1024


def dot(a, b):
    return jnp.dot(a, b, preferred_element_type=F32)


def dot_nt(a, b):
    return lax.dot_general(a, b, NT, preferred_element_type=F32)


def dot_exact(a, b):
    return jnp.dot(a, b, preferred_element_type=F32, precision=lax.Precision.HIGHEST)


def sigmoid(v):
    return 0.5 * jnp.tanh(0.5 * v) + 0.5


def iota(shape, dim):
    return lax.broadcasted_iota(jnp.int32, shape, dim)


def lane_lo():
    return iota((BLOCK, BLOCK), 1) < HEADDIM


def expand_pair(x, j, lo):
    rows = x.shape[0]
    a = jnp.broadcast_to(x[:, 2 * j : 2 * j + 1], (rows, BLOCK))
    b = jnp.broadcast_to(x[:, 2 * j + 1 : 2 * j + 2], (rows, BLOCK))
    return jnp.where(lo, a, b), a, b


def block_diag(v):
    lo = iota(v.shape, 1) < HEADDIM
    zero = jnp.zeros_like(v)
    return jnp.concatenate([jnp.where(lo, v, zero), jnp.where(lo, zero, v)], axis=0)


def pair(j):
    return slice(j * BLOCK, (j + 1) * BLOCK)


MESH = pl.DeviceIdType.MESH
ANY = pl.BlockSpec(memory_space=pl.ANY)
WC = CH + BLOCK
TN = (((0,), (0,)), ((), ()))


def dot_tn(a, b):
    return lax.dot_general(a, b, TN, preferred_element_type=F32)


def sizes():
    return {"z": lax.axis_size("dp") // 2, "x": 2, "y": lax.axis_size("seq") // 2, "c": 2}


def place():
    dp, seq = lax.axis_index("dp"), lax.axis_index("seq")
    return {"z": dp // 2, "x": lax.rem(dp, 2), "y": seq // 2, "c": lax.rem(seq, 2)}


def device(at):
    return {"dp": at["z"] * 2 + at["x"], "seq": at["y"] * 2 + at["c"]}


def peers(at, axis):
    n = sizes()[axis]
    return [dict(at, **{axis: lax.rem(at[axis] + o, n)}) for o in range(1, n)]


def greet(at, axes, by=0):
    sem = pltpu.get_barrier_semaphore()
    count = 0
    for axis in axes:
        for peer in peers(at, axis):
            pl.semaphore_signal(sem, inc=1, device_id=device(peer), device_id_type=MESH)
            count += 1
    if not by:
        pl.semaphore_wait(sem, count)
        return
    seq, n = lax.axis_index("seq"), lax.axis_size("seq")

    @pl.when((seq + by >= 0) & (seq + by < n))
    def _():
        pl.semaphore_signal(sem, inc=1, device_id={"seq": seq + by}, device_id_type=MESH)

    heard = (seq - by >= 0) & (seq - by < n)

    @pl.when(heard)
    def _():
        pl.semaphore_wait(sem, count + 1)

    @pl.when(jnp.logical_not(heard))
    def _():
        pl.semaphore_wait(sem, count)


def greet_neighbours():
    seq, n = lax.axis_index("seq"), lax.axis_size("seq")
    sem = pltpu.get_barrier_semaphore()

    @pl.when(seq > 0)
    def _():
        pl.semaphore_signal(sem, inc=1, device_id={"seq": seq - 1}, device_id_type=MESH)

    @pl.when(seq < n - 1)
    def _():
        pl.semaphore_signal(sem, inc=1, device_id={"seq": seq + 1}, device_id_type=MESH)

    @pl.when((seq > 0) & (seq < n - 1))
    def _():
        pl.semaphore_wait(sem, 2)

    @pl.when((seq == 0) | (seq == n - 1))
    def _():
        pl.semaphore_wait(sem, 1)


def remote(src, dst, send, recv, peer):
    return pltpu.make_async_remote_copy(
        src_ref=src, dst_ref=dst, send_sem=send, recv_sem=recv, device_id=device(peer), device_id_type=MESH
    )


class Gather:
    def __init__(self, slab, spot, order, sems):
        self.slab, self.spot, self.order = slab, spot, order
        self.send, self.recv = sems
        self.at = place()

    def copies(self, stage):
        at, (a, b) = self.at, self.order
        n = sizes()
        out = []
        every = slice(None)
        nz = n["z"] - 1
        if stage == 0:
            for o, peer in enumerate(peers(at, "z")):
                out.append((self.slab, self.spot(at), o, peer))
        elif stage == 1:
            index = dict(at, z=every)
            out.append((self.spot(index), self.spot(index), nz, peers(at, a)[0]))
        elif stage == 2:
            index = dict(at, z=every)
            index[a] = every
            for o, peer in enumerate(peers(at, b)):
                out.append((self.spot(index), self.spot(index), nz + 1 + o, peer))
            out.append((self.spot(index), self.spot(index), nz + 1 + n[b] - 1, peers(at, "c")[0]))
        else:
            for o in range(1, n[b]):
                index = dict(at, z=every)
                index[a] = every
                index[b] = lax.rem(at[b] + o, n[b])
                out.append((self.spot(index), self.spot(index), nz + 1 + n[b] + o - 1, peers(at, "c")[0]))
        return [remote(s, d, self.send.at[k], self.recv.at[k], p) for s, d, k, p in out]

    def start(self, stage):
        for c in self.copies(stage):
            c.start()

    def wait(self, stage):
        for c in self.copies(stage):
            c.wait()


def spots(buf, lanes=slice(None)):
    return lambda index: buf.at[index["z"], index["x"], index["y"], index["c"], :, lanes]


def gather_sems():
    count = sizes()["z"] + 2 * sizes()["y"] + 4
    return [pltpu.SemaphoreType.DMA((count,)), pltpu.SemaphoreType.DMA((count,))]


class Scatter:
    def __init__(self, grads, order, scratch, own=None, local=None):
        self.grads, self.order, self.own_ref, self.local = grads, order, own, local
        self.rc, self.r1, self.r2, self.rz, self.send, self.recv = scratch
        self.at = place()
        self.own = self

    def spot(self, z, x, y):
        if self.own_ref is not None:
            return self.own_ref.at[z, x, y]
        return self.grads.at[z, x, y, self.at["c"]]

    def add(self, z, x, y, got):
        mine = self.spot(z, x, y)
        mine[...] = (mine[...].astype(F32) + got.astype(F32)).astype(BF16)

    def copies(self, stage):
        at, (a, b) = self.at, self.order
        every = slice(None)
        out = []

        def spot(index):
            return self.spot(index["z"], index["x"], index["y"])

        if stage == 0:
            out.append((self.grads.at[:, :, :, 1 - at["c"]], self.rc, 0, peers(at, "c")[0]))
        elif stage == 1:
            index = {"z": every, "x": every, "y": every}
            index[a] = 1 - at[a]
            out.append((spot(index), self.r1, 1, peers(at, a)[0]))
        elif stage == 2:
            index = {"z": every, a: at[a], b: 1 - at[b]}
            out.append((spot(index), self.r2, 2, peers(at, b)[0]))
        else:
            for o, peer in enumerate(peers(at, "z")):
                out.append((self.spot(peer["z"], at["x"], at["y"]), self.rz.at[o], 3 + o, peer))
        return [remote(s, d, self.send.at[k], self.recv.at[k], p) for s, d, k, p in out]

    def mine(self):
        return pltpu.make_async_copy(self.grads.at[:, :, :, self.at["c"]], self.own_ref, self.local)

    def start(self, stage):
        if stage == 0 and self.own_ref is not None:
            self.mine().start()
        for c in self.copies(stage):
            c.start()

    def finish(self, stage):
        at, (a, b) = self.at, self.order
        for c in self.copies(stage):
            c.wait()
        nz = sizes()["z"]
        if stage == 0:
            if self.own_ref is not None:
                self.mine().wait()

            def body(z, _):
                for x in range(2):
                    for y in range(2):
                        self.add(z, x, y, self.rc[z, x, y])
                return _

        elif stage == 1:

            def body(z, _):
                for k in range(2):
                    index = {a: at[a], b: k}
                    self.add(z, index["x"], index["y"], self.r1[z, k])
                return _

        else:

            def body(z, _):
                self.add(z, at["x"], at["y"], self.r2[z])
                return _

        lax.fori_loop(0, nz, body, 0)

    def result(self):
        for c in self.copies(3):
            c.wait()
        total = self.spot(self.at["z"], self.at["x"], self.at["y"])[...].astype(F32)
        for o in range(sizes()["z"] - 1):
            total = total + self.rz[o].astype(F32)
        return total


def scatter_scratch(rows, width):
    nz = sizes()["z"]
    return [
        pltpu.VMEM((nz, 2, 2, rows, width), BF16), pltpu.VMEM((nz, 2, rows, width), BF16),
        pltpu.VMEM((nz, rows, width), BF16), pltpu.VMEM((nz - 1, rows, width), BF16),
        pltpu.SemaphoreType.DMA((nz + 2,)), pltpu.SemaphoreType.DMA((nz + 2,)),
    ]


NSC = 6


def own_scratch(rows, width):
    return [pltpu.VMEM((sizes()["z"], 2, 2, rows, width), BF16), pltpu.SemaphoreType.DMA(())]


class Chain:
    def __init__(self, leave, inc, decay, bufs, reverse):
        self.leave, self.inc, self.decay, self.reverse = leave, inc, decay, reverse
        self.got, self.put, self.send, self.recv = bufs
        self.n = lax.axis_size("seq")
        seq = lax.axis_index("seq")
        self.rank = self.n - 1 - seq if reverse else seq
        self.to = seq - 1 if reverse else seq + 1

    def copy(self):
        return pltpu.make_async_remote_copy(
            src_ref=self.put, dst_ref=self.got, send_sem=self.send, recv_sem=self.recv,
            device_id={"seq": self.to}, device_id_type=MESH,
        )

    def step(self, k):
        @pl.when(self.rank == k)
        def _():
            if k == 0:
                self.inc[...] = jnp.zeros_like(self.inc)
                self.put[...] = self.leave[...].astype(BF16)
            else:
                self.copy().wait_recv()
                got = self.got[...].astype(F32)
                self.inc[...] = got
                if k < self.n - 1:
                    self.put[...] = (got * self.decay[0:1] + self.leave[...]).astype(BF16)
            if k < self.n - 1:
                self.copy().start()

    def done(self):
        @pl.when(self.rank < self.n - 1)
        def _():
            self.copy().wait_send()


def chain_scratch():
    return [
        pltpu.VMEM((NSTATE, DI), BF16), pltpu.VMEM((NSTATE, DI), BF16), pltpu.SemaphoreType.DMA(()),
        pltpu.SemaphoreType.DMA(()),
    ]


def expand_row(row, dst):
    lo = iota((8, BLOCK), 1) < HEADDIM
    wide = jnp.broadcast_to(row, (8, BLOCK))
    for j in range(PAIRS):
        dst[:, pair(j)] = expand_pair(wide, j, lo)[0]


CHUNKS = ((0, 512), (512, 512), (1024, 512), (1536, 384))
ORDERS = ("xy", "yx", "xy", "yx")


def gate_kernel(normed_ref, wg_ref, cot_ref, wo_ref, gain_ref, leave_ref, tot_ref, gate_ref, ng_ref, inc_ref, decay, *bufs):
    i = pl.program_id(0)
    chain = Chain(leave_ref, inc_ref, decay, bufs, False)
    last = pl.num_programs(0) - 1

    @pl.when(i == 0)
    def _():
        expand_row(jnp.exp2(tot_ref[0:1]), decay)
        greet_neighbours()
        chain.step(0)

    for c in range(DI // 256):
        cs = slice(c * 256, (c + 1) * 256)
        gate_ref[:, cs] = dot(normed_ref[...], wg_ref[:, cs]).astype(BF16)
        ng_ref[:, cs] = (dot_nt(cot_ref[...], wo_ref[cs, :]) * gain_ref[1:2, cs]).astype(BF16)
    for k in range(1, chain.n):
        @pl.when(i == (0, 2, 3)[min(k, 3) - 1])
        def _():
            chain.step(k)

    @pl.when(i == last)
    def _():
        chain.done()


def gate_pass(normed, wg, cot, wo, gain, leave, tot, T=512):
    L = normed.shape[0]
    row = lambda w: pl.BlockSpec((T, w), lambda i: (i, 0))
    return pl.pallas_call(
        gate_kernel,
        grid=(L // T,),
        in_specs=[
            row(D), full((D, DI)), row(D), full((DI, D)), full((8, DI)), full((NSTATE, DI)), full((8, BLOCK)),
        ],
        out_specs=[row(DI), row(DI), full((NSTATE, DI))],
        out_shape=[sds((L, DI), BF16), sds((L, DI), BF16), sds((NSTATE, DI), F32)],
        scratch_shapes=[pltpu.VMEM((8, DI), F32)] + chain_scratch(),
        compiler_params=params(collective_id=2),
        name="gate_pass",
    )(normed, wg, cot, wo, gain, leave, tot)


def grads_kernel(nout_ref, cot_ref, xt_ref, ggrad_ref, back_ref, tot_ref, gout_ref, ggate_ref, inc_ref, decay, *bufs):
    i = pl.program_id(0)
    chain = Chain(back_ref, inc_ref, decay, bufs, True)
    last = pl.num_programs(0) - 1

    @pl.when(i == 0)
    def _():
        expand_row(jnp.exp2(tot_ref[0:1]), decay)
        greet_neighbours()
        chain.step(0)

    gout_ref[...] = dot_tn(nout_ref[...], cot_ref[...]).astype(BF16)
    ggate_ref[...] = dot(xt_ref[...], ggrad_ref[...]).astype(BF16)
    for k in range(1, chain.n):
        @pl.when(i == (0, 3, 5)[min(k, 3) - 1])
        def _():
            chain.step(k)

    @pl.when(i == last)
    def _():
        chain.done()


def grads_pass(nout, cot, xt, ggrad, back, tot):
    L = nout.shape[0]
    col = lambda w: pl.BlockSpec((L, w), lambda i: (0, i))
    return pl.pallas_call(
        grads_kernel,
        grid=(6,),
        in_specs=[
            col(256), full((L, D)), pl.BlockSpec((128, L), lambda i: (i, 0)), full((L, DI)), full((NSTATE, DI)),
            full((8, BLOCK)),
        ],
        out_specs=[
            pl.BlockSpec((256, D), lambda i: (i, 0)), pl.BlockSpec((128, DI), lambda i: (i, 0)), full((NSTATE, DI)),
        ],
        out_shape=[sds((DI, D), BF16), sds((D, DI), BF16), sds((NSTATE, DI), F32)],
        scratch_shapes=[pltpu.VMEM((8, DI), F32)] + chain_scratch(),
        compiler_params=params(collective_id=3),
        name="grads_pass",
    )(nout, cot, xt, ggrad, back, tot)


def last_kernel(
    T, xt_any, pg_any, wg_any, wc_any, tail_ref, ggrad_ref, tok_ref, cot_ref, gain_ref, small_ref,
    tgrad_ref, gout_ref, sums_ref, xt, wg, wc, pg, g0, g1, g2, g3, lsem, smalls, ssend, srecv, *scratch,
):
    i = pl.program_id(0)
    nc = len(CHUNKS)
    grads = (g0, g1, g2, g3)
    sc = [Scatter(grads[k], ORDERS[k][::-1], scratch[NSC * k : NSC * k + NSC]) for k in range(nc)]
    dp, seq = lax.axis_index("dp"), lax.axis_index("seq")
    n_dp, n_seq = lax.axis_size("dp"), lax.axis_size("seq")
    total = n_dp * n_seq
    me = dp * n_seq + seq
    L = pg.shape[0]

    whole = ((xt_any, xt), (wg_any, wg), (wc_any, wc))

    def load(k):
        if k >= nc:
            return pltpu.make_async_copy(*whole[k - nc], lsem.at[k])
        lanes = pl.ds(CHUNKS[k][0], CHUNKS[k][1])
        return pltpu.make_async_copy(pg_any.at[:, lanes], pg.at[:, lanes], lsem.at[k])

    def far(o):
        r = lax.rem(me + o, total)
        return {"dp": r // n_seq, "seq": lax.rem(r, n_seq)}

    def small(o):
        r = lax.rem(me + o, total)
        return pltpu.make_async_remote_copy(
            src_ref=small_ref.at[r], dst_ref=smalls.at[o - 1], send_sem=ssend.at[o - 1], recv_sem=srecv.at[o - 1],
            device_id=far(o), device_id_type=MESH,
        )

    @pl.when(i == 0)
    def _():
        load(nc).start()
        load(0).start()
        sem = pltpu.get_barrier_semaphore()
        for o in range(1, total):
            pl.semaphore_signal(sem, inc=1, device_id=far(o), device_id_type=MESH)

    for k in range(nc):
        @pl.when(i == k)
        def _():
            lane, width = CHUNKS[k]
            if k == 0:
                load(nc).wait()
            load(k).wait()
            if k + 1 < nc:
                load(k + 1).start()
            if k >= nc - 2:
                load(nc + 1 + k - (nc - 2)).start()
            skip = BLOCK if k == 0 else 0
            pg[L - 16 :, lane + skip : lane + width] = tail_ref[:, lane + skip : lane + width]
            rows = grads[k].shape[4]
            for q in range(2):
                half = D // 2
                g = dot(xt[q * half : (q + 1) * half], pg[:, lane : lane + width])
                for r in range(half // rows):
                    s = r + q * (half // rows)
                    grads[k][s // 8, (s // 4) % 2, (s // 2) % 2, s % 2] = g[r * rows : (r + 1) * rows].astype(BF16)
            if k == 0:
                pl.semaphore_wait(pltpu.get_barrier_semaphore(), total - 1)
                sc[0].start(0)
                for o in range(1, total):
                    small(o).start()
            else:
                sc[k - 1].finish(0)
                sc[k - 1].start(1)
                sc[k].start(0)

    @pl.when(i >= nc)
    def _():
        r0 = pl.multiple_of((i - nc) * T, T)

        @pl.when(i == nc)
        def _():
            load(nc + 1).wait()
            load(nc + 2).wait()

        u = dot_nt(ggrad_ref[...], wg[...]) + dot_nt(pg[pl.ds(r0, T), :], wc[...])
        u = u * gain_ref[0:1]
        x = tok_ref[...].astype(F32)
        inv = lax.rsqrt(jnp.mean(x * x, axis=-1, keepdims=True) + EPS)
        xi = x * inv
        coef = inv * jnp.mean(u * xi, axis=-1, keepdims=True)
        tgrad_ref[...] = (cot_ref[...].astype(F32) + inv * u - xi * coef).astype(BF16)

    def after(step, what):
        @pl.when(i == step)
        def _():
            for k, stage in what:
                sc[k].finish(stage)
                sc[k].start(stage + 1)

    after(nc + 1, [(3, 0)])
    after(nc + 3, [(0, 1)])
    after(nc + 4, [(1, 1)])
    after(nc + 5, [(2, 1)])
    after(nc + 6, [(3, 1), (0, 2)])
    after(nc + 7, [(1, 2), (2, 2), (3, 2)])

    @pl.when(i == pl.num_programs(0) - 1)
    def _():
        for o in range(1, total):
            small(o).wait()
        acc = small_ref[me]
        for o in range(1, total):
            acc = acc + smalls[o - 1]
        sums_ref[...] = acc
        for k in range(nc):
            lane, width = CHUNKS[k]
            gout_ref[:, lane : lane + width] = sc[k].result()


def last_pass(xt, pg, tail, ggrad, tok, cot, wg, wc, gain, small):
    L = tok.shape[0]
    T = L // 8
    n = sizes()
    nc = len(CHUNKS)
    total = lax.axis_size("dp") * lax.axis_size("seq")
    rows = D // total
    row = lambda w: pl.BlockSpec((T, w), lambda i: (jnp.maximum(i - nc, 0), 0))
    scratch = []
    for _, w in CHUNKS:
        scratch += scatter_scratch(rows, w)
    return pl.pallas_call(
        functools.partial(last_kernel, T),
        grid=(nc + L // T,),
        in_specs=[
            ANY, ANY, ANY, ANY, once((16, WC)), row(DI), row(D), row(D), once((8, D)), once((total, 8, BLOCK)),
        ],
        out_specs=[row(D), full((rows, WC)), full((8, BLOCK))],
        out_shape=[sds((L, D), BF16), sds((rows, WC), F32), sds((8, BLOCK), F32)],
        scratch_shapes=[
            pltpu.VMEM((D, L), BF16), pltpu.VMEM((D, DI), BF16), pltpu.VMEM((D, WC), BF16), pltpu.VMEM((L, WC), BF16),
        ]
        + [pltpu.VMEM((n["z"], 2, n["y"], 2, rows, w), BF16) for _, w in CHUNKS]
        + [
            pltpu.SemaphoreType.DMA((nc + 3,)), pltpu.VMEM((total - 1, 8, BLOCK), F32),
            pltpu.SemaphoreType.DMA((total - 1,)), pltpu.SemaphoreType.DMA((total - 1,)),
        ] + scratch,
        compiler_params=params(collective_id=5),
        name="last_pass",
    )(xt, pg, wg, wc, tail, ggrad, tok, cot, gain, small)


def finish_kernel(
    gate_ref, conv_ref, out_ref, sums_ref, w_ref, wo_ref, own_ref, tgrad_ref,
    in_grad, ngain, ggain, taps, bias, step, decay, skip, out_grad, tgrad_out,
):
    tgrad_out[...] = tgrad_ref[...]

    @pl.when(pl.program_id(0) == 0)
    def _():
        finish_small(
            gate_ref, conv_ref, out_ref, sums_ref, w_ref, wo_ref, own_ref, in_grad, ngain, ggain, taps, bias,
            step, decay, skip, out_grad,
        )


def finish_small(
    gate_ref, conv_ref, out_ref, sums_ref, w_ref, wo_ref, own_ref,
    in_grad, ngain, ggain, taps, bias, step, decay, skip, out_grad,
):
    conv = conv_ref[...]
    raw = jnp.concatenate([gate_ref[...], conv[:, BLOCK:], conv[:, :HEADS]], axis=1)
    in_grad[...] = raw
    ngain[...] = jnp.sum(raw * w_ref[...].astype(F32), axis=1) / own_ref[0, 5, : ngain.shape[0]]
    o = out_ref[...]
    out_grad[...] = o
    ggain[...] = jnp.sum(o * wo_ref[...].astype(F32), axis=1) / own_ref[0, 6, : ggain.shape[0]]
    s = sums_ref[...]
    n = bias.shape[0]
    taps[...] = s[:CONV, :n]
    bias[...] = s[4, :n]
    step[...] = s[7, :HEADS]
    decay[...] = s[7, HEADS : 2 * HEADS]
    skip[...] = s[7, 2 * HEADS : 3 * HEADS]


def finish_pass(gate_cols, conv_cols, out_raw, sums, w, wo, own, tgrad, channels):
    vec = lambda n: sds((n,), F32)
    rows = pl.BlockSpec((512, D), lambda i: (i, 0))
    small = [
        sds(w.shape, F32), vec(w.shape[0]), vec(wo.shape[0]), sds((CONV, channels), F32),
        vec(channels), vec(HEADS), vec(HEADS), vec(HEADS), sds(out_raw.shape, F32),
    ]
    ins = (gate_cols, conv_cols, out_raw, sums, w, wo, own)
    return pl.pallas_call(
        finish_kernel,
        grid=(tgrad.shape[0] // 512,),
        in_specs=[once(x.shape) for x in ins] + [rows],
        out_specs=[once(x.shape) for x in small] + [rows],
        out_shape=small + [sds(tgrad.shape, BF16)],
        name="finish_pass",
    )(*ins, tgrad)


def rms_rows(tok, gain):
    x = tok.astype(F32)
    return (x * lax.rsqrt(jnp.mean(x * x, axis=-1, keepdims=True) + EPS) * gain).astype(BF16)


def first_kernel(
    T, win_ref, small, tok_any, so_ref,
    xhat_any, xt_any, wc_any, p_any, hp_ref, conv_ref, gain_ref, row_ref,
    act_ref, slope_ref, dt_ref, cum_ref, sig_ref, bst_ref, leave_ref, tot_ref, bg_ref, bo_ref,
    slab, tok, halo, xhat, xt, wc, wide, p, smalls, b0, b1, b2, b3, ext, state, weighted, lsem, hsend, hrecv, ssend, srecv,
    *sems,
):
    i = pl.program_id(0)
    steps = pl.num_programs(0)
    at = place()
    seq, n = lax.axis_index("seq"), lax.axis_size("seq")
    L = tok.shape[0]
    bufs = (b0, b1, b2, b3)
    nc = len(CHUNKS)
    gets = []
    for (lane, width), order, buf, k in zip(CHUNKS, ORDERS, bufs, range(nc)):
        gets.append(Gather(slab.at[:, pl.ds(lane, width)], spots(buf), order, sems[2 * k : 2 * k + 2]))
    for k in range(4):
        buf = (bg_ref, bo_ref)[k % 2]
        width = buf.shape[5] // 2
        lanes = pl.ds((k // 2) * width, width)
        q = 2 * (nc + k)
        src = win_ref if k % 2 == 0 else so_ref
        gets.append(Gather(src.at[:, lanes], spots(buf, lanes), ORDERS[k], sems[q : q + 2]))
    own = []
    for k, (src, buf) in enumerate(((win_ref.at[:, pl.ds(0, DI)], bg_ref), (so_ref, bo_ref))):
        own.append(pltpu.make_async_copy(src, buf.at[at["z"], at["x"], at["y"], at["c"]], lsem.at[k]))
    halo_copy = pltpu.make_async_remote_copy(
        src_ref=tok_any.at[pl.ds(L - 16, 16)], dst_ref=halo, send_sem=hsend, recv_sem=hrecv,
        device_id={"seq": seq + 1}, device_id_type=MESH,
    )
    outs = [pltpu.make_async_copy(xhat, xhat_any, lsem.at[3]), pltpu.make_async_copy(xt, xt_any, lsem.at[4])]
    for k, (lane, width) in enumerate(CHUNKS):
        for j, (src, dst) in enumerate(((p, p_any), (wc, wc_any))):
            lanes = pl.ds(lane, width)
            outs.append(pltpu.make_async_copy(src.at[:, lanes], dst.at[:, lanes], lsem.at[5 + 2 * k + j]))

    def advance(*what):
        for k, stage in what:
            if stage > 0:
                gets[k].wait(stage - 1)
            if stage < 4:
                gets[k].start(stage)

    def project(k):
        lane, width = CHUNKS[k]
        buf = bufs[k]
        nz, rows_k = buf.shape[0], buf.shape[4]
        for z in range(nz):
            for m in range(8):
                r = z * 8 + m
                wide[r * rows_k : (r + 1) * rows_k, :width] = buf[z, m // 4, (m // 2) % 2, m % 2].astype(F32)
        wc[:, lane : lane + width] = wide[:, :width].astype(BF16)
        for r in range(L // 512):
            rows = slice(r * 512, (r + 1) * 512)
            p[rows, lane : lane + width] = dot(xhat[rows], wc[:, lane : lane + width]).astype(BF16)
        hp_ref[:, lane : lane + width] = dot(halo[...], wc[:, lane : lane + width]).astype(BF16)
        for c in outs[2 + 2 * k : 4 + 2 * k]:
            c.start()

    @pl.when(i == 0)
    def _():
        dp = lax.axis_index("dp")
        n_dp = lax.axis_size("dp")
        total = n_dp * n
        me = dp * n + seq
        load = pltpu.make_async_copy(tok_any, tok, lsem.at[2])
        load.start()
        sem = pltpu.get_barrier_semaphore()
        k_rows = slab.shape[0]
        steps_w = win_ref[:, DI + CH :]
        slab[:, :BLOCK] = jnp.concatenate([steps_w, jnp.zeros((k_rows, BLOCK - HEADS), BF16)], axis=1)
        slab[:, BLOCK:] = win_ref[:, DI : DI + CH]

        def far(o):
            r = lax.rem(me + o, total)
            return {"dp": r // n, "seq": lax.rem(r, n)}

        for o in range(1, total):
            pl.semaphore_signal(sem, inc=1, device_id=far(o), device_id_type=MESH)
        pl.semaphore_wait(sem, total - 1)
        advance((0, 0), (1, 0))

        @pl.when(seq < n - 1)
        def _():
            halo_copy.start()

        sends = []
        for o in range(1, total):
            c = pltpu.make_async_remote_copy(
                src_ref=small.at[0], dst_ref=smalls.at[me], send_sem=ssend.at[o - 1], recv_sem=srecv.at[o - 1],
                device_id=far(o), device_id_type=MESH,
            )
            c.start()
            sends.append(c)
        for c in own:
            c.start()
        smalls[me] = small[0]
        expand_row(small[1, 2:3], row_ref)
        for (lane, width), buf in zip(CHUNKS, bufs):
            buf[at["z"], at["x"], at["y"], at["c"]] = slab[:, lane : lane + width]
        conv_ref[...] = jnp.zeros_like(conv_ref)
        state[...] = jnp.zeros_like(state)
        tot_ref[...] = jnp.zeros_like(tot_ref)
        advance((0, 1), (2, 0), (1, 1), (3, 0))
        load.wait()
        for c in sends:
            c.wait()
        taps, ks, gs = CH // total, D // total, DI // total
        for r in range(total):
            conv_ref[0:5, r * taps : (r + 1) * taps] = smalls[r, 0:5, :taps]
            gain_ref[:, r * ks : (r + 1) * ks] = jnp.broadcast_to(smalls[r, 5:6, :ks], (8, ks))
            row_ref[1:2, r * gs : (r + 1) * gs] = smalls[r, 6:7, :gs]

        def norm(r, _):
            rows = pl.ds(pl.multiple_of(r * 256, 256), 256)
            h = rms_rows(tok[rows], gain_ref[0:1])
            xhat[rows] = h
            xt[:, rows] = h.T
            return _

        lax.fori_loop(0, L // 512, norm, 0)
        advance((0, 2), (1, 2), (2, 1), (4, 0), (3, 1), (5, 0), (6, 0), (7, 0))
        lax.fori_loop(L // 512, L // 256, norm, 0)
        for c in outs[:2]:
            c.start()

        @pl.when(seq == 0)
        def _():
            halo[...] = jnp.zeros_like(halo)

        @pl.when(seq > 0)
        def _():
            halo_copy.wait_recv()

        @pl.when(seq < n - 1)
        def _():
            halo_copy.wait_send()

        halo[...] = rms_rows(halo[...], gain_ref[0:1])
        for c in own:
            c.wait()
        advance((0, 3), (1, 3), (2, 2), (3, 2), (0, 4))
        project(0)
        advance((1, 4), (4, 1), (5, 1))
        project(1)
        advance((2, 3), (3, 3), (4, 2), (5, 2), (6, 1), (7, 1), (2, 4))
        project(2)
        advance((3, 4))
        project(3)
        for c in range(CH // 128):
            ext[c, 0:8] = hp_ref[:, BLOCK + c * 128 : BLOCK + (c + 1) * 128].astype(F32)[8:16]

    def tile(r0):
        for c in range(CH // 128):
            cs = slice(c * 128, (c + 1) * 128)
            ext[c, 8 : 8 + T] = p[pl.ds(r0, T), BLOCK + c * 128 : BLOCK + (c + 1) * 128].astype(F32)
            for r in range(0, T, 64):
                total = conv_ref[4:5, cs]
                for k in range(CONV):
                    total = total + ext[c, 5 + k + r : 5 + k + r + 64] * conv_ref[k : k + 1, cs]
                sg = sigmoid(total)
                v = total * sg
                act_ref[r : r + 64, cs] = v.astype(BF16)
                slope_ref[r : r + 64, cs] = (sg + v * (1.0 - sg)).astype(BF16)
        raw = p[pl.ds(r0, T), :BLOCK].astype(F32) + small[1, 0:1]
        dt_all = jnp.maximum(raw, 0.0) + jnp.log1p(jnp.exp(-jnp.abs(raw)))
        dt_ref[...] = dt_all
        sig_ref[...] = sigmoid_exact(raw)
        tril = (iota((BLOCK, BLOCK), 0) >= iota((BLOCK, BLOCK), 1)).astype(F32)
        lo = lane_lo()
        for blk in range(T // BLOCK):
            rows = slice(blk * BLOCK, (blk + 1) * BLOCK)
            dt = dt_all[rows]
            cum = dot_exact(tril, dt * -jnp.exp(small[1, 1:2])) * LOG2E
            cum_ref[rows] = cum
            end = cum[BLOCK - 1 : BLOCK]
            tot_ref[...] += jnp.broadcast_to(end, tot_ref.shape)
            wfac = jnp.exp2(end - cum) * dt
            decay = jnp.broadcast_to(jnp.exp2(end), (8, BLOCK))
            write_t = act_ref[rows, DI : DI + NSTATE].T
            for j in range(PAIRS):
                w, _, _ = expand_pair(wfac, j, lo)
                weighted[:, pair(j)] = (act_ref[rows, pair(j)].astype(F32) * w).astype(BF16)
            for q in range(PAIRS // 2):
                cs = slice(q * 256, (q + 1) * 256)
                new = dot(write_t, weighted[:, cs])
                bst_ref[blk, :, cs] = new.astype(BF16)
                d0, _, _ = expand_pair(decay, 2 * q, lo[:8])
                d1, _, _ = expand_pair(decay, 2 * q + 1, lo[:8])
                dd = jnp.concatenate([d0, d1], axis=1)[0:1]
                state[:, cs] = state[:, cs] * dd + new

    def after(step, *what):
        @pl.when(i == step)
        def _():
            advance(*what)

    after(2, (6, 2), (7, 2))
    after(4, (4, 3), (5, 3))
    after(6, (6, 3), (7, 3))

    @pl.when(i > 1)
    def _():
        ext[:, 0:8] = ext[:, T : T + 8]

    @pl.when(i > 0)
    def _():
        tile(pl.multiple_of((i - 1) * T, T))

    @pl.when(i == steps - 1)
    def _():
        leave_ref[...] = state[...]
        advance((4, 4), (5, 4), (6, 4), (7, 4))
        for c in outs:
            c.wait()


def sigmoid_exact(v):
    return 1.0 / (1.0 + jnp.exp(-v))


def second_kernel(
    T, gate_s, ng, act_ref, dt_ref, cum_ref, bst_ref, inc_ref, tok_ref, wo_ref, row_ref, et_ref,
    mixed_ref, nout_ref, ggrad_ref, mlow_ref, dcum_ref, ent_ref, egrad_ref, rg_ref, leave_ref, back_ref, cols_ref,
    ms, growth, rlow, prod, plow, state, exg, lows,
):
    i = pl.program_id(0)

    @pl.when(i == 0)
    def _():
        state[...] = inc_ref[...]
        exg[...] = jnp.ones_like(exg)
        back_ref[...] = jnp.zeros_like(back_ref)
        cols_ref[...] = jnp.zeros_like(cols_ref)

    lo = lane_lo()
    lower = iota((BLOCK, BLOCK), 0) >= iota((BLOCK, BLOCK), 1)
    nblk = T // BLOCK
    for blk in range(nblk):
        rows = slice(blk * BLOCK, (blk + 1) * BLOCK)
        cum = cum_ref[rows]
        cum_t = cum.T
        dt = dt_ref[rows]
        write = act_ref[rows, DI : DI + NSTATE]
        read = act_ref[rows, DI + NSTATE :]
        inner = jnp.where(lower, dot_nt(read, write), 0.0)
        lows[blk] = state[...].astype(BF16)
        ent_ref[blk] = lows[blk]
        for j in range(PAIRS):
            cols, a, b = expand_pair(cum, j, lo)
            ga = jnp.exp2(jnp.minimum(a - cum_t[2 * j : 2 * j + 1], 0.0)) * inner
            gb = jnp.exp2(jnp.minimum(b - cum_t[2 * j + 1 : 2 * j + 2], 0.0)) * inner
            scores = jnp.concatenate([ga.astype(BF16), gb.astype(BF16)], axis=1)
            vals = act_ref[rows, pair(j)].astype(F32)
            dtp, _, _ = expand_pair(dt, j, lo)
            vdt = (vals * dtp).astype(BF16)
            grow = jnp.exp2(cols)
            growth[rows, pair(j)] = grow
            diag = dot(scores, block_diag(vdt))
            if j % 2 == 0:
                outs = dot(read, lows[blk, :, j * BLOCK : (j + 2) * BLOCK])
            out = outs[:, (j % 2) * BLOCK : (j % 2 + 1) * BLOCK]
            ms[rows, pair(j)] = diag + grow * out + row_ref[0:1, pair(j)] * vals
            dec = grow[BLOCK - 1 : BLOCK]
            state[:, pair(j)] = state[:, pair(j)] * dec + bst_ref[blk, :, pair(j)].astype(F32)

    sq = jnp.zeros((T, BLOCK), F32)
    ug = jnp.zeros((T, BLOCK), F32)
    for j in range(PAIRS):
        g = gate_s[:, pair(j)].astype(F32)
        gated = ms[:, pair(j)] * (g * sigmoid(g))
        sq = sq + gated * gated
        ug = ug + gated * ng[:, pair(j)].astype(F32)
    inv = lax.rsqrt(jnp.sum(sq, axis=-1, keepdims=True) * (1.0 / DI) + EPS)
    coef = jnp.sum(ug, axis=-1, keepdims=True) * (1.0 / DI) * (inv * inv * inv)
    for j in range(PAIRS):
        g = gate_s[:, pair(j)].astype(F32)
        sg = sigmoid(g)
        silu = g * sg
        m = ms[:, pair(j)]
        gated = m * silu
        nout_ref[:, pair(j)] = (gated * inv * row_ref[1:2, pair(j)]).astype(BF16)
        dg = inv * ng[:, pair(j)].astype(F32) - gated * coef
        low = (dg * silu).astype(BF16)
        mlow_ref[:, pair(j)] = low
        ggrad_ref[:, pair(j)] = (dg * m * (sg + silu * (1.0 - sg))).astype(BF16)
        vals = act_ref[:, pair(j)].astype(F32)
        lowf = low.astype(F32)
        mv = lowf * vals
        pr = lowf * m - row_ref[0:1, pair(j)] * mv
        hi = pr.astype(BF16)
        prod[:, pair(j)] = hi
        plow[:, pair(j)] = (pr - hi.astype(F32)).astype(BF16)
        rlow[:, pair(j)] = (lowf * growth[:, pair(j)]).astype(BF16)
        cols_ref[:, pair(j)] += jnp.sum(mv.reshape(T // 8, 8, BLOCK), axis=0)
    dcum_ref[...] = dot(prod[...], et_ref[...]) + dot(plow[...], et_ref[...])
    mixed_ref[...] = (tok_ref[...].astype(F32) + dot(nout_ref[...], wo_ref[...])).astype(BF16)
    for blk in range(nblk):
        rows = slice(blk * BLOCK, (blk + 1) * BLOCK)
        read_t = act_ref[rows, DI + NSTATE :].T
        for q in range(PAIRS // 2):
            cs = slice(q * 256, (q + 1) * 256)
            eg = dot(read_t, rlow[rows, cs])
            egrad_ref[blk, :, cs] = eg.astype(BF16)
            back_ref[:, cs] += eg * exg[0:1, cs]
        exg[...] = exg[...] * growth[blk * BLOCK + BLOCK - 1 : blk * BLOCK + BLOCK, :]
        rg_ref[rows] = dot_nt(rlow[rows, :], lows[blk])

    @pl.when(i == pl.num_programs(0) - 1)
    def _():
        leave_ref[...] = state[...].astype(BF16)


def third_kernel(
    T, act_ref, convin_ref, slope_ref, dt_ref, cum_ref, sig_ref, dcum_ref, mlow_ref, ent_ref, leave_ref,
    egrad_ref, rg_ref, inc_ref, row_ref, conv_ref, head_ref, et_ref, cols_ref, go_ref, gg_ref,
    pg_ref, small_ref, tail_ref, so_ref, sg_ref,
    cgrad_ref, hgrad_ref, sums8, glast, xlast, gafter, hsend, hrecv, carry, dact, vprod, prod, plow, weighted, lows, dec, nxt, gext, *scratch,
):
    i = pl.program_id(0)
    steps = pl.num_programs(0)
    sca = Scatter(go_ref, "yx", scratch[2 : 2 + NSC], *scratch[:2])
    scb = Scatter(gg_ref, "xy", scratch[4 + NSC :], *scratch[2 + NSC : 4 + NSC])
    seq, nseq = lax.axis_index("seq"), lax.axis_size("seq")
    after = pltpu.make_async_remote_copy(
        src_ref=gext.at[:, pl.ds(0, 8)], dst_ref=gafter, send_sem=hsend, recv_sem=hrecv, device_id={"seq": seq - 1},
        device_id_type=MESH,
    )

    @pl.when(i == 0)
    def _():
        greet(place(), "zxyc", 1)
        sca.start(0)
        scb.start(0)

    for stage, when in enumerate((1, 3, 5)):
        @pl.when(i == when)
        def _():
            sca.finish(stage)
            sca.start(stage + 1)
            scb.finish(stage)
            scb.start(stage + 1)


    @pl.when(i == 0)
    def _():
        carry[...] = inc_ref[...]
        nxt[...] = leave_ref[...]
        cgrad_ref[...] = jnp.zeros_like(cgrad_ref)
        hgrad_ref[...] = jnp.zeros_like(hgrad_ref)

    lo = lane_lo()
    upper = iota((BLOCK, BLOCK), 0) <= iota((BLOCK, BLOCK), 1)
    triu = upper.astype(F32)
    last = iota((BLOCK, BLOCK), 0) == BLOCK - 1
    for blk in reversed(range(T // BLOCK)):
        rows = slice(blk * BLOCK, (blk + 1) * BLOCK)
        cum = cum_ref[rows]
        cum_t = cum.T
        dt = dt_ref[rows]
        end = cum[BLOCK - 1 : BLOCK]
        write = act_ref[rows, DI : DI + NSTATE]
        read = act_ref[rows, DI + NSTATE :]
        inner = jnp.where(upper, dot_nt(write, read), 0.0)
        lows[...] = carry[...].astype(BF16)
        acc = jnp.zeros((BLOCK, BLOCK), F32)
        for j in range(PAIRS):
            cols, a, b = expand_pair(cum, j, lo)
            ends = jnp.where(lo[:1], end[:, 2 * j : 2 * j + 1], end[:, 2 * j + 1 : 2 * j + 2])
            wexp = jnp.exp2(ends - cols)
            da = jnp.exp2(jnp.minimum(cum_t[2 * j : 2 * j + 1] - a, 0.0))
            db = jnp.exp2(jnp.minimum(cum_t[2 * j + 1 : 2 * j + 2] - b, 0.0))
            scores = jnp.concatenate([(da * inner).astype(BF16), (db * inner).astype(BF16)], axis=1)
            m = mlow_ref[rows, pair(j)]
            diag = block_diag(m)
            z = dot(scores, diag)
            vals = act_ref[rows, pair(j)].astype(F32)
            dtp, _, _ = expand_pair(dt, j, lo)
            vdt = vals * dtp
            vdtb = vdt.astype(BF16)
            wtb = (vdt * wexp).astype(BF16)
            g = dot_nt(vdtb, diag)
            acc = acc + g[:, :BLOCK] * da + g[:, BLOCK:] * db
            if j % 2 == 0:
                wgs = dot(write, lows[:, j * BLOCK : (j + 2) * BLOCK])
            wg = wgs[:, (j % 2) * BLOCK : (j % 2 + 1) * BLOCK]
            pr = vdtb.astype(F32) * z + wtb.astype(F32) * wg
            z = z + wg * wexp
            dact[rows, pair(j)] = row_ref[0:1, pair(j)] * m.astype(F32) + dtp * z
            vprod[:, pair(j)] = (vals * z).astype(BF16)
            hi = pr.astype(BF16)
            prod[:, pair(j)] = hi
            plow[:, pair(j)] = (pr - hi.astype(F32)).astype(BF16)
            weighted[:, pair(j)] = wtb
            dec[0:1, pair(j)] = jnp.exp2(cols[BLOCK - 1 : BLOCK])
        low = jnp.where(upper, acc, 0.0).astype(BF16)
        dact[rows, DI : DI + NSTATE] = dot_nt(weighted[...], lows[...]) + dot(low, read)
        dact[rows, DI + NSTATE :] = rg_ref[rows] + dot(low.T, write)
        c = dot(vprod[...], et_ref[...])
        used = dot(prod[...], et_ref[...]) + dot(plow[...], et_ref[...])
        ends = jnp.sum((lows[...].astype(F32) * nxt[...].astype(F32)).reshape(16, 8, DI), axis=0)
        ends_hi = ends.astype(BF16)
        ends_lo = (ends - ends_hi.astype(F32)).astype(BF16)
        de = jnp.sum(dot(ends_hi, et_ref[...]) + dot(ends_lo, et_ref[...]), axis=0, keepdims=True)
        dc = dcum_ref[rows] - used + jnp.where(last, de, 0.0)
        da_log = dot_exact(triu, dc)
        decay = -jnp.exp(head_ref[1, 1:2])
        draw = (c + da_log * decay) * sig_ref[rows]
        pg_ref[rows, :BLOCK] = draw.astype(BF16)
        hgrad_ref[0:8] += jnp.sum(draw.reshape(16, 8, BLOCK), axis=0)
        hgrad_ref[8:16] += jnp.sum((da_log * dt).reshape(16, 8, BLOCK), axis=0) * decay
        nxt[...] = ent_ref[blk]
        for q in range(PAIRS // 2):
            cs = slice(q * 256, (q + 1) * 256)
            carry[:, cs] = carry[:, cs] * dec[0:1, cs] + egrad_ref[blk, :, cs].astype(F32)

    for c in range(CH // 128):
        cs = slice(c * 128, (c + 1) * 128)
        ps = slice(BLOCK + c * 128, BLOCK + (c + 1) * 128)

        @pl.when(i == 0)
        def _():
            gext[c, T : T + 8] = jnp.zeros((8, 128), F32)
            xlast[:, cs] = convin_ref[T - 16 :, ps].astype(F32)

        @pl.when(i > 0)
        def _():
            gext[c, T : T + 8] = gext[c, 0:8]

        for r in range(0, T, 64):
            gext[c, r : r + 64] = dact[r : r + 64, cs] * slope_ref[r : r + 64, cs].astype(F32)
        sums = [jnp.zeros((8, 128), F32)] * 5
        for r in range(0, T, 64):
            x = convin_ref[r : r + 64, ps].astype(F32)
            g = gext[c, r : r + 64]
            back = g * conv_ref[3:4, cs]
            sums[4] = sums[4] + jnp.sum(g.reshape(8, 8, 128), axis=0)
            sums[3] = sums[3] + jnp.sum((g * x).reshape(8, 8, 128), axis=0)
            for k in range(CONV - 1):
                gk = gext[c, 3 - k + r : 3 - k + r + 64]
                back = back + gk * conv_ref[k : k + 1, cs]
                sums[k] = sums[k] + jnp.sum((gk * x).reshape(8, 8, 128), axis=0)
            pg_ref[r : r + 64, ps] = back.astype(BF16)
            if r + 64 == T:
                @pl.when(i == 0)
                def _():
                    glast[:, cs] = back[48:]
        for k in range(5):
            cgrad_ref[8 * k : 8 * k + 8, cs] += sums[k]

    @pl.when(i == steps - 1)
    def _():
        @pl.when(seq > 0)
        def _():
            after.start()

        so_ref[...] = sca.result()
        sg_ref[...] = scb.result()

        @pl.when(seq == nseq - 1)
        def _():
            gafter[...] = jnp.zeros_like(gafter)

        @pl.when(seq < nseq - 1)
        def _():
            after.wait_recv()

        row16, row8 = iota((16, 128), 0), iota((8, 128), 0)
        for c in range(CH // 128):
            cs = slice(c * 128, (c + 1) * 128)
            ps = slice(BLOCK + c * 128, BLOCK + (c + 1) * 128)
            tail = glast[:, cs]
            for j in range(CONV - 1):
                for k in range(j + 1):
                    g = gafter[c, j - k : j - k + 1]
                    tail = tail + jnp.where(row16 == 13 + j, g * conv_ref[k : k + 1, cs], 0.0)
                    cgrad_ref[8 * k : 8 * k + 8, cs] += jnp.where(row8 == 0, g * xlast[13 + j : 14 + j, cs], 0.0)
            tail_ref[:, ps] = tail.astype(BF16)
        tail_ref[:, :BLOCK] = jnp.zeros((16, BLOCK), BF16)
        for k in range(5):
            sums8[k : k + 1] = jnp.sum(cgrad_ref[8 * k : 8 * k + 8], axis=0, keepdims=True)
        steps8 = jnp.broadcast_to(jnp.sum(hgrad_ref[0:8], axis=0, keepdims=True), (8, BLOCK))
        decay8 = jnp.broadcast_to(jnp.sum(hgrad_ref[8:16], axis=0, keepdims=True), (8, BLOCK))
        high = cols_ref[...].astype(BF16)
        low8 = (cols_ref[...] - high.astype(F32)).astype(BF16)
        skip8 = jnp.sum(dot(high, et_ref[...]) + dot(low8, et_ref[...]), axis=0, keepdims=True)
        skip8 = jnp.broadcast_to(skip8, (8, BLOCK))
        lane = iota((8, BLOCK), 1)
        heads = jnp.where(lane < HEADS, steps8, pltpu.roll(decay8, HEADS, 1))
        heads = jnp.where(lane < 2 * HEADS, heads, pltpu.roll(skip8, 2 * HEADS, 1))
        heads = jnp.where((iota((8, BLOCK), 0) == 7) & (lane < 3 * HEADS), heads, 0.0)
        take = CH // small_ref.shape[0]
        for r in range(small_ref.shape[0]):
            small_ref[r] = heads
            small_ref[r, 0:5, :take] = sums8[0:5, r * take : (r + 1) * take]

        @pl.when(seq > 0)
        def _():
            after.wait_send()


def once(shape):
    return pl.BlockSpec(shape, lambda i: (0,) * len(shape), pipeline_mode=pl.Buffered(1))


def full(shape):
    return pl.BlockSpec(shape, lambda i: (0,) * len(shape))


def params(collective_id=None):
    return pltpu.CompilerParams(
        dimension_semantics=("arbitrary",), vmem_limit_bytes=VMEM_LIMIT, collective_id=collective_id,
        has_side_effects=collective_id is not None,
    )


def head_columns():
    et = np.zeros((DI, BLOCK), np.float32)
    et[np.arange(DI), np.arange(DI) // HEADDIM] = 1.0
    return et


def sds(shape, dtype):
    return jax.ShapeDtypeStruct(shape, dtype)


def first_pass(w_in, small, tok, slab_o, T=256):
    L = tok.shape[0]
    nb, per = L // BLOCK, T // BLOCK
    n = sizes()
    k_rows = w_in.shape[0]
    total = lax.axis_size("dp") * lax.axis_size("seq")
    row = lambda w: pl.BlockSpec((T, w), lambda i: (jnp.maximum(i - 1, 0), 0))
    dims = (n["z"], n["x"], n["y"], n["c"])
    sems = []
    for _ in range(len(CHUNKS) + 4):
        sems += gather_sems()
    return pl.pallas_call(
        functools.partial(first_kernel, T),
        grid=(1 + L // T,),
        in_specs=[once(w_in.shape), once((2, 8, BLOCK)), ANY, ANY],
        out_specs=[
            ANY, ANY, ANY, ANY, full((16, WC)), full((8, CH)), full((8, D)), full((8, DI)),
            row(CH), row(CH), row(BLOCK), row(BLOCK), row(BLOCK),
            pl.BlockSpec((per, NSTATE, DI), lambda i: (jnp.maximum(i - 1, 0), 0, 0)), full((NSTATE, DI)),
            full((8, BLOCK)), ANY, ANY,
        ],
        out_shape=[
            sds((L, D), BF16), sds((D, L), BF16), sds((D, WC), BF16), sds((L, WC), BF16), sds((16, WC), BF16),
            sds((8, CH), F32), sds((8, D), F32), sds((8, DI), F32),
            sds((L, CH), BF16), sds((L, CH), BF16), sds((L, BLOCK), F32), sds((L, BLOCK), F32), sds((L, BLOCK), F32),
            sds((nb, NSTATE, DI), BF16), sds((NSTATE, DI), F32), sds((8, BLOCK), F32),
            sds(dims + (k_rows, DI), BF16), sds(dims + slab_o.shape, BF16),
        ],
        scratch_shapes=[
            pltpu.VMEM((k_rows, WC), BF16), pltpu.VMEM((L, D), BF16), pltpu.VMEM((16, D), BF16), pltpu.VMEM((L, D), BF16), pltpu.VMEM((D, L), BF16),
            pltpu.VMEM((D, WC), BF16), pltpu.VMEM((D, 512), F32), pltpu.VMEM((L, WC), BF16),
            pltpu.VMEM((total, 8, BLOCK), F32),
        ] + [pltpu.VMEM(dims + (k_rows, w), BF16) for _, w in CHUNKS] + [
            pltpu.VMEM((CH // 128, T + 8, 128), F32), pltpu.VMEM((NSTATE, DI), F32), pltpu.VMEM((BLOCK, DI), BF16),
            pltpu.SemaphoreType.DMA((5 + 2 * len(CHUNKS),)), pltpu.SemaphoreType.DMA(()), pltpu.SemaphoreType.DMA(()),
            pltpu.SemaphoreType.DMA((total - 1,)), pltpu.SemaphoreType.DMA((total - 1,)),
        ] + sems,
        compiler_params=params(collective_id=1),
        name="first_pass",
    )(w_in, small, tok, slab_o)


def second_pass(gate, ng, act, dt, cum, bst, inc, tok, wo, rows, et, T=256):
    L = tok.shape[0]
    nb, per = L // BLOCK, T // BLOCK
    row = lambda w: pl.BlockSpec((T, w), lambda i: (i, 0))
    blk = pl.BlockSpec((per, NSTATE, DI), lambda i: (i, 0, 0))
    return pl.pallas_call(
        functools.partial(second_kernel, T),
        grid=(L // T,),
        in_specs=[
            row(DI), row(DI), row(CH), row(BLOCK), row(BLOCK), blk, full((NSTATE, DI)), row(D), full((DI, D)), full((8, DI)), full((DI, BLOCK)),
        ],
        out_specs=[
            row(D), row(DI), row(DI), row(DI), row(BLOCK), blk, blk, row(BLOCK), full((NSTATE, DI)),
            full((NSTATE, DI)), full((8, DI)),
        ],
        out_shape=[
            sds((L, D), BF16), sds((L, DI), BF16), sds((L, DI), BF16), sds((L, DI), BF16), sds((L, BLOCK), F32),
            sds((nb, NSTATE, DI), BF16), sds((nb, NSTATE, DI), BF16), sds((L, BLOCK), F32), sds((NSTATE, DI), BF16),
            sds((NSTATE, DI), F32), sds((8, DI), F32),
        ],
        scratch_shapes=[
            pltpu.VMEM((T, DI), F32), pltpu.VMEM((T, DI), F32),
            pltpu.VMEM((T, DI), BF16), pltpu.VMEM((T, DI), BF16), pltpu.VMEM((T, DI), BF16), pltpu.VMEM((NSTATE, DI), F32),
            pltpu.VMEM((8, DI), F32), pltpu.VMEM((per, NSTATE, DI), BF16),
        ],
        compiler_params=params(),
        name="second_pass",
    )(gate, ng, act, dt, cum, bst, inc, tok, wo, rows, et)


def third_pass(
    act, convin, slope, dt, cum, sig, dcum, mlow, ent, leave, egrad, rg, inc, rows, conv, head, et, cols, go, gg, T=256
):
    L = act.shape[0]
    m = sizes()
    dims = (m["z"], m["x"], m["y"], m["c"])
    total = m["z"] * m["y"] * 4
    ro, rg_rows = DI // total, D // total
    go = go.reshape(dims + (ro, D))
    gg = gg.reshape(dims + (rg_rows, DI))
    n, per = L // T, T // BLOCK
    row = lambda w: pl.BlockSpec((T, w), lambda i: (n - 1 - i, 0))
    blk = pl.BlockSpec((per, NSTATE, DI), lambda i: (n - 1 - i, 0, 0))
    return pl.pallas_call(
        functools.partial(third_kernel, T),
        grid=(n,),
        in_specs=[
            row(CH), row(WC), row(CH), row(BLOCK), row(BLOCK), row(BLOCK), row(BLOCK), row(DI), blk,
            full((NSTATE, DI)), blk, row(BLOCK), full((NSTATE, DI)), full((8, DI)), full((8, CH)), full((2, 8, BLOCK)),
            full((DI, BLOCK)), full((8, DI)), ANY, ANY,
        ],
        out_specs=[
            row(WC), full((total, 8, BLOCK)), full((16, WC)), full((ro, D)), full((rg_rows, DI)),
        ],
        out_shape=[
            sds((L, WC), BF16), sds((total, 8, BLOCK), F32), sds((16, WC), BF16), sds((ro, D), F32),
            sds((rg_rows, DI), F32),
        ],
        scratch_shapes=[
            pltpu.VMEM((40, CH), F32), pltpu.VMEM((16, BLOCK), F32), pltpu.VMEM((8, CH), F32),
            pltpu.VMEM((16, CH), F32), pltpu.VMEM((16, CH), F32), pltpu.VMEM((CH // 128, 8, 128), F32),
            pltpu.SemaphoreType.DMA(()), pltpu.SemaphoreType.DMA(()),
            pltpu.VMEM((NSTATE, DI), F32), pltpu.VMEM((T, CH), F32), pltpu.VMEM((BLOCK, DI), BF16), pltpu.VMEM((BLOCK, DI), BF16), pltpu.VMEM((BLOCK, DI), BF16),
            pltpu.VMEM((BLOCK, DI), BF16), pltpu.VMEM((NSTATE, DI), BF16), pltpu.VMEM((8, DI), F32),
            pltpu.VMEM((NSTATE, DI), BF16), pltpu.VMEM((CH // 128, T + 8, 128), F32),
        ] + own_scratch(ro, D) + scatter_scratch(ro, D) + own_scratch(rg_rows, DI) + scatter_scratch(rg_rows, DI),
        compiler_params=params(collective_id=4),
        name="third_pass",
    )(act, convin, slope, dt, cum, sig, dcum, mlow, ent, leave, egrad, rg, inc, rows, conv, head, et, cols, go, gg)


def on_device(
    tokens, cotangent, norm_gain, in_weight, conv_weight, conv_bias, step_bias, decay_log, skip_gain, gate_gain,
    out_weight,
):
    tok, cot = tokens[0], cotangent[0]
    L = tok.shape[0]
    k_rows, c_rows = in_weight.shape[0], conv_weight.shape[0]
    total = D // k_rows
    lanes = lambda x: jnp.pad(x, ((0, 0),) * (x.ndim - 1) + ((0, BLOCK - x.shape[-1]),))

    def put(x, row):
        x = x.astype(F32)
        return jnp.pad(x, ((row, 16 - row - x.shape[0]), (0, BLOCK - x.shape[1])))

    own = put(conv_weight.T, 0) + put(conv_bias[None], 4) + put(norm_gain[None], 5) + put(gate_gain[None], 6)
    own = own + put(step_bias[None], 8) + put(decay_log[None], 9) + put(skip_gain[None], 10)
    own = own.reshape(2, 8, BLOCK)
    et = jnp.asarray(head_columns(), BF16)

    (xhat, xt, wc, p, hp, conv, gain, rows, act, slope, dt, cum, sig, bst, leave, tot, buf_g, buf_o) = first_pass(
        in_weight, own, tok, out_weight
    )
    wg, wo = buf_g.reshape(D, DI), buf_o.reshape(DI, D)
    gate, ng, inc = gate_pass(xhat, wg, cot, wo, rows, leave, tot)
    mixed, nout, ggrad, mlow, dcum, ent, egrad, rg, leave2, back, cols = second_pass(
        gate, ng, act, dt, cum, bst, inc, tok, wo, rows, et
    )
    g_out, g_gate, later = grads_pass(nout, cot, xt, ggrad, back, tot)
    pg, small, tail, out_raw, gate_cols = third_pass(
        act, p, slope, dt, cum, sig, dcum, mlow, ent, leave2, egrad, rg, later, rows, conv, own, et, cols, g_out,
        g_gate,
    )
    tgrad, conv_cols, sums = last_pass(xt, pg, tail, ggrad, tok, cot, wg, wc, gain, small)
    in_grad, ngain_grad, ggain_grad, taps, bias, step, decay, skip, out_grad, tgrad = finish_pass(
        gate_cols, conv_cols, out_raw, sums, in_weight, out_weight, own, tgrad, c_rows
    )
    return (
        mixed[None], tgrad[None], ngain_grad, in_grad, taps.T, bias, step, decay, skip, ggain_grad, out_grad,
    )


def solution(mesh):
    both = ("dp", "seq")
    vec, mat, tok, rep = P(both), P(both, None), P("dp", "seq", None), P()
    return jax.shard_map(
        on_device,
        mesh=mesh,
        in_specs=(tok, tok, vec, mat, mat, vec, rep, rep, rep, vec, mat),
        out_specs=(tok, tok, vec, mat, mat, vec, rep, rep, rep, vec, mat),
        check_vma=False,
    )
```

```python
import functools

import jax
import jax.numpy as jnp
import numpy as np
from jax import lax
from jax.experimental import pallas as pl
from jax.experimental.pallas import tpu as pltpu
from jax.sharding import PartitionSpec as P

D = 768
HEADS = 24
HEADDIM = 64
NSTATE = 128
CONV = 4
BLOCK = 128
DI = 1536
CH = 1792
PAIRS = HEADS // 2
EPS = 1e-05
LOG2E = 1.4426950408889634
F32 = jnp.float32
BF16 = jnp.bfloat16
NT = (((1,), (1,)), ((), ()))
VMEM_LIMIT = 60 * 1024 * 1024


def dot(a, b):
    return jnp.dot(a, b, preferred_element_type=F32)


def dot_nt(a, b):
    return lax.dot_general(a, b, NT, preferred_element_type=F32)


def dot_exact(a, b):
    return jnp.dot(a, b, preferred_element_type=F32, precision=lax.Precision.HIGHEST)


def sigmoid(v):
    return 0.5 * jnp.tanh(0.5 * v) + 0.5


def iota(shape, dim):
    return lax.broadcasted_iota(jnp.int32, shape, dim)


def lane_lo():
    return iota((BLOCK, BLOCK), 1) < HEADDIM


def expand_pair(x, j, lo):
    rows = x.shape[0]
    a = jnp.broadcast_to(x[:, 2 * j : 2 * j + 1], (rows, BLOCK))
    b = jnp.broadcast_to(x[:, 2 * j + 1 : 2 * j + 2], (rows, BLOCK))
    return jnp.where(lo, a, b), a, b


def block_diag(v):
    lo = iota(v.shape, 1) < HEADDIM
    zero = jnp.zeros_like(v)
    return jnp.concatenate([jnp.where(lo, v, zero), jnp.where(lo, zero, v)], axis=0)


def pair(j):
    return slice(j * BLOCK, (j + 1) * BLOCK)


MESH = pl.DeviceIdType.MESH
ANY = pl.BlockSpec(memory_space=pl.ANY)
WC = CH + BLOCK
TN = (((0,), (0,)), ((), ()))


def dot_tn(a, b):
    return lax.dot_general(a, b, TN, preferred_element_type=F32)


def sizes():
    return {"z": lax.axis_size("dp") // 2, "x": 2, "y": lax.axis_size("seq") // 2, "c": 2}


def place():
    dp, seq = lax.axis_index("dp"), lax.axis_index("seq")
    return {"z": dp // 2, "x": lax.rem(dp, 2), "y": seq // 2, "c": lax.rem(seq, 2)}


def device(at):
    return {"dp": at["z"] * 2 + at["x"], "seq": at["y"] * 2 + at["c"]}


def peers(at, axis):
    n = sizes()[axis]
    return [dict(at, **{axis: lax.rem(at[axis] + o, n)}) for o in range(1, n)]


def greet(at, axes, by=0):
    sem = pltpu.get_barrier_semaphore()
    count = 0
    for axis in axes:
        for peer in peers(at, axis):
            pl.semaphore_signal(sem, inc=1, device_id=device(peer), device_id_type=MESH)
            count += 1
    if not by:
        pl.semaphore_wait(sem, count)
        return
    seq, n = lax.axis_index("seq"), lax.axis_size("seq")

    @pl.when((seq + by >= 0) & (seq + by < n))
    def _():
        pl.semaphore_signal(sem, inc=1, device_id={"seq": seq + by}, device_id_type=MESH)

    heard = (seq - by >= 0) & (seq - by < n)

    @pl.when(heard)
    def _():
        pl.semaphore_wait(sem, count + 1)

    @pl.when(jnp.logical_not(heard))
    def _():
        pl.semaphore_wait(sem, count)


def greet_neighbours():
    seq, n = lax.axis_index("seq"), lax.axis_size("seq")
    sem = pltpu.get_barrier_semaphore()

    @pl.when(seq > 0)
    def _():
        pl.semaphore_signal(sem, inc=1, device_id={"seq": seq - 1}, device_id_type=MESH)

    @pl.when(seq < n - 1)
    def _():
        pl.semaphore_signal(sem, inc=1, device_id={"seq": seq + 1}, device_id_type=MESH)

    @pl.when((seq > 0) & (seq < n - 1))
    def _():
        pl.semaphore_wait(sem, 2)

    @pl.when((seq == 0) | (seq == n - 1))
    def _():
        pl.semaphore_wait(sem, 1)


def remote(src, dst, send, recv, peer):
    return pltpu.make_async_remote_copy(
        src_ref=src, dst_ref=dst, send_sem=send, recv_sem=recv, device_id=device(peer), device_id_type=MESH
    )


class Gather:
    def __init__(self, slab, spot, order, sems):
        self.slab, self.spot, self.order = slab, spot, order
        self.send, self.recv = sems
        self.at = place()

    def copies(self, stage):
        at, (a, b) = self.at, self.order
        n = sizes()
        out = []
        every = slice(None)
        nz = n["z"] - 1
        if stage == 0:
            for o, peer in enumerate(peers(at, "z")):
                out.append((self.slab, self.spot(at), o, peer))
        elif stage == 1:
            index = dict(at, z=every)
            out.append((self.spot(index), self.spot(index), nz, peers(at, a)[0]))
        elif stage == 2:
            index = dict(at, z=every)
            index[a] = every
            for o, peer in enumerate(peers(at, b)):
                out.append((self.spot(index), self.spot(index), nz + 1 + o, peer))
            out.append((self.spot(index), self.spot(index), nz + 1 + n[b] - 1, peers(at, "c")[0]))
        else:
            for o in range(1, n[b]):
                index = dict(at, z=every)
                index[a] = every
                index[b] = lax.rem(at[b] + o, n[b])
                out.append((self.spot(index), self.spot(index), nz + 1 + n[b] + o - 1, peers(at, "c")[0]))
        return [remote(s, d, self.send.at[k], self.recv.at[k], p) for s, d, k, p in out]

    def start(self, stage):
        for c in self.copies(stage):
            c.start()

    def wait(self, stage):
        for c in self.copies(stage):
            c.wait()


def spots(buf, lanes=slice(None)):
    return lambda index: buf.at[index["z"], index["x"], index["y"], index["c"], :, lanes]


def gather_sems():
    count = sizes()["z"] + 2 * sizes()["y"] + 4
    return [pltpu.SemaphoreType.DMA((count,)), pltpu.SemaphoreType.DMA((count,))]


class Scatter:
    def __init__(self, grads, order, scratch, own=None, local=None):
        self.grads, self.order, self.own_ref, self.local = grads, order, own, local
        self.rc, self.r1, self.r2, self.rz, self.send, self.recv = scratch
        self.at = place()
        self.own = self

    def spot(self, z, x, y):
        if self.own_ref is not None:
            return self.own_ref.at[z, x, y]
        return self.grads.at[z, x, y, self.at["c"]]

    def add(self, z, x, y, got):
        mine = self.spot(z, x, y)
        mine[...] = (mine[...].astype(F32) + got.astype(F32)).astype(BF16)

    def copies(self, stage):
        at, (a, b) = self.at, self.order
        every = slice(None)
        out = []

        def spot(index):
            return self.spot(index["z"], index["x"], index["y"])

        if stage == 0:
            out.append((self.grads.at[:, :, :, 1 - at["c"]], self.rc, 0, peers(at, "c")[0]))
        elif stage == 1:
            index = {"z": every, "x": every, "y": every}
            index[a] = 1 - at[a]
            out.append((spot(index), self.r1, 1, peers(at, a)[0]))
        elif stage == 2:
            index = {"z": every, a: at[a], b: 1 - at[b]}
            out.append((spot(index), self.r2, 2, peers(at, b)[0]))
        else:
            for o, peer in enumerate(peers(at, "z")):
                out.append((self.spot(peer["z"], at["x"], at["y"]), self.rz.at[o], 3 + o, peer))
        return [remote(s, d, self.send.at[k], self.recv.at[k], p) for s, d, k, p in out]

    def mine(self):
        return pltpu.make_async_copy(self.grads.at[:, :, :, self.at["c"]], self.own_ref, self.local)

    def start(self, stage):
        if stage == 0 and self.own_ref is not None:
            self.mine().start()
        for c in self.copies(stage):
            c.start()

    def finish(self, stage):
        at, (a, b) = self.at, self.order
        for c in self.copies(stage):
            c.wait()
        nz = sizes()["z"]
        if stage == 0:
            if self.own_ref is not None:
                self.mine().wait()

            def body(z, _):
                for x in range(2):
                    for y in range(2):
                        self.add(z, x, y, self.rc[z, x, y])
                return _

        elif stage == 1:

            def body(z, _):
                for k in range(2):
                    index = {a: at[a], b: k}
                    self.add(z, index["x"], index["y"], self.r1[z, k])
                return _

        else:

            def body(z, _):
                self.add(z, at["x"], at["y"], self.r2[z])
                return _

        lax.fori_loop(0, nz, body, 0)

    def result(self):
        for c in self.copies(3):
            c.wait()
        total = self.spot(self.at["z"], self.at["x"], self.at["y"])[...].astype(F32)
        for o in range(sizes()["z"] - 1):
            total = total + self.rz[o].astype(F32)
        return total


def scatter_scratch(rows, width):
    nz = sizes()["z"]
    return [
        pltpu.VMEM((nz, 2, 2, rows, width), BF16), pltpu.VMEM((nz, 2, rows, width), BF16),
        pltpu.VMEM((nz, rows, width), BF16), pltpu.VMEM((nz - 1, rows, width), BF16),
        pltpu.SemaphoreType.DMA((nz + 2,)), pltpu.SemaphoreType.DMA((nz + 2,)),
    ]


NSC = 6


def own_scratch(rows, width):
    return [pltpu.VMEM((sizes()["z"], 2, 2, rows, width), BF16), pltpu.SemaphoreType.DMA(())]


class Chain:
    def __init__(self, leave, inc, decay, bufs, reverse):
        self.leave, self.inc, self.decay, self.reverse = leave, inc, decay, reverse
        self.got, self.put, self.send, self.recv = bufs
        self.n = lax.axis_size("seq")
        seq = lax.axis_index("seq")
        self.rank = self.n - 1 - seq if reverse else seq
        self.to = seq - 1 if reverse else seq + 1

    def copy(self):
        return pltpu.make_async_remote_copy(
            src_ref=self.put, dst_ref=self.got, send_sem=self.send, recv_sem=self.recv,
            device_id={"seq": self.to}, device_id_type=MESH,
        )

    def step(self, k):
        @pl.when(self.rank == k)
        def _():
            if k == 0:
                self.inc[...] = jnp.zeros_like(self.inc)
                self.put[...] = self.leave[...].astype(BF16)
            else:
                self.copy().wait_recv()
                got = self.got[...].astype(F32)
                self.inc[...] = got
                if k < self.n - 1:
                    self.put[...] = (got * self.decay[0:1] + self.leave[...]).astype(BF16)
            if k < self.n - 1:
                self.copy().start()

    def done(self):
        @pl.when(self.rank < self.n - 1)
        def _():
            self.copy().wait_send()


def chain_scratch():
    return [
        pltpu.VMEM((NSTATE, DI), BF16), pltpu.VMEM((NSTATE, DI), BF16), pltpu.SemaphoreType.DMA(()),
        pltpu.SemaphoreType.DMA(()),
    ]


def expand_row(row, dst):
    lo = iota((8, BLOCK), 1) < HEADDIM
    wide = jnp.broadcast_to(row, (8, BLOCK))
    for j in range(PAIRS):
        dst[:, pair(j)] = expand_pair(wide, j, lo)[0]


CHUNKS = ((0, 512), (512, 512), (1024, 512), (1536, 384))
ORDERS = ("xy", "yx", "xy", "yx")


def gate_kernel(normed_ref, wg_ref, cot_ref, wo_ref, gain_ref, leave_ref, tot_ref, gate_ref, ng_ref, inc_ref, decay, *bufs):
    i = pl.program_id(0)
    chain = Chain(leave_ref, inc_ref, decay, bufs, False)
    last = pl.num_programs(0) - 1

    @pl.when(i == 0)
    def _():
        expand_row(jnp.exp2(tot_ref[0:1]), decay)
        greet_neighbours()
        chain.step(0)

    for c in range(DI // 256):
        cs = slice(c * 256, (c + 1) * 256)
        gate_ref[:, cs] = dot(normed_ref[...], wg_ref[:, cs]).astype(BF16)
        ng_ref[:, cs] = (dot_nt(cot_ref[...], wo_ref[cs, :]) * gain_ref[1:2, cs]).astype(BF16)
    for k in range(1, chain.n):
        @pl.when(i == (0, 2, 3)[min(k, 3) - 1])
        def _():
            chain.step(k)

    @pl.when(i == last)
    def _():
        chain.done()


def gate_pass(normed, wg, cot, wo, gain, leave, tot, T=512):
    L = normed.shape[0]
    row = lambda w: pl.BlockSpec((T, w), lambda i: (i, 0))
    return pl.pallas_call(
        gate_kernel,
        grid=(L // T,),
        in_specs=[
            row(D), full((D, DI)), row(D), full((DI, D)), full((8, DI)), full((NSTATE, DI)), full((8, BLOCK)),
        ],
        out_specs=[row(DI), row(DI), full((NSTATE, DI))],
        out_shape=[sds((L, DI), BF16), sds((L, DI), BF16), sds((NSTATE, DI), F32)],
        scratch_shapes=[pltpu.VMEM((8, DI), F32)] + chain_scratch(),
        compiler_params=params(collective_id=2),
        name="gate_pass",
    )(normed, wg, cot, wo, gain, leave, tot)


def grads_kernel(nout_ref, cot_ref, xt_ref, ggrad_ref, back_ref, tot_ref, gout_ref, ggate_ref, inc_ref, decay, *bufs):
    i = pl.program_id(0)
    chain = Chain(back_ref, inc_ref, decay, bufs, True)
    last = pl.num_programs(0) - 1

    @pl.when(i == 0)
    def _():
        expand_row(jnp.exp2(tot_ref[0:1]), decay)
        greet_neighbours()
        chain.step(0)

    gout_ref[...] = dot_tn(nout_ref[...], cot_ref[...]).astype(BF16)
    ggate_ref[...] = dot(xt_ref[...], ggrad_ref[...]).astype(BF16)
    for k in range(1, chain.n):
        @pl.when(i == (0, 3, 5)[min(k, 3) - 1])
        def _():
            chain.step(k)

    @pl.when(i == last)
    def _():
        chain.done()


def grads_pass(nout, cot, xt, ggrad, back, tot):
    L = nout.shape[0]
    col = lambda w: pl.BlockSpec((L, w), lambda i: (0, i))
    return pl.pallas_call(
        grads_kernel,
        grid=(6,),
        in_specs=[
            col(256), once((L, D)), once((D, L)), col(256), full((NSTATE, DI)),
            full((8, BLOCK)),
        ],
        out_specs=[
            pl.BlockSpec((256, D), lambda i: (i, 0)), pl.BlockSpec((D, 256), lambda i: (0, i)), full((NSTATE, DI)),
        ],
        out_shape=[sds((DI, D), BF16), sds((D, DI), BF16), sds((NSTATE, DI), F32)],
        scratch_shapes=[pltpu.VMEM((8, DI), F32)] + chain_scratch(),
        compiler_params=params(collective_id=3),
        name="grads_pass",
    )(nout, cot, xt, ggrad, back, tot)


def last_kernel(
    T, xt_any, pg_any, wg_any, wc_any, tail_ref, ggrad_ref, tok_ref, cot_ref, gain_ref, small_ref,
    tgrad_ref, gout_ref, sums_ref, xt, wg, wc, pg, g0, g1, g2, g3, lsem, smalls, ssend, srecv, *scratch,
):
    i = pl.program_id(0)
    nc = len(CHUNKS)
    grads = (g0, g1, g2, g3)
    sc = [Scatter(grads[k], ORDERS[k][::-1], scratch[NSC * k : NSC * k + NSC]) for k in range(nc)]
    dp, seq = lax.axis_index("dp"), lax.axis_index("seq")
    n_dp, n_seq = lax.axis_size("dp"), lax.axis_size("seq")
    total = n_dp * n_seq
    me = dp * n_seq + seq
    L = pg.shape[0]

    whole = ((xt_any, xt), (wg_any, wg), (wc_any, wc))

    def load(k):
        if k >= nc:
            return pltpu.make_async_copy(*whole[k - nc], lsem.at[k])
        lanes = pl.ds(CHUNKS[k][0], CHUNKS[k][1])
        return pltpu.make_async_copy(pg_any.at[:, lanes], pg.at[:, lanes], lsem.at[k])

    def far(o):
        r = lax.rem(me + o, total)
        return {"dp": r // n_seq, "seq": lax.rem(r, n_seq)}

    def small(o):
        r = lax.rem(me + o, total)
        return pltpu.make_async_remote_copy(
            src_ref=small_ref.at[r], dst_ref=smalls.at[o - 1], send_sem=ssend.at[o - 1], recv_sem=srecv.at[o - 1],
            device_id=far(o), device_id_type=MESH,
        )

    @pl.when(i == 0)
    def _():
        load(nc).start()
        load(0).start()
        sem = pltpu.get_barrier_semaphore()
        for o in range(1, total):
            pl.semaphore_signal(sem, inc=1, device_id=far(o), device_id_type=MESH)

    for k in range(nc):
        @pl.when(i == k)
        def _():
            lane, width = CHUNKS[k]
            if k == 0:
                load(nc).wait()
            load(k).wait()
            if k + 1 < nc:
                load(k + 1).start()
            if k >= nc - 2:
                load(nc + 1 + k - (nc - 2)).start()
            skip = BLOCK if k == 0 else 0
            pg[L - 16 :, lane + skip : lane + width] = tail_ref[:, lane + skip : lane + width]
            rows = grads[k].shape[4]
            for q in range(2):
                half = D // 2
                g = dot(xt[q * half : (q + 1) * half], pg[:, lane : lane + width])
                for r in range(half // rows):
                    s = r + q * (half // rows)
                    grads[k][s // 8, (s // 4) % 2, (s // 2) % 2, s % 2] = g[r * rows : (r + 1) * rows].astype(BF16)
            if k == 0:
                pl.semaphore_wait(pltpu.get_barrier_semaphore(), total - 1)
                sc[0].start(0)
                for o in range(1, total):
                    small(o).start()
            else:
                sc[k - 1].finish(0)
                sc[k - 1].start(1)
                sc[k].start(0)

    @pl.when(i >= nc)
    def _():
        r0 = pl.multiple_of((i - nc) * T, T)

        @pl.when(i == nc)
        def _():
            load(nc + 1).wait()
            load(nc + 2).wait()

        u = dot_nt(ggrad_ref[...], wg[...]) + dot_nt(pg[pl.ds(r0, T), :], wc[...])
        u = u * gain_ref[0:1]
        x = tok_ref[...].astype(F32)
        inv = lax.rsqrt(jnp.mean(x * x, axis=-1, keepdims=True) + EPS)
        xi = x * inv
        coef = inv * jnp.mean(u * xi, axis=-1, keepdims=True)
        tgrad_ref[...] = (cot_ref[...].astype(F32) + inv * u - xi * coef).astype(BF16)

    def after(step, what):
        @pl.when(i == step)
        def _():
            for k, stage in what:
                sc[k].finish(stage)
                sc[k].start(stage + 1)

    after(nc, [(3, 0)])
    after(nc + 1, [(0, 1)])
    after(nc + 2, [(1, 1)])
    after(nc + 3, [(2, 1), (0, 2)])
    after(nc + 4, [(3, 1), (1, 2)])
    after(nc + 5, [(2, 2), (3, 2)])

    @pl.when(i == pl.num_programs(0) - 1)
    def _():
        for o in range(1, total):
            small(o).wait()
        acc = small_ref[me]
        for o in range(1, total):
            acc = acc + smalls[o - 1]
        sums_ref[...] = acc
        for k in range(nc):
            lane, width = CHUNKS[k]
            gout_ref[:, lane : lane + width] = sc[k].result()


def last_pass(xt, pg, tail, ggrad, tok, cot, wg, wc, gain, small):
    L = tok.shape[0]
    T = L // 8
    n = sizes()
    nc = len(CHUNKS)
    total = lax.axis_size("dp") * lax.axis_size("seq")
    rows = D // total
    row = lambda w: pl.BlockSpec((T, w), lambda i: (jnp.maximum(i - nc, 0), 0))
    scratch = []
    for _, w in CHUNKS:
        scratch += scatter_scratch(rows, w)
    return pl.pallas_call(
        functools.partial(last_kernel, T),
        grid=(nc + L // T,),
        in_specs=[
            ANY, ANY, ANY, ANY, once((16, WC)), row(DI), row(D), row(D), once((8, D)), once((total, 8, BLOCK)),
        ],
        out_specs=[row(D), full((rows, WC)), full((8, BLOCK))],
        out_shape=[sds((L, D), BF16), sds((rows, WC), F32), sds((8, BLOCK), F32)],
        scratch_shapes=[
            pltpu.VMEM((D, L), BF16), pltpu.VMEM((D, DI), BF16), pltpu.VMEM((D, WC), BF16), pltpu.VMEM((L, WC), BF16),
        ]
        + [pltpu.VMEM((n["z"], 2, n["y"], 2, rows, w), BF16) for _, w in CHUNKS]
        + [
            pltpu.SemaphoreType.DMA((nc + 3,)), pltpu.VMEM((total - 1, 8, BLOCK), F32),
            pltpu.SemaphoreType.DMA((total - 1,)), pltpu.SemaphoreType.DMA((total - 1,)),
        ] + scratch,
        compiler_params=params(collective_id=5),
        name="last_pass",
    )(xt, pg, wg, wc, tail, ggrad, tok, cot, gain, small)


def finish_kernel(
    gate_ref, conv_ref, out_ref, sums_ref, w_ref, wo_ref, own_ref, tgrad_ref,
    in_grad, ngain, ggain, taps, bias, step, decay, skip, out_grad, tgrad_out,
):
    tgrad_out[...] = tgrad_ref[...]

    @pl.when(pl.program_id(0) == 0)
    def _():
        finish_small(
            gate_ref, conv_ref, out_ref, sums_ref, w_ref, wo_ref, own_ref, in_grad, ngain, ggain, taps, bias,
            step, decay, skip, out_grad,
        )


def finish_small(
    gate_ref, conv_ref, out_ref, sums_ref, w_ref, wo_ref, own_ref,
    in_grad, ngain, ggain, taps, bias, step, decay, skip, out_grad,
):
    conv = conv_ref[...]
    raw = jnp.concatenate([gate_ref[...], conv[:, BLOCK:], conv[:, :HEADS]], axis=1)
    in_grad[...] = raw
    ngain[...] = jnp.sum(raw * w_ref[...].astype(F32), axis=1) / own_ref[0, 5, : ngain.shape[0]]
    o = out_ref[...]
    out_grad[...] = o
    ggain[...] = jnp.sum(o * wo_ref[...].astype(F32), axis=1) / own_ref[0, 6, : ggain.shape[0]]
    s = sums_ref[...]
    n = bias.shape[0]
    taps[...] = s[:CONV, :n]
    bias[...] = s[4, :n]
    step[...] = s[7, :HEADS]
    decay[...] = s[7, HEADS : 2 * HEADS]
    skip[...] = s[7, 2 * HEADS : 3 * HEADS]


def finish_pass(gate_cols, conv_cols, out_raw, sums, w, wo, own, tgrad, channels):
    vec = lambda n: sds((n,), F32)
    rows = pl.BlockSpec((512, D), lambda i: (i, 0))
    small = [
        sds(w.shape, F32), vec(w.shape[0]), vec(wo.shape[0]), sds((CONV, channels), F32),
        vec(channels), vec(HEADS), vec(HEADS), vec(HEADS), sds(out_raw.shape, F32),
    ]
    ins = (gate_cols, conv_cols, out_raw, sums, w, wo, own)
    return pl.pallas_call(
        finish_kernel,
        grid=(tgrad.shape[0] // 512,),
        in_specs=[once(x.shape) for x in ins] + [rows],
        out_specs=[once(x.shape) for x in small] + [rows],
        out_shape=small + [sds(tgrad.shape, BF16)],
        name="finish_pass",
    )(*ins, tgrad)


def rms_rows(tok, gain):
    x = tok.astype(F32)
    return (x * lax.rsqrt(jnp.mean(x * x, axis=-1, keepdims=True) + EPS) * gain).astype(BF16)


def first_kernel(
    T, win_ref, small, tok_any, so_ref,
    xhat_any, xt_any, wc_any, p_any, hp_ref, conv_ref, gain_ref, row_ref,
    act_ref, slope_ref, dt_ref, cum_ref, sig_ref, bst_ref, leave_ref, tot_ref, bg_ref, bo_ref,
    slab, tok, halo, xhat, xt, wc, wide, p, smalls, b0, b1, b2, b3, ext, state, weighted, lsem, hsend, hrecv, ssend, srecv,
    *sems,
):
    i = pl.program_id(0)
    steps = pl.num_programs(0)
    at = place()
    seq, n = lax.axis_index("seq"), lax.axis_size("seq")
    L = tok.shape[0]
    bufs = (b0, b1, b2, b3)
    nc = len(CHUNKS)
    gets = []
    for (lane, width), order, buf, k in zip(CHUNKS, ORDERS, bufs, range(nc)):
        gets.append(Gather(slab.at[:, pl.ds(lane, width)], spots(buf), order, sems[2 * k : 2 * k + 2]))
    for k in range(4):
        buf = (bg_ref, bo_ref)[k % 2]
        width = buf.shape[5] // 2
        lanes = pl.ds((k // 2) * width, width)
        q = 2 * (nc + k)
        src = win_ref if k % 2 == 0 else so_ref
        gets.append(Gather(src.at[:, lanes], spots(buf, lanes), ORDERS[k], sems[q : q + 2]))
    own = []
    for k, (src, buf) in enumerate(((win_ref.at[:, pl.ds(0, DI)], bg_ref), (so_ref, bo_ref))):
        own.append(pltpu.make_async_copy(src, buf.at[at["z"], at["x"], at["y"], at["c"]], lsem.at[k]))
    halo_copy = pltpu.make_async_remote_copy(
        src_ref=tok_any.at[pl.ds(L - 16, 16)], dst_ref=halo, send_sem=hsend, recv_sem=hrecv,
        device_id={"seq": seq + 1}, device_id_type=MESH,
    )
    outs = [pltpu.make_async_copy(xhat, xhat_any, lsem.at[3]), pltpu.make_async_copy(xt, xt_any, lsem.at[4])]
    for k, (lane, width) in enumerate(CHUNKS):
        for j, (src, dst) in enumerate(((p, p_any), (wc, wc_any))):
            lanes = pl.ds(lane, width)
            outs.append(pltpu.make_async_copy(src.at[:, lanes], dst.at[:, lanes], lsem.at[5 + 2 * k + j]))

    def advance(*what):
        for k, stage in what:
            if stage > 0:
                gets[k].wait(stage - 1)
            if stage < 4:
                gets[k].start(stage)

    def project(k):
        lane, width = CHUNKS[k]
        buf = bufs[k]
        nz, rows_k = buf.shape[0], buf.shape[4]
        for z in range(nz):
            for m in range(8):
                r = z * 8 + m
                wide[r * rows_k : (r + 1) * rows_k, :width] = buf[z, m // 4, (m // 2) % 2, m % 2].astype(F32)
        wc[:, lane : lane + width] = wide[:, :width].astype(BF16)
        for r in range(L // 512):
            rows = slice(r * 512, (r + 1) * 512)
            p[rows, lane : lane + width] = dot(xhat[rows], wc[:, lane : lane + width]).astype(BF16)
        hp_ref[:, lane : lane + width] = dot(halo[...], wc[:, lane : lane + width]).astype(BF16)
        for c in outs[2 + 2 * k : 4 + 2 * k]:
            c.start()

    @pl.when(i == 0)
    def _():
        dp = lax.axis_index("dp")
        n_dp = lax.axis_size("dp")
        total = n_dp * n
        me = dp * n + seq
        load = pltpu.make_async_copy(tok_any, tok, lsem.at[2])
        load.start()
        sem = pltpu.get_barrier_semaphore()
        k_rows = slab.shape[0]
        steps_w = win_ref[:, DI + CH :]
        slab[:, :BLOCK] = jnp.concatenate([steps_w, jnp.zeros((k_rows, BLOCK - HEADS), BF16)], axis=1)
        slab[:, BLOCK:] = win_ref[:, DI : DI + CH]

        def far(o):
            r = lax.rem(me + o, total)
            return {"dp": r // n, "seq": lax.rem(r, n)}

        for o in range(1, total):
            pl.semaphore_signal(sem, inc=1, device_id=far(o), device_id_type=MESH)
        pl.semaphore_wait(sem, total - 1)
        advance((0, 0), (1, 0))

        @pl.when(seq < n - 1)
        def _():
            halo_copy.start()

        sends = []
        for o in range(1, total):
            c = pltpu.make_async_remote_copy(
                src_ref=small.at[0], dst_ref=smalls.at[me], send_sem=ssend.at[o - 1], recv_sem=srecv.at[o - 1],
                device_id=far(o), device_id_type=MESH,
            )
            c.start()
            sends.append(c)
        for c in own:
            c.start()
        smalls[me] = small[0]
        expand_row(small[1, 2:3], row_ref)
        for (lane, width), buf in zip(CHUNKS, bufs):
            buf[at["z"], at["x"], at["y"], at["c"]] = slab[:, lane : lane + width]
        conv_ref[...] = jnp.zeros_like(conv_ref)
        state[...] = jnp.zeros_like(state)
        tot_ref[...] = jnp.zeros_like(tot_ref)
        advance((0, 1), (2, 0), (1, 1), (3, 0))
        load.wait()
        for c in sends:
            c.wait()
        taps, ks, gs = CH // total, D // total, DI // total
        for r in range(total):
            conv_ref[0:5, r * taps : (r + 1) * taps] = smalls[r, 0:5, :taps]
            gain_ref[:, r * ks : (r + 1) * ks] = jnp.broadcast_to(smalls[r, 5:6, :ks], (8, ks))
            row_ref[1:2, r * gs : (r + 1) * gs] = smalls[r, 6:7, :gs]

        def norm(r, _):
            rows = pl.ds(pl.multiple_of(r * 256, 256), 256)
            h = rms_rows(tok[rows], gain_ref[0:1])
            xhat[rows] = h
            xt[:, rows] = h.T
            return _

        lax.fori_loop(0, L // 512, norm, 0)
        advance((0, 2), (1, 2), (2, 1), (4, 0), (3, 1), (5, 0), (6, 0), (7, 0))
        lax.fori_loop(L // 512, L // 256, norm, 0)
        for c in outs[:2]:
            c.start()

        @pl.when(seq == 0)
        def _():
            halo[...] = jnp.zeros_like(halo)

        @pl.when(seq > 0)
        def _():
            halo_copy.wait_recv()

        @pl.when(seq < n - 1)
        def _():
            halo_copy.wait_send()

        halo[...] = rms_rows(halo[...], gain_ref[0:1])
        for c in own:
            c.wait()
        advance((0, 3), (1, 3), (2, 2), (3, 2), (0, 4))
        project(0)
        advance((1, 4), (4, 1), (5, 1))
        project(1)
        advance((2, 3), (3, 3), (4, 2), (5, 2), (6, 1), (7, 1), (2, 4))
        project(2)
        advance((3, 4))
        project(3)
        for c in range(CH // 128):
            ext[c, 0:8] = hp_ref[:, BLOCK + c * 128 : BLOCK + (c + 1) * 128].astype(F32)[8:16]

    def tile(r0):
        for c in range(CH // 128):
            cs = slice(c * 128, (c + 1) * 128)
            ext[c, 8 : 8 + T] = p[pl.ds(r0, T), BLOCK + c * 128 : BLOCK + (c + 1) * 128].astype(F32)
            for r in range(0, T, 64):
                total = conv_ref[4:5, cs]
                for k in range(CONV):
                    total = total + ext[c, 5 + k + r : 5 + k + r + 64] * conv_ref[k : k + 1, cs]
                sg = sigmoid(total)
                v = total * sg
                act_ref[r : r + 64, cs] = v.astype(BF16)
                slope_ref[r : r + 64, cs] = (sg + v * (1.0 - sg)).astype(BF16)
        raw = p[pl.ds(r0, T), :BLOCK].astype(F32) + small[1, 0:1]
        dt_all = jnp.maximum(raw, 0.0) + jnp.log1p(jnp.exp(-jnp.abs(raw)))
        dt_ref[...] = dt_all
        sig_ref[...] = sigmoid_exact(raw)
        tril = (iota((BLOCK, BLOCK), 0) >= iota((BLOCK, BLOCK), 1)).astype(F32)
        lo = lane_lo()
        for blk in range(T // BLOCK):
            rows = slice(blk * BLOCK, (blk + 1) * BLOCK)
            dt = dt_all[rows]
            cum = dot_exact(tril, dt * -jnp.exp(small[1, 1:2])) * LOG2E
            cum_ref[rows] = cum
            end = cum[BLOCK - 1 : BLOCK]
            tot_ref[...] += jnp.broadcast_to(end, tot_ref.shape)
            wfac = jnp.exp2(end - cum) * dt
            decay = jnp.broadcast_to(jnp.exp2(end), (8, BLOCK))
            write_t = act_ref[rows, DI : DI + NSTATE].T
            for j in range(PAIRS):
                w, _, _ = expand_pair(wfac, j, lo)
                weighted[:, pair(j)] = (act_ref[rows, pair(j)].astype(F32) * w).astype(BF16)
            for q in range(PAIRS // 2):
                cs = slice(q * 256, (q + 1) * 256)
                new = dot(write_t, weighted[:, cs])
                bst_ref[blk, :, cs] = new.astype(BF16)
                d0, _, _ = expand_pair(decay, 2 * q, lo[:8])
                d1, _, _ = expand_pair(decay, 2 * q + 1, lo[:8])
                dd = jnp.concatenate([d0, d1], axis=1)[0:1]
                state[:, cs] = state[:, cs] * dd + new

    def after(step, *what):
        @pl.when(i == step)
        def _():
            advance(*what)

    after(4, (6, 2), (7, 2), (4, 3), (5, 3))
    after(7, (6, 3), (7, 3))

    @pl.when(i > 1)
    def _():
        ext[:, 0:8] = ext[:, T : T + 8]

    @pl.when(i > 0)
    def _():
        tile(pl.multiple_of((i - 1) * T, T))

    @pl.when(i == steps - 1)
    def _():
        leave_ref[...] = state[...]
        advance((4, 4), (5, 4), (6, 4), (7, 4))
        for c in outs:
            c.wait()


def sigmoid_exact(v):
    return 1.0 / (1.0 + jnp.exp(-v))


def second_kernel(
    T, gate_s, ng, act_ref, dt_ref, cum_ref, bst_ref, inc_ref, tok_ref, wo_ref, row_ref, et_ref,
    mixed_ref, nout_ref, ggrad_ref, mlow_ref, dcum_ref, ent_ref, egrad_ref, rg_ref, leave_ref, back_ref, cols_ref,
    ms, growth, rlow, prod, plow, state, exg, lows,
):
    i = pl.program_id(0)

    @pl.when(i == 0)
    def _():
        state[...] = inc_ref[...]
        exg[...] = jnp.ones_like(exg)
        back_ref[...] = jnp.zeros_like(back_ref)
        cols_ref[...] = jnp.zeros_like(cols_ref)

    lo = lane_lo()
    lower = iota((BLOCK, BLOCK), 0) >= iota((BLOCK, BLOCK), 1)
    nblk = T // BLOCK
    for blk in range(nblk):
        rows = slice(blk * BLOCK, (blk + 1) * BLOCK)
        cum = cum_ref[rows]
        cum_t = cum.T
        dt = dt_ref[rows]
        write = act_ref[rows, DI : DI + NSTATE]
        read = act_ref[rows, DI + NSTATE :]
        inner = jnp.where(lower, dot_nt(read, write), 0.0)
        lows[blk] = state[...].astype(BF16)
        ent_ref[blk] = lows[blk]
        for j in range(PAIRS):
            cols, a, b = expand_pair(cum, j, lo)
            ga = jnp.exp2(jnp.minimum(a - cum_t[2 * j : 2 * j + 1], 0.0)) * inner
            gb = jnp.exp2(jnp.minimum(b - cum_t[2 * j + 1 : 2 * j + 2], 0.0)) * inner
            scores = jnp.concatenate([ga.astype(BF16), gb.astype(BF16)], axis=1)
            vals = act_ref[rows, pair(j)].astype(F32)
            dtp, _, _ = expand_pair(dt, j, lo)
            vdt = (vals * dtp).astype(BF16)
            grow = jnp.exp2(cols)
            growth[rows, pair(j)] = grow
            diag = dot(scores, block_diag(vdt))
            if j % 2 == 0:
                outs = dot(read, lows[blk, :, j * BLOCK : (j + 2) * BLOCK])
            out = outs[:, (j % 2) * BLOCK : (j % 2 + 1) * BLOCK]
            ms[rows, pair(j)] = diag + grow * out + row_ref[0:1, pair(j)] * vals
            dec = grow[BLOCK - 1 : BLOCK]
            state[:, pair(j)] = state[:, pair(j)] * dec + bst_ref[blk, :, pair(j)].astype(F32)

    sq = jnp.zeros((T, BLOCK), F32)
    ug = jnp.zeros((T, BLOCK), F32)
    for j in range(PAIRS):
        g = gate_s[:, pair(j)].astype(F32)
        gated = ms[:, pair(j)] * (g * sigmoid(g))
        sq = sq + gated * gated
        ug = ug + gated * ng[:, pair(j)].astype(F32)
    inv = lax.rsqrt(jnp.sum(sq, axis=-1, keepdims=True) * (1.0 / DI) + EPS)
    coef = jnp.sum(ug, axis=-1, keepdims=True) * (1.0 / DI) * (inv * inv * inv)
    for j in range(PAIRS):
        g = gate_s[:, pair(j)].astype(F32)
        sg = sigmoid(g)
        silu = g * sg
        m = ms[:, pair(j)]
        gated = m * silu
        nout_ref[:, pair(j)] = (gated * inv * row_ref[1:2, pair(j)]).astype(BF16)
        dg = inv * ng[:, pair(j)].astype(F32) - gated * coef
        low = (dg * silu).astype(BF16)
        mlow_ref[:, pair(j)] = low
        ggrad_ref[:, pair(j)] = (dg * m * (sg + silu * (1.0 - sg))).astype(BF16)
        vals = act_ref[:, pair(j)].astype(F32)
        lowf = low.astype(F32)
        mv = lowf * vals
        pr = lowf * m - row_ref[0:1, pair(j)] * mv
        hi = pr.astype(BF16)
        prod[:, pair(j)] = hi
        plow[:, pair(j)] = (pr - hi.astype(F32)).astype(BF16)
        rlow[:, pair(j)] = (lowf * growth[:, pair(j)]).astype(BF16)
        cols_ref[:, pair(j)] += jnp.sum(mv.reshape(T // 8, 8, BLOCK), axis=0)
    dcum_ref[...] = dot(prod[...], et_ref[...]) + dot(plow[...], et_ref[...])
    mixed_ref[...] = (tok_ref[...].astype(F32) + dot(nout_ref[...], wo_ref[...])).astype(BF16)
    for blk in range(nblk):
        rows = slice(blk * BLOCK, (blk + 1) * BLOCK)
        read_t = act_ref[rows, DI + NSTATE :].T
        for q in range(PAIRS // 2):
            cs = slice(q * 256, (q + 1) * 256)
            eg = dot(read_t, rlow[rows, cs])
            egrad_ref[blk, :, cs] = eg.astype(BF16)
            back_ref[:, cs] += eg * exg[0:1, cs]
        exg[...] = exg[...] * growth[blk * BLOCK + BLOCK - 1 : blk * BLOCK + BLOCK, :]
        rg_ref[rows] = dot_nt(rlow[rows, :], lows[blk])

    @pl.when(i == pl.num_programs(0) - 1)
    def _():
        leave_ref[...] = state[...].astype(BF16)


def third_kernel(
    T, act_ref, convin_ref, slope_ref, dt_ref, cum_ref, sig_ref, dcum_ref, mlow_ref, ent_ref, leave_ref,
    egrad_ref, rg_ref, inc_ref, row_ref, conv_ref, head_ref, et_ref, cols_ref, go_ref, gg_ref,
    pg_ref, small_ref, tail_ref, so_ref, sg_ref,
    cgrad_ref, hgrad_ref, sums8, glast, xlast, gafter, hsend, hrecv, carry, dact, vprod, prod, plow, weighted, lows, dec, nxt, gext, *scratch,
):
    i = pl.program_id(0)
    steps = pl.num_programs(0)
    sca = Scatter(go_ref, "yx", scratch[2 : 2 + NSC], *scratch[:2])
    scb = Scatter(gg_ref, "xy", scratch[4 + NSC :], *scratch[2 + NSC : 4 + NSC])
    seq, nseq = lax.axis_index("seq"), lax.axis_size("seq")
    after = pltpu.make_async_remote_copy(
        src_ref=gext.at[:, pl.ds(0, 8)], dst_ref=gafter, send_sem=hsend, recv_sem=hrecv, device_id={"seq": seq - 1},
        device_id_type=MESH,
    )

    @pl.when(i == 0)
    def _():
        greet(place(), "zxyc", 1)
        sca.start(0)
        scb.start(0)

    for stage, when in enumerate((1, 4, 6)):
        @pl.when(i == when)
        def _():
            sca.finish(stage)
            sca.start(stage + 1)
            scb.finish(stage)
            scb.start(stage + 1)


    @pl.when(i == 0)
    def _():
        carry[...] = inc_ref[...]
        nxt[...] = leave_ref[...]
        cgrad_ref[...] = jnp.zeros_like(cgrad_ref)
        hgrad_ref[...] = jnp.zeros_like(hgrad_ref)

    lo = lane_lo()
    upper = iota((BLOCK, BLOCK), 0) <= iota((BLOCK, BLOCK), 1)
    triu = upper.astype(F32)
    last = iota((BLOCK, BLOCK), 0) == BLOCK - 1
    for blk in reversed(range(T // BLOCK)):
        rows = slice(blk * BLOCK, (blk + 1) * BLOCK)
        cum = cum_ref[rows]
        cum_t = cum.T
        dt = dt_ref[rows]
        end = cum[BLOCK - 1 : BLOCK]
        write = act_ref[rows, DI : DI + NSTATE]
        read = act_ref[rows, DI + NSTATE :]
        inner = jnp.where(upper, dot_nt(write, read), 0.0)
        lows[...] = carry[...].astype(BF16)
        acc = jnp.zeros((BLOCK, BLOCK), F32)
        for j in range(PAIRS):
            cols, a, b = expand_pair(cum, j, lo)
            ends = jnp.where(lo[:1], end[:, 2 * j : 2 * j + 1], end[:, 2 * j + 1 : 2 * j + 2])
            wexp = jnp.exp2(ends - cols)
            da = jnp.exp2(jnp.minimum(cum_t[2 * j : 2 * j + 1] - a, 0.0))
            db = jnp.exp2(jnp.minimum(cum_t[2 * j + 1 : 2 * j + 2] - b, 0.0))
            scores = jnp.concatenate([(da * inner).astype(BF16), (db * inner).astype(BF16)], axis=1)
            m = mlow_ref[rows, pair(j)]
            diag = block_diag(m)
            z = dot(scores, diag)
            vals = act_ref[rows, pair(j)].astype(F32)
            dtp, _, _ = expand_pair(dt, j, lo)
            vdt = vals * dtp
            vdtb = vdt.astype(BF16)
            wtb = (vdt * wexp).astype(BF16)
            g = dot_nt(vdtb, diag)
            acc = acc + g[:, :BLOCK] * da + g[:, BLOCK:] * db
            if j % 2 == 0:
                wgs = dot(write, lows[:, j * BLOCK : (j + 2) * BLOCK])
            wg = wgs[:, (j % 2) * BLOCK : (j % 2 + 1) * BLOCK]
            pr = vdtb.astype(F32) * z + wtb.astype(F32) * wg
            z = z + wg * wexp
            dact[rows, pair(j)] = row_ref[0:1, pair(j)] * m.astype(F32) + dtp * z
            vprod[:, pair(j)] = (vals * z).astype(BF16)
            hi = pr.astype(BF16)
            prod[:, pair(j)] = hi
            plow[:, pair(j)] = (pr - hi.astype(F32)).astype(BF16)
            weighted[:, pair(j)] = wtb
            dec[0:1, pair(j)] = jnp.exp2(cols[BLOCK - 1 : BLOCK])
        low = jnp.where(upper, acc, 0.0).astype(BF16)
        dact[rows, DI : DI + NSTATE] = dot_nt(weighted[...], lows[...]) + dot(low, read)
        dact[rows, DI + NSTATE :] = rg_ref[rows] + dot(low.T, write)
        c = dot(vprod[...], et_ref[...])
        used = dot(prod[...], et_ref[...]) + dot(plow[...], et_ref[...])
        ends = jnp.sum((lows[...].astype(F32) * nxt[...].astype(F32)).reshape(16, 8, DI), axis=0)
        ends_hi = ends.astype(BF16)
        ends_lo = (ends - ends_hi.astype(F32)).astype(BF16)
        de = jnp.sum(dot(ends_hi, et_ref[...]) + dot(ends_lo, et_ref[...]), axis=0, keepdims=True)
        dc = dcum_ref[rows] - used + jnp.where(last, de, 0.0)
        da_log = dot_exact(triu, dc)
        decay = -jnp.exp(head_ref[1, 1:2])
        draw = (c + da_log * decay) * sig_ref[rows]
        pg_ref[rows, :BLOCK] = draw.astype(BF16)
        hgrad_ref[0:8] += jnp.sum(draw.reshape(16, 8, BLOCK), axis=0)
        hgrad_ref[8:16] += jnp.sum((da_log * dt).reshape(16, 8, BLOCK), axis=0) * decay
        nxt[...] = ent_ref[blk]
        for q in range(PAIRS // 2):
            cs = slice(q * 256, (q + 1) * 256)
            carry[:, cs] = carry[:, cs] * dec[0:1, cs] + egrad_ref[blk, :, cs].astype(F32)

    for c in range(CH // 128):
        cs = slice(c * 128, (c + 1) * 128)
        ps = slice(BLOCK + c * 128, BLOCK + (c + 1) * 128)

        @pl.when(i == 0)
        def _():
            gext[c, T : T + 8] = jnp.zeros((8, 128), F32)
            xlast[:, cs] = convin_ref[T - 16 :, ps].astype(F32)

        @pl.when(i > 0)
        def _():
            gext[c, T : T + 8] = gext[c, 0:8]

        for r in range(0, T, 64):
            gext[c, r : r + 64] = dact[r : r + 64, cs] * slope_ref[r : r + 64, cs].astype(F32)
        sums = [jnp.zeros((8, 128), F32)] * 5
        for r in range(0, T, 64):
            x = convin_ref[r : r + 64, ps].astype(F32)
            g = gext[c, r : r + 64]
            back = g * conv_ref[3:4, cs]
            sums[4] = sums[4] + jnp.sum(g.reshape(8, 8, 128), axis=0)
            sums[3] = sums[3] + jnp.sum((g * x).reshape(8, 8, 128), axis=0)
            for k in range(CONV - 1):
                gk = gext[c, 3 - k + r : 3 - k + r + 64]
                back = back + gk * conv_ref[k : k + 1, cs]
                sums[k] = sums[k] + jnp.sum((gk * x).reshape(8, 8, 128), axis=0)
            pg_ref[r : r + 64, ps] = back.astype(BF16)
            if r + 64 == T:
                @pl.when(i == 0)
                def _():
                    glast[:, cs] = back[48:]
        for k in range(5):
            cgrad_ref[8 * k : 8 * k + 8, cs] += sums[k]

    @pl.when(i == steps - 1)
    def _():
        @pl.when(seq > 0)
        def _():
            after.start()

        so_ref[...] = sca.result()
        sg_ref[...] = scb.result()

        @pl.when(seq == nseq - 1)
        def _():
            gafter[...] = jnp.zeros_like(gafter)

        @pl.when(seq < nseq - 1)
        def _():
            after.wait_recv()

        row16, row8 = iota((16, 128), 0), iota((8, 128), 0)
        for c in range(CH // 128):
            cs = slice(c * 128, (c + 1) * 128)
            ps = slice(BLOCK + c * 128, BLOCK + (c + 1) * 128)
            tail = glast[:, cs]
            for j in range(CONV - 1):
                for k in range(j + 1):
                    g = gafter[c, j - k : j - k + 1]
                    tail = tail + jnp.where(row16 == 13 + j, g * conv_ref[k : k + 1, cs], 0.0)
                    cgrad_ref[8 * k : 8 * k + 8, cs] += jnp.where(row8 == 0, g * xlast[13 + j : 14 + j, cs], 0.0)
            tail_ref[:, ps] = tail.astype(BF16)
        tail_ref[:, :BLOCK] = jnp.zeros((16, BLOCK), BF16)
        for k in range(5):
            sums8[k : k + 1] = jnp.sum(cgrad_ref[8 * k : 8 * k + 8], axis=0, keepdims=True)
        steps8 = jnp.broadcast_to(jnp.sum(hgrad_ref[0:8], axis=0, keepdims=True), (8, BLOCK))
        decay8 = jnp.broadcast_to(jnp.sum(hgrad_ref[8:16], axis=0, keepdims=True), (8, BLOCK))
        high = cols_ref[...].astype(BF16)
        low8 = (cols_ref[...] - high.astype(F32)).astype(BF16)
        skip8 = jnp.sum(dot(high, et_ref[...]) + dot(low8, et_ref[...]), axis=0, keepdims=True)
        skip8 = jnp.broadcast_to(skip8, (8, BLOCK))
        lane = iota((8, BLOCK), 1)
        heads = jnp.where(lane < HEADS, steps8, pltpu.roll(decay8, HEADS, 1))
        heads = jnp.where(lane < 2 * HEADS, heads, pltpu.roll(skip8, 2 * HEADS, 1))
        heads = jnp.where((iota((8, BLOCK), 0) == 7) & (lane < 3 * HEADS), heads, 0.0)
        take = CH // small_ref.shape[0]
        for r in range(small_ref.shape[0]):
            small_ref[r] = heads
            small_ref[r, 0:5, :take] = sums8[0:5, r * take : (r + 1) * take]

        @pl.when(seq > 0)
        def _():
            after.wait_send()


def once(shape):
    return pl.BlockSpec(shape, lambda i: (0,) * len(shape), pipeline_mode=pl.Buffered(1))


def full(shape):
    return pl.BlockSpec(shape, lambda i: (0,) * len(shape))


def params(collective_id=None):
    return pltpu.CompilerParams(
        dimension_semantics=("arbitrary",), vmem_limit_bytes=VMEM_LIMIT, collective_id=collective_id,
        has_side_effects=collective_id is not None,
    )


def head_columns():
    et = np.zeros((DI, BLOCK), np.float32)
    et[np.arange(DI), np.arange(DI) // HEADDIM] = 1.0
    return et


def sds(shape, dtype):
    return jax.ShapeDtypeStruct(shape, dtype)


def first_pass(w_in, small, tok, slab_o, T=256):
    L = tok.shape[0]
    nb, per = L // BLOCK, T // BLOCK
    n = sizes()
    k_rows = w_in.shape[0]
    total = lax.axis_size("dp") * lax.axis_size("seq")
    row = lambda w: pl.BlockSpec((T, w), lambda i: (jnp.maximum(i - 1, 0), 0))
    dims = (n["z"], n["x"], n["y"], n["c"])
    sems = []
    for _ in range(len(CHUNKS) + 4):
        sems += gather_sems()
    return pl.pallas_call(
        functools.partial(first_kernel, T),
        grid=(1 + L // T,),
        in_specs=[once(w_in.shape), once((2, 8, BLOCK)), ANY, ANY],
        out_specs=[
            ANY, ANY, ANY, ANY, full((16, WC)), full((8, CH)), full((8, D)), full((8, DI)),
            row(CH), row(CH), row(BLOCK), row(BLOCK), row(BLOCK),
            pl.BlockSpec((per, NSTATE, DI), lambda i: (jnp.maximum(i - 1, 0), 0, 0)), full((NSTATE, DI)),
            full((8, BLOCK)), ANY, ANY,
        ],
        out_shape=[
            sds((L, D), BF16), sds((D, L), BF16), sds((D, WC), BF16), sds((L, WC), BF16), sds((16, WC), BF16),
            sds((8, CH), F32), sds((8, D), F32), sds((8, DI), F32),
            sds((L, CH), BF16), sds((L, CH), BF16), sds((L, BLOCK), F32), sds((L, BLOCK), F32), sds((L, BLOCK), F32),
            sds((nb, NSTATE, DI), BF16), sds((NSTATE, DI), F32), sds((8, BLOCK), F32),
            sds(dims + (k_rows, DI), BF16), sds(dims + slab_o.shape, BF16),
        ],
        scratch_shapes=[
            pltpu.VMEM((k_rows, WC), BF16), pltpu.VMEM((L, D), BF16), pltpu.VMEM((16, D), BF16), pltpu.VMEM((L, D), BF16), pltpu.VMEM((D, L), BF16),
            pltpu.VMEM((D, WC), BF16), pltpu.VMEM((D, 512), F32), pltpu.VMEM((L, WC), BF16),
            pltpu.VMEM((total, 8, BLOCK), F32),
        ] + [pltpu.VMEM(dims + (k_rows, w), BF16) for _, w in CHUNKS] + [
            pltpu.VMEM((CH // 128, T + 8, 128), F32), pltpu.VMEM((NSTATE, DI), F32), pltpu.VMEM((BLOCK, DI), BF16),
            pltpu.SemaphoreType.DMA((5 + 2 * len(CHUNKS),)), pltpu.SemaphoreType.DMA(()), pltpu.SemaphoreType.DMA(()),
            pltpu.SemaphoreType.DMA((total - 1,)), pltpu.SemaphoreType.DMA((total - 1,)),
        ] + sems,
        compiler_params=params(collective_id=1),
        name="first_pass",
    )(w_in, small, tok, slab_o)


def second_pass(gate, ng, act, dt, cum, bst, inc, tok, wo, rows, et, T=256):
    L = tok.shape[0]
    nb, per = L // BLOCK, T // BLOCK
    row = lambda w: pl.BlockSpec((T, w), lambda i: (i, 0))
    blk = pl.BlockSpec((per, NSTATE, DI), lambda i: (i, 0, 0))
    return pl.pallas_call(
        functools.partial(second_kernel, T),
        grid=(L // T,),
        in_specs=[
            row(DI), row(DI), row(CH), row(BLOCK), row(BLOCK), blk, full((NSTATE, DI)), row(D), full((DI, D)), full((8, DI)), full((DI, BLOCK)),
        ],
        out_specs=[
            row(D), row(DI), row(DI), row(DI), row(BLOCK), blk, blk, row(BLOCK), full((NSTATE, DI)),
            full((NSTATE, DI)), full((8, DI)),
        ],
        out_shape=[
            sds((L, D), BF16), sds((L, DI), BF16), sds((L, DI), BF16), sds((L, DI), BF16), sds((L, BLOCK), F32),
            sds((nb, NSTATE, DI), BF16), sds((nb, NSTATE, DI), BF16), sds((L, BLOCK), F32), sds((NSTATE, DI), BF16),
            sds((NSTATE, DI), F32), sds((8, DI), F32),
        ],
        scratch_shapes=[
            pltpu.VMEM((T, DI), F32), pltpu.VMEM((T, DI), F32),
            pltpu.VMEM((T, DI), BF16), pltpu.VMEM((T, DI), BF16), pltpu.VMEM((T, DI), BF16), pltpu.VMEM((NSTATE, DI), F32),
            pltpu.VMEM((8, DI), F32), pltpu.VMEM((per, NSTATE, DI), BF16),
        ],
        compiler_params=params(),
        name="second_pass",
    )(gate, ng, act, dt, cum, bst, inc, tok, wo, rows, et)


def third_pass(
    act, convin, slope, dt, cum, sig, dcum, mlow, ent, leave, egrad, rg, inc, rows, conv, head, et, cols, go, gg, T=256
):
    L = act.shape[0]
    m = sizes()
    dims = (m["z"], m["x"], m["y"], m["c"])
    total = m["z"] * m["y"] * 4
    ro, rg_rows = DI // total, D // total
    go = go.reshape(dims + (ro, D))
    gg = gg.reshape(dims + (rg_rows, DI))
    n, per = L // T, T // BLOCK
    row = lambda w: pl.BlockSpec((T, w), lambda i: (n - 1 - i, 0))
    blk = pl.BlockSpec((per, NSTATE, DI), lambda i: (n - 1 - i, 0, 0))
    return pl.pallas_call(
        functools.partial(third_kernel, T),
        grid=(n,),
        in_specs=[
            row(CH), row(WC), row(CH), row(BLOCK), row(BLOCK), row(BLOCK), row(BLOCK), row(DI), blk,
            full((NSTATE, DI)), blk, row(BLOCK), full((NSTATE, DI)), full((8, DI)), full((8, CH)), full((2, 8, BLOCK)),
            full((DI, BLOCK)), full((8, DI)), ANY, ANY,
        ],
        out_specs=[
            row(WC), full((total, 8, BLOCK)), full((16, WC)), full((ro, D)), full((rg_rows, DI)),
        ],
        out_shape=[
            sds((L, WC), BF16), sds((total, 8, BLOCK), F32), sds((16, WC), BF16), sds((ro, D), F32),
            sds((rg_rows, DI), F32),
        ],
        scratch_shapes=[
            pltpu.VMEM((40, CH), F32), pltpu.VMEM((16, BLOCK), F32), pltpu.VMEM((8, CH), F32),
            pltpu.VMEM((16, CH), F32), pltpu.VMEM((16, CH), F32), pltpu.VMEM((CH // 128, 8, 128), F32),
            pltpu.SemaphoreType.DMA(()), pltpu.SemaphoreType.DMA(()),
            pltpu.VMEM((NSTATE, DI), F32), pltpu.VMEM((T, CH), F32), pltpu.VMEM((BLOCK, DI), BF16), pltpu.VMEM((BLOCK, DI), BF16), pltpu.VMEM((BLOCK, DI), BF16),
            pltpu.VMEM((BLOCK, DI), BF16), pltpu.VMEM((NSTATE, DI), BF16), pltpu.VMEM((8, DI), F32),
            pltpu.VMEM((NSTATE, DI), BF16), pltpu.VMEM((CH // 128, T + 8, 128), F32),
        ] + own_scratch(ro, D) + scatter_scratch(ro, D) + own_scratch(rg_rows, DI) + scatter_scratch(rg_rows, DI),
        compiler_params=params(collective_id=4),
        name="third_pass",
    )(act, convin, slope, dt, cum, sig, dcum, mlow, ent, leave, egrad, rg, inc, rows, conv, head, et, cols, go, gg)


def on_device(
    tokens, cotangent, norm_gain, in_weight, conv_weight, conv_bias, step_bias, decay_log, skip_gain, gate_gain,
    out_weight,
):
    tok, cot = tokens[0], cotangent[0]
    L = tok.shape[0]
    k_rows, c_rows = in_weight.shape[0], conv_weight.shape[0]
    total = D // k_rows
    lanes = lambda x: jnp.pad(x, ((0, 0),) * (x.ndim - 1) + ((0, BLOCK - x.shape[-1]),))

    def put(x, row):
        x = x.astype(F32)
        return jnp.pad(x, ((row, 16 - row - x.shape[0]), (0, BLOCK - x.shape[1])))

    own = put(conv_weight.T, 0) + put(conv_bias[None], 4) + put(norm_gain[None], 5) + put(gate_gain[None], 6)
    own = own + put(step_bias[None], 8) + put(decay_log[None], 9) + put(skip_gain[None], 10)
    own = own.reshape(2, 8, BLOCK)
    et = jnp.asarray(head_columns(), BF16)

    (xhat, xt, wc, p, hp, conv, gain, rows, act, slope, dt, cum, sig, bst, leave, tot, buf_g, buf_o) = first_pass(
        in_weight, own, tok, out_weight
    )
    wg, wo = buf_g.reshape(D, DI), buf_o.reshape(DI, D)
    gate, ng, inc = gate_pass(xhat, wg, cot, wo, rows, leave, tot)
    mixed, nout, ggrad, mlow, dcum, ent, egrad, rg, leave2, back, cols = second_pass(
        gate, ng, act, dt, cum, bst, inc, tok, wo, rows, et
    )
    g_out, g_gate, later = grads_pass(nout, cot, xt, ggrad, back, tot)
    pg, small, tail, out_raw, gate_cols = third_pass(
        act, p, slope, dt, cum, sig, dcum, mlow, ent, leave2, egrad, rg, later, rows, conv, own, et, cols, g_out,
        g_gate,
    )
    tgrad, conv_cols, sums = last_pass(xt, pg, tail, ggrad, tok, cot, wg, wc, gain, small)
    in_grad, ngain_grad, ggain_grad, taps, bias, step, decay, skip, out_grad, tgrad = finish_pass(
        gate_cols, conv_cols, out_raw, sums, in_weight, out_weight, own, tgrad, c_rows
    )
    return (
        mixed[None], tgrad[None], ngain_grad, in_grad, taps.T, bias, step, decay, skip, ggain_grad, out_grad,
    )


def solution(mesh):
    both = ("dp", "seq")
    vec, mat, tok, rep = P(both), P(both, None), P("dp", "seq", None), P()
    return jax.shard_map(
        on_device,
        mesh=mesh,
        in_specs=(tok, tok, vec, mat, mat, vec, rep, rep, rep, vec, mat),
        out_specs=(tok, tok, vec, mat, mat, vec, rep, rep, rep, vec, mat),
        check_vma=False,
    )
```

```python
import functools

import jax
import jax.numpy as jnp
import numpy as np
from jax import lax
from jax.experimental import pallas as pl
from jax.experimental.pallas import tpu as pltpu
from jax.sharding import PartitionSpec as P

D = 768
HEADS = 24
HEADDIM = 64
NSTATE = 128
CONV = 4
BLOCK = 128
DI = 1536
CH = 1792
PAIRS = HEADS // 2
EPS = 1e-05
LOG2E = 1.4426950408889634
F32 = jnp.float32
BF16 = jnp.bfloat16
NT = (((1,), (1,)), ((), ()))
VMEM_LIMIT = 60 * 1024 * 1024


def dot(a, b):
    return jnp.dot(a, b, preferred_element_type=F32)


def dot_nt(a, b):
    return lax.dot_general(a, b, NT, preferred_element_type=F32)


def dot_exact(a, b):
    return jnp.dot(a, b, preferred_element_type=F32, precision=lax.Precision.HIGHEST)


def sigmoid(v):
    return 0.5 * jnp.tanh(0.5 * v) + 0.5


def iota(shape, dim):
    return lax.broadcasted_iota(jnp.int32, shape, dim)


def lane_lo():
    return iota((BLOCK, BLOCK), 1) < HEADDIM


def expand_pair(x, j, lo):
    rows = x.shape[0]
    a = jnp.broadcast_to(x[:, 2 * j : 2 * j + 1], (rows, BLOCK))
    b = jnp.broadcast_to(x[:, 2 * j + 1 : 2 * j + 2], (rows, BLOCK))
    return jnp.where(lo, a, b), a, b


def block_diag(v):
    lo = iota(v.shape, 1) < HEADDIM
    zero = jnp.zeros_like(v)
    return jnp.concatenate([jnp.where(lo, v, zero), jnp.where(lo, zero, v)], axis=0)


def pair(j):
    return slice(j * BLOCK, (j + 1) * BLOCK)


MESH = pl.DeviceIdType.MESH
ANY = pl.BlockSpec(memory_space=pl.ANY)
WC = CH + BLOCK
TN = (((0,), (0,)), ((), ()))


def dot_tn(a, b):
    return lax.dot_general(a, b, TN, preferred_element_type=F32)


def sizes():
    return {"z": lax.axis_size("dp") // 2, "x": 2, "y": lax.axis_size("seq") // 2, "c": 2}


def place():
    dp, seq = lax.axis_index("dp"), lax.axis_index("seq")
    return {"z": dp // 2, "x": lax.rem(dp, 2), "y": seq // 2, "c": lax.rem(seq, 2)}


def device(at):
    return {"dp": at["z"] * 2 + at["x"], "seq": at["y"] * 2 + at["c"]}


def peers(at, axis):
    n = sizes()[axis]
    return [dict(at, **{axis: lax.rem(at[axis] + o, n)}) for o in range(1, n)]


def greet(at, axes, by=0):
    sem = pltpu.get_barrier_semaphore()
    count = 0
    for axis in axes:
        for peer in peers(at, axis):
            pl.semaphore_signal(sem, inc=1, device_id=device(peer), device_id_type=MESH)
            count += 1
    if not by:
        pl.semaphore_wait(sem, count)
        return
    seq, n = lax.axis_index("seq"), lax.axis_size("seq")

    @pl.when((seq + by >= 0) & (seq + by < n))
    def _():
        pl.semaphore_signal(sem, inc=1, device_id={"seq": seq + by}, device_id_type=MESH)

    heard = (seq - by >= 0) & (seq - by < n)

    @pl.when(heard)
    def _():
        pl.semaphore_wait(sem, count + 1)

    @pl.when(jnp.logical_not(heard))
    def _():
        pl.semaphore_wait(sem, count)


def greet_neighbours():
    seq, n = lax.axis_index("seq"), lax.axis_size("seq")
    sem = pltpu.get_barrier_semaphore()

    @pl.when(seq > 0)
    def _():
        pl.semaphore_signal(sem, inc=1, device_id={"seq": seq - 1}, device_id_type=MESH)

    @pl.when(seq < n - 1)
    def _():
        pl.semaphore_signal(sem, inc=1, device_id={"seq": seq + 1}, device_id_type=MESH)

    @pl.when((seq > 0) & (seq < n - 1))
    def _():
        pl.semaphore_wait(sem, 2)

    @pl.when((seq == 0) | (seq == n - 1))
    def _():
        pl.semaphore_wait(sem, 1)


def remote(src, dst, send, recv, peer):
    return pltpu.make_async_remote_copy(
        src_ref=src, dst_ref=dst, send_sem=send, recv_sem=recv, device_id=device(peer), device_id_type=MESH
    )


class Gather:
    def __init__(self, slab, spot, order, sems):
        self.slab, self.spot, self.order = slab, spot, order
        self.send, self.recv = sems
        self.at = place()

    def copies(self, stage):
        at, (a, b) = self.at, self.order
        n = sizes()
        out = []
        every = slice(None)
        nz = n["z"] - 1
        if stage == 0:
            for o, peer in enumerate(peers(at, "z")):
                out.append((self.slab, self.spot(at), o, peer))
        elif stage == 1:
            index = dict(at, z=every)
            out.append((self.spot(index), self.spot(index), nz, peers(at, a)[0]))
        elif stage == 2:
            index = dict(at, z=every)
            index[a] = every
            for o, peer in enumerate(peers(at, b)):
                out.append((self.spot(index), self.spot(index), nz + 1 + o, peer))
            out.append((self.spot(index), self.spot(index), nz + 1 + n[b] - 1, peers(at, "c")[0]))
        else:
            for o in range(1, n[b]):
                index = dict(at, z=every)
                index[a] = every
                index[b] = lax.rem(at[b] + o, n[b])
                out.append((self.spot(index), self.spot(index), nz + 1 + n[b] + o - 1, peers(at, "c")[0]))
        return [remote(s, d, self.send.at[k], self.recv.at[k], p) for s, d, k, p in out]

    def start(self, stage):
        for c in self.copies(stage):
            c.start()

    def wait(self, stage):
        for c in self.copies(stage):
            c.wait()


def spots(buf, lanes=slice(None)):
    return lambda index: buf.at[index["z"], index["x"], index["y"], index["c"], :, lanes]


def gather_sems():
    count = sizes()["z"] + 2 * sizes()["y"] + 4
    return [pltpu.SemaphoreType.DMA((count,)), pltpu.SemaphoreType.DMA((count,))]


class Scatter:
    def __init__(self, grads, order, scratch, own=None, local=None):
        self.grads, self.order, self.own_ref, self.local = grads, order, own, local
        self.rc, self.r1, self.r2, self.rz, self.send, self.recv = scratch
        self.at = place()
        self.own = self

    def spot(self, z, x, y):
        if self.own_ref is not None:
            return self.own_ref.at[z, x, y]
        return self.grads.at[z, x, y, self.at["c"]]

    def add(self, z, x, y, got):
        mine = self.spot(z, x, y)
        mine[...] = (mine[...].astype(F32) + got.astype(F32)).astype(BF16)

    def copies(self, stage):
        at, (a, b) = self.at, self.order
        every = slice(None)
        out = []

        def spot(index):
            return self.spot(index["z"], index["x"], index["y"])

        if stage == 0:
            out.append((self.grads.at[:, :, :, 1 - at["c"]], self.rc, 0, peers(at, "c")[0]))
        elif stage == 1:
            index = {"z": every, "x": every, "y": every}
            index[a] = 1 - at[a]
            out.append((spot(index), self.r1, 1, peers(at, a)[0]))
        elif stage == 2:
            index = {"z": every, a: at[a], b: 1 - at[b]}
            out.append((spot(index), self.r2, 2, peers(at, b)[0]))
        else:
            for o, peer in enumerate(peers(at, "z")):
                out.append((self.spot(peer["z"], at["x"], at["y"]), self.rz.at[o], 3 + o, peer))
        return [remote(s, d, self.send.at[k], self.recv.at[k], p) for s, d, k, p in out]

    def mine(self):
        return pltpu.make_async_copy(self.grads.at[:, :, :, self.at["c"]], self.own_ref, self.local)

    def start(self, stage):
        if stage == 0 and self.own_ref is not None:
            self.mine().start()
        for c in self.copies(stage):
            c.start()

    def finish(self, stage):
        at, (a, b) = self.at, self.order
        for c in self.copies(stage):
            c.wait()
        nz = sizes()["z"]
        if stage == 0:
            if self.own_ref is not None:
                self.mine().wait()

            def body(z, _):
                for x in range(2):
                    for y in range(2):
                        self.add(z, x, y, self.rc[z, x, y])
                return _

        elif stage == 1:

            def body(z, _):
                for k in range(2):
                    index = {a: at[a], b: k}
                    self.add(z, index["x"], index["y"], self.r1[z, k])
                return _

        else:

            def body(z, _):
                self.add(z, at["x"], at["y"], self.r2[z])
                return _

        lax.fori_loop(0, nz, body, 0)

    def result(self):
        for c in self.copies(3):
            c.wait()
        total = self.spot(self.at["z"], self.at["x"], self.at["y"])[...].astype(F32)
        for o in range(sizes()["z"] - 1):
            total = total + self.rz[o].astype(F32)
        return total


def scatter_scratch(rows, width):
    nz = sizes()["z"]
    return [
        pltpu.VMEM((nz, 2, 2, rows, width), BF16), pltpu.VMEM((nz, 2, rows, width), BF16),
        pltpu.VMEM((nz, rows, width), BF16), pltpu.VMEM((nz - 1, rows, width), BF16),
        pltpu.SemaphoreType.DMA((nz + 2,)), pltpu.SemaphoreType.DMA((nz + 2,)),
    ]


NSC = 6


def own_scratch(rows, width):
    return [pltpu.VMEM((sizes()["z"], 2, 2, rows, width), BF16), pltpu.SemaphoreType.DMA(())]


class Chain:
    def __init__(self, leave, inc, decay, bufs, reverse):
        self.leave, self.inc, self.decay, self.reverse = leave, inc, decay, reverse
        self.got, self.put, self.send, self.recv = bufs
        self.n = lax.axis_size("seq")
        seq = lax.axis_index("seq")
        self.rank = self.n - 1 - seq if reverse else seq
        self.to = seq - 1 if reverse else seq + 1

    def copy(self):
        return pltpu.make_async_remote_copy(
            src_ref=self.put, dst_ref=self.got, send_sem=self.send, recv_sem=self.recv,
            device_id={"seq": self.to}, device_id_type=MESH,
        )

    def step(self, k):
        @pl.when(self.rank == k)
        def _():
            if k == 0:
                self.inc[...] = jnp.zeros_like(self.inc)
                self.put[...] = self.leave[...].astype(BF16)
            else:
                self.copy().wait_recv()
                got = self.got[...].astype(F32)
                self.inc[...] = got
                if k < self.n - 1:
                    self.put[...] = (got * self.decay[0:1] + self.leave[...]).astype(BF16)
            if k < self.n - 1:
                self.copy().start()

    def done(self):
        @pl.when(self.rank < self.n - 1)
        def _():
            self.copy().wait_send()


def chain_scratch():
    return [
        pltpu.VMEM((NSTATE, DI), BF16), pltpu.VMEM((NSTATE, DI), BF16), pltpu.SemaphoreType.DMA(()),
        pltpu.SemaphoreType.DMA(()),
    ]


def expand_row(row, dst):
    lo = iota((8, BLOCK), 1) < HEADDIM
    wide = jnp.broadcast_to(row, (8, BLOCK))
    for j in range(PAIRS):
        dst[:, pair(j)] = expand_pair(wide, j, lo)[0]


CHUNKS = ((0, 512), (512, 512), (1024, 512), (1536, 384))
ORDERS = ("xy", "yx", "xy", "yx")


def gate_kernel(normed_ref, wg_ref, cot_ref, wo_ref, gain_ref, leave_ref, tot_ref, gate_ref, ng_ref, inc_ref, decay, *bufs):
    i = pl.program_id(0)
    chain = Chain(leave_ref, inc_ref, decay, bufs, False)
    last = pl.num_programs(0) - 1

    @pl.when(i == 0)
    def _():
        expand_row(jnp.exp2(tot_ref[0:1]), decay)
        greet_neighbours()
        chain.step(0)

    for c in range(DI // 256):
        cs = slice(c * 256, (c + 1) * 256)
        gate_ref[:, cs] = dot(normed_ref[...], wg_ref[:, cs]).astype(BF16)
        ng_ref[:, cs] = (dot_nt(cot_ref[...], wo_ref[cs, :]) * gain_ref[1:2, cs]).astype(BF16)
    for k in range(1, chain.n):
        @pl.when(i == (0, 2, 3)[min(k, 3) - 1])
        def _():
            chain.step(k)

    @pl.when(i == last)
    def _():
        chain.done()


def gate_pass(normed, wg, cot, wo, gain, leave, tot, T=512):
    L = normed.shape[0]
    row = lambda w: pl.BlockSpec((T, w), lambda i: (i, 0))
    return pl.pallas_call(
        gate_kernel,
        grid=(L // T,),
        in_specs=[
            row(D), full((D, DI)), row(D), full((DI, D)), full((8, DI)), full((NSTATE, DI)), full((8, BLOCK)),
        ],
        out_specs=[row(DI), row(DI), full((NSTATE, DI))],
        out_shape=[sds((L, DI), BF16), sds((L, DI), BF16), sds((NSTATE, DI), F32)],
        scratch_shapes=[pltpu.VMEM((8, DI), F32)] + chain_scratch(),
        compiler_params=params(collective_id=2),
        name="gate_pass",
    )(normed, wg, cot, wo, gain, leave, tot)


def grads_kernel(nout_ref, cot_ref, xt_ref, ggrad_ref, back_ref, tot_ref, gout_ref, ggate_ref, inc_ref, decay, *bufs):
    i = pl.program_id(0)
    chain = Chain(back_ref, inc_ref, decay, bufs, True)
    last = pl.num_programs(0) - 1

    @pl.when(i == 0)
    def _():
        expand_row(jnp.exp2(tot_ref[0:1]), decay)
        greet_neighbours()
        chain.step(0)

    gout_ref[...] = dot_tn(nout_ref[...], cot_ref[...]).astype(BF16)
    ggate_ref[...] = dot(xt_ref[...], ggrad_ref[...]).astype(BF16)
    for k in range(1, chain.n):
        @pl.when(i == (0, 3, 5)[min(k, 3) - 1])
        def _():
            chain.step(k)

    @pl.when(i == last)
    def _():
        chain.done()


def grads_pass(nout, cot, xt, ggrad, back, tot):
    L = nout.shape[0]
    col = lambda w: pl.BlockSpec((L, w), lambda i: (0, i))
    return pl.pallas_call(
        grads_kernel,
        grid=(6,),
        in_specs=[
            col(256), once((L, D)), once((D, L)), col(256), full((NSTATE, DI)),
            full((8, BLOCK)),
        ],
        out_specs=[
            pl.BlockSpec((256, D), lambda i: (i, 0)), pl.BlockSpec((D, 256), lambda i: (0, i)), full((NSTATE, DI)),
        ],
        out_shape=[sds((DI, D), BF16), sds((D, DI), BF16), sds((NSTATE, DI), F32)],
        scratch_shapes=[pltpu.VMEM((8, DI), F32)] + chain_scratch(),
        compiler_params=params(collective_id=3),
        name="grads_pass",
    )(nout, cot, xt, ggrad, back, tot)


def last_kernel(
    T, xt_any, pg_any, wg_any, wc_any, tail_ref, ggrad_ref, tok_ref, cot_ref, gain_ref, small_ref,
    tgrad_ref, gout_ref, sums_ref, xt, wg, wc, pg, g0, g1, g2, g3, lsem, smalls, ssend, srecv, *scratch,
):
    i = pl.program_id(0)
    nc = len(CHUNKS)
    grads = (g0, g1, g2, g3)
    sc = [Scatter(grads[k], ORDERS[k][::-1], scratch[NSC * k : NSC * k + NSC]) for k in range(nc)]
    dp, seq = lax.axis_index("dp"), lax.axis_index("seq")
    n_dp, n_seq = lax.axis_size("dp"), lax.axis_size("seq")
    total = n_dp * n_seq
    me = dp * n_seq + seq
    L = pg.shape[0]

    whole = ((xt_any, xt), (wg_any, wg), (wc_any, wc))

    def load(k):
        if k >= nc:
            return pltpu.make_async_copy(*whole[k - nc], lsem.at[k])
        lanes = pl.ds(CHUNKS[k][0], CHUNKS[k][1])
        return pltpu.make_async_copy(pg_any.at[:, lanes], pg.at[:, lanes], lsem.at[k])

    def far(o):
        r = lax.rem(me + o, total)
        return {"dp": r // n_seq, "seq": lax.rem(r, n_seq)}

    def small(o):
        r = lax.rem(me + o, total)
        return pltpu.make_async_remote_copy(
            src_ref=small_ref.at[r], dst_ref=smalls.at[o - 1], send_sem=ssend.at[o - 1], recv_sem=srecv.at[o - 1],
            device_id=far(o), device_id_type=MESH,
        )

    @pl.when(i == 0)
    def _():
        load(nc).start()
        load(0).start()
        sem = pltpu.get_barrier_semaphore()
        for o in range(1, total):
            pl.semaphore_signal(sem, inc=1, device_id=far(o), device_id_type=MESH)

    for k in range(nc):
        @pl.when(i == k)
        def _():
            lane, width = CHUNKS[k]
            if k == 0:
                load(nc).wait()
            load(k).wait()
            if k + 1 < nc:
                load(k + 1).start()
            if k >= nc - 2:
                load(nc + 1 + k - (nc - 2)).start()
            skip = BLOCK if k == 0 else 0
            pg[L - 16 :, lane + skip : lane + width] = tail_ref[:, lane + skip : lane + width]
            rows = grads[k].shape[4]
            for q in range(2):
                half = D // 2
                g = dot(xt[q * half : (q + 1) * half], pg[:, lane : lane + width])
                for r in range(half // rows):
                    s = r + q * (half // rows)
                    grads[k][s // 8, (s // 4) % 2, (s // 2) % 2, s % 2] = g[r * rows : (r + 1) * rows].astype(BF16)
            if k == 0:
                pl.semaphore_wait(pltpu.get_barrier_semaphore(), total - 1)
                sc[0].start(0)
                for o in range(1, total):
                    small(o).start()
            else:
                sc[k - 1].finish(0)
                sc[k - 1].start(1)
                sc[k].start(0)

    @pl.when(i >= nc)
    def _():
        r0 = pl.multiple_of((i - nc) * T, T)

        @pl.when(i == nc)
        def _():
            load(nc + 1).wait()
            load(nc + 2).wait()

        u = dot_nt(ggrad_ref[...], wg[...]) + dot_nt(pg[pl.ds(r0, T), :], wc[...])
        u = u * gain_ref[0:1]
        x = tok_ref[...].astype(F32)
        inv = lax.rsqrt(jnp.mean(x * x, axis=-1, keepdims=True) + EPS)
        xi = x * inv
        coef = inv * jnp.mean(u * xi, axis=-1, keepdims=True)
        tgrad_ref[...] = (cot_ref[...].astype(F32) + inv * u - xi * coef).astype(BF16)

    def after(step, what):
        @pl.when(i == step)
        def _():
            for k, stage in what:
                sc[k].finish(stage)
                sc[k].start(stage + 1)

    after(nc, [(3, 0)])
    after(nc + 1, [(0, 1)])
    after(nc + 2, [(1, 1), (2, 1), (0, 2)])
    after(nc + 3, [(3, 1), (1, 2)])
    after(nc + 4, [(2, 2), (3, 2)])

    @pl.when(i == pl.num_programs(0) - 1)
    def _():
        for o in range(1, total):
            small(o).wait()
        acc = small_ref[me]
        for o in range(1, total):
            acc = acc + smalls[o - 1]
        sums_ref[...] = acc
        for k in range(nc):
            lane, width = CHUNKS[k]
            gout_ref[:, lane : lane + width] = sc[k].result()


def last_pass(xt, pg, tail, ggrad, tok, cot, wg, wc, gain, small):
    L = tok.shape[0]
    T = L // 8
    n = sizes()
    nc = len(CHUNKS)
    total = lax.axis_size("dp") * lax.axis_size("seq")
    rows = D // total
    row = lambda w: pl.BlockSpec((T, w), lambda i: (jnp.maximum(i - nc, 0), 0))
    scratch = []
    for _, w in CHUNKS:
        scratch += scatter_scratch(rows, w)
    return pl.pallas_call(
        functools.partial(last_kernel, T),
        grid=(nc + L // T,),
        in_specs=[
            ANY, ANY, ANY, ANY, once((16, WC)), row(DI), row(D), row(D), once((8, D)), once((total, 8, BLOCK)),
        ],
        out_specs=[row(D), full((rows, WC)), full((8, BLOCK))],
        out_shape=[sds((L, D), BF16), sds((rows, WC), F32), sds((8, BLOCK), F32)],
        scratch_shapes=[
            pltpu.VMEM((D, L), BF16), pltpu.VMEM((D, DI), BF16), pltpu.VMEM((D, WC), BF16), pltpu.VMEM((L, WC), BF16),
        ]
        + [pltpu.VMEM((n["z"], 2, n["y"], 2, rows, w), BF16) for _, w in CHUNKS]
        + [
            pltpu.SemaphoreType.DMA((nc + 3,)), pltpu.VMEM((total - 1, 8, BLOCK), F32),
            pltpu.SemaphoreType.DMA((total - 1,)), pltpu.SemaphoreType.DMA((total - 1,)),
        ] + scratch,
        compiler_params=params(collective_id=5),
        name="last_pass",
    )(xt, pg, wg, wc, tail, ggrad, tok, cot, gain, small)


def finish_kernel(
    gate_ref, conv_ref, out_ref, sums_ref, w_ref, wo_ref, own_ref, tgrad_ref,
    in_grad, ngain, ggain, taps, bias, step, decay, skip, out_grad, tgrad_out,
):
    tgrad_out[...] = tgrad_ref[...]

    @pl.when(pl.program_id(0) == 0)
    def _():
        finish_small(
            gate_ref, conv_ref, out_ref, sums_ref, w_ref, wo_ref, own_ref, in_grad, ngain, ggain, taps, bias,
            step, decay, skip, out_grad,
        )


def finish_small(
    gate_ref, conv_ref, out_ref, sums_ref, w_ref, wo_ref, own_ref,
    in_grad, ngain, ggain, taps, bias, step, decay, skip, out_grad,
):
    conv = conv_ref[...]
    raw = jnp.concatenate([gate_ref[...], conv[:, BLOCK:], conv[:, :HEADS]], axis=1)
    in_grad[...] = raw
    ngain[...] = jnp.sum(raw * w_ref[...].astype(F32), axis=1) / own_ref[0, 5, : ngain.shape[0]]
    o = out_ref[...]
    out_grad[...] = o
    ggain[...] = jnp.sum(o * wo_ref[...].astype(F32), axis=1) / own_ref[0, 6, : ggain.shape[0]]
    s = sums_ref[...]
    n = bias.shape[0]
    taps[...] = s[:CONV, :n]
    bias[...] = s[4, :n]
    step[...] = s[7, :HEADS]
    decay[...] = s[7, HEADS : 2 * HEADS]
    skip[...] = s[7, 2 * HEADS : 3 * HEADS]


def finish_pass(gate_cols, conv_cols, out_raw, sums, w, wo, own, tgrad, channels):
    vec = lambda n: sds((n,), F32)
    rows = pl.BlockSpec((512, D), lambda i: (i, 0))
    small = [
        sds(w.shape, F32), vec(w.shape[0]), vec(wo.shape[0]), sds((CONV, channels), F32),
        vec(channels), vec(HEADS), vec(HEADS), vec(HEADS), sds(out_raw.shape, F32),
    ]
    ins = (gate_cols, conv_cols, out_raw, sums, w, wo, own)
    return pl.pallas_call(
        finish_kernel,
        grid=(tgrad.shape[0] // 512,),
        in_specs=[once(x.shape) for x in ins] + [rows],
        out_specs=[once(x.shape) for x in small] + [rows],
        out_shape=small + [sds(tgrad.shape, BF16)],
        name="finish_pass",
    )(*ins, tgrad)


def rms_rows(tok, gain):
    x = tok.astype(F32)
    return (x * lax.rsqrt(jnp.mean(x * x, axis=-1, keepdims=True) + EPS) * gain).astype(BF16)


def first_kernel(
    T, win_ref, small, tok_any, so_ref,
    xhat_any, xt_any, wc_any, p_any, hp_ref, conv_ref, gain_ref, row_ref,
    act_ref, slope_ref, dt_ref, cum_ref, sig_ref, bst_ref, leave_ref, tot_ref, bg_ref, bo_ref,
    slab, tok, halo, xhat, xt, wc, wide, p, smalls, b0, b1, b2, b3, ext, state, weighted, lsem, hsend, hrecv, ssend, srecv,
    *sems,
):
    i = pl.program_id(0)
    steps = pl.num_programs(0)
    at = place()
    seq, n = lax.axis_index("seq"), lax.axis_size("seq")
    L = tok.shape[0]
    bufs = (b0, b1, b2, b3)
    nc = len(CHUNKS)
    gets = []
    for (lane, width), order, buf, k in zip(CHUNKS, ORDERS, bufs, range(nc)):
        gets.append(Gather(slab.at[:, pl.ds(lane, width)], spots(buf), order, sems[2 * k : 2 * k + 2]))
    for k in range(4):
        buf = (bg_ref, bo_ref)[k % 2]
        width = buf.shape[5] // 2
        lanes = pl.ds((k // 2) * width, width)
        q = 2 * (nc + k)
        src = win_ref if k % 2 == 0 else so_ref
        gets.append(Gather(src.at[:, lanes], spots(buf, lanes), ORDERS[k], sems[q : q + 2]))
    own = []
    for k, (src, buf) in enumerate(((win_ref.at[:, pl.ds(0, DI)], bg_ref), (so_ref, bo_ref))):
        own.append(pltpu.make_async_copy(src, buf.at[at["z"], at["x"], at["y"], at["c"]], lsem.at[k]))
    halo_copy = pltpu.make_async_remote_copy(
        src_ref=tok_any.at[pl.ds(L - 16, 16)], dst_ref=halo, send_sem=hsend, recv_sem=hrecv,
        device_id={"seq": seq + 1}, device_id_type=MESH,
    )
    outs = [pltpu.make_async_copy(xhat, xhat_any, lsem.at[3]), pltpu.make_async_copy(xt, xt_any, lsem.at[4])]
    for k, (lane, width) in enumerate(CHUNKS):
        for j, (src, dst) in enumerate(((p, p_any), (wc, wc_any))):
            lanes = pl.ds(lane, width)
            outs.append(pltpu.make_async_copy(src.at[:, lanes], dst.at[:, lanes], lsem.at[5 + 2 * k + j]))

    def advance(*what):
        for k, stage in what:
            if stage > 0:
                gets[k].wait(stage - 1)
            if stage < 4:
                gets[k].start(stage)

    def project(k):
        lane, width = CHUNKS[k]
        buf = bufs[k]
        nz, rows_k = buf.shape[0], buf.shape[4]
        for z in range(nz):
            for m in range(8):
                r = z * 8 + m
                wide[r * rows_k : (r + 1) * rows_k, :width] = buf[z, m // 4, (m // 2) % 2, m % 2].astype(F32)
        wc[:, lane : lane + width] = wide[:, :width].astype(BF16)
        for r in range(L // 512):
            rows = slice(r * 512, (r + 1) * 512)
            p[rows, lane : lane + width] = dot(xhat[rows], wc[:, lane : lane + width]).astype(BF16)
        hp_ref[:, lane : lane + width] = dot(halo[...], wc[:, lane : lane + width]).astype(BF16)
        for c in outs[2 + 2 * k : 4 + 2 * k]:
            c.start()

    @pl.when(i == 0)
    def _():
        dp = lax.axis_index("dp")
        n_dp = lax.axis_size("dp")
        total = n_dp * n
        me = dp * n + seq
        load = pltpu.make_async_copy(tok_any, tok, lsem.at[2])
        load.start()
        sem = pltpu.get_barrier_semaphore()
        k_rows = slab.shape[0]
        steps_w = win_ref[:, DI + CH :]
        slab[:, :BLOCK] = jnp.concatenate([steps_w, jnp.zeros((k_rows, BLOCK - HEADS), BF16)], axis=1)
        slab[:, BLOCK:] = win_ref[:, DI : DI + CH]

        def far(o):
            r = lax.rem(me + o, total)
            return {"dp": r // n, "seq": lax.rem(r, n)}

        for o in range(1, total):
            pl.semaphore_signal(sem, inc=1, device_id=far(o), device_id_type=MESH)
        pl.semaphore_wait(sem, total - 1)
        advance((0, 0), (1, 0))

        @pl.when(seq < n - 1)
        def _():
            halo_copy.start()

        sends = []
        for o in range(1, total):
            c = pltpu.make_async_remote_copy(
                src_ref=small.at[0], dst_ref=smalls.at[me], send_sem=ssend.at[o - 1], recv_sem=srecv.at[o - 1],
                device_id=far(o), device_id_type=MESH,
            )
            c.start()
            sends.append(c)
        for c in own:
            c.start()
        smalls[me] = small[0]
        expand_row(small[1, 2:3], row_ref)
        for (lane, width), buf in zip(CHUNKS, bufs):
            buf[at["z"], at["x"], at["y"], at["c"]] = slab[:, lane : lane + width]
        conv_ref[...] = jnp.zeros_like(conv_ref)
        state[...] = jnp.zeros_like(state)
        tot_ref[...] = jnp.zeros_like(tot_ref)
        advance((0, 1), (2, 0), (1, 1), (3, 0))
        load.wait()
        for c in sends:
            c.wait()
        taps, ks, gs = CH // total, D // total, DI // total
        for r in range(total):
            conv_ref[0:5, r * taps : (r + 1) * taps] = smalls[r, 0:5, :taps]
            gain_ref[:, r * ks : (r + 1) * ks] = jnp.broadcast_to(smalls[r, 5:6, :ks], (8, ks))
            row_ref[1:2, r * gs : (r + 1) * gs] = smalls[r, 6:7, :gs]

        def norm(r, _):
            rows = pl.ds(pl.multiple_of(r * 256, 256), 256)
            h = rms_rows(tok[rows], gain_ref[0:1])
            xhat[rows] = h
            xt[:, rows] = h.T
            return _

        lax.fori_loop(0, L // 512, norm, 0)
        advance((0, 2), (1, 2), (2, 1), (4, 0), (3, 1), (5, 0), (6, 0), (7, 0))
        lax.fori_loop(L // 512, L // 256, norm, 0)
        for c in outs[:2]:
            c.start()

        @pl.when(seq == 0)
        def _():
            halo[...] = jnp.zeros_like(halo)

        @pl.when(seq > 0)
        def _():
            halo_copy.wait_recv()

        @pl.when(seq < n - 1)
        def _():
            halo_copy.wait_send()

        halo[...] = rms_rows(halo[...], gain_ref[0:1])
        for c in own:
            c.wait()
        advance((0, 3), (1, 3), (2, 2), (3, 2), (0, 4))
        project(0)
        advance((1, 4), (4, 1), (5, 1))
        project(1)
        advance((2, 3), (3, 3), (4, 2), (5, 2), (6, 1), (7, 1), (2, 4))
        project(2)
        advance((3, 4))
        project(3)
        for c in range(CH // 128):
            ext[c, 0:8] = hp_ref[:, BLOCK + c * 128 : BLOCK + (c + 1) * 128].astype(F32)[8:16]

    def tile(r0):
        for c in range(CH // 128):
            cs = slice(c * 128, (c + 1) * 128)
            ext[c, 8 : 8 + T] = p[pl.ds(r0, T), BLOCK + c * 128 : BLOCK + (c + 1) * 128].astype(F32)
            for r in range(0, T, 64):
                total = conv_ref[4:5, cs]
                for k in range(CONV):
                    total = total + ext[c, 5 + k + r : 5 + k + r + 64] * conv_ref[k : k + 1, cs]
                sg = sigmoid(total)
                v = total * sg
                act_ref[r : r + 64, cs] = v.astype(BF16)
                slope_ref[r : r + 64, cs] = (sg + v * (1.0 - sg)).astype(BF16)
        raw = p[pl.ds(r0, T), :BLOCK].astype(F32) + small[1, 0:1]
        dt_all = jnp.maximum(raw, 0.0) + jnp.log1p(jnp.exp(-jnp.abs(raw)))
        dt_ref[...] = dt_all
        sig_ref[...] = sigmoid_exact(raw)
        tril = (iota((BLOCK, BLOCK), 0) >= iota((BLOCK, BLOCK), 1)).astype(F32)
        lo = lane_lo()
        for blk in range(T // BLOCK):
            rows = slice(blk * BLOCK, (blk + 1) * BLOCK)
            dt = dt_all[rows]
            cum = dot_exact(tril, dt * -jnp.exp(small[1, 1:2])) * LOG2E
            cum_ref[rows] = cum
            end = cum[BLOCK - 1 : BLOCK]
            tot_ref[...] += jnp.broadcast_to(end, tot_ref.shape)
            wfac = jnp.exp2(end - cum) * dt
            decay = jnp.broadcast_to(jnp.exp2(end), (8, BLOCK))
            write_t = act_ref[rows, DI : DI + NSTATE].T
            for j in range(PAIRS):
                w, _, _ = expand_pair(wfac, j, lo)
                weighted[:, pair(j)] = (act_ref[rows, pair(j)].astype(F32) * w).astype(BF16)
            for q in range(PAIRS // 2):
                cs = slice(q * 256, (q + 1) * 256)
                new = dot(write_t, weighted[:, cs])
                bst_ref[blk, :, cs] = new.astype(BF16)
                d0, _, _ = expand_pair(decay, 2 * q, lo[:8])
                d1, _, _ = expand_pair(decay, 2 * q + 1, lo[:8])
                dd = jnp.concatenate([d0, d1], axis=1)[0:1]
                state[:, cs] = state[:, cs] * dd + new

    def after(step, *what):
        @pl.when(i == step)
        def _():
            advance(*what)

    after(4, (6, 2), (7, 2), (4, 3), (5, 3))
    after(7, (6, 3), (7, 3))

    @pl.when(i > 1)
    def _():
        ext[:, 0:8] = ext[:, T : T + 8]

    @pl.when(i > 0)
    def _():
        tile(pl.multiple_of((i - 1) * T, T))

    @pl.when(i == steps - 1)
    def _():
        leave_ref[...] = state[...]
        advance((4, 4), (5, 4), (6, 4), (7, 4))
        for c in outs:
            c.wait()


def sigmoid_exact(v):
    return 1.0 / (1.0 + jnp.exp(-v))


def second_kernel(
    T, gate_s, ng, act_ref, dt_ref, cum_ref, bst_ref, inc_ref, tok_ref, wo_ref, row_ref, et_ref,
    mixed_ref, nout_ref, ggrad_ref, mlow_ref, dcum_ref, ent_ref, egrad_ref, rg_ref, leave_ref, back_ref, cols_ref,
    ms, growth, rlow, prod, plow, state, exg, lows,
):
    i = pl.program_id(0)

    @pl.when(i == 0)
    def _():
        state[...] = inc_ref[...]
        exg[...] = jnp.ones_like(exg)
        back_ref[...] = jnp.zeros_like(back_ref)
        cols_ref[...] = jnp.zeros_like(cols_ref)

    lo = lane_lo()
    lower = iota((BLOCK, BLOCK), 0) >= iota((BLOCK, BLOCK), 1)
    nblk = T // BLOCK
    for blk in range(nblk):
        rows = slice(blk * BLOCK, (blk + 1) * BLOCK)
        cum = cum_ref[rows]
        cum_t = cum.T
        dt = dt_ref[rows]
        write = act_ref[rows, DI : DI + NSTATE]
        read = act_ref[rows, DI + NSTATE :]
        inner = jnp.where(lower, dot_nt(read, write), 0.0)
        lows[blk] = state[...].astype(BF16)
        ent_ref[blk] = lows[blk]
        for j in range(PAIRS):
            cols, a, b = expand_pair(cum, j, lo)
            ga = jnp.exp2(jnp.minimum(a - cum_t[2 * j : 2 * j + 1], 0.0)) * inner
            gb = jnp.exp2(jnp.minimum(b - cum_t[2 * j + 1 : 2 * j + 2], 0.0)) * inner
            scores = jnp.concatenate([ga.astype(BF16), gb.astype(BF16)], axis=1)
            vals = act_ref[rows, pair(j)].astype(F32)
            dtp, _, _ = expand_pair(dt, j, lo)
            vdt = (vals * dtp).astype(BF16)
            grow = jnp.exp2(cols)
            growth[rows, pair(j)] = grow
            diag = dot(scores, block_diag(vdt))
            if j % 2 == 0:
                outs = dot(read, lows[blk, :, j * BLOCK : (j + 2) * BLOCK])
            out = outs[:, (j % 2) * BLOCK : (j % 2 + 1) * BLOCK]
            ms[rows, pair(j)] = diag + grow * out + row_ref[0:1, pair(j)] * vals
            dec = grow[BLOCK - 1 : BLOCK]
            state[:, pair(j)] = state[:, pair(j)] * dec + bst_ref[blk, :, pair(j)].astype(F32)

    sq = jnp.zeros((T, BLOCK), F32)
    ug = jnp.zeros((T, BLOCK), F32)
    for j in range(PAIRS):
        g = gate_s[:, pair(j)].astype(F32)
        gated = ms[:, pair(j)] * (g * sigmoid(g))
        sq = sq + gated * gated
        ug = ug + gated * ng[:, pair(j)].astype(F32)
    inv = lax.rsqrt(jnp.sum(sq, axis=-1, keepdims=True) * (1.0 / DI) + EPS)
    coef = jnp.sum(ug, axis=-1, keepdims=True) * (1.0 / DI) * (inv * inv * inv)
    for j in range(PAIRS):
        g = gate_s[:, pair(j)].astype(F32)
        sg = sigmoid(g)
        silu = g * sg
        m = ms[:, pair(j)]
        gated = m * silu
        nout_ref[:, pair(j)] = (gated * inv * row_ref[1:2, pair(j)]).astype(BF16)
        dg = inv * ng[:, pair(j)].astype(F32) - gated * coef
        low = (dg * silu).astype(BF16)
        mlow_ref[:, pair(j)] = low
        ggrad_ref[:, pair(j)] = (dg * m * (sg + silu * (1.0 - sg))).astype(BF16)
        vals = act_ref[:, pair(j)].astype(F32)
        lowf = low.astype(F32)
        mv = lowf * vals
        pr = lowf * m - row_ref[0:1, pair(j)] * mv
        hi = pr.astype(BF16)
        prod[:, pair(j)] = hi
        plow[:, pair(j)] = (pr - hi.astype(F32)).astype(BF16)
        rlow[:, pair(j)] = (lowf * growth[:, pair(j)]).astype(BF16)
        cols_ref[:, pair(j)] += jnp.sum(mv.reshape(T // 8, 8, BLOCK), axis=0)
    dcum_ref[...] = dot(prod[...], et_ref[...]) + dot(plow[...], et_ref[...])
    mixed_ref[...] = (tok_ref[...].astype(F32) + dot(nout_ref[...], wo_ref[...])).astype(BF16)
    for blk in range(nblk):
        rows = slice(blk * BLOCK, (blk + 1) * BLOCK)
        read_t = act_ref[rows, DI + NSTATE :].T
        for q in range(PAIRS // 2):
            cs = slice(q * 256, (q + 1) * 256)
            eg = dot(read_t, rlow[rows, cs])
            egrad_ref[blk, :, cs] = eg.astype(BF16)
            back_ref[:, cs] += eg * exg[0:1, cs]
        exg[...] = exg[...] * growth[blk * BLOCK + BLOCK - 1 : blk * BLOCK + BLOCK, :]
        rg_ref[rows] = dot_nt(rlow[rows, :], lows[blk])

    @pl.when(i == pl.num_programs(0) - 1)
    def _():
        leave_ref[...] = state[...].astype(BF16)


def third_kernel(
    T, act_ref, convin_ref, slope_ref, dt_ref, cum_ref, sig_ref, dcum_ref, mlow_ref, ent_ref, leave_ref,
    egrad_ref, rg_ref, inc_ref, row_ref, conv_ref, head_ref, et_ref, cols_ref, go_ref, gg_ref,
    pg_ref, small_ref, tail_ref, so_ref, sg_ref,
    cgrad_ref, hgrad_ref, sums8, glast, xlast, gafter, hsend, hrecv, carry, dact, vprod, prod, plow, weighted, lows, dec, nxt, gext, *scratch,
):
    i = pl.program_id(0)
    steps = pl.num_programs(0)
    sca = Scatter(go_ref, "yx", scratch[2 : 2 + NSC], *scratch[:2])
    scb = Scatter(gg_ref, "xy", scratch[4 + NSC :], *scratch[2 + NSC : 4 + NSC])
    seq, nseq = lax.axis_index("seq"), lax.axis_size("seq")
    after = pltpu.make_async_remote_copy(
        src_ref=gext.at[:, pl.ds(0, 8)], dst_ref=gafter, send_sem=hsend, recv_sem=hrecv, device_id={"seq": seq - 1},
        device_id_type=MESH,
    )

    @pl.when(i == 0)
    def _():
        greet(place(), "zxyc", 1)
        sca.start(0)
        scb.start(0)

    for stage, when in enumerate((1, 4, 6)):
        @pl.when(i == when)
        def _():
            sca.finish(stage)
            sca.start(stage + 1)
            scb.finish(stage)
            scb.start(stage + 1)


    @pl.when(i == 0)
    def _():
        carry[...] = inc_ref[...]
        nxt[...] = leave_ref[...]
        cgrad_ref[...] = jnp.zeros_like(cgrad_ref)
        hgrad_ref[...] = jnp.zeros_like(hgrad_ref)

    lo = lane_lo()
    upper = iota((BLOCK, BLOCK), 0) <= iota((BLOCK, BLOCK), 1)
    triu = upper.astype(F32)
    last = iota((BLOCK, BLOCK), 0) == BLOCK - 1
    for blk in reversed(range(T // BLOCK)):
        rows = slice(blk * BLOCK, (blk + 1) * BLOCK)
        cum = cum_ref[rows]
        cum_t = cum.T
        dt = dt_ref[rows]
        end = cum[BLOCK - 1 : BLOCK]
        write = act_ref[rows, DI : DI + NSTATE]
        read = act_ref[rows, DI + NSTATE :]
        inner = jnp.where(upper, dot_nt(write, read), 0.0)
        lows[...] = carry[...].astype(BF16)
        acc = jnp.zeros((BLOCK, BLOCK), F32)
        for j in range(PAIRS):
            cols, a, b = expand_pair(cum, j, lo)
            ends = jnp.where(lo[:1], end[:, 2 * j : 2 * j + 1], end[:, 2 * j + 1 : 2 * j + 2])
            wexp = jnp.exp2(ends - cols)
            da = jnp.exp2(jnp.minimum(cum_t[2 * j : 2 * j + 1] - a, 0.0))
            db = jnp.exp2(jnp.minimum(cum_t[2 * j + 1 : 2 * j + 2] - b, 0.0))
            scores = jnp.concatenate([(da * inner).astype(BF16), (db * inner).astype(BF16)], axis=1)
            m = mlow_ref[rows, pair(j)]
            diag = block_diag(m)
            z = dot(scores, diag)
            vals = act_ref[rows, pair(j)].astype(F32)
            dtp, _, _ = expand_pair(dt, j, lo)
            vdt = vals * dtp
            vdtb = vdt.astype(BF16)
            wtb = (vdt * wexp).astype(BF16)
            g = dot_nt(vdtb, diag)
            acc = acc + g[:, :BLOCK] * da + g[:, BLOCK:] * db
            if j % 2 == 0:
                wgs = dot(write, lows[:, j * BLOCK : (j + 2) * BLOCK])
            wg = wgs[:, (j % 2) * BLOCK : (j % 2 + 1) * BLOCK]
            pr = vdtb.astype(F32) * z + wtb.astype(F32) * wg
            z = z + wg * wexp
            dact[rows, pair(j)] = row_ref[0:1, pair(j)] * m.astype(F32) + dtp * z
            vprod[:, pair(j)] = (vals * z).astype(BF16)
            hi = pr.astype(BF16)
            prod[:, pair(j)] = hi
            plow[:, pair(j)] = (pr - hi.astype(F32)).astype(BF16)
            weighted[:, pair(j)] = wtb
            dec[0:1, pair(j)] = jnp.exp2(cols[BLOCK - 1 : BLOCK])
        low = jnp.where(upper, acc, 0.0).astype(BF16)
        dact[rows, DI : DI + NSTATE] = dot_nt(weighted[...], lows[...]) + dot(low, read)
        dact[rows, DI + NSTATE :] = rg_ref[rows] + dot(low.T, write)
        c = dot(vprod[...], et_ref[...])
        used = dot(prod[...], et_ref[...]) + dot(plow[...], et_ref[...])
        ends = jnp.sum((lows[...].astype(F32) * nxt[...].astype(F32)).reshape(16, 8, DI), axis=0)
        ends_hi = ends.astype(BF16)
        ends_lo = (ends - ends_hi.astype(F32)).astype(BF16)
        de = jnp.sum(dot(ends_hi, et_ref[...]) + dot(ends_lo, et_ref[...]), axis=0, keepdims=True)
        dc = dcum_ref[rows] - used + jnp.where(last, de, 0.0)
        da_log = dot_exact(triu, dc)
        decay = -jnp.exp(head_ref[1, 1:2])
        draw = (c + da_log * decay) * sig_ref[rows]
        pg_ref[rows, :BLOCK] = draw.astype(BF16)
        hgrad_ref[0:8] += jnp.sum(draw.reshape(16, 8, BLOCK), axis=0)
        hgrad_ref[8:16] += jnp.sum((da_log * dt).reshape(16, 8, BLOCK), axis=0) * decay
        nxt[...] = ent_ref[blk]
        for q in range(PAIRS // 2):
            cs = slice(q * 256, (q + 1) * 256)
            carry[:, cs] = carry[:, cs] * dec[0:1, cs] + egrad_ref[blk, :, cs].astype(F32)

    for c in range(CH // 128):
        cs = slice(c * 128, (c + 1) * 128)
        ps = slice(BLOCK + c * 128, BLOCK + (c + 1) * 128)

        @pl.when(i == 0)
        def _():
            gext[c, T : T + 8] = jnp.zeros((8, 128), F32)
            xlast[:, cs] = convin_ref[T - 16 :, ps].astype(F32)

        @pl.when(i > 0)
        def _():
            gext[c, T : T + 8] = gext[c, 0:8]

        for r in range(0, T, 64):
            gext[c, r : r + 64] = dact[r : r + 64, cs] * slope_ref[r : r + 64, cs].astype(F32)
        sums = [jnp.zeros((8, 128), F32)] * 5
        for r in range(0, T, 64):
            x = convin_ref[r : r + 64, ps].astype(F32)
            g = gext[c, r : r + 64]
            back = g * conv_ref[3:4, cs]
            sums[4] = sums[4] + jnp.sum(g.reshape(8, 8, 128), axis=0)
            sums[3] = sums[3] + jnp.sum((g * x).reshape(8, 8, 128), axis=0)
            for k in range(CONV - 1):
                gk = gext[c, 3 - k + r : 3 - k + r + 64]
                back = back + gk * conv_ref[k : k + 1, cs]
                sums[k] = sums[k] + jnp.sum((gk * x).reshape(8, 8, 128), axis=0)
            pg_ref[r : r + 64, ps] = back.astype(BF16)
            if r + 64 == T:
                @pl.when(i == 0)
                def _():
                    glast[:, cs] = back[48:]
        for k in range(5):
            cgrad_ref[8 * k : 8 * k + 8, cs] += sums[k]

    @pl.when(i == steps - 1)
    def _():
        @pl.when(seq > 0)
        def _():
            after.start()

        so_ref[...] = sca.result()
        sg_ref[...] = scb.result()

        @pl.when(seq == nseq - 1)
        def _():
            gafter[...] = jnp.zeros_like(gafter)

        @pl.when(seq < nseq - 1)
        def _():
            after.wait_recv()

        row16, row8 = iota((16, 128), 0), iota((8, 128), 0)
        for c in range(CH // 128):
            cs = slice(c * 128, (c + 1) * 128)
            ps = slice(BLOCK + c * 128, BLOCK + (c + 1) * 128)
            tail = glast[:, cs]
            for j in range(CONV - 1):
                for k in range(j + 1):
                    g = gafter[c, j - k : j - k + 1]
                    tail = tail + jnp.where(row16 == 13 + j, g * conv_ref[k : k + 1, cs], 0.0)
                    cgrad_ref[8 * k : 8 * k + 8, cs] += jnp.where(row8 == 0, g * xlast[13 + j : 14 + j, cs], 0.0)
            tail_ref[:, ps] = tail.astype(BF16)
        tail_ref[:, :BLOCK] = jnp.zeros((16, BLOCK), BF16)
        for k in range(5):
            sums8[k : k + 1] = jnp.sum(cgrad_ref[8 * k : 8 * k + 8], axis=0, keepdims=True)
        steps8 = jnp.broadcast_to(jnp.sum(hgrad_ref[0:8], axis=0, keepdims=True), (8, BLOCK))
        decay8 = jnp.broadcast_to(jnp.sum(hgrad_ref[8:16], axis=0, keepdims=True), (8, BLOCK))
        high = cols_ref[...].astype(BF16)
        low8 = (cols_ref[...] - high.astype(F32)).astype(BF16)
        skip8 = jnp.sum(dot(high, et_ref[...]) + dot(low8, et_ref[...]), axis=0, keepdims=True)
        skip8 = jnp.broadcast_to(skip8, (8, BLOCK))
        lane = iota((8, BLOCK), 1)
        heads = jnp.where(lane < HEADS, steps8, pltpu.roll(decay8, HEADS, 1))
        heads = jnp.where(lane < 2 * HEADS, heads, pltpu.roll(skip8, 2 * HEADS, 1))
        heads = jnp.where((iota((8, BLOCK), 0) == 7) & (lane < 3 * HEADS), heads, 0.0)
        take = CH // small_ref.shape[0]
        for r in range(small_ref.shape[0]):
            small_ref[r] = heads
            small_ref[r, 0:5, :take] = sums8[0:5, r * take : (r + 1) * take]

        @pl.when(seq > 0)
        def _():
            after.wait_send()


def once(shape):
    return pl.BlockSpec(shape, lambda i: (0,) * len(shape), pipeline_mode=pl.Buffered(1))


def full(shape):
    return pl.BlockSpec(shape, lambda i: (0,) * len(shape))


def params(collective_id=None):
    return pltpu.CompilerParams(
        dimension_semantics=("arbitrary",), vmem_limit_bytes=VMEM_LIMIT, collective_id=collective_id,
        has_side_effects=collective_id is not None,
    )


def head_columns():
    et = np.zeros((DI, BLOCK), np.float32)
    et[np.arange(DI), np.arange(DI) // HEADDIM] = 1.0
    return et


def sds(shape, dtype):
    return jax.ShapeDtypeStruct(shape, dtype)


def first_pass(w_in, small, tok, slab_o, T=256):
    L = tok.shape[0]
    nb, per = L // BLOCK, T // BLOCK
    n = sizes()
    k_rows = w_in.shape[0]
    total = lax.axis_size("dp") * lax.axis_size("seq")
    row = lambda w: pl.BlockSpec((T, w), lambda i: (jnp.maximum(i - 1, 0), 0))
    dims = (n["z"], n["x"], n["y"], n["c"])
    sems = []
    for _ in range(len(CHUNKS) + 4):
        sems += gather_sems()
    return pl.pallas_call(
        functools.partial(first_kernel, T),
        grid=(1 + L // T,),
        in_specs=[once(w_in.shape), once((2, 8, BLOCK)), ANY, ANY],
        out_specs=[
            ANY, ANY, ANY, ANY, full((16, WC)), full((8, CH)), full((8, D)), full((8, DI)),
            row(CH), row(CH), row(BLOCK), row(BLOCK), row(BLOCK),
            pl.BlockSpec((per, NSTATE, DI), lambda i: (jnp.maximum(i - 1, 0), 0, 0)), full((NSTATE, DI)),
            full((8, BLOCK)), ANY, ANY,
        ],
        out_shape=[
            sds((L, D), BF16), sds((D, L), BF16), sds((D, WC), BF16), sds((L, WC), BF16), sds((16, WC), BF16),
            sds((8, CH), F32), sds((8, D), F32), sds((8, DI), F32),
            sds((L, CH), BF16), sds((L, CH), BF16), sds((L, BLOCK), F32), sds((L, BLOCK), F32), sds((L, BLOCK), F32),
            sds((nb, NSTATE, DI), BF16), sds((NSTATE, DI), F32), sds((8, BLOCK), F32),
            sds(dims + (k_rows, DI), BF16), sds(dims + slab_o.shape, BF16),
        ],
        scratch_shapes=[
            pltpu.VMEM((k_rows, WC), BF16), pltpu.VMEM((L, D), BF16), pltpu.VMEM((16, D), BF16), pltpu.VMEM((L, D), BF16), pltpu.VMEM((D, L), BF16),
            pltpu.VMEM((D, WC), BF16), pltpu.VMEM((D, 512), F32), pltpu.VMEM((L, WC), BF16),
            pltpu.VMEM((total, 8, BLOCK), F32),
        ] + [pltpu.VMEM(dims + (k_rows, w), BF16) for _, w in CHUNKS] + [
            pltpu.VMEM((CH // 128, T + 8, 128), F32), pltpu.VMEM((NSTATE, DI), F32), pltpu.VMEM((BLOCK, DI), BF16),
            pltpu.SemaphoreType.DMA((5 + 2 * len(CHUNKS),)), pltpu.SemaphoreType.DMA(()), pltpu.SemaphoreType.DMA(()),
            pltpu.SemaphoreType.DMA((total - 1,)), pltpu.SemaphoreType.DMA((total - 1,)),
        ] + sems,
        compiler_params=params(collective_id=1),
        name="first_pass",
    )(w_in, small, tok, slab_o)


def second_pass(gate, ng, act, dt, cum, bst, inc, tok, wo, rows, et, T=256):
    L = tok.shape[0]
    nb, per = L // BLOCK, T // BLOCK
    row = lambda w: pl.BlockSpec((T, w), lambda i: (i, 0))
    blk = pl.BlockSpec((per, NSTATE, DI), lambda i: (i, 0, 0))
    return pl.pallas_call(
        functools.partial(second_kernel, T),
        grid=(L // T,),
        in_specs=[
            row(DI), row(DI), row(CH), row(BLOCK), row(BLOCK), blk, full((NSTATE, DI)), row(D), full((DI, D)), full((8, DI)), full((DI, BLOCK)),
        ],
        out_specs=[
            row(D), row(DI), row(DI), row(DI), row(BLOCK), blk, blk, row(BLOCK), full((NSTATE, DI)),
            full((NSTATE, DI)), full((8, DI)),
        ],
        out_shape=[
            sds((L, D), BF16), sds((L, DI), BF16), sds((L, DI), BF16), sds((L, DI), BF16), sds((L, BLOCK), F32),
            sds((nb, NSTATE, DI), BF16), sds((nb, NSTATE, DI), BF16), sds((L, BLOCK), F32), sds((NSTATE, DI), BF16),
            sds((NSTATE, DI), F32), sds((8, DI), F32),
        ],
        scratch_shapes=[
            pltpu.VMEM((T, DI), F32), pltpu.VMEM((T, DI), F32),
            pltpu.VMEM((T, DI), BF16), pltpu.VMEM((T, DI), BF16), pltpu.VMEM((T, DI), BF16), pltpu.VMEM((NSTATE, DI), F32),
            pltpu.VMEM((8, DI), F32), pltpu.VMEM((per, NSTATE, DI), BF16),
        ],
        compiler_params=params(),
        name="second_pass",
    )(gate, ng, act, dt, cum, bst, inc, tok, wo, rows, et)


def third_pass(
    act, convin, slope, dt, cum, sig, dcum, mlow, ent, leave, egrad, rg, inc, rows, conv, head, et, cols, go, gg, T=256
):
    L = act.shape[0]
    m = sizes()
    dims = (m["z"], m["x"], m["y"], m["c"])
    total = m["z"] * m["y"] * 4
    ro, rg_rows = DI // total, D // total
    go = go.reshape(dims + (ro, D))
    gg = gg.reshape(dims + (rg_rows, DI))
    n, per = L // T, T // BLOCK
    row = lambda w: pl.BlockSpec((T, w), lambda i: (n - 1 - i, 0))
    blk = pl.BlockSpec((per, NSTATE, DI), lambda i: (n - 1 - i, 0, 0))
    return pl.pallas_call(
        functools.partial(third_kernel, T),
        grid=(n,),
        in_specs=[
            row(CH), row(WC), row(CH), row(BLOCK), row(BLOCK), row(BLOCK), row(BLOCK), row(DI), blk,
            full((NSTATE, DI)), blk, row(BLOCK), full((NSTATE, DI)), full((8, DI)), full((8, CH)), full((2, 8, BLOCK)),
            full((DI, BLOCK)), full((8, DI)), ANY, ANY,
        ],
        out_specs=[
            row(WC), full((total, 8, BLOCK)), full((16, WC)), full((ro, D)), full((rg_rows, DI)),
        ],
        out_shape=[
            sds((L, WC), BF16), sds((total, 8, BLOCK), F32), sds((16, WC), BF16), sds((ro, D), F32),
            sds((rg_rows, DI), F32),
        ],
        scratch_shapes=[
            pltpu.VMEM((40, CH), F32), pltpu.VMEM((16, BLOCK), F32), pltpu.VMEM((8, CH), F32),
            pltpu.VMEM((16, CH), F32), pltpu.VMEM((16, CH), F32), pltpu.VMEM((CH // 128, 8, 128), F32),
            pltpu.SemaphoreType.DMA(()), pltpu.SemaphoreType.DMA(()),
            pltpu.VMEM((NSTATE, DI), F32), pltpu.VMEM((T, CH), F32), pltpu.VMEM((BLOCK, DI), BF16), pltpu.VMEM((BLOCK, DI), BF16), pltpu.VMEM((BLOCK, DI), BF16),
            pltpu.VMEM((BLOCK, DI), BF16), pltpu.VMEM((NSTATE, DI), BF16), pltpu.VMEM((8, DI), F32),
            pltpu.VMEM((NSTATE, DI), BF16), pltpu.VMEM((CH // 128, T + 8, 128), F32),
        ] + own_scratch(ro, D) + scatter_scratch(ro, D) + own_scratch(rg_rows, DI) + scatter_scratch(rg_rows, DI),
        compiler_params=params(collective_id=4),
        name="third_pass",
    )(act, convin, slope, dt, cum, sig, dcum, mlow, ent, leave, egrad, rg, inc, rows, conv, head, et, cols, go, gg)


def on_device(
    tokens, cotangent, norm_gain, in_weight, conv_weight, conv_bias, step_bias, decay_log, skip_gain, gate_gain,
    out_weight,
):
    tok, cot = tokens[0], cotangent[0]
    L = tok.shape[0]
    k_rows, c_rows = in_weight.shape[0], conv_weight.shape[0]
    total = D // k_rows
    lanes = lambda x: jnp.pad(x, ((0, 0),) * (x.ndim - 1) + ((0, BLOCK - x.shape[-1]),))

    def put(x, row):
        x = x.astype(F32)
        return jnp.pad(x, ((row, 16 - row - x.shape[0]), (0, BLOCK - x.shape[1])))

    own = put(conv_weight.T, 0) + put(conv_bias[None], 4) + put(norm_gain[None], 5) + put(gate_gain[None], 6)
    own = own + put(step_bias[None], 8) + put(decay_log[None], 9) + put(skip_gain[None], 10)
    own = own.reshape(2, 8, BLOCK)
    et = jnp.asarray(head_columns(), BF16)

    (xhat, xt, wc, p, hp, conv, gain, rows, act, slope, dt, cum, sig, bst, leave, tot, buf_g, buf_o) = first_pass(
        in_weight, own, tok, out_weight
    )
    wg, wo = buf_g.reshape(D, DI), buf_o.reshape(DI, D)
    gate, ng, inc = gate_pass(xhat, wg, cot, wo, rows, leave, tot)
    mixed, nout, ggrad, mlow, dcum, ent, egrad, rg, leave2, back, cols = second_pass(
        gate, ng, act, dt, cum, bst, inc, tok, wo, rows, et
    )
    g_out, g_gate, later = grads_pass(nout, cot, xt, ggrad, back, tot)
    pg, small, tail, out_raw, gate_cols = third_pass(
        act, p, slope, dt, cum, sig, dcum, mlow, ent, leave2, egrad, rg, later, rows, conv, own, et, cols, g_out,
        g_gate,
    )
    tgrad, conv_cols, sums = last_pass(xt, pg, tail, ggrad, tok, cot, wg, wc, gain, small)
    in_grad, ngain_grad, ggain_grad, taps, bias, step, decay, skip, out_grad, tgrad = finish_pass(
        gate_cols, conv_cols, out_raw, sums, in_weight, out_weight, own, tgrad, c_rows
    )
    return (
        mixed[None], tgrad[None], ngain_grad, in_grad, taps.T, bias, step, decay, skip, ggain_grad, out_grad,
    )


def solution(mesh):
    both = ("dp", "seq")
    vec, mat, tok, rep = P(both), P(both, None), P("dp", "seq", None), P()
    return jax.shard_map(
        on_device,
        mesh=mesh,
        in_specs=(tok, tok, vec, mat, mat, vec, rep, rep, rep, vec, mat),
        out_specs=(tok, tok, vec, mat, mat, vec, rep, rep, rep, vec, mat),
        check_vma=False,
    )
```
